32 devices in a mesh: tile: 8 (over y, x, core), member: 4 (over z).
Axes of the slice: x: 2, y: 2, z: 4, core: 2. Of those that a mesh axis runs over, the one named last changes fastest.
Arguments:
- residual_in: float32 [64, 128, 512], P(None, 'tile', 'member'), may hold values from -6 to 6
- members: bfloat16 [8, 64, 128, 512], P('member', None, 'tile'), may hold values from -6 to 6
- wind_x: float32 [64], replicated, may hold values from 0.05 to 0.25
- wind_y: float32 [64], replicated, may hold values from 0.05 to 0.25
Outputs:
- analysis: float32 [64, 128, 512], P(None, 'tile', 'member')
- residual: float32 [64, 128, 512], P(None, 'tile', 'member')
The draws below stay inside these ranges and needn't reach their ends.
All inputs are finite; a program needn't handle non-finite values.
Results may differ from the reference program's by a relative error of at most 0.006.
Values may be sent and summed in bfloat16 or wider, within the bound.
No kernel may reach another device: no remote copies, remote signals or barrier semaphores. Data moves between devices by JAX's collectives and lax.ppermute only.
A program may use at most 64 MiB of HBM per device.

```python
import jax
import jax.numpy as jnp
from jax import lax

LEVELS = 64
ITERS = 2
MODEL_STEPS = 4
NX = 128
NY = 512
MEMBERS = 8


def strengthened(values, rng, source, target, shards_of, factor):
    owner, partner = [(jnp.arange(values.shape[dim]) // (values.shape[dim] // shards_of)).reshape([-1 if axis == dim else 1 for axis in range(values.ndim)]) for dim in (source, target)]
    chosen = jax.random.permutation(rng, shards_of)[partner]
    strong = (owner == chosen) | (owner == (partner + shards_of // 2) % shards_of)
    return jnp.where(strong, factor * values, values)


def block_scale(stream_key, shape, cuts, smallest, largest):
    level, own = 1.0, jax.random.fold_in(stream_key, 6)
    for dim, parts in cuts:
        steps = jnp.exp(jax.random.uniform(jax.random.fold_in(own, dim), (parts,), jnp.float32, smallest / len(cuts), largest / len(cuts)))
        level = level * jnp.repeat(steps, shape[dim] // parts).reshape([-1 if axis == dim else 1 for axis in range(len(shape))])
    return level


def bell_draw(rng, shape, width, most, split=(), kind=jnp.bfloat16):
    level = block_scale(rng, shape, split, -0.22, 0.18) if split else 1.0
    values = jax.random.normal(rng, shape, jnp.float32) * width * level
    return jnp.minimum(jnp.maximum(values, -most), most).astype(kind)


def noise_with(own_key, shape, spread, reach, shards, heavy, kind=jnp.bfloat16):
    values = spread * jax.random.normal(own_key, shape, jnp.float32)
    if shards:
        values = values * block_scale(own_key, shape, shards, -0.22, 0.18)
    return jnp.clip(strengthened(values, jax.random.fold_in(own_key, 3), *heavy), -reach, reach).astype(kind)


def setup_inputs(seed: int = 0) -> dict:
    splits = jax.random.split(jax.random.key(seed), 5)
    return {
        "residual_in": bell_draw(splits[0], (LEVELS, NX, NY), 1.0, 6.0, ((1, 8), (2, 4)), jnp.float32),
        "members": noise_with(splits[1], (MEMBERS, LEVELS, NX, NY), 1.0, 6.0, ((0, 4), (2, 8)), (0, 3, 4, 2.0)),
        "wind_x": jnp.clip(jax.random.uniform(splits[2], (LEVELS,), jnp.float32, 0.05, 0.25), 0.05, 0.25),
        "wind_y": jnp.clip(jax.random.uniform(splits[3], (LEVELS,), jnp.float32, 0.05, 0.25), 0.05, 0.25),
    }


diffusion = 0.1
relax = 0.5


def taper_weights():
    raw = [1.0 - (k / 17.0) ** 2 for k in range(-16, 17)]
    total = sum(raw)
    return [value / total for value in raw]


def adjoint_step(field, wind_x, wind_y):
    padded = jnp.pad(field, ((0, 0), (1, 1), (1, 1)))
    center = padded[:, 1:-1, 1:-1]
    ahead_x = padded[:, 2:, 1:-1]
    behind_x = padded[:, :-2, 1:-1]
    ahead_y = padded[:, 1:-1, 2:]
    behind_y = padded[:, 1:-1, :-2]
    result = center + diffusion * (ahead_x + behind_x + ahead_y + behind_y - 4.0 * center)
    result = result - wind_x[:, None, None] * (center - ahead_x)
    return result - wind_y[:, None, None] * (center - ahead_y)


def smooth_axis(padded, count, axis):
    weights = taper_weights()
    total = weights[0] * lax.slice_in_dim(padded, 0, count, axis=axis)
    for offset in range(1, len(weights)):
        total = total + weights[offset] * lax.slice_in_dim(padded, offset, offset + count, axis=axis)
    return total


def localize(field):
    rows = field.shape[0]
    columns = field.shape[1]
    smoothed = smooth_axis(jnp.pad(field, ((16, 16), (0, 0))), rows, 0)
    return smooth_axis(jnp.pad(smoothed, ((0, 0), (16, 16))), columns, 1)


def reference(residual_in, members, wind_x, wind_y):
    residual = residual_in
    analysis = jnp.zeros_like(residual_in)
    for iteration in range(ITERS):
        field = residual
        for sweep in range(MODEL_STEPS):
            field = adjoint_step(field, wind_x, wind_y)
        grad = field.astype(jnp.bfloat16).astype(jnp.float32)

        def accumulate(carry, member):
            member_f = member.astype(jnp.float32)
            project = jnp.sum(member_f * grad, axis=0)
            localized = localize(project)
            return carry + member_f * localized[None], None

        increment, unused = lax.scan(accumulate, jnp.zeros_like(residual_in), members)
        analysis = analysis + increment
        residual = residual - relax * increment
    return analysis, residual
```

```python
import functools

import jax
import jax.numpy as jnp
from jax import lax
from jax.experimental import pallas as pl
from jax.experimental.pallas import tpu as pltpu
from jax.sharding import PartitionSpec as P

ITERS = 2
MODEL_STEPS = 4
DIFFUSION = 0.1
RELAX = 0.5
REACH = 16
TAPER_TOTAL = sum(1.0 - (k / 17.0) ** 2 for k in range(-REACH, REACH + 1))
F32 = jnp.float32
BF16 = jnp.bfloat16
LANES = 128
SUB = 8

VMEM = pl.BlockSpec(memory_space=pltpu.VMEM)
SMEM = pl.BlockSpec(memory_space=pltpu.SMEM)
PARAMS = pltpu.CompilerParams(vmem_limit_bytes=48 * 1024 * 1024)


def call(body, out_shape, *args, in_specs=None, scratch=()):
    return pl.pallas_call(
        body,
        out_shape=out_shape,
        in_specs=in_specs or [VMEM] * len(args),
        out_specs=jax.tree.map(lambda _: VMEM, out_shape),
        scratch_shapes=scratch,
        compiler_params=PARAMS,
    )(*args)


def lane_iota(shape):
    return lax.broadcasted_iota(jnp.int32, shape, len(shape) - 1)


def sub_iota(shape):
    return lax.broadcasted_iota(jnp.int32, shape, len(shape) - 2)


def split_body(in_ref, out_ref):
    out_ref[0] = in_ref[...]


def split_columns(members, parts):
    own, levels, rows, ny = members.shape
    cols = ny // parts
    return pl.pallas_call(
        split_body,
        out_shape=jax.ShapeDtypeStruct((parts, own, levels, rows, cols), members.dtype),
        grid=(parts,),
        in_specs=[pl.BlockSpec((own, levels, rows, cols), lambda c: (0, 0, 0, c))],
        out_specs=pl.BlockSpec((1, own, levels, rows, cols), lambda c: (c, 0, 0, 0, 0)),
        compiler_params=PARAMS,
    )(members)


def edge_body(x_ref, first_ref, last_ref):
    levels, rows, cols = x_ref.shape
    group = LANES // MODEL_STEPS
    slot = lane_iota((rows, LANES)) // MODEL_STEPS
    for g in range(levels // group):
        first = jnp.zeros((rows, LANES), F32)
        last = jnp.zeros((rows, LANES), F32)
        for k in range(group):
            x = x_ref[g * group + k]
            here = slot == k
            first = jnp.where(here, pltpu.roll(x, (MODEL_STEPS * k) % LANES, 1), first)
            last = jnp.where(here, pltpu.roll(x, (MODEL_STEPS * (k + 1)) % LANES, 1), last)
        first_ref[g] = first
        last_ref[g] = last


def edge_columns(x):
    levels, rows, cols = x.shape
    out = jax.ShapeDtypeStruct((levels * MODEL_STEPS // LANES, rows, LANES), F32)
    return call(edge_body, (out, out), x)


def rows_body(x_ref, left_ref, right_ref, top_ref, bottom_ref):
    upper = sub_iota((SUB, LANES)) < MODEL_STEPS
    at = 0
    for ref in (x_ref, left_ref, right_ref):
        count, rows, _ = ref.shape
        for q in range(count // 2):
            top_ref[at] = jnp.where(upper, ref[2 * q, :SUB], pltpu.roll(ref[2 * q + 1, :SUB], MODEL_STEPS, 0))
            bottom_ref[at] = jnp.where(
                upper, pltpu.roll(ref[2 * q, rows - SUB :], MODEL_STEPS, 0), ref[2 * q + 1, rows - SUB :]
            )
            at += 1


def edge_rows(x, left, right):
    count = (x.shape[0] + left.shape[0] + right.shape[0]) // 2
    out = jax.ShapeDtypeStruct((count, SUB, LANES), F32)
    return call(rows_body, (out, out), x, left, right)


def shift(x, axis, step):
    count = lax.axis_size(axis)
    pairs = [(i, i + step) for i in range(count) if 0 <= i + step < count]
    return lax.ppermute(x, axis, pairs)


def halo_of(x):
    first, last = edge_columns(x)
    left = shift(last, "member", 1)
    right = shift(first, "member", -1)
    return left, right


def halo_rows_of(x, left, right):
    top, bottom = edge_rows(x, left, right)
    above = shift(bottom, "tile", 1)
    below = shift(top, "tile", -1)
    return above, below


def third_tile(below, above, odd):
    upper = sub_iota((SUB, LANES)) < MODEL_STEPS
    if odd:
        return jnp.where(upper, pltpu.roll(below, MODEL_STEPS, 0), above)
    return jnp.where(upper, below, pltpu.roll(above, MODEL_STEPS, 0))


def sweep_block(level_pair, x_ref, sides, above_ref, below_ref, wx_ref, wy_ref, mask, emit):
    lanes = lane_iota((x_ref.shape[1] + SUB, LANES))
    group = LANES // MODEL_STEPS
    rows = x_ref.shape[1]
    ext_rows = rows + SUB
    ext_cols = 2 * LANES
    above = above_ref[level_pair]
    below = below_ref[level_pair]
    for odd in range(2):
        level = 2 * level_pair + odd
        g = level // group
        k = level % group
        left = sides[0][g]
        right = sides[1][g]
        at = (LANES - MODEL_STEPS * k) % LANES
        side_right = pltpu.roll(right, at, 1)
        side_left = pltpu.roll(left, (at + LANES - MODEL_STEPS) % LANES, 1)
        side = jnp.where(lanes < MODEL_STEPS, side_right, side_left)
        center = jnp.concatenate([x_ref[level], third_tile(below, above, odd)], axis=0)
        field = jnp.concatenate([center, side], axis=1) * mask
        wx = wx_ref[level]
        wy = wy_ref[level]
        own = 1.0 - 4.0 * DIFFUSION - wx - wy
        ahead_x = DIFFUSION + wx
        ahead_y = DIFFUSION + wy
        for _ in range(MODEL_STEPS):
            field = (
                own * field
                + ahead_x * pltpu.roll(field, ext_rows - 1, 0)
                + ahead_y * pltpu.roll(field, ext_cols - 1, 1)
                + DIFFUSION * (pltpu.roll(field, 1, 0) + pltpu.roll(field, 1, 1))
            ) * mask
        emit(level, field[:rows, :LANES])


def block_mask(place_ref, rows, cols):
    tile, tiles, member, parts = (place_ref[i] for i in range(4))
    shape = (rows + SUB, 2 * LANES)
    r = sub_iota(shape)
    c = lane_iota(shape)
    r = jnp.where(r < rows + MODEL_STEPS, r, r - rows - SUB)
    near = (c < cols + MODEL_STEPS) | (c >= 2 * LANES - MODEL_STEPS)
    c = jnp.where(c < cols + MODEL_STEPS, c, c - 2 * LANES)
    gr = r + tile * rows
    gc = c + member * cols
    inside = (gr >= 0) & (gr < tiles * rows) & (gc >= 0) & (gc < parts * cols) & near
    return jnp.where(inside, 1.0, 0.0).astype(F32)


def make_sides(left_ref, right_ref, above_ref, below_ref, levels, sides_ref):
    groups, rows, _ = left_ref.shape
    for s, ref in enumerate((left_ref, right_ref)):
        for g in range(groups):
            at = (levels + s * groups + g) // 2
            sides_ref[s, g, :rows] = ref[g]
            sides_ref[s, g, rows:] = third_tile(below_ref[at], above_ref[at], g % 2)


def model_body(place_ref, wx_ref, wy_ref, x_ref, left_ref, right_ref, above_ref, below_ref, grad_ref, sides_ref):
    levels, rows, cols = x_ref.shape
    mask = block_mask(place_ref, rows, cols)
    make_sides(left_ref, right_ref, above_ref, below_ref, levels, sides_ref)
    sides = (sides_ref.at[0], sides_ref.at[1])

    def emit(level, value):
        grad_ref[level] = value

    def step(q, carry):
        for u in range(2):
            sweep_block(2 * q + u, x_ref, sides, above_ref, below_ref, wx_ref, wy_ref, mask, emit)
        return carry

    lax.fori_loop(0, levels // 4, step, 0)


def model(place, wind_x, wind_y, x, left, right, above, below):
    levels, rows, cols = x.shape
    groups = left.shape[0]
    return call(
        model_body,
        jax.ShapeDtypeStruct(x.shape, F32),
        place, wind_x, wind_y, x, left, right, above, below,
        in_specs=[SMEM] * 3 + [VMEM] * 5,
        scratch=[pltpu.VMEM((2, groups, rows + SUB, LANES), F32)],
    )


def project_body(members_ref, grad_ref, out_ref):
    parts, own, levels, rows, cols = members_ref.shape
    count = parts * own

    def step(q, carry):
        carry = list(carry)
        for u in range(2):
            level = 2 * q + u
            g = grad_ref[level]
            for m in range(count):
                carry[m] = carry[m] + members_ref[m // own, m % own, level].astype(F32) * g
        return tuple(carry)

    zero = jnp.zeros((rows, cols), F32)
    total = lax.fori_loop(0, levels // 2, step, (zero,) * count)
    for m in range(count):
        out_ref[m] = total[m].astype(out_ref.dtype)


def project(members, grad, dtype):
    parts, own, levels, rows, cols = members.shape
    return call(project_body, jax.ShapeDtypeStruct((parts * own, rows, cols), dtype), members, grad)


def taper(offset):
    k = offset.astype(F32)
    w = (1.0 - (k / 17.0) * (k / 17.0)) * (1.0 / TAPER_TOTAL)
    return jnp.where(jnp.abs(offset) <= REACH, w, 0.0)


def halves(x):
    high = x.astype(BF16)
    return high, (x - high.astype(F32)).astype(BF16)


def sharp_dot(a, b):
    ah, al = halves(a)
    bh, bl = halves(b)
    dot = functools.partial(jnp.dot, preferred_element_type=F32)
    return dot(ah, bh) + dot(al, bh) + dot(ah, bl)


def smooth_columns(wide, cols):
    shape = (3 * cols, cols)
    band = taper(sub_iota(shape) - lane_iota(shape) - cols)
    return sharp_dot(wide, band)


def smooth_rows(tall, rows):
    shape = (rows, 3 * rows)
    band = taper(lane_iota(shape) - sub_iota(shape) - rows)
    return sharp_dot(band, tall)


def columns_body(left_ref, mid_ref, right_ref, out_ref):
    count, rows, cols = mid_ref.shape
    wide = jnp.concatenate([r[...].reshape(count * rows, cols).astype(F32) for r in (left_ref, mid_ref, right_ref)], axis=1)
    out_ref[...] = smooth_columns(wide, cols).reshape(count, rows, cols)


def increments(members_ref, local_ref, emit):
    parts, own, levels, rows, cols = members_ref.shape
    local = [local_ref[m] for m in range(parts * own)]

    def step(q, carry):
        for u in range(2):
            level = 2 * q + u
            total = members_ref[0, 0, level].astype(F32) * local[0]
            for m in range(1, parts * own):
                total = total + members_ref[m // own, m % own, level].astype(F32) * local[m]
            emit(level, total)
        return carry

    lax.fori_loop(0, levels // 2, step, 0)


def update_body(members_ref, residual_ref, above_ref, mid_ref, below_ref, analysis_ref, out_ref, local_ref):
    count, rows, cols = mid_ref.shape
    for m in range(count):
        local_ref[m] = smooth_rows(jnp.concatenate([above_ref[m], mid_ref[m], below_ref[m]], axis=0), rows)

    def emit(level, value):
        analysis_ref[level] = value
        out_ref[level] = residual_ref[level] - RELAX * value

    increments(members_ref, local_ref, emit)


def final_body(place_ref, members_ref, residual_ref, before_ref, all_ref, analysis_ref, out_ref, local_ref, wide_ref):
    _, count, rows, cols = all_ref.shape
    tile, tiles, member, parts = (place_ref[i] for i in range(4))
    for i in range(3):
        for j in range(3):
            t = tile + i - 1
            c = member + j - 1
            ok = (t >= 0) & (t < tiles) & (c >= 0) & (c < parts)
            at = jnp.clip(t, 0, tiles - 1) * parts + jnp.clip(c, 0, parts - 1)
            block = all_ref[at].astype(F32) * jnp.where(ok, 1.0, 0.0)
            wide_ref[:, i * rows : (i + 1) * rows, j * cols : (j + 1) * cols] = block
    wide = wide_ref[...].reshape(count * 3 * rows, 3 * cols)
    tall = smooth_columns(wide, cols).reshape(count, 3 * rows, cols)
    for m in range(count):
        local_ref[m] = smooth_rows(tall[m], rows)

    def emit(level, value):
        analysis_ref[level] = before_ref[level] + value
        out_ref[level] = residual_ref[level] - RELAX * value

    increments(members_ref, local_ref, emit)


def per_device(residual_in, members, wind_x, wind_y):
    levels, rows, cols = residual_in.shape
    tiles = lax.axis_size("tile")
    parts = lax.axis_size("member")
    place = jnp.stack([lax.axis_index("tile"), jnp.int32(tiles), lax.axis_index("member"), jnp.int32(parts)])
    count = members.shape[0] * parts
    like = jax.ShapeDtypeStruct(residual_in.shape, F32)
    small = jax.ShapeDtypeStruct((count, rows, cols), F32)

    left, right = halo_of(residual_in)
    outgoing = split_columns(members, parts)
    block = lax.all_to_all(outgoing, "member", split_axis=0, concat_axis=0, tiled=True)
    above, below = halo_rows_of(residual_in, left, right)
    grad = model(place, wind_x, wind_y, residual_in, left, right, above, below)

    mid = project(block, grad, F32)
    smooth = call(columns_body, small, shift(mid, "member", 1), mid, shift(mid, "member", -1))
    analysis, residual = call(
        update_body, (like, like),
        block, residual_in, shift(smooth, "tile", 1), smooth, shift(smooth, "tile", -1),
        scratch=[pltpu.VMEM((count, rows, cols), F32)],
    )

    left, right = halo_of(residual)
    above, below = halo_rows_of(residual, left, right)
    grad = model(place, wind_x, wind_y, residual, left, right, above, below)
    mid = project(block, grad, BF16)
    everywhere = lax.all_gather(mid, ("tile", "member"), axis=0, tiled=False)
    return call(
        final_body, (like, like),
        place, block, residual, analysis, everywhere,
        in_specs=[SMEM] + [VMEM] * 4,
        scratch=[pltpu.VMEM((count, rows, cols), F32), pltpu.VMEM((count, 3 * rows, 3 * cols), F32)],
    )


def solution(mesh):
    return jax.shard_map(
        per_device,
        mesh=mesh,
        in_specs=(P(None, "tile", "member"), P("member", None, "tile", None), P(), P()),
        out_specs=(P(None, "tile", "member"), P(None, "tile", "member")),
        check_vma=False,
    )
```

```python
import functools

import jax
import jax.numpy as jnp
from jax import lax
from jax.experimental import pallas as pl
from jax.experimental.pallas import tpu as pltpu
from jax.sharding import PartitionSpec as P

ITERS = 2
MODEL_STEPS = 4
DIFFUSION = 0.1
RELAX = 0.5
REACH = 16
TAPER_TOTAL = sum(1.0 - (k / 17.0) ** 2 for k in range(-REACH, REACH + 1))
F32 = jnp.float32
BF16 = jnp.bfloat16
LANES = 128
SUB = 8

VMEM = pl.BlockSpec(memory_space=pltpu.VMEM)
SMEM = pl.BlockSpec(memory_space=pltpu.SMEM)
PARAMS = pltpu.CompilerParams(vmem_limit_bytes=48 * 1024 * 1024)


def call(body, out_shape, *args, in_specs=None, scratch=()):
    return pl.pallas_call(
        body,
        out_shape=out_shape,
        in_specs=in_specs or [VMEM] * len(args),
        out_specs=jax.tree.map(lambda _: VMEM, out_shape),
        scratch_shapes=scratch,
        compiler_params=PARAMS,
    )(*args)


def lane_iota(shape):
    return lax.broadcasted_iota(jnp.int32, shape, len(shape) - 1)


def sub_iota(shape):
    return lax.broadcasted_iota(jnp.int32, shape, len(shape) - 2)


def split_body(in_ref, out_ref, sems):
    parts = out_ref.shape[0]
    cols = out_ref.shape[-1]
    copies = [
        pltpu.make_async_copy(in_ref.at[:, :, :, pl.ds(c * cols, cols)], out_ref.at[c], sems.at[c]) for c in range(parts)
    ]
    for copy in copies:
        copy.start()
    for copy in copies:
        copy.wait()


def split_columns(members, parts):
    own, levels, rows, ny = members.shape
    cols = ny // parts
    return pl.pallas_call(
        split_body,
        out_shape=jax.ShapeDtypeStruct((parts, own, levels, rows, cols), members.dtype),
        in_specs=[pl.BlockSpec(memory_space=pltpu.HBM)],
        out_specs=pl.BlockSpec(memory_space=pltpu.HBM),
        scratch_shapes=[pltpu.SemaphoreType.DMA((parts,))],
        compiler_params=PARAMS,
    )(members)


def edge_body(x_ref, first_ref, last_ref):
    levels, rows, cols = x_ref.shape
    group = LANES // MODEL_STEPS
    slot = lane_iota((rows, LANES)) // MODEL_STEPS
    for g in range(levels // group):
        first = jnp.zeros((rows, LANES), F32)
        last = jnp.zeros((rows, LANES), F32)
        for k in range(group):
            x = x_ref[g * group + k]
            here = slot == k
            first = jnp.where(here, pltpu.roll(x, (MODEL_STEPS * k) % LANES, 1), first)
            last = jnp.where(here, pltpu.roll(x, (MODEL_STEPS * (k + 1)) % LANES, 1), last)
        first_ref[g] = first
        last_ref[g] = last


def edge_columns(x):
    levels, rows, cols = x.shape
    out = jax.ShapeDtypeStruct((levels * MODEL_STEPS // LANES, rows, LANES), F32)
    return call(edge_body, (out, out), x)


def rows_body(x_ref, left_ref, right_ref, top_ref, bottom_ref):
    upper = sub_iota((SUB, LANES)) < MODEL_STEPS
    at = 0
    for ref in (x_ref, left_ref, right_ref):
        count, rows, _ = ref.shape
        for q in range(count // 2):
            top_ref[at] = jnp.where(upper, ref[2 * q, :SUB], pltpu.roll(ref[2 * q + 1, :SUB], MODEL_STEPS, 0))
            bottom_ref[at] = jnp.where(
                upper, pltpu.roll(ref[2 * q, rows - SUB :], MODEL_STEPS, 0), ref[2 * q + 1, rows - SUB :]
            )
            at += 1


def edge_rows(x, left, right):
    count = (x.shape[0] + left.shape[0] + right.shape[0]) // 2
    out = jax.ShapeDtypeStruct((count, SUB, LANES), F32)
    return call(rows_body, (out, out), x, left, right)


def shift(x, axis, step):
    count = lax.axis_size(axis)
    pairs = [(i, i + step) for i in range(count) if 0 <= i + step < count]
    return lax.ppermute(x, axis, pairs)


def halo_of(x):
    first, last = edge_columns(x)
    left = shift(last, "member", 1)
    right = shift(first, "member", -1)
    return left, right


def halo_rows_of(x, left, right):
    top, bottom = edge_rows(x, left, right)
    above = shift(bottom, "tile", 1)
    below = shift(top, "tile", -1)
    return above, below


def third_tile(below, above, odd):
    upper = sub_iota((SUB, LANES)) < MODEL_STEPS
    if odd:
        return jnp.where(upper, pltpu.roll(below, MODEL_STEPS, 0), above)
    return jnp.where(upper, below, pltpu.roll(above, MODEL_STEPS, 0))


def sweep_block(level_pair, x_ref, sides, above_ref, below_ref, wx_ref, wy_ref, mask, emit):
    lanes = lane_iota((x_ref.shape[1] + SUB, LANES))
    group = LANES // MODEL_STEPS
    rows = x_ref.shape[1]
    ext_rows = rows + SUB
    ext_cols = 2 * LANES
    above = above_ref[level_pair]
    below = below_ref[level_pair]
    for odd in range(2):
        level = 2 * level_pair + odd
        g = level // group
        k = level % group
        left = sides[0][g]
        right = sides[1][g]
        at = (LANES - MODEL_STEPS * k) % LANES
        side_right = pltpu.roll(right, at, 1)
        side_left = pltpu.roll(left, (at + LANES - MODEL_STEPS) % LANES, 1)
        side = jnp.where(lanes < MODEL_STEPS, side_right, side_left)
        center = jnp.concatenate([x_ref[level], third_tile(below, above, odd)], axis=0)
        field = jnp.concatenate([center, side], axis=1) * mask
        wx = wx_ref[level]
        wy = wy_ref[level]
        own = 1.0 - 4.0 * DIFFUSION - wx - wy
        ahead_x = DIFFUSION + wx
        ahead_y = DIFFUSION + wy
        for _ in range(MODEL_STEPS):
            field = (
                own * field
                + ahead_x * pltpu.roll(field, ext_rows - 1, 0)
                + ahead_y * pltpu.roll(field, ext_cols - 1, 1)
                + DIFFUSION * (pltpu.roll(field, 1, 0) + pltpu.roll(field, 1, 1))
            ) * mask
        emit(level, field[:rows, :LANES])


def block_mask(place_ref, rows, cols):
    tile, tiles, member, parts = (place_ref[i] for i in range(4))
    shape = (rows + SUB, 2 * LANES)
    r = sub_iota(shape)
    c = lane_iota(shape)
    r = jnp.where(r < rows + MODEL_STEPS, r, r - rows - SUB)
    near = (c < cols + MODEL_STEPS) | (c >= 2 * LANES - MODEL_STEPS)
    c = jnp.where(c < cols + MODEL_STEPS, c, c - 2 * LANES)
    gr = r + tile * rows
    gc = c + member * cols
    inside = (gr >= 0) & (gr < tiles * rows) & (gc >= 0) & (gc < parts * cols) & near
    return jnp.where(inside, 1.0, 0.0).astype(F32)


def make_sides(left_ref, right_ref, above_ref, below_ref, levels, sides_ref):
    groups, rows, _ = left_ref.shape
    for s, ref in enumerate((left_ref, right_ref)):
        for g in range(groups):
            at = (levels + s * groups + g) // 2
            sides_ref[s, g, :rows] = ref[g]
            sides_ref[s, g, rows:] = third_tile(below_ref[at], above_ref[at], g % 2)


def model_body(place_ref, wx_ref, wy_ref, x_ref, left_ref, right_ref, above_ref, below_ref, grad_ref, sides_ref):
    levels, rows, cols = x_ref.shape
    mask = block_mask(place_ref, rows, cols)
    make_sides(left_ref, right_ref, above_ref, below_ref, levels, sides_ref)
    sides = (sides_ref.at[0], sides_ref.at[1])

    def emit(level, value):
        grad_ref[level] = value

    def step(q, carry):
        for u in range(2):
            sweep_block(2 * q + u, x_ref, sides, above_ref, below_ref, wx_ref, wy_ref, mask, emit)
        return carry

    lax.fori_loop(0, levels // 4, step, 0)


def model(place, wind_x, wind_y, x, left, right, above, below):
    levels, rows, cols = x.shape
    groups = left.shape[0]
    return call(
        model_body,
        jax.ShapeDtypeStruct(x.shape, F32),
        place, wind_x, wind_y, x, left, right, above, below,
        in_specs=[SMEM] * 3 + [VMEM] * 5,
        scratch=[pltpu.VMEM((2, groups, rows + SUB, LANES), F32)],
    )


def project_body(members_ref, grad_ref, out_ref):
    parts, own, levels, rows, cols = members_ref.shape
    count = parts * own

    def step(q, carry):
        carry = list(carry)
        for u in range(2):
            level = 2 * q + u
            g = grad_ref[level]
            for m in range(count):
                carry[m] = carry[m] + members_ref[m // own, m % own, level].astype(F32) * g
        return tuple(carry)

    zero = jnp.zeros((rows, cols), F32)
    total = lax.fori_loop(0, levels // 2, step, (zero,) * count)
    for m in range(count):
        out_ref[m] = total[m].astype(out_ref.dtype)


def project(members, grad, dtype):
    parts, own, levels, rows, cols = members.shape
    return call(project_body, jax.ShapeDtypeStruct((parts * own, rows, cols), dtype), members, grad)


def taper(offset):
    k = offset.astype(F32)
    w = (1.0 - (k / 17.0) * (k / 17.0)) * (1.0 / TAPER_TOTAL)
    return jnp.where(jnp.abs(offset) <= REACH, w, 0.0)


def halves(x):
    high = x.astype(BF16)
    return high, (x - high.astype(F32)).astype(BF16)


def sharp_dot(a, b):
    ah, al = halves(a)
    bh, bl = halves(b)
    dot = functools.partial(jnp.dot, preferred_element_type=F32)
    return dot(ah, bh) + dot(al, bh) + dot(ah, bl)


def smooth_columns(wide, cols):
    shape = (3 * cols, cols)
    band = taper(sub_iota(shape) - lane_iota(shape) - cols)
    return sharp_dot(wide, band)


def smooth_rows(tall, rows):
    shape = (rows, 3 * rows)
    band = taper(lane_iota(shape) - sub_iota(shape) - rows)
    return sharp_dot(band, tall)


def columns_body(left_ref, mid_ref, right_ref, out_ref):
    count, rows, cols = mid_ref.shape
    wide = jnp.concatenate([r[...].reshape(count * rows, cols).astype(F32) for r in (left_ref, mid_ref, right_ref)], axis=1)
    out_ref[...] = smooth_columns(wide, cols).reshape(count, rows, cols)


def increments(members_ref, local_ref, emit):
    parts, own, levels, rows, cols = members_ref.shape
    local = [local_ref[m] for m in range(parts * own)]

    def step(q, carry):
        for u in range(2):
            level = 2 * q + u
            total = members_ref[0, 0, level].astype(F32) * local[0]
            for m in range(1, parts * own):
                total = total + members_ref[m // own, m % own, level].astype(F32) * local[m]
            emit(level, total)
        return carry

    lax.fori_loop(0, levels // 2, step, 0)


def update_body(members_ref, residual_ref, above_ref, mid_ref, below_ref, analysis_ref, out_ref, local_ref):
    count, rows, cols = mid_ref.shape
    for m in range(count):
        local_ref[m] = smooth_rows(jnp.concatenate([above_ref[m], mid_ref[m], below_ref[m]], axis=0), rows)

    def emit(level, value):
        analysis_ref[level] = value
        out_ref[level] = residual_ref[level] - RELAX * value

    increments(members_ref, local_ref, emit)


def final_body(members_ref, residual_ref, before_ref, above_ref, mid_ref, below_ref, analysis_ref, out_ref, local_ref):
    count, rows, cols = mid_ref.shape
    for m in range(count):
        local_ref[m] = smooth_rows(jnp.concatenate([above_ref[m], mid_ref[m], below_ref[m]], axis=0), rows)

    def emit(level, value):
        analysis_ref[level] = before_ref[level] + value
        out_ref[level] = residual_ref[level] - RELAX * value

    increments(members_ref, local_ref, emit)


def per_device(residual_in, members, wind_x, wind_y):
    levels, rows, cols = residual_in.shape
    tiles = lax.axis_size("tile")
    parts = lax.axis_size("member")
    place = jnp.stack([lax.axis_index("tile"), jnp.int32(tiles), lax.axis_index("member"), jnp.int32(parts)])
    count = members.shape[0] * parts
    like = jax.ShapeDtypeStruct(residual_in.shape, F32)
    small = jax.ShapeDtypeStruct((count, rows, cols), F32)

    left, right = halo_of(residual_in)
    outgoing = split_columns(members, parts)
    outgoing, left, right = lax.optimization_barrier((outgoing, left, right))
    block = lax.all_to_all(outgoing, "member", split_axis=0, concat_axis=0, tiled=True)
    above, below = halo_rows_of(residual_in, left, right)
    grad = model(place, wind_x, wind_y, residual_in, left, right, above, below)

    def smoothed(grad):
        mid = project(block, grad, F32)
        smooth = call(columns_body, small, shift(mid, "member", 1), mid, shift(mid, "member", -1))
        return shift(smooth, "tile", 1), smooth, shift(smooth, "tile", -1)

    local = [pltpu.VMEM((count, rows, cols), F32)]
    analysis, residual = call(update_body, (like, like), block, residual_in, *smoothed(grad), scratch=local)

    left, right = halo_of(residual)
    above, below = halo_rows_of(residual, left, right)
    grad = model(place, wind_x, wind_y, residual, left, right, above, below)
    return call(final_body, (like, like), block, residual, analysis, *smoothed(grad), scratch=local)


def solution(mesh):
    return jax.shard_map(
        per_device,
        mesh=mesh,
        in_specs=(P(None, "tile", "member"), P("member", None, "tile", None), P(), P()),
        out_specs=(P(None, "tile", "member"), P(None, "tile", "member")),
        check_vma=False,
    )
```

```python
import functools

import jax
import jax.numpy as jnp
from jax import lax
from jax.experimental import pallas as pl
from jax.experimental.pallas import tpu as pltpu
from jax.sharding import PartitionSpec as P

ITERS = 2
MODEL_STEPS = 4
DIFFUSION = 0.1
RELAX = 0.5
REACH = 16
TAPER_TOTAL = sum(1.0 - (k / 17.0) ** 2 for k in range(-REACH, REACH + 1))
F32 = jnp.float32
BF16 = jnp.bfloat16
LANES = 128
SUB = 8
GROUP = LANES // (2 * MODEL_STEPS)

VMEM = pl.BlockSpec(memory_space=pltpu.VMEM)
SMEM = pl.BlockSpec(memory_space=pltpu.SMEM)
PARAMS = pltpu.CompilerParams(vmem_limit_bytes=48 * 1024 * 1024)
BIG = pltpu.CompilerParams(vmem_limit_bytes=60 * 1024 * 1024)


def call(body, out_shape, *args, in_specs=None, scratch=()):
    return pl.pallas_call(
        body,
        out_shape=out_shape,
        in_specs=in_specs or [VMEM] * len(args),
        out_specs=jax.tree.map(lambda _: VMEM, out_shape),
        scratch_shapes=scratch,
        compiler_params=PARAMS,
    )(*args)


def lane_iota(shape):
    return lax.broadcasted_iota(jnp.int32, shape, len(shape) - 1)


def sub_iota(shape):
    return lax.broadcasted_iota(jnp.int32, shape, len(shape) - 2)


def split_body(start, in_ref, out_ref, sems):
    parts, own, levels, rows, cols = out_ref.shape
    copies = [
        pltpu.make_async_copy(
            in_ref.at[:, pl.ds(start, levels), :, pl.ds(c * cols, cols)], out_ref.at[c], sems.at[c]
        )
        for c in range(parts)
    ]
    for copy in copies:
        copy.start()
    for copy in copies:
        copy.wait()


def split_columns(members, parts, count):
    own, levels, rows, ny = members.shape
    return pl.pallas_call(
        functools.partial(split_body, 0),
        out_shape=jax.ShapeDtypeStruct((parts, own, count, rows, ny // parts), members.dtype),
        in_specs=[pl.BlockSpec(memory_space=pl.ANY)],
        out_specs=pl.BlockSpec(memory_space=pl.ANY),
        scratch_shapes=[pltpu.SemaphoreType.DMA((parts,))],
        compiler_params=BIG,
    )(members)


def sided_body(start, left_ref, mid_ref, right_ref, out_ref):
    own, levels, rows, cols = mid_ref.shape
    rest = levels - start
    slot = lane_iota((rows, LANES)) // MODEL_STEPS
    out_ref[0, :, :rest] = mid_ref[:, start:]
    for m in range(own):

        def step(g, carry):
            total = jnp.zeros((rows, LANES), F32)
            for k in range(GROUP):
                left = left_ref[m, g * GROUP + k].astype(F32)
                right = right_ref[m, g * GROUP + k].astype(F32)
                total = jnp.where(slot == k, pltpu.roll(left, MODEL_STEPS * (k + 1), 1), total)
                total = jnp.where(slot == GROUP + k, pltpu.roll(right, MODEL_STEPS * (GROUP + k), 1), total)
            out_ref[0, m, rest + g] = total.astype(out_ref.dtype)
            return carry

        lax.fori_loop(0, levels // GROUP, step, 0)


def split_with_sides(members, parts, start):
    own, levels, rows, ny = members.shape
    cols = ny // parts
    block = (own, levels, rows, cols)
    planes = levels - start + levels // GROUP
    return pl.pallas_call(
        functools.partial(sided_body, start),
        out_shape=jax.ShapeDtypeStruct((parts, own, planes, rows, cols), members.dtype),
        grid=(parts,),
        in_specs=[
            pl.BlockSpec(block, lambda c: (0, 0, 0, (c + parts - 1) % parts)),
            pl.BlockSpec(block, lambda c: (0, 0, 0, c)),
            pl.BlockSpec(block, lambda c: (0, 0, 0, (c + 1) % parts)),
        ],
        out_specs=pl.BlockSpec((1, own, planes, rows, cols), lambda c: (c, 0, 0, 0, 0)),
        compiler_params=PARAMS,
    )(members, members, members)


def third_tile(below, above, odd):
    upper = sub_iota((SUB, LANES)) < MODEL_STEPS
    if odd:
        return jnp.where(upper, pltpu.roll(below, MODEL_STEPS, 0), above)
    return jnp.where(upper, below, pltpu.roll(above, MODEL_STEPS, 0))


def pack_rows(ref, at, top_ref, bottom_ref):
    upper = sub_iota((SUB, LANES)) < MODEL_STEPS
    count, rows, _ = ref.shape
    for q in range(count // 2):
        top_ref[at + q] = jnp.where(upper, ref[2 * q, :SUB], pltpu.roll(ref[2 * q + 1, :SUB], MODEL_STEPS, 0))
        bottom_ref[at + q] = jnp.where(
            upper, pltpu.roll(ref[2 * q, rows - SUB :], MODEL_STEPS, 0), ref[2 * q + 1, rows - SUB :]
        )


def rows_body(x_ref, top_ref, bottom_ref):
    pack_rows(x_ref, 0, top_ref, bottom_ref)


def edge_rows(x):
    out = jax.ShapeDtypeStruct((x.shape[0] // 2, SUB, LANES), F32)
    return call(rows_body, (out, out), x)


def columns_edge_body(x_ref, above_ref, below_ref, first_ref, last_ref):
    levels, rows, cols = x_ref.shape
    slot = lane_iota((rows + SUB, LANES)) // MODEL_STEPS

    def step(g, carry):
        first = jnp.zeros((rows + SUB, LANES), F32)
        last = jnp.zeros((rows + SUB, LANES), F32)
        for k in range(GROUP):
            level = g * GROUP + k
            pair = g * (GROUP // 2) + k // 2
            x = jnp.concatenate([x_ref[level], third_tile(below_ref[pair], above_ref[pair], k % 2)], axis=0)
            last = jnp.where(slot == k, pltpu.roll(x, MODEL_STEPS * (k + 1), 1), last)
            first = jnp.where(slot == GROUP + k, pltpu.roll(x, MODEL_STEPS * (GROUP + k), 1), first)
        first_ref[g] = first
        last_ref[g] = last
        return carry

    lax.fori_loop(0, levels // GROUP, step, 0)


def edge_columns(x, above, below):
    levels, rows, cols = x.shape
    out = jax.ShapeDtypeStruct((levels // GROUP, rows + SUB, LANES), F32)
    return call(columns_edge_body, (out, out), x, above, below)


def shift(x, axis, step):
    count = lax.axis_size(axis)
    pairs = [(i, i + step) for i in range(count) if 0 <= i + step < count]
    return lax.ppermute(x, axis, pairs)


def sweep_block(level_pair, x_ref, sides_ref, above_ref, below_ref, wx_ref, wy_ref, mask):
    rows = x_ref.shape[1]
    lanes = lane_iota((rows + SUB, LANES))
    ext_rows = rows + SUB
    ext_cols = 2 * LANES
    above = above_ref[level_pair]
    below = below_ref[level_pair]
    results = []
    for odd in range(2):
        level = 2 * level_pair + odd
        k = level % GROUP
        packed = sides_ref[level // GROUP]
        side_right = pltpu.roll(packed, (LANES + LANES // 2 - MODEL_STEPS * k) % LANES, 1)
        side_left = pltpu.roll(packed, LANES - MODEL_STEPS * (k + 1), 1)
        side = jnp.where(lanes < MODEL_STEPS, side_right, side_left)
        center = jnp.concatenate([x_ref[level], third_tile(below, above, odd)], axis=0)
        field = jnp.concatenate([center, side], axis=1) * mask
        wx = wx_ref[level]
        wy = wy_ref[level]
        own = 1.0 - 4.0 * DIFFUSION - wx - wy
        ahead_x = DIFFUSION + wx
        ahead_y = DIFFUSION + wy
        for _ in range(MODEL_STEPS):
            field = (
                own * field
                + ahead_x * pltpu.roll(field, ext_rows - 1, 0)
                + ahead_y * pltpu.roll(field, ext_cols - 1, 1)
                + DIFFUSION * (pltpu.roll(field, 1, 0) + pltpu.roll(field, 1, 1))
            ) * mask
        results.append(field[:rows, :LANES])
    return results


def block_mask(place_ref, rows, cols):
    tile, tiles, member, parts = (place_ref[i] for i in range(4))
    shape = (rows + SUB, 2 * LANES)
    r = sub_iota(shape)
    c = lane_iota(shape)
    r = jnp.where(r < rows + MODEL_STEPS, r, r - rows - SUB)
    near = (c < cols + MODEL_STEPS) | (c >= 2 * LANES - MODEL_STEPS)
    c = jnp.where(c < cols + MODEL_STEPS, c, c - 2 * LANES)
    gr = r + tile * rows
    gc = c + member * cols
    inside = (gr >= 0) & (gr < tiles * rows) & (gc >= 0) & (gc < parts * cols) & near
    return jnp.where(inside, 1.0, 0.0).astype(F32)


def first_model_body(place_ref, wx_ref, wy_ref, x_ref, left_ref, right_ref, above_ref, below_ref, grad_ref, sides_ref):
    levels, rows, cols = x_ref.shape
    mask = block_mask(place_ref, rows, cols)
    sides_ref[...] = left_ref[...] + right_ref[...]

    def step(q, carry):
        for u in range(2):
            pair = 2 * q + u
            for odd, value in enumerate(
                sweep_block(pair, x_ref, sides_ref, above_ref, below_ref, wx_ref, wy_ref, mask)
            ):
                grad_ref[2 * pair + odd] = value
        return carry

    lax.fori_loop(0, levels // 4, step, 0)


def second_model_body(
    place_ref, wx_ref, wy_ref, one_ref, two_ref, x_ref, beside_ref, above_ref, below_ref, wide_ref, thin_ref, grad_ref, sides_ref
):
    levels, rows, cols = x_ref.shape
    groups = beside_ref.shape[0]
    mask = block_mask(place_ref, rows, cols)
    for g in range(groups):
        at = (levels + g) // 2
        sides_ref[g, :rows] = beside_ref[g]
        sides_ref[g, rows:] = third_tile(below_ref[at], above_ref[at], g % 2)

    def step(q, carry):
        for u in range(2):
            pair = 2 * q + u
            for odd, value in enumerate(
                sweep_block(pair, x_ref, sides_ref, above_ref, below_ref, wx_ref, wy_ref, mask)
            ):
                grad_ref[2 * pair + odd] = value
        return carry

    lax.fori_loop(0, levels // 4, step, 0)
    project_body(one_ref, two_ref, grad_ref, wide_ref, thin_ref)


def project_body(one_ref, two_ref, grad_ref, wide_ref, thin_ref):
    parts, own, early, rows, cols = one_ref.shape
    levels = grad_ref.shape[0]
    count = parts * own
    total = (jnp.zeros((rows, cols), F32),) * count
    for ref, start, stop in ((one_ref, 0, early), (two_ref, early, levels)):

        def step(q, carry):
            carry = list(carry)
            for u in range(2):
                level = 2 * q + u
                g = grad_ref[start + level]
                for m in range(count):
                    carry[m] = carry[m] + ref[m // own, m % own, level].astype(F32) * g
            return tuple(carry)

        total = lax.fori_loop(0, (stop - start) // 2, step, total)
    for m in range(count):
        wide_ref[m] = total[m]
        thin_ref[m] = total[m].astype(BF16)


def taper(offset):
    k = offset.astype(F32)
    w = (1.0 - (k / 17.0) * (k / 17.0)) * (1.0 / TAPER_TOTAL)
    return jnp.where(jnp.abs(offset) <= REACH, w, 0.0)


def halves(x):
    high = x.astype(BF16)
    return high, (x - high.astype(F32)).astype(BF16)


def sharp_dot(a, b):
    ah, al = halves(a)
    bh, bl = halves(b)
    dot = functools.partial(jnp.dot, preferred_element_type=F32)
    return dot(ah, bh) + dot(al, bh) + dot(ah, bl)


def columns_body(left_ref, mid_ref, right_ref, wide_ref, thin_ref):
    count, rows, cols = mid_ref.shape
    wide = jnp.concatenate(
        [r[...].astype(F32).reshape(count * rows, cols) for r in (left_ref, mid_ref, right_ref)], axis=1
    )
    shape = (3 * cols, wide_ref.shape[0] // count * cols)
    lane = lane_iota(shape)
    beside = lane % MODEL_STEPS + jnp.where(lane < cols + LANES // 2, -MODEL_STEPS, cols)
    target = jnp.where(lane < cols, lane, beside)
    out = sharp_dot(wide, taper(sub_iota(shape) - cols - target))
    for i in range(shape[1] // cols):
        part = out[:, i * cols : (i + 1) * cols].reshape(count, rows, cols)
        wide_ref[i * count : (i + 1) * count] = part
        thin_ref[i * count : (i + 1) * count] = part.astype(BF16)


def smooth_rows(above_ref, mid_ref, below_ref):
    count, rows, cols = mid_ref.shape
    tall = jnp.concatenate(
        [
            jnp.concatenate([above_ref[m].astype(F32), mid_ref[m], below_ref[m].astype(F32)], axis=0)
            for m in range(count)
        ],
        axis=1,
    )
    shape = (rows, 3 * rows)
    out = sharp_dot(taper(lane_iota(shape) - sub_iota(shape) - rows), tall)
    return [out[:, m * cols : (m + 1) * cols] for m in range(count)]


def increments(one_ref, two_ref, levels, local, emit):
    parts, own, early, rows, cols = one_ref.shape

    def at(ref, level):
        total = ref[0, 0, level].astype(F32) * local[0]
        for m in range(1, parts * own):
            total = total + ref[m // own, m % own, level].astype(F32) * local[m]
        return total

    for ref, start, stop in ((one_ref, 0, early), (two_ref, early, levels)):

        def step(q, carry):
            for u in range(2):
                emit(start + 2 * q + u, at(ref, 2 * q + u))
            return carry

        lax.fori_loop(0, (stop - start) // 2, step, 0)


def update_body(
    one_ref, two_ref, residual_ref, left_ref, right_ref, above_ref, mid_ref, below_ref,
    analysis_ref, out_ref, beside_ref, top_ref, bottom_ref,
):
    levels, rows, cols = residual_ref.shape
    parts, own, early = one_ref.shape[:3]
    count = parts * own
    local = smooth_rows(above_ref, mid_ref, below_ref)

    def emit(level, value):
        analysis_ref[level] = value
        out_ref[level] = residual_ref[level] - RELAX * value

    increments(one_ref, two_ref, levels, local[:count], emit)
    for g in range(levels // GROUP):
        total = jnp.zeros((rows, LANES), F32)
        for m in range(count):
            total = total + two_ref[m // own, m % own, levels - early + g].astype(F32) * local[count + m]
        beside_ref[g] = left_ref[g, :rows] + right_ref[g, :rows] - RELAX * total
    pack_rows(out_ref, 0, top_ref, bottom_ref)
    pack_rows(beside_ref, levels // 2, top_ref, bottom_ref)


def final_body(one_ref, two_ref, residual_ref, before_ref, above_ref, mid_ref, below_ref, analysis_ref, out_ref):
    local = smooth_rows(above_ref, mid_ref, below_ref)

    def emit(level, value):
        analysis_ref[level] = before_ref[level] + value
        out_ref[level] = residual_ref[level] - RELAX * value

    increments(one_ref, two_ref, residual_ref.shape[0], local, emit)


def per_device(residual_in, members, wind_x, wind_y):
    levels, rows, cols = residual_in.shape
    tiles = lax.axis_size("tile")
    parts = lax.axis_size("member")
    place = jnp.stack([lax.axis_index("tile"), jnp.int32(tiles), lax.axis_index("member"), jnp.int32(parts)])
    count = members.shape[0] * parts
    groups = levels // GROUP
    early = levels * 5 // 8

    def shape(*dims, kind=F32):
        return jax.ShapeDtypeStruct(dims, kind)

    def both(*dims):
        return shape(*dims), shape(*dims, kind=BF16)

    def exchange(x):
        return lax.all_to_all(x, "member", split_axis=0, concat_axis=0, tiled=True)

    def smoothed(wide, thin, planes):
        wide, thin = call(
            columns_body, both(planes, rows, cols), shift(thin, "member", 1), wide, shift(thin, "member", -1)
        )
        return shift(thin, "tile", 1), wide, shift(thin, "tile", -1)

    like = shape(levels, rows, cols)
    sides = [pltpu.VMEM((groups, rows + SUB, LANES), F32)]

    soon, residual_in = lax.optimization_barrier((split_columns(members, parts, early), residual_in))
    one = exchange(soon)
    top, bottom = edge_rows(residual_in)
    above, below = shift(bottom, "tile", 1), shift(top, "tile", -1)
    first, last = edge_columns(residual_in, above, below)
    rest, first, last = lax.optimization_barrier((split_with_sides(members, parts, early), first, last))
    left, right = shift(last, "member", 1), shift(first, "member", -1)
    two = exchange(rest)
    grad = call(
        first_model_body, like,
        place, wind_x, wind_y, residual_in, left, right, above, below,
        in_specs=[SMEM] * 3 + [VMEM] * 5, scratch=sides,
    )
    wide, thin = call(project_body, both(count, rows, cols), one, two, grad)

    halo = shape((levels + groups) // 2, SUB, LANES)
    analysis, residual, beside, top, bottom = call(
        update_body, (like, like, shape(groups, rows, LANES), halo, halo),
        one, two, residual_in, left, right, *smoothed(wide, thin, 2 * count),
    )
    above, below = shift(bottom, "tile", 1), shift(top, "tile", -1)
    wide, thin = call(
        second_model_body, both(count, rows, cols),
        place, wind_x, wind_y, one, two, residual, beside, above, below,
        in_specs=[SMEM] * 3 + [VMEM] * 6, scratch=[pltpu.VMEM((levels, rows, cols), F32)] + sides,
    )
    return call(final_body, (like, like), one, two, residual, analysis, *smoothed(wide, thin, count))


def solution(mesh):
    return jax.shard_map(
        per_device,
        mesh=mesh,
        in_specs=(P(None, "tile", "member"), P("member", None, "tile", None), P(), P()),
        out_specs=(P(None, "tile", "member"), P(None, "tile", "member")),
        check_vma=False,
    )
```

```python
import functools

import jax
import jax.numpy as jnp
from jax import lax
from jax.experimental import pallas as pl
from jax.experimental.pallas import tpu as pltpu
from jax.sharding import PartitionSpec as P

ITERS = 2
MODEL_STEPS = 4
DIFFUSION = 0.1
RELAX = 0.5
REACH = 16
TAPER_TOTAL = sum(1.0 - (k / 17.0) ** 2 for k in range(-REACH, REACH + 1))
F32 = jnp.float32
BF16 = jnp.bfloat16
LANES = 128
SUB = 8
GROUP = LANES // (2 * MODEL_STEPS)

VMEM = pl.BlockSpec(memory_space=pltpu.VMEM)
SMEM = pl.BlockSpec(memory_space=pltpu.SMEM)
PARAMS = pltpu.CompilerParams(vmem_limit_bytes=48 * 1024 * 1024)


def call(body, out_shape, *args, in_specs=None, scratch=()):
    return pl.pallas_call(
        body,
        out_shape=out_shape,
        in_specs=in_specs or [VMEM] * len(args),
        out_specs=jax.tree.map(lambda _: VMEM, out_shape),
        scratch_shapes=scratch,
        compiler_params=PARAMS,
    )(*args)


def lane_iota(shape):
    return lax.broadcasted_iota(jnp.int32, shape, len(shape) - 1)


def sub_iota(shape):
    return lax.broadcasted_iota(jnp.int32, shape, len(shape) - 2)


def neighbor_of(place_ref, step):
    member, parts = place_ref[2], place_ref[3]
    return lax.rem(member + parts + step, parts)


def split_body(turns, place_ref, in_ref, *out_refs):
    own, planes, rows, cols = out_refs[0].shape
    levels = in_ref.shape[1]
    slot = lane_iota((rows, LANES)) // MODEL_STEPS

    def block(step):
        return pl.ds(pl.multiple_of(neighbor_of(place_ref, step) * cols, cols), cols)

    for r, out_ref in zip(turns, out_refs):
        before, here, after = block(r - 1), block(r), block(r + 1)
        for m in range(own):

            def step(g, carry):
                total = jnp.zeros((rows, LANES), F32)
                for k in range(GROUP):
                    level = g * GROUP + k
                    out_ref[m, level] = in_ref[m, level, :, here]
                    left = in_ref[m, level, :, before].astype(F32)
                    right = in_ref[m, level, :, after].astype(F32)
                    total = jnp.where(slot == k, pltpu.roll(left, MODEL_STEPS * (k + 1), 1), total)
                    total = jnp.where(slot == GROUP + k, pltpu.roll(right, MODEL_STEPS * (GROUP + k), 1), total)
                out_ref[m, levels + g] = total.astype(out_ref.dtype)
                return carry

            lax.fori_loop(0, levels // GROUP, step, 0)


def split_columns(place, members, parts, turns):
    own, levels, rows, ny = members.shape
    out = jax.ShapeDtypeStruct((own, levels + levels // GROUP, rows, ny // parts), members.dtype)
    return call(functools.partial(split_body, turns), (out,) * len(turns), place, members, in_specs=[SMEM, VMEM])


def third_tile(below, above, odd):
    upper = sub_iota((SUB, LANES)) < MODEL_STEPS
    if odd:
        return jnp.where(upper, pltpu.roll(below, MODEL_STEPS, 0), above)
    return jnp.where(upper, below, pltpu.roll(above, MODEL_STEPS, 0))


def pack_rows(ref, at, top_ref, bottom_ref):
    upper = sub_iota((SUB, LANES)) < MODEL_STEPS
    count, rows, _ = ref.shape
    for q in range(count // 2):
        top_ref[at + q] = jnp.where(upper, ref[2 * q, :SUB], pltpu.roll(ref[2 * q + 1, :SUB], MODEL_STEPS, 0))
        bottom_ref[at + q] = jnp.where(
            upper, pltpu.roll(ref[2 * q, rows - SUB :], MODEL_STEPS, 0), ref[2 * q + 1, rows - SUB :]
        )


def rows_body(x_ref, top_ref, bottom_ref):
    pack_rows(x_ref, 0, top_ref, bottom_ref)


def edge_rows(x):
    out = jax.ShapeDtypeStruct((x.shape[0] // 2, SUB, LANES), F32)
    return call(rows_body, (out, out), x)


def columns_edge_body(x_ref, above_ref, below_ref, first_ref, last_ref):
    levels, rows, cols = x_ref.shape
    slot = lane_iota((rows + SUB, LANES)) // MODEL_STEPS

    def step(g, carry):
        first = jnp.zeros((rows + SUB, LANES), F32)
        last = jnp.zeros((rows + SUB, LANES), F32)
        for k in range(GROUP):
            level = g * GROUP + k
            pair = g * (GROUP // 2) + k // 2
            x = jnp.concatenate([x_ref[level], third_tile(below_ref[pair], above_ref[pair], k % 2)], axis=0)
            last = jnp.where(slot == k, pltpu.roll(x, MODEL_STEPS * (k + 1), 1), last)
            first = jnp.where(slot == GROUP + k, pltpu.roll(x, MODEL_STEPS * (GROUP + k), 1), first)
        first_ref[g] = first
        last_ref[g] = last
        return carry

    lax.fori_loop(0, levels // GROUP, step, 0)


def edge_columns(x, above, below):
    levels, rows, cols = x.shape
    out = jax.ShapeDtypeStruct((levels // GROUP, rows + SUB, LANES), F32)
    return call(columns_edge_body, (out, out), x, above, below)


def shift(x, axis, step):
    count = lax.axis_size(axis)
    pairs = [(i, i + step) for i in range(count) if 0 <= i + step < count]
    return lax.ppermute(x, axis, pairs)


def sweep_block(level_pair, x_ref, sides_ref, above_ref, below_ref, wx_ref, wy_ref, mask):
    rows = x_ref.shape[1]
    lanes = lane_iota((rows + SUB, LANES))
    ext_rows = rows + SUB
    ext_cols = 2 * LANES
    above = above_ref[level_pair]
    below = below_ref[level_pair]
    results = []
    for odd in range(2):
        level = 2 * level_pair + odd
        k = level % GROUP
        packed = sides_ref[level // GROUP]
        side_right = pltpu.roll(packed, (LANES + LANES // 2 - MODEL_STEPS * k) % LANES, 1)
        side_left = pltpu.roll(packed, LANES - MODEL_STEPS * (k + 1), 1)
        side = jnp.where(lanes < MODEL_STEPS, side_right, side_left)
        center = jnp.concatenate([x_ref[level], third_tile(below, above, odd)], axis=0)
        field = jnp.concatenate([center, side], axis=1) * mask
        wx = wx_ref[level]
        wy = wy_ref[level]
        own = 1.0 - 4.0 * DIFFUSION - wx - wy
        ahead_x = DIFFUSION + wx
        ahead_y = DIFFUSION + wy
        for _ in range(MODEL_STEPS):
            field = (
                own * field
                + ahead_x * pltpu.roll(field, ext_rows - 1, 0)
                + ahead_y * pltpu.roll(field, ext_cols - 1, 1)
                + DIFFUSION * (pltpu.roll(field, 1, 0) + pltpu.roll(field, 1, 1))
            ) * mask
        results.append(field[:rows, :LANES])
    return results


def block_mask(place_ref, rows, cols):
    tile, tiles, member, parts = (place_ref[i] for i in range(4))
    shape = (rows + SUB, 2 * LANES)
    r = sub_iota(shape)
    c = lane_iota(shape)
    r = jnp.where(r < rows + MODEL_STEPS, r, r - rows - SUB)
    near = (c < cols + MODEL_STEPS) | (c >= 2 * LANES - MODEL_STEPS)
    c = jnp.where(c < cols + MODEL_STEPS, c, c - 2 * LANES)
    gr = r + tile * rows
    gc = c + member * cols
    inside = (gr >= 0) & (gr < tiles * rows) & (gc >= 0) & (gc < parts * cols) & near
    return jnp.where(inside, 1.0, 0.0).astype(F32)


def first_model_body(place_ref, wx_ref, wy_ref, x_ref, left_ref, right_ref, above_ref, below_ref, grad_ref, sides_ref):
    levels, rows, cols = x_ref.shape
    mask = block_mask(place_ref, rows, cols)
    sides_ref[...] = left_ref[...] + right_ref[...]

    def step(q, carry):
        for u in range(2):
            pair = 2 * q + u
            for odd, value in enumerate(
                sweep_block(pair, x_ref, sides_ref, above_ref, below_ref, wx_ref, wy_ref, mask)
            ):
                grad_ref[2 * pair + odd] = value
        return carry

    lax.fori_loop(0, levels // 4, step, 0)


def second_model_body(
    place_ref, wx_ref, wy_ref, x_ref, beside_ref, above_ref, below_ref, *refs
):
    *others, grad_ref, sides_ref = refs
    levels, rows, cols = x_ref.shape
    groups = beside_ref.shape[0]
    mask = block_mask(place_ref, rows, cols)
    for g in range(groups):
        at = (levels + g) // 2
        sides_ref[g, :rows] = beside_ref[g]
        sides_ref[g, rows:] = third_tile(below_ref[at], above_ref[at], g % 2)

    def step(q, carry):
        for u in range(2):
            pair = 2 * q + u
            for odd, value in enumerate(
                sweep_block(pair, x_ref, sides_ref, above_ref, below_ref, wx_ref, wy_ref, mask)
            ):
                grad_ref[2 * pair + odd] = value
        return carry

    lax.fori_loop(0, levels // 4, step, 0)
    project_body(place_ref, grad_ref, *others)


def project_body(place_ref, grad_ref, *refs):
    *member_refs, wide_ref, thin_ref = refs
    own, _, rows, cols = member_refs[0].shape
    count = len(member_refs) * own

    def step(q, carry):
        carry = list(carry)
        for u in range(2):
            g = grad_ref[2 * q + u]
            for m in range(count):
                carry[m] = carry[m] + member_refs[m // own][m % own, 2 * q + u].astype(F32) * g
        return tuple(carry)

    total = lax.fori_loop(0, grad_ref.shape[0] // 2, step, (jnp.zeros((rows, cols), F32),) * count)
    for m in range(count):
        at = neighbor_of(place_ref, -(m // own)) * own + m % own
        wide_ref[at] = total[m]
        thin_ref[at] = total[m].astype(BF16)


def taper(offset):
    k = offset.astype(F32)
    w = (1.0 - (k / 17.0) * (k / 17.0)) * (1.0 / TAPER_TOTAL)
    return jnp.where(jnp.abs(offset) <= REACH, w, 0.0)


def halves(x):
    high = x.astype(BF16)
    return high, (x - high.astype(F32)).astype(BF16)


def sharp_dot(a, b):
    ah, al = halves(a)
    bh, bl = halves(b)
    dot = functools.partial(jnp.dot, preferred_element_type=F32)
    return dot(ah, bh) + dot(al, bh) + dot(ah, bl)


def columns_body(left_ref, mid_ref, right_ref, wide_ref, thin_ref):
    count, rows, cols = mid_ref.shape
    wide = jnp.concatenate(
        [r[...].astype(F32).reshape(count * rows, cols) for r in (left_ref, mid_ref, right_ref)], axis=1
    )
    shape = (3 * cols, wide_ref.shape[0] // count * cols)
    lane = lane_iota(shape)
    beside = lane % MODEL_STEPS + jnp.where(lane < cols + LANES // 2, -MODEL_STEPS, cols)
    target = jnp.where(lane < cols, lane, beside)
    out = sharp_dot(wide, taper(sub_iota(shape) - cols - target))
    for i in range(shape[1] // cols):
        part = out[:, i * cols : (i + 1) * cols].reshape(count, rows, cols)
        wide_ref[i * count : (i + 1) * count] = part
        thin_ref[i * count : (i + 1) * count] = part.astype(BF16)


def smooth_rows(above_ref, mid_ref, below_ref):
    count, rows, cols = mid_ref.shape
    tall = jnp.concatenate(
        [
            jnp.concatenate([above_ref[m].astype(F32), mid_ref[m], below_ref[m].astype(F32)], axis=0)
            for m in range(count)
        ],
        axis=1,
    )
    shape = (rows, 3 * rows)
    out = sharp_dot(taper(lane_iota(shape) - sub_iota(shape) - rows), tall)
    return [out[:, m * cols : (m + 1) * cols] for m in range(count)]


def increments(place_ref, member_refs, local_ref, levels, emit):
    own = member_refs[0].shape[0]
    count = len(member_refs) * own
    local = [local_ref[neighbor_of(place_ref, -(m // own)) * own + m % own] for m in range(count)]

    def step(q, carry):
        for u in range(2):
            level = 2 * q + u
            total = member_refs[0][0, level].astype(F32) * local[0]
            for m in range(1, count):
                total = total + member_refs[m // own][m % own, level].astype(F32) * local[m]
            emit(level, total)
        return carry

    lax.fori_loop(0, levels // 2, step, 0)


def update_body(parts, place_ref, residual_ref, left_ref, right_ref, above_ref, mid_ref, below_ref, *refs):
    member_refs = refs[:parts]
    analysis_ref, out_ref, beside_ref, top_ref, bottom_ref, local_ref = refs[parts:]
    levels, rows, cols = residual_ref.shape
    own = member_refs[0].shape[0]
    count = parts * own
    for m, value in enumerate(smooth_rows(above_ref, mid_ref, below_ref)):
        local_ref[m] = value

    def emit(level, value):
        analysis_ref[level] = value
        out_ref[level] = residual_ref[level] - RELAX * value

    increments(place_ref, member_refs, local_ref, levels, emit)
    for g in range(levels // GROUP):
        total = jnp.zeros((rows, LANES), F32)
        for m in range(count):
            at = neighbor_of(place_ref, -(m // own)) * own + m % own
            total = total + member_refs[m // own][m % own, levels + g].astype(F32) * local_ref[count + at]
        beside_ref[g] = left_ref[g, :rows] + right_ref[g, :rows] - RELAX * total
    pack_rows(out_ref, 0, top_ref, bottom_ref)
    pack_rows(beside_ref, levels // 2, top_ref, bottom_ref)


def final_body(parts, place_ref, residual_ref, before_ref, above_ref, mid_ref, below_ref, *refs):
    member_refs = refs[:parts]
    analysis_ref, out_ref, local_ref = refs[parts:]
    for m, value in enumerate(smooth_rows(above_ref, mid_ref, below_ref)):
        local_ref[m] = value

    def emit(level, value):
        analysis_ref[level] = before_ref[level] + value
        out_ref[level] = residual_ref[level] - RELAX * value

    increments(place_ref, member_refs, local_ref, residual_ref.shape[0], emit)


def per_device(residual_in, members, wind_x, wind_y):
    levels, rows, cols = residual_in.shape
    tiles = lax.axis_size("tile")
    parts = lax.axis_size("member")
    place = jnp.stack([lax.axis_index("tile"), jnp.int32(tiles), lax.axis_index("member"), jnp.int32(parts)])
    count = members.shape[0] * parts
    groups = levels // GROUP

    def shape(*dims, kind=F32):
        return jax.ShapeDtypeStruct(dims, kind)

    def both(*dims):
        return shape(*dims), shape(*dims, kind=BF16)

    def turned(x, step):
        return lax.ppermute(x, "member", [(i, (i + step) % parts) for i in range(parts)])

    def smoothed(wide, thin, planes):
        wide, thin = call(
            columns_body, both(planes, rows, cols), shift(thin, "member", 1), wide, shift(thin, "member", -1)
        )
        return shift(thin, "tile", 1), wide, shift(thin, "tile", -1)

    like = shape(levels, rows, cols)
    sides = [pltpu.VMEM((groups, rows + SUB, LANES), F32)]

    far = parts // 2
    (soon,) = split_columns(place, members, parts, (far,))
    soon, residual_in = lax.optimization_barrier((soon, residual_in))
    blocks = {far: turned(soon, far)}
    top, bottom = edge_rows(residual_in)
    above, below = shift(bottom, "tile", 1), shift(top, "tile", -1)
    first, last = edge_columns(residual_in, above, below)
    left, right = shift(last, "member", 1), shift(first, "member", -1)
    members, first = lax.optimization_barrier((members, first))
    turns = [r for r in range(parts) if r != far]
    later = split_columns(place, members, parts, turns)
    later, left, right = lax.optimization_barrier((later, left, right))
    for r, block in zip(turns, later):
        blocks[r] = turned(block, r) if r else block
    blocks = [blocks[r] for r in range(parts)]
    grad = call(
        first_model_body, like,
        place, wind_x, wind_y, residual_in, left, right, above, below,
        in_specs=[SMEM] * 3 + [VMEM] * 5, scratch=sides,
    )
    wide, thin = call(
        project_body, both(count, rows, cols), place, grad, *blocks, in_specs=[SMEM] + [VMEM] * (1 + parts)
    )

    halo = shape((levels + groups) // 2, SUB, LANES)
    analysis, residual, beside, top, bottom = call(
        functools.partial(update_body, parts), (like, like, shape(groups, rows, LANES), halo, halo),
        place, residual_in, left, right, *smoothed(wide, thin, 2 * count), *blocks,
        in_specs=[SMEM] + [VMEM] * (6 + parts), scratch=[pltpu.VMEM((2 * count, rows, cols), F32)],
    )
    above, below = shift(bottom, "tile", 1), shift(top, "tile", -1)
    wide, thin = call(
        second_model_body, both(count, rows, cols),
        place, wind_x, wind_y, residual, beside, above, below, *blocks,
        in_specs=[SMEM] * 3 + [VMEM] * (4 + parts), scratch=[pltpu.VMEM((levels, rows, cols), F32)] + sides,
    )
    return call(
        functools.partial(final_body, parts), (like, like),
        place, residual, analysis, *smoothed(wide, thin, count), *blocks,
        in_specs=[SMEM] + [VMEM] * (5 + parts), scratch=[pltpu.VMEM((count, rows, cols), F32)],
    )


def solution(mesh):
    return jax.shard_map(
        per_device,
        mesh=mesh,
        in_specs=(P(None, "tile", "member"), P("member", None, "tile", None), P(), P()),
        out_specs=(P(None, "tile", "member"), P(None, "tile", "member")),
        check_vma=False,
    )
```

```python
import functools

import jax
import jax.numpy as jnp
from jax import lax
from jax.experimental import pallas as pl
from jax.experimental.pallas import tpu as pltpu
from jax.sharding import PartitionSpec as P

ITERS = 2
MODEL_STEPS = 4
DIFFUSION = 0.1
RELAX = 0.5
REACH = 16
TAPER_TOTAL = sum(1.0 - (k / 17.0) ** 2 for k in range(-REACH, REACH + 1))
F32 = jnp.float32
BF16 = jnp.bfloat16
LANES = 128
SUB = 8
GROUP = LANES // (2 * MODEL_STEPS)

VMEM = pl.BlockSpec(memory_space=pltpu.VMEM)
SMEM = pl.BlockSpec(memory_space=pltpu.SMEM)
PARAMS = pltpu.CompilerParams(vmem_limit_bytes=48 * 1024 * 1024)


def call(body, out_shape, *args, in_specs=None, scratch=()):
    return pl.pallas_call(
        body,
        out_shape=out_shape,
        in_specs=in_specs or [VMEM] * len(args),
        out_specs=jax.tree.map(lambda _: VMEM, out_shape),
        scratch_shapes=scratch,
        compiler_params=PARAMS,
    )(*args)


def lane_iota(shape):
    return lax.broadcasted_iota(jnp.int32, shape, len(shape) - 1)


def sub_iota(shape):
    return lax.broadcasted_iota(jnp.int32, shape, len(shape) - 2)


def neighbor_of(place_ref, step):
    member, parts = place_ref[2], place_ref[3]
    return lax.rem(member + parts + step, parts)


def early_body(in_ref, out_ref):
    parts, own, levels, rows, cols = out_ref.shape
    for c in range(parts):
        out_ref[c] = in_ref[:, :levels, :, c * cols : (c + 1) * cols]


def split_body(turns, early, place_ref, in_ref, *out_refs):
    own, planes, rows, cols = out_refs[0].shape
    levels = in_ref.shape[1]
    late = levels - early
    slot = lane_iota((rows, LANES)) // MODEL_STEPS

    def block(step):
        return pl.ds(pl.multiple_of(neighbor_of(place_ref, step) * cols, cols), cols)

    for r, out_ref in zip(turns, out_refs):
        before, here, after = block(r - 1), block(r), block(r + 1)
        for m in range(own):
            out_ref[m, :late] = in_ref[m, early:, :, here]

            def step(g, carry):
                total = jnp.zeros((rows, LANES), F32)
                for k in range(GROUP):
                    left = in_ref[m, g * GROUP + k, :, before].astype(F32)
                    right = in_ref[m, g * GROUP + k, :, after].astype(F32)
                    total = jnp.where(slot == k, pltpu.roll(left, MODEL_STEPS * (k + 1), 1), total)
                    total = jnp.where(slot == GROUP + k, pltpu.roll(right, MODEL_STEPS * (GROUP + k), 1), total)
                out_ref[m, late + g] = total.astype(out_ref.dtype)
                return carry

            lax.fori_loop(0, levels // GROUP, step, 0)


def split_early(members, parts, early):
    own, levels, rows, ny = members.shape
    return call(early_body, jax.ShapeDtypeStruct((parts, own, early, rows, ny // parts), members.dtype), members)


def split_late(place, members, parts, early):
    own, levels, rows, ny = members.shape
    out = jax.ShapeDtypeStruct((own, levels - early + levels // GROUP, rows, ny // parts), members.dtype)
    body = functools.partial(split_body, range(parts), early)
    return call(body, (out,) * parts, place, members, in_specs=[SMEM, VMEM])


def third_tile(below, above, odd):
    upper = sub_iota((SUB, LANES)) < MODEL_STEPS
    if odd:
        return jnp.where(upper, pltpu.roll(below, MODEL_STEPS, 0), above)
    return jnp.where(upper, below, pltpu.roll(above, MODEL_STEPS, 0))


def pack_rows(ref, at, top_ref, bottom_ref):
    upper = sub_iota((SUB, LANES)) < MODEL_STEPS
    count, rows, _ = ref.shape
    for q in range(count // 2):
        top_ref[at + q] = jnp.where(upper, ref[2 * q, :SUB], pltpu.roll(ref[2 * q + 1, :SUB], MODEL_STEPS, 0))
        bottom_ref[at + q] = jnp.where(
            upper, pltpu.roll(ref[2 * q, rows - SUB :], MODEL_STEPS, 0), ref[2 * q + 1, rows - SUB :]
        )


def rows_body(x_ref, top_ref, bottom_ref):
    pack_rows(x_ref, 0, top_ref, bottom_ref)


def edge_rows(x):
    out = jax.ShapeDtypeStruct((x.shape[0] // 2, SUB, LANES), F32)
    return call(rows_body, (out, out), x)


def columns_edge_body(x_ref, above_ref, below_ref, first_ref, last_ref):
    levels, rows, cols = x_ref.shape
    slot = lane_iota((rows + SUB, LANES)) // MODEL_STEPS

    def step(g, carry):
        first = jnp.zeros((rows + SUB, LANES), F32)
        last = jnp.zeros((rows + SUB, LANES), F32)
        for k in range(GROUP):
            level = g * GROUP + k
            pair = g * (GROUP // 2) + k // 2
            x = jnp.concatenate([x_ref[level], third_tile(below_ref[pair], above_ref[pair], k % 2)], axis=0)
            last = jnp.where(slot == k, pltpu.roll(x, MODEL_STEPS * (k + 1), 1), last)
            first = jnp.where(slot == GROUP + k, pltpu.roll(x, MODEL_STEPS * (GROUP + k), 1), first)
        first_ref[g] = first
        last_ref[g] = last
        return carry

    lax.fori_loop(0, levels // GROUP, step, 0)


def edge_columns(x, above, below):
    levels, rows, cols = x.shape
    out = jax.ShapeDtypeStruct((levels // GROUP, rows + SUB, LANES), F32)
    return call(columns_edge_body, (out, out), x, above, below)


def shift(x, axis, step):
    count = lax.axis_size(axis)
    pairs = [(i, i + step) for i in range(count) if 0 <= i + step < count]
    return lax.ppermute(x, axis, pairs)


def sweep_block(level_pair, x_ref, sides_ref, above_ref, below_ref, wx_ref, wy_ref, mask):
    rows = x_ref.shape[1]
    lanes = lane_iota((rows + SUB, LANES))
    ext_rows = rows + SUB
    ext_cols = 2 * LANES
    above = above_ref[level_pair]
    below = below_ref[level_pair]
    results = []
    for odd in range(2):
        level = 2 * level_pair + odd
        k = level % GROUP
        packed = sides_ref[level // GROUP]
        side_right = pltpu.roll(packed, (LANES + LANES // 2 - MODEL_STEPS * k) % LANES, 1)
        side_left = pltpu.roll(packed, LANES - MODEL_STEPS * (k + 1), 1)
        side = jnp.where(lanes < MODEL_STEPS, side_right, side_left)
        center = jnp.concatenate([x_ref[level], third_tile(below, above, odd)], axis=0)
        field = jnp.concatenate([center, side], axis=1) * mask
        wx = wx_ref[level]
        wy = wy_ref[level]
        own = 1.0 - 4.0 * DIFFUSION - wx - wy
        ahead_x = DIFFUSION + wx
        ahead_y = DIFFUSION + wy
        for _ in range(MODEL_STEPS):
            field = (
                own * field
                + ahead_x * pltpu.roll(field, ext_rows - 1, 0)
                + ahead_y * pltpu.roll(field, ext_cols - 1, 1)
                + DIFFUSION * (pltpu.roll(field, 1, 0) + pltpu.roll(field, 1, 1))
            ) * mask
        results.append(field[:rows, :LANES])
    return results


def block_mask(place_ref, rows, cols):
    tile, tiles, member, parts = (place_ref[i] for i in range(4))
    shape = (rows + SUB, 2 * LANES)
    r = sub_iota(shape)
    c = lane_iota(shape)
    r = jnp.where(r < rows + MODEL_STEPS, r, r - rows - SUB)
    near = (c < cols + MODEL_STEPS) | (c >= 2 * LANES - MODEL_STEPS)
    c = jnp.where(c < cols + MODEL_STEPS, c, c - 2 * LANES)
    gr = r + tile * rows
    gc = c + member * cols
    inside = (gr >= 0) & (gr < tiles * rows) & (gc >= 0) & (gc < parts * cols) & near
    return jnp.where(inside, 1.0, 0.0).astype(F32)


def first_model_body(place_ref, wx_ref, wy_ref, x_ref, left_ref, right_ref, above_ref, below_ref, grad_ref, sides_ref):
    levels, rows, cols = x_ref.shape
    mask = block_mask(place_ref, rows, cols)
    sides_ref[...] = left_ref[...] + right_ref[...]

    def step(q, carry):
        for u in range(2):
            pair = 2 * q + u
            for odd, value in enumerate(
                sweep_block(pair, x_ref, sides_ref, above_ref, below_ref, wx_ref, wy_ref, mask)
            ):
                grad_ref[2 * pair + odd] = value
        return carry

    lax.fori_loop(0, levels // 4, step, 0)


def second_model_body(
    place_ref, wx_ref, wy_ref, x_ref, beside_ref, above_ref, below_ref, *refs
):
    *others, grad_ref, sides_ref = refs
    levels, rows, cols = x_ref.shape
    groups = beside_ref.shape[0]
    mask = block_mask(place_ref, rows, cols)
    for g in range(groups):
        at = (levels + g) // 2
        sides_ref[g, :rows] = beside_ref[g]
        sides_ref[g, rows:] = third_tile(below_ref[at], above_ref[at], g % 2)

    def step(q, carry):
        for u in range(2):
            pair = 2 * q + u
            for odd, value in enumerate(
                sweep_block(pair, x_ref, sides_ref, above_ref, below_ref, wx_ref, wy_ref, mask)
            ):
                grad_ref[2 * pair + odd] = value
        return carry

    lax.fori_loop(0, levels // 4, step, 0)
    project_body(place_ref, grad_ref, *others)


def project_body(place_ref, grad_ref, first_ref, *refs):
    *late_refs, wide_ref, thin_ref = refs
    parts, own, early, rows, cols = first_ref.shape
    count = parts * own
    zeros = (jnp.zeros((rows, cols), F32),) * count

    def over(start, stop, member):
        def step(q, carry):
            carry = list(carry)
            for u in range(2):
                level = 2 * q + u
                g = grad_ref[start + level]
                for m in range(count):
                    carry[m] = carry[m] + member(m // own, m % own, level).astype(F32) * g
            return tuple(carry)

        return lax.fori_loop(0, (stop - start) // 2, step, zeros)

    total = over(0, early, lambda r, m, level: first_ref[r, m, level])
    for m in range(count):
        wide_ref[m] = total[m]
    total = over(early, grad_ref.shape[0], lambda r, m, level: late_refs[r][m, level])
    for m in range(count):
        at = neighbor_of(place_ref, -(m // own)) * own + m % own
        value = wide_ref[at] + total[m]
        wide_ref[at] = value
        thin_ref[at] = value.astype(BF16)


def taper(offset):
    k = offset.astype(F32)
    w = (1.0 - (k / 17.0) * (k / 17.0)) * (1.0 / TAPER_TOTAL)
    return jnp.where(jnp.abs(offset) <= REACH, w, 0.0)


def halves(x):
    high = x.astype(BF16)
    return high, (x - high.astype(F32)).astype(BF16)


def sharp_dot(a, b):
    ah, al = halves(a)
    bh, bl = halves(b)
    dot = functools.partial(jnp.dot, preferred_element_type=F32)
    return dot(ah, bh) + dot(al, bh) + dot(ah, bl)


def columns_body(left_ref, mid_ref, right_ref, wide_ref, thin_ref):
    count, rows, cols = mid_ref.shape
    wide = jnp.concatenate(
        [r[...].astype(F32).reshape(count * rows, cols) for r in (left_ref, mid_ref, right_ref)], axis=1
    )
    shape = (3 * cols, wide_ref.shape[0] // count * cols)
    lane = lane_iota(shape)
    beside = lane % MODEL_STEPS + jnp.where(lane < cols + LANES // 2, -MODEL_STEPS, cols)
    target = jnp.where(lane < cols, lane, beside)
    out = sharp_dot(wide, taper(sub_iota(shape) - cols - target))
    for i in range(shape[1] // cols):
        part = out[:, i * cols : (i + 1) * cols].reshape(count, rows, cols)
        wide_ref[i * count : (i + 1) * count] = part
        thin_ref[i * count : (i + 1) * count] = part.astype(BF16)


def smooth_rows(above_ref, mid_ref, below_ref):
    count, rows, cols = mid_ref.shape
    tall = jnp.concatenate(
        [
            jnp.concatenate([above_ref[m].astype(F32), mid_ref[m], below_ref[m].astype(F32)], axis=0)
            for m in range(count)
        ],
        axis=1,
    )
    shape = (rows, 3 * rows)
    out = sharp_dot(taper(lane_iota(shape) - sub_iota(shape) - rows), tall)
    return [out[:, m * cols : (m + 1) * cols] for m in range(count)]


def increments(place_ref, member_refs, local_ref, levels, emit):
    first_ref, *late_refs = member_refs
    parts, own, early, _, _ = first_ref.shape
    count = parts * own

    def over(start, stop, member, local):
        def step(q, carry):
            for u in range(2):
                level = 2 * q + u
                total = member(0, 0, level).astype(F32) * local[0]
                for m in range(1, count):
                    total = total + member(m // own, m % own, level).astype(F32) * local[m]
                emit(start + level, total)
            return carry

        lax.fori_loop(0, (stop - start) // 2, step, 0)

    over(0, early, lambda r, m, level: first_ref[r, m, level], [local_ref[m] for m in range(count)])
    turned = [local_ref[neighbor_of(place_ref, -(m // own)) * own + m % own] for m in range(count)]
    over(early, levels, lambda r, m, level: late_refs[r][m, level], turned)


def update_body(parts, place_ref, residual_ref, left_ref, right_ref, above_ref, mid_ref, below_ref, *refs):
    member_refs = refs[: parts + 1]
    analysis_ref, out_ref, beside_ref, top_ref, bottom_ref, local_ref = refs[parts + 1 :]
    levels, rows, cols = residual_ref.shape
    _, own, early, _, _ = member_refs[0].shape
    count = parts * own
    for m, value in enumerate(smooth_rows(above_ref, mid_ref, below_ref)):
        local_ref[m] = value

    def emit(level, value):
        analysis_ref[level] = value
        out_ref[level] = residual_ref[level] - RELAX * value

    increments(place_ref, member_refs, local_ref, levels, emit)
    for g in range(levels // GROUP):
        total = jnp.zeros((rows, LANES), F32)
        for m in range(count):
            at = neighbor_of(place_ref, -(m // own)) * own + m % own
            member = member_refs[1 + m // own][m % own, levels - early + g]
            total = total + member.astype(F32) * local_ref[count + at]
        beside_ref[g] = left_ref[g, :rows] + right_ref[g, :rows] - RELAX * total
    pack_rows(out_ref, 0, top_ref, bottom_ref)
    pack_rows(beside_ref, levels // 2, top_ref, bottom_ref)


def final_body(parts, place_ref, residual_ref, before_ref, above_ref, mid_ref, below_ref, *refs):
    member_refs = refs[: parts + 1]
    analysis_ref, out_ref, local_ref = refs[parts + 1 :]
    for m, value in enumerate(smooth_rows(above_ref, mid_ref, below_ref)):
        local_ref[m] = value

    def emit(level, value):
        analysis_ref[level] = before_ref[level] + value
        out_ref[level] = residual_ref[level] - RELAX * value

    increments(place_ref, member_refs, local_ref, residual_ref.shape[0], emit)


def per_device(residual_in, members, wind_x, wind_y):
    levels, rows, cols = residual_in.shape
    tiles = lax.axis_size("tile")
    parts = lax.axis_size("member")
    place = jnp.stack([lax.axis_index("tile"), jnp.int32(tiles), lax.axis_index("member"), jnp.int32(parts)])
    count = members.shape[0] * parts
    groups = levels // GROUP

    def shape(*dims, kind=F32):
        return jax.ShapeDtypeStruct(dims, kind)

    def both(*dims):
        return shape(*dims), shape(*dims, kind=BF16)

    def turned(x, step):
        return lax.ppermute(x, "member", [(i, (i + step) % parts) for i in range(parts)])

    def smoothed(wide, thin, planes):
        wide, thin = call(
            columns_body, both(planes, rows, cols), shift(thin, "member", 1), wide, shift(thin, "member", -1)
        )
        return shift(thin, "tile", 1), wide, shift(thin, "tile", -1)

    like = shape(levels, rows, cols)
    sides = [pltpu.VMEM((groups, rows + SUB, LANES), F32)]

    early = levels * 3 // 4
    soon, residual_in = lax.optimization_barrier((split_early(members, parts, early), residual_in))
    blocks = [lax.all_to_all(soon, "member", split_axis=0, concat_axis=0, tiled=True)]
    top, bottom = edge_rows(residual_in)
    above, below = shift(bottom, "tile", 1), shift(top, "tile", -1)
    first, last = edge_columns(residual_in, above, below)
    left, right = shift(last, "member", 1), shift(first, "member", -1)
    members, first = lax.optimization_barrier((members, first))
    later, left, right = lax.optimization_barrier((split_late(place, members, parts, early), left, right))
    blocks += [turned(block, r) if r else block for r, block in enumerate(later)]
    grad = call(
        first_model_body, like,
        place, wind_x, wind_y, residual_in, left, right, above, below,
        in_specs=[SMEM] * 3 + [VMEM] * 5, scratch=sides,
    )
    wide, thin = call(
        project_body, both(count, rows, cols), place, grad, *blocks, in_specs=[SMEM] + [VMEM] * (2 + parts)
    )

    halo = shape((levels + groups) // 2, SUB, LANES)
    analysis, residual, beside, top, bottom = call(
        functools.partial(update_body, parts), (like, like, shape(groups, rows, LANES), halo, halo),
        place, residual_in, left, right, *smoothed(wide, thin, 2 * count), *blocks,
        in_specs=[SMEM] + [VMEM] * (7 + parts), scratch=[pltpu.VMEM((2 * count, rows, cols), F32)],
    )
    above, below = shift(bottom, "tile", 1), shift(top, "tile", -1)
    wide, thin = call(
        second_model_body, both(count, rows, cols),
        place, wind_x, wind_y, residual, beside, above, below, *blocks,
        in_specs=[SMEM] * 3 + [VMEM] * (5 + parts), scratch=[pltpu.VMEM((levels, rows, cols), F32)] + sides,
    )
    return call(
        functools.partial(final_body, parts), (like, like),
        place, residual, analysis, *smoothed(wide, thin, count), *blocks,
        in_specs=[SMEM] + [VMEM] * (6 + parts), scratch=[pltpu.VMEM((count, rows, cols), F32)],
    )


def solution(mesh):
    return jax.shard_map(
        per_device,
        mesh=mesh,
        in_specs=(P(None, "tile", "member"), P("member", None, "tile", None), P(), P()),
        out_specs=(P(None, "tile", "member"), P(None, "tile", "member")),
        check_vma=False,
    )
```

```python
import functools

import jax
import jax.numpy as jnp
from jax import lax
from jax.experimental import pallas as pl
from jax.experimental.pallas import tpu as pltpu
from jax.sharding import PartitionSpec as P

ITERS = 2
MODEL_STEPS = 4
DIFFUSION = 0.1
RELAX = 0.5
REACH = 16
TAPER_TOTAL = sum(1.0 - (k / 17.0) ** 2 for k in range(-REACH, REACH + 1))
F32 = jnp.float32
BF16 = jnp.bfloat16
LANES = 128
SUB = 8
GROUP = LANES // (2 * MODEL_STEPS)

VMEM = pl.BlockSpec(memory_space=pltpu.VMEM)
SMEM = pl.BlockSpec(memory_space=pltpu.SMEM)
PARAMS = pltpu.CompilerParams(vmem_limit_bytes=48 * 1024 * 1024)


def call(body, out_shape, *args, in_specs=None, scratch=()):
    return pl.pallas_call(
        body,
        out_shape=out_shape,
        in_specs=in_specs or [VMEM] * len(args),
        out_specs=jax.tree.map(lambda _: VMEM, out_shape),
        scratch_shapes=scratch,
        compiler_params=PARAMS,
    )(*args)


def lane_iota(shape):
    return lax.broadcasted_iota(jnp.int32, shape, len(shape) - 1)


def sub_iota(shape):
    return lax.broadcasted_iota(jnp.int32, shape, len(shape) - 2)


def neighbor_of(place_ref, step):
    member, parts = place_ref[2], place_ref[3]
    return lax.rem(member + parts + step, parts)


def columns_split_body(in_ref, out_ref):
    parts, own, levels, rows, cols = out_ref.shape
    for c in range(parts):
        out_ref[c] = in_ref[:, :, :, c * cols : (c + 1) * cols]


def split_columns(members, parts):
    own, levels, rows, ny = members.shape
    out = jax.ShapeDtypeStruct((parts, own, levels, rows, ny // parts), members.dtype)
    return call(columns_split_body, out, members)


def put_left(x, k, total):
    here = lane_iota(x.shape) // MODEL_STEPS == GROUP - 1 - k
    return jnp.where(here, pltpu.roll(x, (MODEL_STEPS * (GROUP - k)) % LANES, 1), total)


def put_right(x, k, total):
    here = lane_iota(x.shape) // MODEL_STEPS == 2 * GROUP - 1 - k
    return jnp.where(here, pltpu.roll(x, (MODEL_STEPS * (2 * GROUP - 1 - k)) % LANES, 1), total)


def sides_body(place_ref, in_ref, *out_refs):
    own, groups, rows, _ = out_refs[0].shape
    cols = in_ref.shape[-1] // len(out_refs)

    def block(step):
        return pl.ds(pl.multiple_of(neighbor_of(place_ref, step) * cols, cols), cols)

    for r, out_ref in enumerate(out_refs):
        before, after = block(r - 1), block(r + 1)
        for m in range(own):

            def step(g, carry):
                total = jnp.zeros((rows, LANES), F32)
                for k in range(GROUP):
                    total = put_left(in_ref[m, g * GROUP + k, :, before].astype(F32), k, total)
                    total = put_right(in_ref[m, g * GROUP + k, :, after].astype(F32), k, total)
                out_ref[m, g] = total.astype(out_ref.dtype)
                return carry

            lax.fori_loop(0, groups, step, 0)


def side_columns(place, members, parts):
    own, levels, rows, ny = members.shape
    out = jax.ShapeDtypeStruct((own, levels // GROUP, rows, LANES), members.dtype)
    return call(sides_body, (out,) * parts, place, members, in_specs=[SMEM, VMEM])


def third_tile(below, above, odd):
    upper = sub_iota((SUB, LANES)) < MODEL_STEPS
    if odd:
        return jnp.where(upper, pltpu.roll(below, MODEL_STEPS, 0), above)
    return jnp.where(upper, below, pltpu.roll(above, MODEL_STEPS, 0))


def pack_rows(ref, at, top_ref, bottom_ref):
    upper = sub_iota((SUB, LANES)) < MODEL_STEPS
    count, rows, _ = ref.shape
    for q in range(count // 2):
        top_ref[at + q] = jnp.where(upper, ref[2 * q, :SUB], pltpu.roll(ref[2 * q + 1, :SUB], MODEL_STEPS, 0))
        bottom_ref[at + q] = jnp.where(
            upper, pltpu.roll(ref[2 * q, rows - SUB :], MODEL_STEPS, 0), ref[2 * q + 1, rows - SUB :]
        )


def rows_body(x_ref, top_ref, bottom_ref):
    pack_rows(x_ref, 0, top_ref, bottom_ref)


def edge_rows(x):
    out = jax.ShapeDtypeStruct((x.shape[0] // 2, SUB, LANES), F32)
    return call(rows_body, (out, out), x)


def columns_edge_body(x_ref, above_ref, below_ref, first_ref, last_ref):
    levels, rows, cols = x_ref.shape

    def step(g, carry):
        first = jnp.zeros((rows + SUB, LANES), F32)
        last = jnp.zeros((rows + SUB, LANES), F32)
        for k in range(GROUP):
            level = g * GROUP + k
            pair = g * (GROUP // 2) + k // 2
            x = jnp.concatenate([x_ref[level], third_tile(below_ref[pair], above_ref[pair], k % 2)], axis=0)
            last = put_left(x, k, last)
            first = put_right(x, k, first)
        first_ref[g] = first
        last_ref[g] = last
        return carry

    lax.fori_loop(0, levels // GROUP, step, 0)


def edge_columns(x, above, below):
    levels, rows, cols = x.shape
    out = jax.ShapeDtypeStruct((levels // GROUP, rows + SUB, LANES), F32)
    return call(columns_edge_body, (out, out), x, above, below)


def shift(x, axis, step):
    count = lax.axis_size(axis)
    pairs = [(i, i + step) for i in range(count) if 0 <= i + step < count]
    return lax.ppermute(x, axis, pairs)


def sweep(place_ref, wx_ref, wy_ref, x_ref, above_ref, below_ref, side_row, grad_ref):
    levels, rows, cols = x_ref.shape
    tile, tiles, member, parts = (place_ref[i] for i in range(4))
    x_flat = x_ref.reshape(levels * rows, cols)
    grad_flat = grad_ref.reshape(levels * rows, cols)
    halo = MODEL_STEPS
    pairs = above_ref.shape[0]
    above_flat = above_ref.reshape(pairs * SUB, LANES)
    below_flat = below_ref.reshape(pairs * SUB, LANES)

    lane = lane_iota((SUB, LANES))
    on_right = lane < halo
    is_first = lane == 0
    is_last = lane == LANES - 1
    inside = (on_right & (member < parts - 1)) | ((lane >= LANES - halo) & (member > 0))
    side_mask = jnp.where(inside, 1.0, 0.0).astype(F32)
    has_above = jnp.where(tile > 0, 1.0, 0.0).astype(F32)
    has_below = jnp.where(tile < tiles - 1, 1.0, 0.0).astype(F32)

    def load(g, half, e):
        q = 2 * g + half
        if e < 0:
            center = above_flat[pl.ds(q * SUB * halo + e + halo, SUB, stride=halo), :]
        elif e < rows:
            center = x_flat[pl.ds(q * SUB * rows + e, SUB, stride=rows), :]
        else:
            center = below_flat[pl.ds(q * SUB * halo + e - rows, SUB, stride=halo), :]
        row = jnp.broadcast_to(side_row(g, e), (SUB, LANES))
        start = halo * SUB * half
        right = pltpu.roll(row, start + halo, 1, stride=halo, stride_axis=0)
        left = pltpu.roll(row, start + LANES // 2, 1, stride=halo, stride_axis=0)
        return center, jnp.where(on_right, right, left) * side_mask

    def advance(before, here, after, e, own, ahead_x, ahead_y):
        center, side = here
        fore_c, fore_s = pltpu.roll(center, LANES - 1, 1), pltpu.roll(side, LANES - 1, 1)
        back_c, back_s = pltpu.roll(center, 1, 1), pltpu.roll(side, 1, 1)
        result = []
        for i, mine, fore, back in (
            (0, center, jnp.where(is_last, fore_s, fore_c), jnp.where(is_first, back_s, back_c)),
            (1, side, jnp.where(is_last, fore_c, fore_s), jnp.where(is_first, back_c, back_s)),
        ):
            value = own * mine + ahead_x * after[i] + ahead_y * fore + DIFFUSION * (before[i] + back)
            if e < 0:
                value = value * has_above
            if e >= rows:
                value = value * has_below
            result.append(value * side_mask if i else value)
        return tuple(result)

    def group(g, carry):
        for half in range(2):
            at = pl.ds(pl.multiple_of((2 * g + half) * SUB, SUB), SUB)
            wx, wy = wx_ref[at, :], wy_ref[at, :]
            coefficients = (1.0 - 4.0 * DIFFUSION - wx - wy, DIFFUSION + wx, DIFFUSION + wy)
            fields = [{} for _ in range(halo + 1)]
            for front in range(-halo, rows + halo):
                fields[0][front] = load(g, half, front)
                for n in range(1, halo + 1):
                    e = front - n
                    if -halo + n <= e < rows + halo - n:
                        old = fields[n - 1]
                        fields[n][e] = advance(old[e - 1], old[e], old[e + 1], e, *coefficients)
                        if n == halo:
                            grad_flat[pl.ds((2 * g + half) * SUB * rows + e, SUB, stride=rows), :] = fields[n][e][0]
        return carry

    lax.fori_loop(0, levels // GROUP, group, 0)


def first_model_body(place_ref, wx_ref, wy_ref, x_ref, left_ref, right_ref, above_ref, below_ref, grad_ref):
    rows = x_ref.shape[1]

    def side_row(g, e):
        at = pl.ds(e if e >= 0 else rows + SUB + e, 1)
        return left_ref[g, at, :] + right_ref[g, at, :]

    sweep(place_ref, wx_ref, wy_ref, x_ref, above_ref, below_ref, side_row, grad_ref)


def second_model_body(
    place_ref, wx_ref, wy_ref, x_ref, beside_ref, above_ref, below_ref, members_ref, wide_ref, thin_ref, grad_ref
):
    levels, rows, cols = x_ref.shape

    def side_row(g, e):
        if 0 <= e < rows:
            return beside_ref[g, pl.ds(e, 1), :]
        ref, row = (above_ref, e + MODEL_STEPS) if e < 0 else (below_ref, e - rows)
        flat = ref.reshape(ref.shape[0] * SUB, LANES)
        return flat[pl.ds((levels + g) * MODEL_STEPS + row, 1), :]

    sweep(place_ref, wx_ref, wy_ref, x_ref, above_ref, below_ref, side_row, grad_ref)
    project_body(grad_ref, members_ref, wide_ref, thin_ref)


def project_body(grad_ref, members_ref, wide_ref, thin_ref):
    parts, own, levels, rows, cols = members_ref.shape
    count = parts * own

    def step(q, carry):
        carry = list(carry)
        for u in range(2):
            g = grad_ref[2 * q + u]
            for m in range(count):
                carry[m] = carry[m] + members_ref[m // own, m % own, 2 * q + u].astype(F32) * g
        return tuple(carry)

    total = lax.fori_loop(0, levels // 2, step, (jnp.zeros((rows, cols), F32),) * count)
    for m in range(count):
        wide_ref[m] = total[m]
        thin_ref[m] = total[m].astype(BF16)


def taper(offset):
    k = offset.astype(F32)
    w = (1.0 - (k / 17.0) * (k / 17.0)) * (1.0 / TAPER_TOTAL)
    return jnp.where(jnp.abs(offset) <= REACH, w, 0.0)


def halves(x):
    high = x.astype(BF16)
    return high, (x - high.astype(F32)).astype(BF16)


def sharp_dot(a, b):
    ah, al = halves(a)
    bh, bl = halves(b)
    dot = functools.partial(jnp.dot, preferred_element_type=F32)
    return dot(ah, bh) + dot(al, bh) + dot(ah, bl)


def columns_body(left_ref, mid_ref, right_ref, wide_ref, thin_ref):
    count, rows, cols = mid_ref.shape
    wide = jnp.concatenate(
        [r[...].astype(F32).reshape(count * rows, cols) for r in (left_ref, mid_ref, right_ref)], axis=1
    )
    shape = (3 * cols, wide_ref.shape[0] // count * cols)
    lane = lane_iota(shape)
    beside = lane % MODEL_STEPS + jnp.where(lane < cols + LANES // 2, -MODEL_STEPS, cols)
    target = jnp.where(lane < cols, lane, beside)
    out = sharp_dot(wide, taper(sub_iota(shape) - cols - target))
    for i in range(shape[1] // cols):
        part = out[:, i * cols : (i + 1) * cols].reshape(count, rows, cols)
        wide_ref[i * count : (i + 1) * count] = part
        thin_ref[i * count : (i + 1) * count] = part.astype(BF16)


def smooth_rows(above_ref, mid_ref, below_ref):
    count, rows, cols = mid_ref.shape
    tall = jnp.concatenate(
        [
            jnp.concatenate([above_ref[m].astype(F32), mid_ref[m], below_ref[m].astype(F32)], axis=0)
            for m in range(count)
        ],
        axis=1,
    )
    shape = (rows, 3 * rows)
    out = sharp_dot(taper(lane_iota(shape) - sub_iota(shape) - rows), tall)
    return [out[:, m * cols : (m + 1) * cols] for m in range(count)]


def increments(members_ref, local, emit):
    parts, own, levels, rows, cols = members_ref.shape

    def step(q, carry):
        for u in range(2):
            level = 2 * q + u
            total = members_ref[0, 0, level].astype(F32) * local[0]
            for m in range(1, parts * own):
                total = total + members_ref[m // own, m % own, level].astype(F32) * local[m]
            emit(level, total)
        return carry

    lax.fori_loop(0, levels // 2, step, 0)


def update_body(
    place_ref, members_ref, residual_ref, left_ref, right_ref, above_ref, mid_ref, below_ref, *refs
):
    *side_refs, analysis_ref, out_ref, beside_ref, top_ref, bottom_ref, local_ref = refs
    levels, rows, cols = residual_ref.shape
    parts, own = members_ref.shape[:2]
    count = parts * own
    local = smooth_rows(above_ref, mid_ref, below_ref)
    for m in range(count):
        local_ref[m] = local[count + m]

    def emit(level, value):
        analysis_ref[level] = value
        out_ref[level] = residual_ref[level] - RELAX * value

    increments(members_ref, local, emit)
    for g in range(levels // GROUP):
        total = jnp.zeros((rows, LANES), F32)
        for m in range(count):
            at = neighbor_of(place_ref, -(m // own)) * own + m % own
            total = total + side_refs[m // own][m % own, g].astype(F32) * local_ref[at]
        beside_ref[g] = left_ref[g, :rows] + right_ref[g, :rows] - RELAX * total
    pack_rows(out_ref, 0, top_ref, bottom_ref)
    pack_rows(beside_ref, levels // 2, top_ref, bottom_ref)


def final_body(members_ref, residual_ref, before_ref, above_ref, mid_ref, below_ref, analysis_ref, out_ref):
    local = smooth_rows(above_ref, mid_ref, below_ref)

    def emit(level, value):
        analysis_ref[level] = before_ref[level] + value
        out_ref[level] = residual_ref[level] - RELAX * value

    increments(members_ref, local, emit)


def per_device(residual_in, members, wind_x, wind_y):
    levels, rows, cols = residual_in.shape
    tiles = lax.axis_size("tile")
    parts = lax.axis_size("member")
    place = jnp.stack([lax.axis_index("tile"), jnp.int32(tiles), lax.axis_index("member"), jnp.int32(parts)])
    count = members.shape[0] * parts
    groups = levels // GROUP

    def shape(*dims, kind=F32):
        return jax.ShapeDtypeStruct(dims, kind)

    def both(*dims):
        return shape(*dims), shape(*dims, kind=BF16)

    def turned(x, step):
        return lax.ppermute(x, "member", [(i, (i + step) % parts) for i in range(parts)])

    def smoothed(wide, thin, planes):
        wide, thin = call(
            columns_body, both(planes, rows, cols), shift(thin, "member", 1), wide, shift(thin, "member", -1)
        )
        return shift(thin, "tile", 1), wide, shift(thin, "tile", -1)

    like = shape(levels, rows, cols)
    halo = shape((levels + groups) // 2, SUB, LANES)
    wind_x, wind_y = (jnp.broadcast_to(w[:, None], (levels, LANES)) for w in (wind_x, wind_y))

    soon, residual_in = lax.optimization_barrier((split_columns(members, parts), residual_in))
    block = lax.all_to_all(soon, "member", split_axis=0, concat_axis=0, tiled=True)
    top, bottom = edge_rows(residual_in)
    above, below = shift(bottom, "tile", 1), shift(top, "tile", -1)
    first, last = edge_columns(residual_in, above, below)
    left, right = shift(last, "member", 1), shift(first, "member", -1)
    members, first = lax.optimization_barrier((members, first))
    sides, left, right = lax.optimization_barrier((side_columns(place, members, parts), left, right))
    sides = [turned(x, r) if r else x for r, x in enumerate(sides)]
    grad = call(
        first_model_body, like,
        place, wind_x, wind_y, residual_in, left, right, above, below, in_specs=[SMEM] + [VMEM] * 7,
    )
    grad, sides = lax.optimization_barrier((grad, sides))
    wide, thin = call(project_body, both(count, rows, cols), grad, block)

    analysis, residual, beside, top, bottom = call(
        update_body, (like, like, shape(groups, rows, LANES), halo, halo),
        place, block, residual_in, left, right, *smoothed(wide, thin, 2 * count), *sides,
        in_specs=[SMEM] + [VMEM] * (7 + parts), scratch=[pltpu.VMEM((count, rows, cols), F32)],
    )
    above, below = shift(bottom, "tile", 1), shift(top, "tile", -1)
    wide, thin = call(
        second_model_body, both(count, rows, cols),
        place, wind_x, wind_y, residual, beside, above, below, block,
        in_specs=[SMEM] + [VMEM] * 7, scratch=[pltpu.VMEM((levels, rows, cols), F32)],
    )
    return call(final_body, (like, like), block, residual, analysis, *smoothed(wide, thin, count))


def solution(mesh):
    return jax.shard_map(
        per_device,
        mesh=mesh,
        in_specs=(P(None, "tile", "member"), P("member", None, "tile", None), P(), P()),
        out_specs=(P(None, "tile", "member"), P(None, "tile", "member")),
        check_vma=False,
    )
```

```python
import functools

import jax
import jax.numpy as jnp
from jax import lax
from jax.experimental import pallas as pl
from jax.experimental.pallas import tpu as pltpu
from jax.sharding import PartitionSpec as P

ITERS = 2
MODEL_STEPS = 4
DIFFUSION = 0.1
RELAX = 0.5
REACH = 16
TAPER_TOTAL = sum(1.0 - (k / 17.0) ** 2 for k in range(-REACH, REACH + 1))
F32 = jnp.float32
BF16 = jnp.bfloat16
LANES = 128
SUB = 8
GROUP = LANES // (2 * MODEL_STEPS)

VMEM = pl.BlockSpec(memory_space=pltpu.VMEM)
SMEM = pl.BlockSpec(memory_space=pltpu.SMEM)
PARAMS = pltpu.CompilerParams(vmem_limit_bytes=48 * 1024 * 1024)


def call(body, out_shape, *args, in_specs=None, scratch=()):
    return pl.pallas_call(
        body,
        out_shape=out_shape,
        in_specs=in_specs or [VMEM] * len(args),
        out_specs=jax.tree.map(lambda _: VMEM, out_shape),
        scratch_shapes=scratch,
        compiler_params=PARAMS,
    )(*args)


def lane_iota(shape):
    return lax.broadcasted_iota(jnp.int32, shape, len(shape) - 1)


def sub_iota(shape):
    return lax.broadcasted_iota(jnp.int32, shape, len(shape) - 2)


def neighbor_of(place_ref, step):
    member, parts = place_ref[2], place_ref[3]
    return lax.rem(member + parts + step, parts)


def early_body(in_ref, out_ref):
    parts, own, levels, rows, cols = out_ref.shape
    for c in range(parts):
        out_ref[c] = in_ref[:, :levels, :, c * cols : (c + 1) * cols]


def split_body(turns, early, place_ref, in_ref, *out_refs):
    own, planes, rows, cols = out_refs[0].shape
    levels = in_ref.shape[1]
    late = levels - early
    slot = lane_iota((rows, LANES)) // MODEL_STEPS

    def block(step):
        return pl.ds(pl.multiple_of(neighbor_of(place_ref, step) * cols, cols), cols)

    for r, out_ref in zip(turns, out_refs):
        before, here, after = block(r - 1), block(r), block(r + 1)
        for m in range(own):
            out_ref[m, :late] = in_ref[m, early:, :, here]

            def step(g, carry):
                total = jnp.zeros((rows, LANES), F32)
                for k in range(GROUP):
                    left = in_ref[m, g * GROUP + k, :, before].astype(F32)
                    right = in_ref[m, g * GROUP + k, :, after].astype(F32)
                    total = jnp.where(slot == k, pltpu.roll(left, MODEL_STEPS * (k + 1), 1), total)
                    total = jnp.where(slot == GROUP + k, pltpu.roll(right, MODEL_STEPS * (GROUP + k), 1), total)
                out_ref[m, late + g] = total.astype(out_ref.dtype)
                return carry

            lax.fori_loop(0, levels // GROUP, step, 0)


def split_early(members, parts, early):
    own, levels, rows, ny = members.shape
    return call(early_body, jax.ShapeDtypeStruct((parts, own, early, rows, ny // parts), members.dtype), members)


def split_late(place, members, parts, early):
    own, levels, rows, ny = members.shape
    out = jax.ShapeDtypeStruct((own, levels - early + levels // GROUP, rows, ny // parts), members.dtype)
    body = functools.partial(split_body, range(parts), early)
    return call(body, (out,) * parts, place, members, in_specs=[SMEM, VMEM])


def third_tile(below, above, odd):
    upper = sub_iota((SUB, LANES)) < MODEL_STEPS
    if odd:
        return jnp.where(upper, pltpu.roll(below, MODEL_STEPS, 0), above)
    return jnp.where(upper, below, pltpu.roll(above, MODEL_STEPS, 0))


def pack_rows(ref, at, top_ref, bottom_ref):
    upper = sub_iota((SUB, LANES)) < MODEL_STEPS
    count, rows, _ = ref.shape
    for q in range(count // 2):
        top_ref[at + q] = jnp.where(upper, ref[2 * q, :SUB], pltpu.roll(ref[2 * q + 1, :SUB], MODEL_STEPS, 0))
        bottom_ref[at + q] = jnp.where(
            upper, pltpu.roll(ref[2 * q, rows - SUB :], MODEL_STEPS, 0), ref[2 * q + 1, rows - SUB :]
        )


def rows_body(x_ref, top_ref, bottom_ref):
    pack_rows(x_ref, 0, top_ref, bottom_ref)


def edge_rows(x):
    out = jax.ShapeDtypeStruct((x.shape[0] // 2, SUB, LANES), F32)
    return call(rows_body, (out, out), x)


def columns_edge_body(x_ref, above_ref, below_ref, first_ref, last_ref):
    levels, rows, cols = x_ref.shape
    slot = lane_iota((rows + SUB, LANES)) // MODEL_STEPS

    def step(g, carry):
        first = jnp.zeros((rows + SUB, LANES), F32)
        last = jnp.zeros((rows + SUB, LANES), F32)
        for k in range(GROUP):
            level = g * GROUP + k
            pair = g * (GROUP // 2) + k // 2
            x = jnp.concatenate([x_ref[level], third_tile(below_ref[pair], above_ref[pair], k % 2)], axis=0)
            last = jnp.where(slot == k, pltpu.roll(x, MODEL_STEPS * (k + 1), 1), last)
            first = jnp.where(slot == GROUP + k, pltpu.roll(x, MODEL_STEPS * (GROUP + k), 1), first)
        first_ref[g] = first
        last_ref[g] = last
        return carry

    lax.fori_loop(0, levels // GROUP, step, 0)


def edge_columns(x, above, below):
    levels, rows, cols = x.shape
    out = jax.ShapeDtypeStruct((levels // GROUP, rows + SUB, LANES), F32)
    return call(columns_edge_body, (out, out), x, above, below)


def shift(x, axis, step):
    count = lax.axis_size(axis)
    pairs = [(i, i + step) for i in range(count) if 0 <= i + step < count]
    return lax.ppermute(x, axis, pairs)


def sweep_block(level_pair, x_ref, sides_ref, above_ref, below_ref, wx_ref, wy_ref, mask):
    rows = x_ref.shape[1]
    lanes = lane_iota((rows + SUB, LANES))
    ext_rows = rows + SUB
    ext_cols = 2 * LANES
    above = above_ref[level_pair]
    below = below_ref[level_pair]
    results = []
    for odd in range(2):
        level = 2 * level_pair + odd
        k = level % GROUP
        packed = sides_ref[level // GROUP]
        side_right = pltpu.roll(packed, (LANES + LANES // 2 - MODEL_STEPS * k) % LANES, 1)
        side_left = pltpu.roll(packed, LANES - MODEL_STEPS * (k + 1), 1)
        side = jnp.where(lanes < MODEL_STEPS, side_right, side_left)
        center = jnp.concatenate([x_ref[level], third_tile(below, above, odd)], axis=0)
        field = jnp.concatenate([center, side], axis=1) * mask
        wx = wx_ref[level]
        wy = wy_ref[level]
        own = 1.0 - 4.0 * DIFFUSION - wx - wy
        ahead_x = DIFFUSION + wx
        ahead_y = DIFFUSION + wy
        for _ in range(MODEL_STEPS):
            field = (
                own * field
                + ahead_x * pltpu.roll(field, ext_rows - 1, 0)
                + ahead_y * pltpu.roll(field, ext_cols - 1, 1)
                + DIFFUSION * (pltpu.roll(field, 1, 0) + pltpu.roll(field, 1, 1))
            ) * mask
        results.append(field[:rows, :LANES])
    return results


def block_mask(place_ref, rows, cols):
    tile, tiles, member, parts = (place_ref[i] for i in range(4))
    shape = (rows + SUB, 2 * LANES)
    r = sub_iota(shape)
    c = lane_iota(shape)
    r = jnp.where(r < rows + MODEL_STEPS, r, r - rows - SUB)
    near = (c < cols + MODEL_STEPS) | (c >= 2 * LANES - MODEL_STEPS)
    c = jnp.where(c < cols + MODEL_STEPS, c, c - 2 * LANES)
    gr = r + tile * rows
    gc = c + member * cols
    inside = (gr >= 0) & (gr < tiles * rows) & (gc >= 0) & (gc < parts * cols) & near
    return jnp.where(inside, 1.0, 0.0).astype(F32)


def first_model_body(place_ref, wx_ref, wy_ref, x_ref, left_ref, right_ref, above_ref, below_ref, grad_ref, sides_ref):
    levels, rows, cols = x_ref.shape
    mask = block_mask(place_ref, rows, cols)
    sides_ref[...] = left_ref[...] + right_ref[...]

    def step(q, carry):
        for u in range(2):
            pair = 2 * q + u
            for odd, value in enumerate(
                sweep_block(pair, x_ref, sides_ref, above_ref, below_ref, wx_ref, wy_ref, mask)
            ):
                grad_ref[2 * pair + odd] = value
        return carry

    lax.fori_loop(0, levels // 4, step, 0)


def second_model_body(
    place_ref, wx_ref, wy_ref, x_ref, beside_ref, above_ref, below_ref, *refs
):
    *others, grad_ref, sides_ref = refs
    levels, rows, cols = x_ref.shape
    groups = beside_ref.shape[0]
    mask = block_mask(place_ref, rows, cols)
    for g in range(groups):
        at = (levels + g) // 2
        sides_ref[g, :rows] = beside_ref[g]
        sides_ref[g, rows:] = third_tile(below_ref[at], above_ref[at], g % 2)

    def step(q, carry):
        for u in range(2):
            pair = 2 * q + u
            for odd, value in enumerate(
                sweep_block(pair, x_ref, sides_ref, above_ref, below_ref, wx_ref, wy_ref, mask)
            ):
                grad_ref[2 * pair + odd] = value
        return carry

    lax.fori_loop(0, levels // 4, step, 0)
    project_body(place_ref, grad_ref, *others)


def project_body(place_ref, grad_ref, first_ref, *refs):
    *late_refs, wide_ref, thin_ref = refs
    parts, own, early, rows, cols = first_ref.shape
    count = parts * own
    zeros = (jnp.zeros((rows, cols), F32),) * count

    def over(start, stop, member):
        def step(q, carry):
            carry = list(carry)
            for u in range(2):
                level = 2 * q + u
                g = grad_ref[start + level]
                for m in range(count):
                    carry[m] = carry[m] + member(m // own, m % own, level).astype(F32) * g
            return tuple(carry)

        return lax.fori_loop(0, (stop - start) // 2, step, zeros)

    total = over(0, early, lambda r, m, level: first_ref[r, m, level])
    for m in range(count):
        wide_ref[m] = total[m]
    total = over(early, grad_ref.shape[0], lambda r, m, level: late_refs[r][m, level])
    for m in range(count):
        at = neighbor_of(place_ref, -(m // own)) * own + m % own
        value = wide_ref[at] + total[m]
        wide_ref[at] = value
        thin_ref[at] = value.astype(BF16)


def taper(offset):
    k = offset.astype(F32)
    w = (1.0 - (k / 17.0) * (k / 17.0)) * (1.0 / TAPER_TOTAL)
    return jnp.where(jnp.abs(offset) <= REACH, w, 0.0)


def halves(x):
    high = x.astype(BF16)
    return high, (x - high.astype(F32)).astype(BF16)


def sharp_dot(a, b):
    ah, al = halves(a)
    bh, bl = halves(b)
    dot = functools.partial(jnp.dot, preferred_element_type=F32)
    return dot(ah, bh) + dot(al, bh) + dot(ah, bl)


def columns_body(left_ref, mid_ref, right_ref, wide_ref, thin_ref):
    count, rows, cols = mid_ref.shape
    wide = jnp.concatenate(
        [r[...].astype(F32).reshape(count * rows, cols) for r in (left_ref, mid_ref, right_ref)], axis=1
    )
    shape = (3 * cols, wide_ref.shape[0] // count * cols)
    lane = lane_iota(shape)
    beside = lane % MODEL_STEPS + jnp.where(lane < cols + LANES // 2, -MODEL_STEPS, cols)
    target = jnp.where(lane < cols, lane, beside)
    out = sharp_dot(wide, taper(sub_iota(shape) - cols - target))
    for i in range(shape[1] // cols):
        part = out[:, i * cols : (i + 1) * cols].reshape(count, rows, cols)
        wide_ref[i * count : (i + 1) * count] = part
        thin_ref[i * count : (i + 1) * count] = part.astype(BF16)


def smooth_rows(above_ref, mid_ref, below_ref):
    count, rows, cols = mid_ref.shape
    tall = jnp.concatenate(
        [
            jnp.concatenate([above_ref[m].astype(F32), mid_ref[m], below_ref[m].astype(F32)], axis=0)
            for m in range(count)
        ],
        axis=1,
    )
    shape = (rows, 3 * rows)
    out = sharp_dot(taper(lane_iota(shape) - sub_iota(shape) - rows), tall)
    return [out[:, m * cols : (m + 1) * cols] for m in range(count)]


def increments(place_ref, member_refs, local_ref, levels, emit):
    first_ref, *late_refs = member_refs
    parts, own, early, _, _ = first_ref.shape
    count = parts * own

    def over(start, stop, member, local):
        def step(q, carry):
            for u in range(2):
                level = 2 * q + u
                total = member(0, 0, level).astype(F32) * local[0]
                for m in range(1, count):
                    total = total + member(m // own, m % own, level).astype(F32) * local[m]
                emit(start + level, total)
            return carry

        lax.fori_loop(0, (stop - start) // 2, step, 0)

    over(0, early, lambda r, m, level: first_ref[r, m, level], [local_ref[m] for m in range(count)])
    turned = [local_ref[neighbor_of(place_ref, -(m // own)) * own + m % own] for m in range(count)]
    over(early, levels, lambda r, m, level: late_refs[r][m, level], turned)


def update_body(parts, place_ref, residual_ref, left_ref, right_ref, above_ref, mid_ref, below_ref, *refs):
    member_refs = refs[: parts + 1]
    analysis_ref, out_ref, beside_ref, top_ref, bottom_ref, local_ref = refs[parts + 1 :]
    levels, rows, cols = residual_ref.shape
    _, own, early, _, _ = member_refs[0].shape
    count = parts * own
    for m, value in enumerate(smooth_rows(above_ref, mid_ref, below_ref)):
        local_ref[m] = value

    def emit(level, value):
        analysis_ref[level] = value
        out_ref[level] = residual_ref[level] - RELAX * value

    increments(place_ref, member_refs, local_ref, levels, emit)
    for g in range(levels // GROUP):
        total = jnp.zeros((rows, LANES), F32)
        for m in range(count):
            at = neighbor_of(place_ref, -(m // own)) * own + m % own
            member = member_refs[1 + m // own][m % own, levels - early + g]
            total = total + member.astype(F32) * local_ref[count + at]
        beside_ref[g] = left_ref[g, :rows] + right_ref[g, :rows] - RELAX * total
    pack_rows(out_ref, 0, top_ref, bottom_ref)
    pack_rows(beside_ref, levels // 2, top_ref, bottom_ref)


def final_body(parts, place_ref, residual_ref, before_ref, above_ref, mid_ref, below_ref, *refs):
    member_refs = refs[: parts + 1]
    analysis_ref, out_ref, local_ref = refs[parts + 1 :]
    for m, value in enumerate(smooth_rows(above_ref, mid_ref, below_ref)):
        local_ref[m] = value

    def emit(level, value):
        analysis_ref[level] = before_ref[level] + value
        out_ref[level] = residual_ref[level] - RELAX * value

    increments(place_ref, member_refs, local_ref, residual_ref.shape[0], emit)


def per_device(residual_in, members, wind_x, wind_y):
    levels, rows, cols = residual_in.shape
    tiles = lax.axis_size("tile")
    parts = lax.axis_size("member")
    place = jnp.stack([lax.axis_index("tile"), jnp.int32(tiles), lax.axis_index("member"), jnp.int32(parts)])
    count = members.shape[0] * parts
    groups = levels // GROUP

    def shape(*dims, kind=F32):
        return jax.ShapeDtypeStruct(dims, kind)

    def both(*dims):
        return shape(*dims), shape(*dims, kind=BF16)

    def turned(x, step):
        return lax.ppermute(x, "member", [(i, (i + step) % parts) for i in range(parts)])

    def smoothed(wide, thin, planes):
        wide, thin = call(
            columns_body, both(planes, rows, cols), shift(thin, "member", 1), wide, shift(thin, "member", -1)
        )
        return shift(thin, "tile", 1), wide, shift(thin, "tile", -1)

    like = shape(levels, rows, cols)
    sides = [pltpu.VMEM((groups, rows + SUB, LANES), F32)]

    early = levels * 3 // 4
    soon, residual_in = lax.optimization_barrier((split_early(members, parts, early), residual_in))
    blocks = [lax.all_to_all(soon, "member", split_axis=0, concat_axis=0, tiled=True)]
    top, bottom = edge_rows(residual_in)
    above, below = shift(bottom, "tile", 1), shift(top, "tile", -1)
    first, last = edge_columns(residual_in, above, below)
    left, right = shift(last, "member", 1), shift(first, "member", -1)
    members, first = lax.optimization_barrier((members, first))
    later = split_late(place, members, parts, early)
    blocks += [turned(block, r) if r else block for r, block in enumerate(later)]
    grad = call(
        first_model_body, like,
        place, wind_x, wind_y, residual_in, left, right, above, below,
        in_specs=[SMEM] * 3 + [VMEM] * 5, scratch=sides,
    )
    wide, thin = call(
        project_body, both(count, rows, cols), place, grad, *blocks, in_specs=[SMEM] + [VMEM] * (2 + parts)
    )

    halo = shape((levels + groups) // 2, SUB, LANES)
    analysis, residual, beside, top, bottom = call(
        functools.partial(update_body, parts), (like, like, shape(groups, rows, LANES), halo, halo),
        place, residual_in, left, right, *smoothed(wide, thin, 2 * count), *blocks,
        in_specs=[SMEM] + [VMEM] * (7 + parts), scratch=[pltpu.VMEM((2 * count, rows, cols), F32)],
    )
    above, below = shift(bottom, "tile", 1), shift(top, "tile", -1)
    wide, thin = call(
        second_model_body, both(count, rows, cols),
        place, wind_x, wind_y, residual, beside, above, below, *blocks,
        in_specs=[SMEM] * 3 + [VMEM] * (5 + parts), scratch=[pltpu.VMEM((levels, rows, cols), F32)] + sides,
    )
    return call(
        functools.partial(final_body, parts), (like, like),
        place, residual, analysis, *smoothed(wide, thin, count), *blocks,
        in_specs=[SMEM] + [VMEM] * (6 + parts), scratch=[pltpu.VMEM((count, rows, cols), F32)],
    )


def solution(mesh):
    return jax.shard_map(
        per_device,
        mesh=mesh,
        in_specs=(P(None, "tile", "member"), P("member", None, "tile", None), P(), P()),
        out_specs=(P(None, "tile", "member"), P(None, "tile", "member")),
        check_vma=False,
    )
```

```python
import functools

import jax
import jax.numpy as jnp
from jax import lax
from jax.experimental import pallas as pl
from jax.experimental.pallas import tpu as pltpu
from jax.sharding import PartitionSpec as P

ITERS = 2
MODEL_STEPS = 4
DIFFUSION = 0.1
RELAX = 0.5
REACH = 16
TAPER_TOTAL = sum(1.0 - (k / 17.0) ** 2 for k in range(-REACH, REACH + 1))
F32 = jnp.float32
BF16 = jnp.bfloat16
LANES = 128
SUB = 8
GROUP = LANES // (2 * MODEL_STEPS)

VMEM = pl.BlockSpec(memory_space=pltpu.VMEM)
SMEM = pl.BlockSpec(memory_space=pltpu.SMEM)
PARAMS = pltpu.CompilerParams(vmem_limit_bytes=48 * 1024 * 1024)


def call(body, out_shape, *args, in_specs=None, scratch=()):
    return pl.pallas_call(
        body,
        out_shape=out_shape,
        in_specs=in_specs or [VMEM] * len(args),
        out_specs=jax.tree.map(lambda _: VMEM, out_shape),
        scratch_shapes=scratch,
        compiler_params=PARAMS,
    )(*args)


def lane_iota(shape):
    return lax.broadcasted_iota(jnp.int32, shape, len(shape) - 1)


def sub_iota(shape):
    return lax.broadcasted_iota(jnp.int32, shape, len(shape) - 2)


def neighbor_of(place_ref, step):
    member, parts = place_ref[2], place_ref[3]
    return lax.rem(member + parts + step, parts)


def columns_split_body(in_ref, out_ref):
    parts, own, levels, rows, cols = out_ref.shape
    for c in range(parts):
        out_ref[c] = in_ref[:, :, :, c * cols : (c + 1) * cols]


def split_columns(members, parts):
    own, levels, rows, ny = members.shape
    out = jax.ShapeDtypeStruct((parts, own, levels, rows, ny // parts), members.dtype)
    return call(columns_split_body, out, members)


def put_left(x, k, total):
    here = lane_iota(x.shape) // MODEL_STEPS == GROUP - 1 - k
    return jnp.where(here, pltpu.roll(x, (MODEL_STEPS * (GROUP - k)) % LANES, 1), total)


def put_right(x, k, total):
    here = lane_iota(x.shape) // MODEL_STEPS == 2 * GROUP - 1 - k
    return jnp.where(here, pltpu.roll(x, (MODEL_STEPS * (2 * GROUP - 1 - k)) % LANES, 1), total)


def sides_body(place_ref, in_ref, *out_refs):
    own, groups, rows, _ = out_refs[0].shape
    cols = in_ref.shape[-1] // len(out_refs)

    def block(step):
        return pl.ds(pl.multiple_of(neighbor_of(place_ref, step) * cols, cols), cols)

    for r, out_ref in enumerate(out_refs):
        before, after = block(r - 1), block(r + 1)
        for m in range(own):

            def step(g, carry):
                total = jnp.zeros((rows, LANES), F32)
                for k in range(GROUP):
                    total = put_left(in_ref[m, g * GROUP + k, :, before].astype(F32), k, total)
                    total = put_right(in_ref[m, g * GROUP + k, :, after].astype(F32), k, total)
                out_ref[m, g] = total.astype(out_ref.dtype)
                return carry

            lax.fori_loop(0, groups, step, 0)


def side_columns(place, members, parts):
    own, levels, rows, ny = members.shape
    out = jax.ShapeDtypeStruct((own, levels // GROUP, rows, LANES), members.dtype)
    return call(sides_body, (out,) * parts, place, members, in_specs=[SMEM, VMEM])


def third_tile(below, above, odd):
    upper = sub_iota((SUB, LANES)) < MODEL_STEPS
    if odd:
        return jnp.where(upper, pltpu.roll(below, MODEL_STEPS, 0), above)
    return jnp.where(upper, below, pltpu.roll(above, MODEL_STEPS, 0))


def pack_rows(ref, at, top_ref, bottom_ref):
    upper = sub_iota((SUB, LANES)) < MODEL_STEPS
    count, rows, _ = ref.shape
    for q in range(count // 2):
        top_ref[at + q] = jnp.where(upper, ref[2 * q, :SUB], pltpu.roll(ref[2 * q + 1, :SUB], MODEL_STEPS, 0))
        bottom_ref[at + q] = jnp.where(
            upper, pltpu.roll(ref[2 * q, rows - SUB :], MODEL_STEPS, 0), ref[2 * q + 1, rows - SUB :]
        )


def rows_body(x_ref, top_ref, bottom_ref):
    pack_rows(x_ref, 0, top_ref, bottom_ref)


def edge_rows(x):
    out = jax.ShapeDtypeStruct((x.shape[0] // 2, SUB, LANES), F32)
    return call(rows_body, (out, out), x)


def columns_edge_body(x_ref, above_ref, below_ref, edges_ref):
    levels, rows, cols = x_ref.shape

    def step(g, carry):
        first = jnp.zeros((rows + SUB, LANES), F32)
        last = jnp.zeros((rows + SUB, LANES), F32)
        for k in range(GROUP):
            level = g * GROUP + k
            pair = g * (GROUP // 2) + k // 2
            x = jnp.concatenate([x_ref[level], third_tile(below_ref[pair], above_ref[pair], k % 2)], axis=0)
            last = put_left(x, k, last)
            first = put_right(x, k, first)
        edges_ref[0, g] = first
        edges_ref[1, g] = last
        return carry

    lax.fori_loop(0, levels // GROUP, step, 0)


def edge_columns(x, above, below):
    levels, rows, cols = x.shape
    out = jax.ShapeDtypeStruct((2, levels // GROUP, rows + SUB, LANES), F32)
    return call(columns_edge_body, out, x, above, below)


def shift(x, axis, step):
    count = lax.axis_size(axis)
    pairs = [(i, i + step) for i in range(count) if 0 <= i + step < count]
    return lax.ppermute(x, axis, pairs)


def sweep(place_ref, wx_ref, wy_ref, x_ref, above_ref, below_ref, side_row, grad_ref):
    levels, rows, cols = x_ref.shape
    tile, tiles, member, parts = (place_ref[i] for i in range(4))
    x_flat = x_ref.reshape(levels * rows, cols)
    grad_flat = grad_ref.reshape(levels * rows, cols)
    halo = MODEL_STEPS
    pairs = above_ref.shape[0]
    above_flat = above_ref.reshape(pairs * SUB, LANES)
    below_flat = below_ref.reshape(pairs * SUB, LANES)

    lane = lane_iota((SUB, LANES))
    on_right = lane < halo
    is_first = lane == 0
    is_last = lane == LANES - 1
    inside = (on_right & (member < parts - 1)) | ((lane >= LANES - halo) & (member > 0))
    side_mask = jnp.where(inside, 1.0, 0.0).astype(F32)
    has_above = jnp.where(tile > 0, 1.0, 0.0).astype(F32)
    has_below = jnp.where(tile < tiles - 1, 1.0, 0.0).astype(F32)

    def load(g, half, e):
        q = 2 * g + half
        if e < 0:
            center = above_flat[pl.ds(q * SUB * halo + e + halo, SUB, stride=halo), :]
        elif e < rows:
            center = x_flat[pl.ds(q * SUB * rows + e, SUB, stride=rows), :]
        else:
            center = below_flat[pl.ds(q * SUB * halo + e - rows, SUB, stride=halo), :]
        row = jnp.broadcast_to(side_row(g, e), (SUB, LANES))
        start = halo * SUB * half
        right = pltpu.roll(row, start + halo, 1, stride=halo, stride_axis=0)
        left = pltpu.roll(row, start + LANES // 2, 1, stride=halo, stride_axis=0)
        return center, jnp.where(on_right, right, left) * side_mask

    def advance(before, here, after, e, own, ahead_x, ahead_y):
        center, side = here
        fore_c, fore_s = pltpu.roll(center, LANES - 1, 1), pltpu.roll(side, LANES - 1, 1)
        back_c, back_s = pltpu.roll(center, 1, 1), pltpu.roll(side, 1, 1)
        result = []
        for i, mine, fore, back in (
            (0, center, jnp.where(is_last, fore_s, fore_c), jnp.where(is_first, back_s, back_c)),
            (1, side, jnp.where(is_last, fore_c, fore_s), jnp.where(is_first, back_c, back_s)),
        ):
            value = own * mine + ahead_x * after[i] + ahead_y * fore + DIFFUSION * (before[i] + back)
            if e < 0:
                value = value * has_above
            if e >= rows:
                value = value * has_below
            result.append(value * side_mask if i else value)
        return tuple(result)

    def group(g, carry):
        for half in range(2):
            at = pl.ds(pl.multiple_of((2 * g + half) * SUB, SUB), SUB)
            wx, wy = wx_ref[at, :], wy_ref[at, :]
            coefficients = (1.0 - 4.0 * DIFFUSION - wx - wy, DIFFUSION + wx, DIFFUSION + wy)
            fields = [{} for _ in range(halo + 1)]
            for front in range(-halo, rows + halo):
                fields[0][front] = load(g, half, front)
                for n in range(1, halo + 1):
                    e = front - n
                    if -halo + n <= e < rows + halo - n:
                        old = fields[n - 1]
                        fields[n][e] = advance(old[e - 1], old[e], old[e + 1], e, *coefficients)
                        if n == halo:
                            grad_flat[pl.ds((2 * g + half) * SUB * rows + e, SUB, stride=rows), :] = fields[n][e][0]
        return carry

    lax.fori_loop(0, levels // GROUP, group, 0)


def first_model_body(
    place_ref, wx_ref, wy_ref, x_ref, edges_ref, above_ref, below_ref, grad_ref, beside_ref
):
    rows = x_ref.shape[1]
    member, parts = place_ref[2], place_ref[3]
    has_left = jnp.where(member > 0, 1.0, 0.0).astype(F32)
    has_right = jnp.where(member < parts - 1, 1.0, 0.0).astype(F32)
    left = edges_ref[jnp.maximum(member - 1, 0), 1]
    right = edges_ref[jnp.minimum(member + 1, parts - 1), 0]
    beside_ref[...] = left * has_left + right * has_right

    def side_row(g, e):
        return beside_ref[g, pl.ds(e if e >= 0 else rows + SUB + e, 1), :]

    sweep(place_ref, wx_ref, wy_ref, x_ref, above_ref, below_ref, side_row, grad_ref)


def second_model_body(
    place_ref, wx_ref, wy_ref, x_ref, beside_ref, above_ref, below_ref, members_ref, wide_ref, thin_ref, grad_ref
):
    levels, rows, cols = x_ref.shape

    def side_row(g, e):
        if 0 <= e < rows:
            return beside_ref[g, pl.ds(e, 1), :]
        ref, row = (above_ref, e + MODEL_STEPS) if e < 0 else (below_ref, e - rows)
        flat = ref.reshape(ref.shape[0] * SUB, LANES)
        return flat[pl.ds((levels + g) * MODEL_STEPS + row, 1), :]

    sweep(place_ref, wx_ref, wy_ref, x_ref, above_ref, below_ref, side_row, grad_ref)
    project_body(grad_ref, members_ref, wide_ref, thin_ref)


def project_body(grad_ref, members_ref, wide_ref, thin_ref):
    parts, own, levels, rows, cols = members_ref.shape
    count = parts * own

    def step(q, carry):
        carry = list(carry)
        for u in range(2):
            g = grad_ref[2 * q + u]
            for m in range(count):
                carry[m] = carry[m] + members_ref[m // own, m % own, 2 * q + u].astype(F32) * g
        return tuple(carry)

    total = lax.fori_loop(0, levels // 2, step, (jnp.zeros((rows, cols), F32),) * count)
    for m in range(count):
        wide_ref[m] = total[m]
        thin_ref[m] = total[m].astype(BF16)


def taper(offset):
    k = offset.astype(F32)
    w = (1.0 - (k / 17.0) * (k / 17.0)) * (1.0 / TAPER_TOTAL)
    return jnp.where(jnp.abs(offset) <= REACH, w, 0.0)


def halves(x):
    high = x.astype(BF16)
    return high, (x - high.astype(F32)).astype(BF16)


def sharp_dot(a, b):
    ah, al = halves(a)
    bh, bl = halves(b)
    dot = functools.partial(jnp.dot, preferred_element_type=F32)
    return dot(ah, bh) + dot(al, bh) + dot(ah, bl)


def columns_body(left_ref, mid_ref, right_ref, wide_ref, thin_ref):
    count, rows, cols = mid_ref.shape
    wide = jnp.concatenate(
        [r[...].astype(F32).reshape(count * rows, cols) for r in (left_ref, mid_ref, right_ref)], axis=1
    )
    shape = (3 * cols, wide_ref.shape[0] // count * cols)
    lane = lane_iota(shape)
    beside = lane % MODEL_STEPS + jnp.where(lane < cols + LANES // 2, -MODEL_STEPS, cols)
    target = jnp.where(lane < cols, lane, beside)
    out = sharp_dot(wide, taper(sub_iota(shape) - cols - target))
    for i in range(shape[1] // cols):
        part = out[:, i * cols : (i + 1) * cols].reshape(count, rows, cols)
        wide_ref[i * count : (i + 1) * count] = part
        thin_ref[i * count : (i + 1) * count] = part.astype(BF16)


def smooth_rows(above_ref, mid_ref, below_ref):
    count, rows, cols = mid_ref.shape
    tall = jnp.concatenate(
        [
            jnp.concatenate([above_ref[m].astype(F32), mid_ref[m], below_ref[m].astype(F32)], axis=0)
            for m in range(count)
        ],
        axis=1,
    )
    shape = (rows, 3 * rows)
    out = sharp_dot(taper(lane_iota(shape) - sub_iota(shape) - rows), tall)
    return [out[:, m * cols : (m + 1) * cols] for m in range(count)]


def increments(members_ref, local, emit):
    parts, own, levels, rows, cols = members_ref.shape

    def step(q, carry):
        for u in range(2):
            level = 2 * q + u
            total = members_ref[0, 0, level].astype(F32) * local[0]
            for m in range(1, parts * own):
                total = total + members_ref[m // own, m % own, level].astype(F32) * local[m]
            emit(level, total)
        return carry

    lax.fori_loop(0, levels // 2, step, 0)


def update_body(
    place_ref, members_ref, residual_ref, around_ref, above_ref, mid_ref, below_ref, *refs
):
    *side_refs, analysis_ref, out_ref, beside_ref, top_ref, bottom_ref, local_ref = refs
    levels, rows, cols = residual_ref.shape
    parts, own = members_ref.shape[:2]
    count = parts * own
    local = smooth_rows(above_ref, mid_ref, below_ref)
    for m in range(count):
        local_ref[m] = local[count + m]

    def emit(level, value):
        analysis_ref[level] = value
        out_ref[level] = residual_ref[level] - RELAX * value

    increments(members_ref, local, emit)
    for g in range(levels // GROUP):
        total = jnp.zeros((rows, LANES), F32)
        for m in range(count):
            at = neighbor_of(place_ref, -(m // own)) * own + m % own
            total = total + side_refs[m // own][m % own, g].astype(F32) * local_ref[at]
        beside_ref[g] = around_ref[g, :rows] - RELAX * total
    pack_rows(out_ref, 0, top_ref, bottom_ref)
    pack_rows(beside_ref, levels // 2, top_ref, bottom_ref)


def final_body(members_ref, residual_ref, before_ref, above_ref, mid_ref, below_ref, analysis_ref, out_ref):
    local = smooth_rows(above_ref, mid_ref, below_ref)

    def emit(level, value):
        analysis_ref[level] = before_ref[level] + value
        out_ref[level] = residual_ref[level] - RELAX * value

    increments(members_ref, local, emit)


def per_device(residual_in, members, wind_x, wind_y):
    levels, rows, cols = residual_in.shape
    tiles = lax.axis_size("tile")
    parts = lax.axis_size("member")
    place = jnp.stack([lax.axis_index("tile"), jnp.int32(tiles), lax.axis_index("member"), jnp.int32(parts)])
    count = members.shape[0] * parts
    groups = levels // GROUP

    def shape(*dims, kind=F32):
        return jax.ShapeDtypeStruct(dims, kind)

    def both(*dims):
        return shape(*dims), shape(*dims, kind=BF16)

    def turned(x, step):
        return lax.ppermute(x, "member", [(i, (i + step) % parts) for i in range(parts)])

    def smoothed(wide, thin, planes):
        wide, thin = call(
            columns_body, both(planes, rows, cols), shift(thin, "member", 1), wide, shift(thin, "member", -1)
        )
        return shift(thin, "tile", 1), wide, shift(thin, "tile", -1)

    like = shape(levels, rows, cols)
    halo = shape((levels + groups) // 2, SUB, LANES)
    wind_x, wind_y = (jnp.broadcast_to(w[:, None], (levels, LANES)) for w in (wind_x, wind_y))

    soon, residual_in = lax.optimization_barrier((split_columns(members, parts), residual_in))
    block = lax.all_to_all(soon, "member", split_axis=0, concat_axis=0, tiled=True)
    top, bottom = edge_rows(residual_in)
    above, below = shift(bottom, "tile", 1), shift(top, "tile", -1)
    edges = edge_columns(residual_in, above, below)
    members, edges = lax.optimization_barrier((members, edges))
    edges = lax.all_gather(edges, "member")
    sides = side_columns(place, members, parts)
    sides = [turned(x, r) if r else x for r, x in enumerate(sides)]
    grad, around = call(
        first_model_body, (like, shape(groups, rows + SUB, LANES)),
        place, wind_x, wind_y, residual_in, edges, above, below, in_specs=[SMEM] + [VMEM] * 6,
    )
    grad, sides = lax.optimization_barrier((grad, sides))
    wide, thin = call(project_body, both(count, rows, cols), grad, block)

    analysis, residual, beside, top, bottom = call(
        update_body, (like, like, shape(groups, rows, LANES), halo, halo),
        place, block, residual_in, around, *smoothed(wide, thin, 2 * count), *sides,
        in_specs=[SMEM] + [VMEM] * (6 + parts), scratch=[pltpu.VMEM((count, rows, cols), F32)],
    )
    above, below = shift(bottom, "tile", 1), shift(top, "tile", -1)
    wide, thin = call(
        second_model_body, both(count, rows, cols),
        place, wind_x, wind_y, residual, beside, above, below, block,
        in_specs=[SMEM] + [VMEM] * 7, scratch=[pltpu.VMEM((levels, rows, cols), F32)],
    )
    return call(final_body, (like, like), block, residual, analysis, *smoothed(wide, thin, count))


def solution(mesh):
    return jax.shard_map(
        per_device,
        mesh=mesh,
        in_specs=(P(None, "tile", "member"), P("member", None, "tile", None), P(), P()),
        out_specs=(P(None, "tile", "member"), P(None, "tile", "member")),
        check_vma=False,
    )
```

```python
import functools

import jax
import jax.numpy as jnp
from jax import lax
from jax.experimental import pallas as pl
from jax.experimental.pallas import tpu as pltpu
from jax.sharding import PartitionSpec as P

ITERS = 2
MODEL_STEPS = 4
DIFFUSION = 0.1
RELAX = 0.5
REACH = 16
TAPER_TOTAL = sum(1.0 - (k / 17.0) ** 2 for k in range(-REACH, REACH + 1))
F32 = jnp.float32
BF16 = jnp.bfloat16
LANES = 128
SUB = 8
GROUP = LANES // (2 * MODEL_STEPS)

VMEM = pl.BlockSpec(memory_space=pltpu.VMEM)
SMEM = pl.BlockSpec(memory_space=pltpu.SMEM)
PARAMS = pltpu.CompilerParams(vmem_limit_bytes=48 * 1024 * 1024)


def call(body, out_shape, *args, in_specs=None, scratch=()):
    return pl.pallas_call(
        body,
        out_shape=out_shape,
        in_specs=in_specs or [VMEM] * len(args),
        out_specs=jax.tree.map(lambda _: VMEM, out_shape),
        scratch_shapes=scratch,
        compiler_params=PARAMS,
    )(*args)


def lane_iota(shape):
    return lax.broadcasted_iota(jnp.int32, shape, len(shape) - 1)


def sub_iota(shape):
    return lax.broadcasted_iota(jnp.int32, shape, len(shape) - 2)


def neighbor_of(place_ref, step):
    member, parts = place_ref[2], place_ref[3]
    return lax.rem(member + parts + step, parts)


def columns_split_body(place_ref, in_ref, *out_refs):
    cols = out_refs[0].shape[-1]
    for r, out_ref in enumerate(out_refs):
        out_ref[...] = in_ref[:, :, :, pl.ds(pl.multiple_of(neighbor_of(place_ref, r) * cols, cols), cols)]


def split_columns(place, members, parts):
    own, levels, rows, ny = members.shape
    out = jax.ShapeDtypeStruct((own, levels, rows, ny // parts), members.dtype)
    return call(columns_split_body, (out,) * parts, place, members, in_specs=[SMEM, VMEM])


def left_slot(k):
    return 3 * SUB - 1 - k % SUB - GROUP * (k // SUB)


def put_left(x, k, total):
    here = lane_iota(x.shape) // MODEL_STEPS == left_slot(k)
    return jnp.where(here, pltpu.roll(x, (MODEL_STEPS * (left_slot(k) + 1)) % LANES, 1), total)


def put_right(x, k, total):
    here = lane_iota(x.shape) // MODEL_STEPS == left_slot(k) + SUB
    return jnp.where(here, pltpu.roll(x, MODEL_STEPS * (left_slot(k) + SUB), 1), total)


def sides_body(place_ref, in_ref, *out_refs):
    own, groups, rows, _ = out_refs[0].shape
    cols = in_ref.shape[-1] // len(out_refs)

    def block(step):
        return pl.ds(pl.multiple_of(neighbor_of(place_ref, step) * cols, cols), cols)

    for r, out_ref in enumerate(out_refs):
        before, after = block(r - 1), block(r + 1)
        for m in range(own):

            def step(g, carry):
                total = jnp.zeros((rows, LANES), F32)
                for k in range(GROUP):
                    total = put_left(in_ref[m, g * GROUP + k, :, before].astype(F32), k, total)
                    total = put_right(in_ref[m, g * GROUP + k, :, after].astype(F32), k, total)
                out_ref[m, g] = total.astype(out_ref.dtype)
                return carry

            lax.fori_loop(0, groups, step, 0)


def side_columns(place, members, parts):
    own, levels, rows, ny = members.shape
    out = jax.ShapeDtypeStruct((own, levels // GROUP, rows, LANES), members.dtype)
    return call(sides_body, (out,) * parts, place, members, in_specs=[SMEM, VMEM])


def pack_rows(ref, at, top_ref, bottom_ref):
    upper = sub_iota((SUB, LANES)) < MODEL_STEPS
    count, rows, _ = ref.shape
    for q in range(count // 2):
        top_ref[at + q] = jnp.where(upper, ref[2 * q, :SUB], pltpu.roll(ref[2 * q + 1, :SUB], MODEL_STEPS, 0))
        bottom_ref[at + q] = jnp.where(
            upper, pltpu.roll(ref[2 * q, rows - SUB :], MODEL_STEPS, 0), ref[2 * q + 1, rows - SUB :]
        )


def rows_body(x_ref, left_ref, right_ref, beside_ref, top_ref, bottom_ref):
    beside_ref[...] = left_ref[...] + right_ref[...]
    pack_rows(x_ref, 0, top_ref, bottom_ref)
    pack_rows(beside_ref, x_ref.shape[0] // 2, top_ref, bottom_ref)


def columns_edge_body(x_ref, first_ref, last_ref):
    levels, rows, cols = x_ref.shape
    for g in range(levels // GROUP):
        first = jnp.zeros((rows, LANES), F32)
        last = jnp.zeros((rows, LANES), F32)
        for k in range(GROUP):
            last = put_left(x_ref[g * GROUP + k], k, last)
            first = put_right(x_ref[g * GROUP + k], k, first)
        first_ref[g] = first
        last_ref[g] = last


def shift(x, axis, step):
    count = lax.axis_size(axis)
    pairs = [(i, i + step) for i in range(count) if 0 <= i + step < count]
    return lax.ppermute(x, axis, pairs)


def sweep(place_ref, wx_ref, wy_ref, x_ref, above_ref, below_ref, side_row, grad_ref):
    levels, rows, cols = x_ref.shape
    tile, tiles, member, parts = (place_ref[i] for i in range(4))
    x_flat = x_ref.reshape(levels * rows, cols)
    grad_flat = grad_ref.reshape(levels * rows, cols)
    halo = MODEL_STEPS
    pairs = above_ref.shape[0]
    above_flat = above_ref.reshape(pairs * SUB, LANES)
    below_flat = below_ref.reshape(pairs * SUB, LANES)

    half = LANES // 2
    lane = lane_iota((SUB, LANES))
    on_right = lane % half < halo
    first_of = (lane == 0, lane == half)
    last_of = (lane == LANES - 1, lane == half - 1)
    second = (lane >= half // 2) & (lane < half + half // 2)
    inside = (on_right & (member < parts - 1)) | ((lane % half >= half - halo) & (member > 0))
    side_mask = jnp.where(inside, 1.0, 0.0).astype(F32)
    has_above = jnp.where(tile > 0, 1.0, 0.0).astype(F32)
    has_below = jnp.where(tile < tiles - 1, 1.0, 0.0).astype(F32)

    def load(g, e):
        centers = []
        for q in (2 * g, 2 * g + 1):
            if e < 0:
                centers.append(above_flat[pl.ds(q * SUB * halo + e + halo, SUB, stride=halo), :])
            elif e < rows:
                centers.append(x_flat[pl.ds(q * SUB * rows + e, SUB, stride=rows), :])
            else:
                centers.append(below_flat[pl.ds(q * SUB * halo + e - rows, SUB, stride=halo), :])
        row = jnp.broadcast_to(side_row(g, e), (SUB, LANES))
        right = pltpu.roll(row, halo, 1, stride=halo, stride_axis=0)
        left = pltpu.roll(row, LANES // 4, 1, stride=halo, stride_axis=0)
        side = jnp.where(on_right, right, left) * side_mask
        return centers[0], pltpu.roll(centers[1], half, 1), side

    def advance(before, here, after, e, coefficients):
        fore = [pltpu.roll(x, LANES - 1, 1) for x in here]
        back = [pltpu.roll(x, 1, 1) for x in here]
        fore_side = jnp.where(last_of[0], fore[0], jnp.where(last_of[1], fore[1], fore[2]))
        back_side = jnp.where(first_of[0], back[0], jnp.where(first_of[1], back[1], back[2]))
        fores = [jnp.where(last_of[i], fore[2], fore[i]) for i in range(2)] + [fore_side]
        backs = [jnp.where(first_of[i], back[2], back[i]) for i in range(2)] + [back_side]
        result = []
        for i, (own, ahead_x, ahead_y) in enumerate(coefficients):
            value = own * here[i] + ahead_x * after[i] + ahead_y * fores[i] + DIFFUSION * (before[i] + backs[i])
            if e < 0:
                value = value * has_above
            if e >= rows:
                value = value * has_below
            result.append(value * side_mask if i == 2 else value)
        return tuple(result)

    def group(g, carry):
        coefficients = []
        for q in (2 * g, 2 * g + 1):
            at = pl.ds(pl.multiple_of(q * SUB, SUB), SUB)
            wx, wy = wx_ref[at, :], wy_ref[at, :]
            coefficients.append((1.0 - 4.0 * DIFFUSION - wx - wy, DIFFUSION + wx, DIFFUSION + wy))
        coefficients.append(tuple(jnp.where(second, b, a) for a, b in zip(*coefficients)))
        fields = [{} for _ in range(halo + 1)]
        for front in range(-halo, rows + halo):
            fields[0][front] = load(g, front)
            for n in range(1, halo + 1):
                e = front - n
                if -halo + n <= e < rows + halo - n:
                    old = fields[n - 1]
                    fields[n][e] = advance(old[e - 1], old[e], old[e + 1], e, coefficients)
            e = front - halo
            if 0 <= e < rows:
                grad_flat[pl.ds(2 * g * SUB * rows + e, SUB, stride=rows), :] = fields[halo][e][0]
                grad_flat[pl.ds((2 * g + 1) * SUB * rows + e, SUB, stride=rows), :] = pltpu.roll(fields[halo][e][1], half, 1)
        return carry

    lax.fori_loop(0, levels // GROUP, group, 0)


def side_rows(levels, rows, beside_ref, above_ref, below_ref):
    above_flat, below_flat = (ref.reshape(ref.shape[0] * SUB, LANES) for ref in (above_ref, below_ref))

    def side_row(g, e):
        if 0 <= e < rows:
            return beside_ref[g, pl.ds(e, 1), :]
        flat, row = (above_flat, e + MODEL_STEPS) if e < 0 else (below_flat, e - rows)
        return flat[pl.ds((levels + g) * MODEL_STEPS + row, 1), :]

    return side_row


def first_model_body(place_ref, wx_ref, wy_ref, x_ref, beside_ref, above_ref, below_ref, grad_ref):
    levels, rows, cols = x_ref.shape
    side_row = side_rows(levels, rows, beside_ref, above_ref, below_ref)
    sweep(place_ref, wx_ref, wy_ref, x_ref, above_ref, below_ref, side_row, grad_ref)


def second_model_body(place_ref, wx_ref, wy_ref, x_ref, beside_ref, above_thin_ref, below_thin_ref, *refs):
    *others, grad_ref, above_ref, below_ref = refs
    levels, rows, cols = x_ref.shape
    above_ref[...] = above_thin_ref[...].astype(F32).reshape(above_ref.shape)
    below_ref[...] = below_thin_ref[...].astype(F32).reshape(below_ref.shape)
    side_row = side_rows(levels, rows, beside_ref, above_ref, below_ref)
    sweep(place_ref, wx_ref, wy_ref, x_ref, above_ref, below_ref, side_row, grad_ref)
    project_body(place_ref, grad_ref, *others)


def project_body(place_ref, grad_ref, *refs):
    *member_refs, wide_ref, thin_ref = refs
    own, _, rows, cols = member_refs[0].shape
    count = len(member_refs) * own

    def step(q, carry):
        carry = list(carry)
        for u in range(2):
            g = grad_ref[2 * q + u]
            for m in range(count):
                carry[m] = carry[m] + member_refs[m // own][m % own, 2 * q + u].astype(F32) * g
        return tuple(carry)

    total = lax.fori_loop(0, grad_ref.shape[0] // 2, step, (jnp.zeros((rows, cols), F32),) * count)
    for m in range(count):
        at = neighbor_of(place_ref, -(m // own)) * own + m % own
        wide_ref[at] = total[m]
        thin_ref[at] = total[m].astype(BF16)


def taper(offset):
    k = offset.astype(F32)
    w = (1.0 - (k / 17.0) * (k / 17.0)) * (1.0 / TAPER_TOTAL)
    return jnp.where(jnp.abs(offset) <= REACH, w, 0.0)


def halves(x):
    high = x.astype(BF16)
    return high, (x - high.astype(F32)).astype(BF16)


def sharp_dot(a, b):
    ah, al = halves(a)
    bh, bl = halves(b)
    dot = functools.partial(jnp.dot, preferred_element_type=F32)
    return dot(ah, bh) + dot(al, bh) + dot(ah, bl)


def columns_body(left_ref, mid_ref, right_ref, wide_ref, thin_ref):
    count, rows, cols = mid_ref.shape
    wide = jnp.concatenate(
        [r[...].astype(F32).reshape(count * rows, cols) for r in (left_ref, mid_ref, right_ref)], axis=1
    )
    shape = (3 * cols, wide_ref.shape[0] // count * cols)
    lane = lane_iota(shape)
    beside = lane % MODEL_STEPS + jnp.where((lane // (SUB * MODEL_STEPS)) % 2 == 0, -MODEL_STEPS, cols)
    target = jnp.where(lane < cols, lane, beside)
    out = sharp_dot(wide, taper(sub_iota(shape) - cols - target))
    for i in range(shape[1] // cols):
        part = out[:, i * cols : (i + 1) * cols].reshape(count, rows, cols)
        wide_ref[i * count : (i + 1) * count] = part
        thin_ref[i * count : (i + 1) * count] = part.astype(BF16)


def smooth_rows(above_ref, mid_ref, below_ref):
    count, rows, cols = mid_ref.shape
    tall = jnp.concatenate(
        [
            jnp.concatenate([above_ref[m].astype(F32), mid_ref[m], below_ref[m].astype(F32)], axis=0)
            for m in range(count)
        ],
        axis=1,
    )
    shape = (rows, 3 * rows)
    out = sharp_dot(taper(lane_iota(shape) - sub_iota(shape) - rows), tall)
    return [out[:, m * cols : (m + 1) * cols] for m in range(count)]


def increments(place_ref, member_refs, local_ref, levels, emit):
    own = member_refs[0].shape[0]
    count = len(member_refs) * own
    local = [local_ref[neighbor_of(place_ref, -(m // own)) * own + m % own] for m in range(count)]

    def step(q, carry):
        for u in range(2):
            level = 2 * q + u
            total = member_refs[0][0, level].astype(F32) * local[0]
            for m in range(1, count):
                total = total + member_refs[m // own][m % own, level].astype(F32) * local[m]
            emit(level, total)
        return carry

    lax.fori_loop(0, levels // 2, step, 0)


def update_body(parts, place_ref, residual_ref, around_ref, above_ref, mid_ref, below_ref, *refs):
    member_refs, side_refs = refs[:parts], refs[parts : 2 * parts]
    analysis_ref, out_ref, beside_ref, top_ref, bottom_ref, local_ref, top_wide_ref, bottom_wide_ref = refs[2 * parts :]
    levels, rows, cols = residual_ref.shape
    own = member_refs[0].shape[0]
    count = parts * own
    for m, value in enumerate(smooth_rows(above_ref, mid_ref, below_ref)):
        local_ref[m] = value

    def emit(level, value):
        analysis_ref[level] = value
        out_ref[level] = residual_ref[level] - RELAX * value

    increments(place_ref, member_refs, local_ref, levels, emit)
    for g in range(levels // GROUP):
        total = jnp.zeros((rows, LANES), F32)
        for m in range(count):
            at = neighbor_of(place_ref, -(m // own)) * own + m % own
            total = total + side_refs[m // own][m % own, g].astype(F32) * local_ref[count + at]
        beside_ref[g] = around_ref[g] - RELAX * total
    pack_rows(out_ref, 0, top_wide_ref, bottom_wide_ref)
    pack_rows(beside_ref, levels // 2, top_wide_ref, bottom_wide_ref)
    top_ref[...] = top_wide_ref[...].reshape(top_ref.shape).astype(BF16)
    bottom_ref[...] = bottom_wide_ref[...].reshape(bottom_ref.shape).astype(BF16)


def final_body(parts, place_ref, residual_ref, before_ref, above_ref, mid_ref, below_ref, *refs):
    member_refs = refs[:parts]
    analysis_ref, out_ref, local_ref = refs[parts:]
    for m, value in enumerate(smooth_rows(above_ref, mid_ref, below_ref)):
        local_ref[m] = value

    def emit(level, value):
        analysis_ref[level] = before_ref[level] + value
        out_ref[level] = residual_ref[level] - RELAX * value

    increments(place_ref, member_refs, local_ref, residual_ref.shape[0], emit)


def per_device(residual_in, members, wind_x, wind_y):
    levels, rows, cols = residual_in.shape
    tiles = lax.axis_size("tile")
    parts = lax.axis_size("member")
    place = jnp.stack([lax.axis_index("tile"), jnp.int32(tiles), lax.axis_index("member"), jnp.int32(parts)])
    count = members.shape[0] * parts
    groups = levels // GROUP

    def shape(*dims, kind=F32):
        return jax.ShapeDtypeStruct(dims, kind)

    def both(*dims):
        return shape(*dims), shape(*dims, kind=BF16)

    def turned(x, step):
        return lax.ppermute(x, "member", [(i, (i + step) % parts) for i in range(parts)])

    def smoothed(wide, thin, planes):
        wide, thin = call(
            columns_body, both(planes, rows, cols), shift(thin, "member", 1), wide, shift(thin, "member", -1)
        )
        return shift(thin, "tile", 1), wide, shift(thin, "tile", -1)

    like = shape(levels, rows, cols)
    halo = shape((levels + groups) // 2, SUB, LANES)
    thin_halo = shape((levels + groups) // 4, 2 * SUB, LANES, kind=BF16)
    wide_halo = [pltpu.VMEM(halo.shape, F32)] * 2
    packed = shape(groups, rows, LANES)
    wind_x, wind_y = (jnp.broadcast_to(w[:, None], (levels, LANES)) for w in (wind_x, wind_y))

    first, last = call(columns_edge_body, (packed, packed), residual_in)
    left, right = shift(last, "member", 1), shift(first, "member", -1)
    blocks, left, right = lax.optimization_barrier((split_columns(place, members, parts), left, right))
    blocks = [turned(x, r) if r else x for r, x in enumerate(blocks)]
    around, top, bottom = call(rows_body, (packed, halo, halo), residual_in, left, right)
    members, around = lax.optimization_barrier((members, around))
    sides = side_columns(place, members, parts)
    above, below = shift(bottom, "tile", 1), shift(top, "tile", -1)
    grad = call(
        first_model_body, like,
        place, wind_x, wind_y, residual_in, around, above, below, in_specs=[SMEM] + [VMEM] * 6,
    )
    grad, sides = lax.optimization_barrier((grad, sides))
    grad, sides = lax.optimization_barrier((grad, [turned(x, r) if r else x for r, x in enumerate(sides)]))
    wide, thin = call(
        project_body, both(count, rows, cols), place, grad, *blocks, in_specs=[SMEM] + [VMEM] * (1 + parts)
    )

    analysis, residual, beside, top, bottom = call(
        functools.partial(update_body, parts), (like, like, packed, thin_halo, thin_halo),
        place, residual_in, around, *smoothed(wide, thin, 2 * count), *blocks, *sides,
        in_specs=[SMEM] + [VMEM] * (5 + 2 * parts),
        scratch=[pltpu.VMEM((2 * count, rows, cols), F32)] + wide_halo,
    )
    above, below = shift(bottom, "tile", 1), shift(top, "tile", -1)
    wide, thin = call(
        second_model_body, both(count, rows, cols),
        place, wind_x, wind_y, residual, beside, above, below, *blocks,
        in_specs=[SMEM] + [VMEM] * (6 + parts), scratch=[pltpu.VMEM((levels, rows, cols), F32)] + wide_halo,
    )
    return call(
        functools.partial(final_body, parts), (like, like),
        place, residual, analysis, *smoothed(wide, thin, count), *blocks,
        in_specs=[SMEM] + [VMEM] * (5 + parts), scratch=[pltpu.VMEM((count, rows, cols), F32)],
    )


def solution(mesh):
    return jax.shard_map(
        per_device,
        mesh=mesh,
        in_specs=(P(None, "tile", "member"), P("member", None, "tile", None), P(), P()),
        out_specs=(P(None, "tile", "member"), P(None, "tile", "member")),
        check_vma=False,
    )
```

```python
import functools

import jax
import jax.numpy as jnp
from jax import lax
from jax.experimental import pallas as pl
from jax.experimental.pallas import tpu as pltpu
from jax.sharding import PartitionSpec as P

ITERS = 2
MODEL_STEPS = 4
DIFFUSION = 0.1
RELAX = 0.5
REACH = 16
TAPER_TOTAL = sum(1.0 - (k / 17.0) ** 2 for k in range(-REACH, REACH + 1))
F32 = jnp.float32
BF16 = jnp.bfloat16
LANES = 128
SUB = 8
GROUP = LANES // (2 * MODEL_STEPS)

VMEM = pl.BlockSpec(memory_space=pltpu.VMEM)
SMEM = pl.BlockSpec(memory_space=pltpu.SMEM)
PARAMS = pltpu.CompilerParams(vmem_limit_bytes=48 * 1024 * 1024)


def call(body, out_shape, *args, in_specs=None, scratch=()):
    return pl.pallas_call(
        body,
        out_shape=out_shape,
        in_specs=in_specs or [VMEM] * len(args),
        out_specs=jax.tree.map(lambda _: VMEM, out_shape),
        scratch_shapes=scratch,
        compiler_params=PARAMS,
    )(*args)


def lane_iota(shape):
    return lax.broadcasted_iota(jnp.int32, shape, len(shape) - 1)


def sub_iota(shape):
    return lax.broadcasted_iota(jnp.int32, shape, len(shape) - 2)


def neighbor_of(place_ref, step):
    member, parts = place_ref[2], place_ref[3]
    return lax.rem(member + parts + step, parts)


def columns_split_body(place_ref, in_ref, *out_refs):
    cols = out_refs[0].shape[-1]
    for r, out_ref in enumerate(out_refs):
        out_ref[...] = in_ref[:, :, :, pl.ds(pl.multiple_of(neighbor_of(place_ref, r) * cols, cols), cols)]


def split_columns(place, members, parts):
    own, levels, rows, ny = members.shape
    out = jax.ShapeDtypeStruct((own, levels, rows, ny // parts), members.dtype)
    return call(columns_split_body, (out,) * parts, place, members, in_specs=[SMEM, VMEM])


def left_slot(k):
    return 3 * SUB - 1 - k % SUB - GROUP * (k // SUB)


def put_left(x, k, total):
    here = lane_iota(x.shape) // MODEL_STEPS == left_slot(k)
    return jnp.where(here, pltpu.roll(x, (MODEL_STEPS * (left_slot(k) + 1)) % LANES, 1), total)


def put_right(x, k, total):
    here = lane_iota(x.shape) // MODEL_STEPS == left_slot(k) + SUB
    return jnp.where(here, pltpu.roll(x, MODEL_STEPS * (left_slot(k) + SUB), 1), total)


def sides_body(in_ref, out_ref):
    parts, own, groups, rows, _ = out_ref.shape
    cols = in_ref.shape[-1] // parts
    for r in range(parts):
        before, after = (pl.ds((r + parts + d) % parts * cols, cols) for d in (-1, 1))
        for m in range(own):

            def step(g, carry):
                total = jnp.zeros((rows, LANES), F32)
                for k in range(GROUP):
                    total = put_left(in_ref[m, g * GROUP + k, :, before].astype(F32), k, total)
                    total = put_right(in_ref[m, g * GROUP + k, :, after].astype(F32), k, total)
                out_ref[r, m, g] = total.astype(out_ref.dtype)
                return carry

            lax.fori_loop(0, groups, step, 0)


def side_columns(members, parts):
    own, levels, rows, ny = members.shape
    return call(sides_body, jax.ShapeDtypeStruct((parts, own, levels // GROUP, rows, LANES), members.dtype), members)


def pack_rows(ref, at, top_ref, bottom_ref):
    upper = sub_iota((SUB, LANES)) < MODEL_STEPS
    count, rows, _ = ref.shape
    for q in range(count // 2):
        top_ref[at + q] = jnp.where(upper, ref[2 * q, :SUB], pltpu.roll(ref[2 * q + 1, :SUB], MODEL_STEPS, 0))
        bottom_ref[at + q] = jnp.where(
            upper, pltpu.roll(ref[2 * q, rows - SUB :], MODEL_STEPS, 0), ref[2 * q + 1, rows - SUB :]
        )


def rows_body(x_ref, left_ref, right_ref, beside_ref, top_ref, bottom_ref):
    beside_ref[...] = left_ref[...] + right_ref[...]
    pack_rows(x_ref, 0, top_ref, bottom_ref)
    pack_rows(beside_ref, x_ref.shape[0] // 2, top_ref, bottom_ref)


def columns_edge_body(x_ref, first_ref, last_ref):
    levels, rows, cols = x_ref.shape
    for g in range(levels // GROUP):
        first = jnp.zeros((rows, LANES), F32)
        last = jnp.zeros((rows, LANES), F32)
        for k in range(GROUP):
            last = put_left(x_ref[g * GROUP + k], k, last)
            first = put_right(x_ref[g * GROUP + k], k, first)
        first_ref[g] = first
        last_ref[g] = last


def shift(x, axis, step):
    count = lax.axis_size(axis)
    pairs = [(i, i + step) for i in range(count) if 0 <= i + step < count]
    return lax.ppermute(x, axis, pairs)


def sweep(place_ref, wx_ref, wy_ref, x_ref, above_ref, below_ref, side_row, grad_ref):
    levels, rows, cols = x_ref.shape
    tile, tiles, member, parts = (place_ref[i] for i in range(4))
    x_flat = x_ref.reshape(levels * rows, cols)
    grad_flat = grad_ref.reshape(levels * rows, cols)
    halo = MODEL_STEPS
    pairs = above_ref.shape[0]
    above_flat = above_ref.reshape(pairs * SUB, LANES)
    below_flat = below_ref.reshape(pairs * SUB, LANES)

    half = LANES // 2
    lane = lane_iota((SUB, LANES))
    on_right = lane % half < halo
    first_of = (lane == 0, lane == half)
    last_of = (lane == LANES - 1, lane == half - 1)
    second = (lane >= half // 2) & (lane < half + half // 2)
    inside = (on_right & (member < parts - 1)) | ((lane % half >= half - halo) & (member > 0))
    side_mask = jnp.where(inside, 1.0, 0.0).astype(F32)
    has_above = jnp.where(tile > 0, 1.0, 0.0).astype(F32)
    has_below = jnp.where(tile < tiles - 1, 1.0, 0.0).astype(F32)

    def load(g, e):
        centers = []
        for q in (2 * g, 2 * g + 1):
            if e < 0:
                centers.append(above_flat[pl.ds(q * SUB * halo + e + halo, SUB, stride=halo), :])
            elif e < rows:
                centers.append(x_flat[pl.ds(q * SUB * rows + e, SUB, stride=rows), :])
            else:
                centers.append(below_flat[pl.ds(q * SUB * halo + e - rows, SUB, stride=halo), :])
        row = jnp.broadcast_to(side_row(g, e), (SUB, LANES))
        right = pltpu.roll(row, halo, 1, stride=halo, stride_axis=0)
        left = pltpu.roll(row, LANES // 4, 1, stride=halo, stride_axis=0)
        side = jnp.where(on_right, right, left) * side_mask
        return centers[0], pltpu.roll(centers[1], half, 1), side

    def advance(before, here, after, e, coefficients):
        fore = [pltpu.roll(x, LANES - 1, 1) for x in here]
        back = [pltpu.roll(x, 1, 1) for x in here]
        fore_side = jnp.where(last_of[0], fore[0], jnp.where(last_of[1], fore[1], fore[2]))
        back_side = jnp.where(first_of[0], back[0], jnp.where(first_of[1], back[1], back[2]))
        fores = [jnp.where(last_of[i], fore[2], fore[i]) for i in range(2)] + [fore_side]
        backs = [jnp.where(first_of[i], back[2], back[i]) for i in range(2)] + [back_side]
        result = []
        for i, (own, ahead_x, ahead_y) in enumerate(coefficients):
            value = own * here[i] + ahead_x * after[i] + ahead_y * fores[i] + DIFFUSION * (before[i] + backs[i])
            if e < 0:
                value = value * has_above
            if e >= rows:
                value = value * has_below
            result.append(value * side_mask if i == 2 else value)
        return tuple(result)

    def group(g, carry):
        coefficients = []
        for q in (2 * g, 2 * g + 1):
            at = pl.ds(pl.multiple_of(q * SUB, SUB), SUB)
            wx, wy = wx_ref[at, :], wy_ref[at, :]
            coefficients.append((1.0 - 4.0 * DIFFUSION - wx - wy, DIFFUSION + wx, DIFFUSION + wy))
        coefficients.append(tuple(jnp.where(second, b, a) for a, b in zip(*coefficients)))
        fields = [{} for _ in range(halo + 1)]
        for front in range(-halo, rows + halo):
            fields[0][front] = load(g, front)
            for n in range(1, halo + 1):
                e = front - n
                if -halo + n <= e < rows + halo - n:
                    old = fields[n - 1]
                    fields[n][e] = advance(old[e - 1], old[e], old[e + 1], e, coefficients)
            e = front - halo
            if 0 <= e < rows:
                grad_flat[pl.ds(2 * g * SUB * rows + e, SUB, stride=rows), :] = fields[halo][e][0]
                grad_flat[pl.ds((2 * g + 1) * SUB * rows + e, SUB, stride=rows), :] = pltpu.roll(fields[halo][e][1], half, 1)
        return carry

    lax.fori_loop(0, levels // GROUP, group, 0)


def side_rows(levels, rows, beside_ref, above_ref, below_ref):
    above_flat, below_flat = (ref.reshape(ref.shape[0] * SUB, LANES) for ref in (above_ref, below_ref))

    def side_row(g, e):
        if 0 <= e < rows:
            return beside_ref[g, pl.ds(e, 1), :]
        flat, row = (above_flat, e + MODEL_STEPS) if e < 0 else (below_flat, e - rows)
        return flat[pl.ds((levels + g) * MODEL_STEPS + row, 1), :]

    return side_row


def first_model_body(place_ref, wx_ref, wy_ref, x_ref, beside_ref, above_ref, below_ref, grad_ref):
    levels, rows, cols = x_ref.shape
    side_row = side_rows(levels, rows, beside_ref, above_ref, below_ref)
    sweep(place_ref, wx_ref, wy_ref, x_ref, above_ref, below_ref, side_row, grad_ref)


def second_model_body(place_ref, wx_ref, wy_ref, x_ref, beside_ref, above_thin_ref, below_thin_ref, *refs):
    *others, grad_ref, above_ref, below_ref = refs
    levels, rows, cols = x_ref.shape
    above_ref[...] = above_thin_ref[...].astype(F32).reshape(above_ref.shape)
    below_ref[...] = below_thin_ref[...].astype(F32).reshape(below_ref.shape)
    side_row = side_rows(levels, rows, beside_ref, above_ref, below_ref)
    sweep(place_ref, wx_ref, wy_ref, x_ref, above_ref, below_ref, side_row, grad_ref)
    project_body(place_ref, grad_ref, *others)


def project_body(place_ref, grad_ref, *refs):
    *member_refs, wide_ref, thin_ref = refs
    own, _, rows, cols = member_refs[0].shape
    count = len(member_refs) * own

    def step(q, carry):
        carry = list(carry)
        for u in range(2):
            g = grad_ref[2 * q + u]
            for m in range(count):
                carry[m] = carry[m] + member_refs[m // own][m % own, 2 * q + u].astype(F32) * g
        return tuple(carry)

    total = lax.fori_loop(0, grad_ref.shape[0] // 2, step, (jnp.zeros((rows, cols), F32),) * count)
    for m in range(count):
        at = neighbor_of(place_ref, -(m // own)) * own + m % own
        wide_ref[at] = total[m]
        thin_ref[at] = total[m].astype(BF16)


def taper(offset):
    k = offset.astype(F32)
    w = (1.0 - (k / 17.0) * (k / 17.0)) * (1.0 / TAPER_TOTAL)
    return jnp.where(jnp.abs(offset) <= REACH, w, 0.0)


def halves(x):
    high = x.astype(BF16)
    return high, (x - high.astype(F32)).astype(BF16)


def sharp_dot(a, b):
    ah, al = halves(a)
    bh, bl = halves(b)
    dot = functools.partial(jnp.dot, preferred_element_type=F32)
    return dot(ah, bh) + dot(al, bh) + dot(ah, bl)


def columns_body(left_ref, mid_ref, right_ref, wide_ref, thin_ref):
    count, rows, cols = mid_ref.shape
    wide = jnp.concatenate(
        [r[...].astype(F32).reshape(count * rows, cols) for r in (left_ref, mid_ref, right_ref)], axis=1
    )
    shape = (3 * cols, wide_ref.shape[0] // count * cols)
    lane = lane_iota(shape)
    beside = lane % MODEL_STEPS + jnp.where((lane // (SUB * MODEL_STEPS)) % 2 == 0, -MODEL_STEPS, cols)
    target = jnp.where(lane < cols, lane, beside)
    out = sharp_dot(wide, taper(sub_iota(shape) - cols - target))
    for i in range(shape[1] // cols):
        part = out[:, i * cols : (i + 1) * cols].reshape(count, rows, cols)
        wide_ref[i * count : (i + 1) * count] = part
        thin_ref[i * count : (i + 1) * count] = part.astype(BF16)


def smooth_rows(above_ref, mid_ref, below_ref):
    count, rows, cols = mid_ref.shape
    tall = jnp.concatenate(
        [
            jnp.concatenate([above_ref[m].astype(F32), mid_ref[m], below_ref[m].astype(F32)], axis=0)
            for m in range(count)
        ],
        axis=1,
    )
    shape = (rows, 3 * rows)
    out = sharp_dot(taper(lane_iota(shape) - sub_iota(shape) - rows), tall)
    return [out[:, m * cols : (m + 1) * cols] for m in range(count)]


def increments(place_ref, member_refs, local_ref, levels, emit):
    own = member_refs[0].shape[0]
    count = len(member_refs) * own
    local = [local_ref[neighbor_of(place_ref, -(m // own)) * own + m % own] for m in range(count)]

    def step(q, carry):
        for u in range(2):
            level = 2 * q + u
            total = member_refs[0][0, level].astype(F32) * local[0]
            for m in range(1, count):
                total = total + member_refs[m // own][m % own, level].astype(F32) * local[m]
            emit(level, total)
        return carry

    lax.fori_loop(0, levels // 2, step, 0)


def update_body(parts, place_ref, residual_ref, around_ref, above_ref, mid_ref, below_ref, *refs):
    member_refs, sides_ref = refs[:parts], refs[parts]
    analysis_ref, out_ref, beside_ref, top_ref, bottom_ref, local_ref, top_wide_ref, bottom_wide_ref = refs[parts + 1 :]
    levels, rows, cols = residual_ref.shape
    own = member_refs[0].shape[0]
    count = parts * own
    for m, value in enumerate(smooth_rows(above_ref, mid_ref, below_ref)):
        local_ref[m] = value

    def emit(level, value):
        analysis_ref[level] = value
        out_ref[level] = residual_ref[level] - RELAX * value

    increments(place_ref, member_refs, local_ref, levels, emit)
    for g in range(levels // GROUP):
        total = jnp.zeros((rows, LANES), F32)
        for m in range(count):
            total = total + sides_ref[m // own, m % own, g].astype(F32) * local_ref[count + m]
        beside_ref[g] = around_ref[g] - RELAX * total
    pack_rows(out_ref, 0, top_wide_ref, bottom_wide_ref)
    pack_rows(beside_ref, levels // 2, top_wide_ref, bottom_wide_ref)
    top_ref[...] = top_wide_ref[...].reshape(top_ref.shape).astype(BF16)
    bottom_ref[...] = bottom_wide_ref[...].reshape(bottom_ref.shape).astype(BF16)


def final_body(parts, place_ref, residual_ref, before_ref, above_ref, mid_ref, below_ref, *refs):
    member_refs = refs[:parts]
    analysis_ref, out_ref, local_ref = refs[parts:]
    for m, value in enumerate(smooth_rows(above_ref, mid_ref, below_ref)):
        local_ref[m] = value

    def emit(level, value):
        analysis_ref[level] = before_ref[level] + value
        out_ref[level] = residual_ref[level] - RELAX * value

    increments(place_ref, member_refs, local_ref, residual_ref.shape[0], emit)


def per_device(residual_in, members, wind_x, wind_y):
    levels, rows, cols = residual_in.shape
    tiles = lax.axis_size("tile")
    parts = lax.axis_size("member")
    place = jnp.stack([lax.axis_index("tile"), jnp.int32(tiles), lax.axis_index("member"), jnp.int32(parts)])
    count = members.shape[0] * parts
    groups = levels // GROUP

    def shape(*dims, kind=F32):
        return jax.ShapeDtypeStruct(dims, kind)

    def both(*dims):
        return shape(*dims), shape(*dims, kind=BF16)

    def turned(x, step):
        return lax.ppermute(x, "member", [(i, (i + step) % parts) for i in range(parts)])

    def smoothed(wide, thin, planes):
        wide, thin = call(
            columns_body, both(planes, rows, cols), shift(thin, "member", 1), wide, shift(thin, "member", -1)
        )
        return shift(thin, "tile", 1), wide, shift(thin, "tile", -1)

    like = shape(levels, rows, cols)
    halo = shape((levels + groups) // 2, SUB, LANES)
    thin_halo = shape((levels + groups) // 4, 2 * SUB, LANES, kind=BF16)
    wide_halo = [pltpu.VMEM(halo.shape, F32)] * 2
    packed = shape(groups, rows, LANES)
    wind_x, wind_y = (jnp.broadcast_to(w[:, None], (levels, LANES)) for w in (wind_x, wind_y))

    first, last = call(columns_edge_body, (packed, packed), residual_in)
    left, right = shift(last, "member", 1), shift(first, "member", -1)
    blocks, left, right = lax.optimization_barrier((split_columns(place, members, parts), left, right))
    blocks = [turned(x, r) if r else x for r, x in enumerate(blocks)]
    around, top, bottom = call(rows_body, (packed, halo, halo), residual_in, left, right)
    members, around = lax.optimization_barrier((members, around))
    sides = side_columns(members, parts)
    above, below = shift(bottom, "tile", 1), shift(top, "tile", -1)
    grad = call(
        first_model_body, like,
        place, wind_x, wind_y, residual_in, around, above, below, in_specs=[SMEM] + [VMEM] * 6,
    )
    grad, sides = lax.optimization_barrier((grad, sides))
    sides = lax.all_to_all(sides, "member", split_axis=0, concat_axis=0, tiled=True)
    grad, sides = lax.optimization_barrier((grad, sides))
    wide, thin = call(
        project_body, both(count, rows, cols), place, grad, *blocks, in_specs=[SMEM] + [VMEM] * (1 + parts)
    )

    analysis, residual, beside, top, bottom = call(
        functools.partial(update_body, parts), (like, like, packed, thin_halo, thin_halo),
        place, residual_in, around, *smoothed(wide, thin, 2 * count), *blocks, sides,
        in_specs=[SMEM] + [VMEM] * (6 + parts),
        scratch=[pltpu.VMEM((2 * count, rows, cols), F32)] + wide_halo,
    )
    above, below = shift(bottom, "tile", 1), shift(top, "tile", -1)
    wide, thin = call(
        second_model_body, both(count, rows, cols),
        place, wind_x, wind_y, residual, beside, above, below, *blocks,
        in_specs=[SMEM] + [VMEM] * (6 + parts), scratch=[pltpu.VMEM((levels, rows, cols), F32)] + wide_halo,
    )
    return call(
        functools.partial(final_body, parts), (like, like),
        place, residual, analysis, *smoothed(wide, thin, count), *blocks,
        in_specs=[SMEM] + [VMEM] * (5 + parts), scratch=[pltpu.VMEM((count, rows, cols), F32)],
    )


def solution(mesh):
    return jax.shard_map(
        per_device,
        mesh=mesh,
        in_specs=(P(None, "tile", "member"), P("member", None, "tile", None), P(), P()),
        out_specs=(P(None, "tile", "member"), P(None, "tile", "member")),
        check_vma=False,
    )
```

```python
import functools

import jax
import jax.numpy as jnp
from jax import lax
from jax.experimental import pallas as pl
from jax.experimental.pallas import tpu as pltpu
from jax.sharding import PartitionSpec as P

ITERS = 2
MODEL_STEPS = 4
DIFFUSION = 0.1
RELAX = 0.5
REACH = 16
TAPER_TOTAL = sum(1.0 - (k / 17.0) ** 2 for k in range(-REACH, REACH + 1))
F32 = jnp.float32
BF16 = jnp.bfloat16
LANES = 128
SUB = 8
GROUP = LANES // (2 * MODEL_STEPS)

VMEM = pl.BlockSpec(memory_space=pltpu.VMEM)
SMEM = pl.BlockSpec(memory_space=pltpu.SMEM)
PARAMS = pltpu.CompilerParams(vmem_limit_bytes=48 * 1024 * 1024)


def call(body, out_shape, *args, in_specs=None, scratch=()):
    return pl.pallas_call(
        body,
        out_shape=out_shape,
        in_specs=in_specs or [VMEM] * len(args),
        out_specs=jax.tree.map(lambda _: VMEM, out_shape),
        scratch_shapes=scratch,
        compiler_params=PARAMS,
    )(*args)


def lane_iota(shape):
    return lax.broadcasted_iota(jnp.int32, shape, len(shape) - 1)


def sub_iota(shape):
    return lax.broadcasted_iota(jnp.int32, shape, len(shape) - 2)


def neighbor_of(place_ref, step):
    member, parts = place_ref[2], place_ref[3]
    at = member + step
    return jnp.where(at < 0, at + parts, jnp.where(at >= parts, at - parts, at))


def left_slot(k):
    return 3 * SUB - 1 - k % SUB - GROUP * (k // SUB)


def put_left(x, k, total):
    here = lane_iota(x.shape) // MODEL_STEPS == left_slot(k)
    return jnp.where(here, pltpu.roll(x, (MODEL_STEPS * (left_slot(k) + 1)) % LANES, 1), total)


def put_right(x, k, total):
    here = lane_iota(x.shape) // MODEL_STEPS == left_slot(k) + SUB
    return jnp.where(here, pltpu.roll(x, MODEL_STEPS * (left_slot(k) + SUB), 1), total)


def sides_body(in_ref, out_ref):
    parts, own, groups, rows, _ = out_ref.shape
    cols = in_ref.shape[-1] // parts
    for r in range(parts):
        before, after = (pl.ds((r + parts + d) % parts * cols, cols) for d in (-1, 1))
        for m in range(own):

            def step(g, carry):
                total = jnp.zeros((rows, LANES), F32)
                for k in range(GROUP):
                    total = put_left(in_ref[m, g * GROUP + k, :, before].astype(F32), k, total)
                    total = put_right(in_ref[m, g * GROUP + k, :, after].astype(F32), k, total)
                out_ref[r, m, g] = total.astype(out_ref.dtype)
                return carry

            lax.fori_loop(0, groups, step, 0)


def side_columns(members, parts):
    own, levels, rows, ny = members.shape
    return call(sides_body, jax.ShapeDtypeStruct((parts, own, levels // GROUP, rows, LANES), members.dtype), members)


def pack_rows(ref, at, top_ref, bottom_ref):
    upper = sub_iota((SUB, LANES)) < MODEL_STEPS
    count, rows, _ = ref.shape
    for q in range(count // 2):
        top_ref[at + q] = jnp.where(upper, ref[2 * q, :SUB], pltpu.roll(ref[2 * q + 1, :SUB], MODEL_STEPS, 0))
        bottom_ref[at + q] = jnp.where(
            upper, pltpu.roll(ref[2 * q, rows - SUB :], MODEL_STEPS, 0), ref[2 * q + 1, rows - SUB :]
        )


def rows_body(x_ref, left_ref, right_ref, beside_ref, top_ref, bottom_ref):
    beside_ref[...] = left_ref[...] + right_ref[...]
    pack_rows(x_ref, 0, top_ref, bottom_ref)
    pack_rows(beside_ref, x_ref.shape[0] // 2, top_ref, bottom_ref)


def opening_body(place_ref, x_ref, members_ref, first_ref, last_ref, *block_refs):
    levels, rows, cols = x_ref.shape
    for g in range(levels // GROUP):
        first = jnp.zeros((rows, LANES), F32)
        last = jnp.zeros((rows, LANES), F32)
        for k in range(GROUP):
            last = put_left(x_ref[g * GROUP + k], k, last)
            first = put_right(x_ref[g * GROUP + k], k, first)
        first_ref[g] = first
        last_ref[g] = last
    for r, block_ref in enumerate(block_refs):
        at = pl.ds(pl.multiple_of(neighbor_of(place_ref, r) * cols, cols), cols)
        block_ref[...] = members_ref[:, :, :, at]


def shift(x, axis, step):
    count = lax.axis_size(axis)
    pairs = [(i, i + step) for i in range(count) if 0 <= i + step < count]
    return lax.ppermute(x, axis, pairs)


def sweep(place_ref, wx_ref, wy_ref, x_ref, above_ref, below_ref, side_row, grad_ref):
    levels, rows, cols = x_ref.shape
    tile, tiles, member, parts = (place_ref[i] for i in range(4))
    x_flat = x_ref.reshape(levels * rows, cols)
    grad_flat = grad_ref.reshape(levels * rows, cols)
    halo = MODEL_STEPS
    pairs = above_ref.shape[0]
    above_flat = above_ref.reshape(pairs * SUB, LANES)
    below_flat = below_ref.reshape(pairs * SUB, LANES)

    half = LANES // 2
    lane = lane_iota((SUB, LANES))
    on_right = lane % half < halo
    first_of = (lane == 0, lane == half)
    last_of = (lane == LANES - 1, lane == half - 1)
    second = (lane >= half // 2) & (lane < half + half // 2)
    inside = (on_right & (member < parts - 1)) | ((lane % half >= half - halo) & (member > 0))
    side_mask = jnp.where(inside, 1.0, 0.0).astype(F32)
    has_above = jnp.where(tile > 0, 1.0, 0.0).astype(F32)
    has_below = jnp.where(tile < tiles - 1, 1.0, 0.0).astype(F32)

    def load(g, e):
        centers = []
        for q in (2 * g, 2 * g + 1):
            if e < 0:
                centers.append(above_flat[pl.ds(q * SUB * halo + e + halo, SUB, stride=halo), :])
            elif e < rows:
                centers.append(x_flat[pl.ds(q * SUB * rows + e, SUB, stride=rows), :])
            else:
                centers.append(below_flat[pl.ds(q * SUB * halo + e - rows, SUB, stride=halo), :])
        row = jnp.broadcast_to(side_row(g, e), (SUB, LANES))
        right = pltpu.roll(row, halo, 1, stride=halo, stride_axis=0)
        left = pltpu.roll(row, LANES // 4, 1, stride=halo, stride_axis=0)
        side = jnp.where(on_right, right, left) * side_mask
        return centers[0], pltpu.roll(centers[1], half, 1), side

    def advance(before, here, after, e, coefficients):
        fore = [pltpu.roll(x, LANES - 1, 1) for x in here]
        back = [pltpu.roll(x, 1, 1) for x in here]
        fore_side = jnp.where(last_of[0], fore[0], jnp.where(last_of[1], fore[1], fore[2]))
        back_side = jnp.where(first_of[0], back[0], jnp.where(first_of[1], back[1], back[2]))
        fores = [jnp.where(last_of[i], fore[2], fore[i]) for i in range(2)] + [fore_side]
        backs = [jnp.where(first_of[i], back[2], back[i]) for i in range(2)] + [back_side]
        result = []
        for i, (own, ahead_x, ahead_y) in enumerate(coefficients):
            value = own * here[i] + ahead_x * after[i] + ahead_y * fores[i] + DIFFUSION * (before[i] + backs[i])
            if e < 0:
                value = value * has_above
            if e >= rows:
                value = value * has_below
            result.append(value * side_mask if i == 2 else value)
        return tuple(result)

    def group(g, carry):
        coefficients = []
        for q in (2 * g, 2 * g + 1):
            at = pl.ds(pl.multiple_of(q * SUB, SUB), SUB)
            wx, wy = wx_ref[at, :], wy_ref[at, :]
            coefficients.append((1.0 - 4.0 * DIFFUSION - wx - wy, DIFFUSION + wx, DIFFUSION + wy))
        coefficients.append(tuple(jnp.where(second, b, a) for a, b in zip(*coefficients)))
        fields = [{} for _ in range(halo + 1)]
        for front in range(-halo, rows + halo):
            fields[0][front] = load(g, front)
            for n in range(1, halo + 1):
                e = front - n
                if -halo + n <= e < rows + halo - n:
                    old = fields[n - 1]
                    fields[n][e] = advance(old[e - 1], old[e], old[e + 1], e, coefficients)
            e = front - halo
            if 0 <= e < rows:
                grad_flat[pl.ds(2 * g * SUB * rows + e, SUB, stride=rows), :] = fields[halo][e][0]
                grad_flat[pl.ds((2 * g + 1) * SUB * rows + e, SUB, stride=rows), :] = pltpu.roll(fields[halo][e][1], half, 1)
        return carry

    lax.fori_loop(0, levels // GROUP, group, 0)


def side_rows(levels, rows, beside_ref, above_ref, below_ref):
    above_flat, below_flat = (ref.reshape(ref.shape[0] * SUB, LANES) for ref in (above_ref, below_ref))

    def side_row(g, e):
        if 0 <= e < rows:
            return beside_ref[g, pl.ds(e, 1), :]
        flat, row = (above_flat, e + MODEL_STEPS) if e < 0 else (below_flat, e - rows)
        return flat[pl.ds((levels + g) * MODEL_STEPS + row, 1), :]

    return side_row


def first_model_body(place_ref, wx_ref, wy_ref, x_ref, beside_ref, above_ref, below_ref, grad_ref):
    levels, rows, cols = x_ref.shape
    side_row = side_rows(levels, rows, beside_ref, above_ref, below_ref)
    sweep(place_ref, wx_ref, wy_ref, x_ref, above_ref, below_ref, side_row, grad_ref)


def second_model_body(place_ref, wx_ref, wy_ref, x_ref, beside_ref, above_thin_ref, below_thin_ref, *refs):
    *others, grad_ref, above_ref, below_ref = refs
    levels, rows, cols = x_ref.shape
    above_ref[...] = above_thin_ref[...].astype(F32).reshape(above_ref.shape)
    below_ref[...] = below_thin_ref[...].astype(F32).reshape(below_ref.shape)
    side_row = side_rows(levels, rows, beside_ref, above_ref, below_ref)
    sweep(place_ref, wx_ref, wy_ref, x_ref, above_ref, below_ref, side_row, grad_ref)
    project_body(place_ref, grad_ref, *others)


def project_body(place_ref, grad_ref, *refs):
    *member_refs, wide_ref, thin_ref = refs
    own, _, rows, cols = member_refs[0].shape
    count = len(member_refs) * own

    def step(q, carry):
        carry = list(carry)
        for u in range(2):
            g = grad_ref[2 * q + u]
            for m in range(count):
                carry[m] = carry[m] + member_refs[m // own][m % own, 2 * q + u].astype(F32) * g
        return tuple(carry)

    total = lax.fori_loop(0, grad_ref.shape[0] // 2, step, (jnp.zeros((rows, cols), F32),) * count)
    for m in range(count):
        at = neighbor_of(place_ref, -(m // own)) * own + m % own
        wide_ref[at] = total[m]
        thin_ref[at] = total[m].astype(BF16)


def taper(offset):
    k = offset.astype(F32)
    w = (1.0 - (k / 17.0) * (k / 17.0)) * (1.0 / TAPER_TOTAL)
    return jnp.where(jnp.abs(offset) <= REACH, w, 0.0)


def halves(x):
    high = x.astype(BF16)
    return high, (x - high.astype(F32)).astype(BF16)


def sharp_dot(a, b):
    ah, al = halves(a)
    bh, bl = halves(b)
    dot = functools.partial(jnp.dot, preferred_element_type=F32)
    return dot(ah, bh) + dot(al, bh) + dot(ah, bl)


def columns_body(left_ref, mid_ref, right_ref, wide_ref, thin_ref):
    count, rows, cols = mid_ref.shape
    wide = jnp.concatenate(
        [r[...].astype(F32).reshape(count * rows, cols) for r in (left_ref, mid_ref, right_ref)], axis=1
    )
    shape = (3 * cols, wide_ref.shape[0] // count * cols)
    lane = lane_iota(shape)
    beside = lane % MODEL_STEPS + jnp.where((lane // (SUB * MODEL_STEPS)) % 2 == 0, -MODEL_STEPS, cols)
    target = jnp.where(lane < cols, lane, beside)
    out = sharp_dot(wide, taper(sub_iota(shape) - cols - target))
    for i in range(shape[1] // cols):
        part = out[:, i * cols : (i + 1) * cols].reshape(count, rows, cols)
        wide_ref[i * count : (i + 1) * count] = part
        thin_ref[i * count : (i + 1) * count] = part.astype(BF16)


def smooth_rows(above_ref, mid_ref, below_ref):
    count, rows, cols = mid_ref.shape
    tall = jnp.concatenate(
        [
            jnp.concatenate([above_ref[m].astype(F32), mid_ref[m], below_ref[m].astype(F32)], axis=0)
            for m in range(count)
        ],
        axis=1,
    )
    shape = (rows, 3 * rows)
    out = sharp_dot(taper(lane_iota(shape) - sub_iota(shape) - rows), tall)
    return [out[:, m * cols : (m + 1) * cols] for m in range(count)]


def increments(place_ref, member_refs, local_ref, levels, emit):
    own = member_refs[0].shape[0]
    count = len(member_refs) * own
    local = [local_ref[neighbor_of(place_ref, -(m // own)) * own + m % own] for m in range(count)]

    def step(q, carry):
        for u in range(2):
            level = 2 * q + u
            total = member_refs[0][0, level].astype(F32) * local[0]
            for m in range(1, count):
                total = total + member_refs[m // own][m % own, level].astype(F32) * local[m]
            emit(level, total)
        return carry

    lax.fori_loop(0, levels // 2, step, 0)


def update_body(parts, place_ref, residual_ref, around_ref, above_ref, mid_ref, below_ref, *refs):
    member_refs, sides_ref = refs[:parts], refs[parts]
    analysis_ref, out_ref, beside_ref, top_ref, bottom_ref, local_ref, top_wide_ref, bottom_wide_ref = refs[parts + 1 :]
    levels, rows, cols = residual_ref.shape
    own = member_refs[0].shape[0]
    count = parts * own
    for m, value in enumerate(smooth_rows(above_ref, mid_ref, below_ref)):
        local_ref[m] = value

    def emit(level, value):
        analysis_ref[level] = value
        out_ref[level] = residual_ref[level] - RELAX * value

    increments(place_ref, member_refs, local_ref, levels, emit)
    for g in range(levels // GROUP):
        total = jnp.zeros((rows, LANES), F32)
        for m in range(count):
            total = total + sides_ref[m // own, m % own, g].astype(F32) * local_ref[count + m]
        beside_ref[g] = around_ref[g] - RELAX * total
    pack_rows(out_ref, 0, top_wide_ref, bottom_wide_ref)
    pack_rows(beside_ref, levels // 2, top_wide_ref, bottom_wide_ref)
    top_ref[...] = top_wide_ref[...].reshape(top_ref.shape).astype(BF16)
    bottom_ref[...] = bottom_wide_ref[...].reshape(bottom_ref.shape).astype(BF16)


def final_body(parts, place_ref, residual_ref, before_ref, above_ref, mid_ref, below_ref, *refs):
    member_refs = refs[:parts]
    analysis_ref, out_ref, local_ref = refs[parts:]
    for m, value in enumerate(smooth_rows(above_ref, mid_ref, below_ref)):
        local_ref[m] = value

    def emit(level, value):
        analysis_ref[level] = before_ref[level] + value
        out_ref[level] = residual_ref[level] - RELAX * value

    increments(place_ref, member_refs, local_ref, residual_ref.shape[0], emit)


def per_device(residual_in, members, wind_x, wind_y):
    levels, rows, cols = residual_in.shape
    tiles = lax.axis_size("tile")
    parts = lax.axis_size("member")
    place = jnp.stack([lax.axis_index("tile"), jnp.int32(tiles), lax.axis_index("member"), jnp.int32(parts)])
    count = members.shape[0] * parts
    groups = levels // GROUP

    def shape(*dims, kind=F32):
        return jax.ShapeDtypeStruct(dims, kind)

    def both(*dims):
        return shape(*dims), shape(*dims, kind=BF16)

    def turned(x, step):
        return lax.ppermute(x, "member", [(i, (i + step) % parts) for i in range(parts)])

    def smoothed(wide, thin, planes):
        wide, thin = call(
            columns_body, both(planes, rows, cols), shift(thin, "member", 1), wide, shift(thin, "member", -1)
        )
        return shift(thin, "tile", 1), wide, shift(thin, "tile", -1)

    like = shape(levels, rows, cols)
    halo = shape((levels + groups) // 2, SUB, LANES)
    thin_halo = shape((levels + groups) // 4, 2 * SUB, LANES, kind=BF16)
    wide_halo = [pltpu.VMEM(halo.shape, F32)] * 2
    packed = shape(groups, rows, LANES)
    wind_x, wind_y = (jnp.broadcast_to(w[:, None], (levels, LANES)) for w in (wind_x, wind_y))

    block = shape(members.shape[0], levels, rows, cols, kind=members.dtype)
    first, last, *blocks = call(
        opening_body, (packed, packed) + (block,) * parts, place, residual_in, members, in_specs=[SMEM, VMEM, VMEM]
    )
    left, right = shift(last, "member", 1), shift(first, "member", -1)
    blocks, left, right = lax.optimization_barrier((blocks, left, right))
    blocks = [turned(x, r) if r else x for r, x in enumerate(blocks)]
    around, top, bottom = call(rows_body, (packed, halo, halo), residual_in, left, right)
    members, around = lax.optimization_barrier((members, around))
    sides = side_columns(members, parts)
    above, below = shift(bottom, "tile", 1), shift(top, "tile", -1)
    grad = call(
        first_model_body, like,
        place, wind_x, wind_y, residual_in, around, above, below, in_specs=[SMEM] + [VMEM] * 6,
    )
    grad, sides = lax.optimization_barrier((grad, sides))
    sides = lax.all_to_all(sides, "member", split_axis=0, concat_axis=0, tiled=True)
    grad, sides = lax.optimization_barrier((grad, sides))
    wide, thin = call(
        project_body, both(count, rows, cols), place, grad, *blocks, in_specs=[SMEM] + [VMEM] * (1 + parts)
    )

    analysis, residual, beside, top, bottom = call(
        functools.partial(update_body, parts), (like, like, packed, thin_halo, thin_halo),
        place, residual_in, around, *smoothed(wide, thin, 2 * count), *blocks, sides,
        in_specs=[SMEM] + [VMEM] * (6 + parts),
        scratch=[pltpu.VMEM((2 * count, rows, cols), F32)] + wide_halo,
    )
    above, below = shift(bottom, "tile", 1), shift(top, "tile", -1)
    wide, thin = call(
        second_model_body, both(count, rows, cols),
        place, wind_x, wind_y, residual, beside, above, below, *blocks,
        in_specs=[SMEM] + [VMEM] * (6 + parts), scratch=[pltpu.VMEM((levels, rows, cols), F32)] + wide_halo,
    )
    return call(
        functools.partial(final_body, parts), (like, like),
        place, residual, analysis, *smoothed(wide, thin, count), *blocks,
        in_specs=[SMEM] + [VMEM] * (5 + parts), scratch=[pltpu.VMEM((count, rows, cols), F32)],
    )


def solution(mesh):
    return jax.shard_map(
        per_device,
        mesh=mesh,
        in_specs=(P(None, "tile", "member"), P("member", None, "tile", None), P(), P()),
        out_specs=(P(None, "tile", "member"), P(None, "tile", "member")),
        check_vma=False,
    )
```

```python
import functools

import jax
import jax.numpy as jnp
from jax import lax
from jax.experimental import pallas as pl
from jax.experimental.pallas import tpu as pltpu
from jax.sharding import PartitionSpec as P

ITERS = 2
MODEL_STEPS = 4
DIFFUSION = 0.1
RELAX = 0.5
REACH = 16
TAPER_TOTAL = sum(1.0 - (k / 17.0) ** 2 for k in range(-REACH, REACH + 1))
F32 = jnp.float32
BF16 = jnp.bfloat16
LANES = 128
SUB = 8
GROUP = LANES // (2 * MODEL_STEPS)

VMEM = pl.BlockSpec(memory_space=pltpu.VMEM)
PARAMS = pltpu.CompilerParams(vmem_limit_bytes=48 * 1024 * 1024)


def call(body, out_shape, *args, in_specs=None, scratch=()):
    return pl.pallas_call(
        body,
        out_shape=out_shape,
        in_specs=in_specs or [VMEM] * len(args),
        out_specs=jax.tree.map(lambda _: VMEM, out_shape),
        scratch_shapes=scratch,
        compiler_params=PARAMS,
    )(*args)


def lane_iota(shape):
    return lax.broadcasted_iota(jnp.int32, shape, len(shape) - 1)


def sub_iota(shape):
    return lax.broadcasted_iota(jnp.int32, shape, len(shape) - 2)


def neighbor_of(step):
    parts = lax.axis_size("member")
    at = lax.axis_index("member") + step
    return jnp.where(at < 0, at + parts, jnp.where(at >= parts, at - parts, at))


def columns_split_body(in_ref, *out_refs):
    cols = out_refs[0].shape[-1]
    for r, out_ref in enumerate(out_refs):
        out_ref[...] = in_ref[:, :, :, pl.ds(pl.multiple_of(neighbor_of(r) * cols, cols), cols)]


def split_columns(members, parts):
    own, levels, rows, ny = members.shape
    out = jax.ShapeDtypeStruct((own, levels, rows, ny // parts), members.dtype)
    return call(columns_split_body, (out,) * parts, members, in_specs=[VMEM])


def left_slot(k):
    return 3 * SUB - 1 - k % SUB - GROUP * (k // SUB)


def put_left(x, k, total):
    here = lane_iota(x.shape) // MODEL_STEPS == left_slot(k)
    return jnp.where(here, pltpu.roll(x, (MODEL_STEPS * (left_slot(k) + 1)) % LANES, 1), total)


def put_right(x, k, total):
    here = lane_iota(x.shape) // MODEL_STEPS == left_slot(k) + SUB
    return jnp.where(here, pltpu.roll(x, MODEL_STEPS * (left_slot(k) + SUB), 1), total)


def sides_body(in_ref, out_ref):
    parts, own, groups, rows, _ = out_ref.shape
    cols = in_ref.shape[-1] // parts
    for r in range(parts):
        before, after = (pl.ds((r + parts + d) % parts * cols, cols) for d in (-1, 1))
        for m in range(own):

            def step(g, carry):
                total = jnp.zeros((rows, LANES), F32)
                for k in range(GROUP):
                    total = put_left(in_ref[m, g * GROUP + k, :, before].astype(F32), k, total)
                    total = put_right(in_ref[m, g * GROUP + k, :, after].astype(F32), k, total)
                out_ref[r, m, g] = total.astype(out_ref.dtype)
                return carry

            lax.fori_loop(0, groups, step, 0)


def side_columns(members, parts):
    own, levels, rows, ny = members.shape
    return call(sides_body, jax.ShapeDtypeStruct((parts, own, levels // GROUP, rows, LANES), members.dtype), members)


def pack_rows(ref, at, top_ref, bottom_ref):
    upper = sub_iota((SUB, LANES)) < MODEL_STEPS
    count, rows, _ = ref.shape
    for q in range(count // 2):
        top_ref[at + q] = jnp.where(upper, ref[2 * q, :SUB], pltpu.roll(ref[2 * q + 1, :SUB], MODEL_STEPS, 0))
        bottom_ref[at + q] = jnp.where(
            upper, pltpu.roll(ref[2 * q, rows - SUB :], MODEL_STEPS, 0), ref[2 * q + 1, rows - SUB :]
        )


def rows_body(x_ref, left_ref, right_ref, beside_ref, top_ref, bottom_ref):
    beside_ref[...] = left_ref[...] + right_ref[...]
    pack_rows(x_ref, 0, top_ref, bottom_ref)
    pack_rows(beside_ref, x_ref.shape[0] // 2, top_ref, bottom_ref)


def columns_edge_body(x_ref, first_ref, last_ref):
    levels, rows, cols = x_ref.shape
    for g in range(levels // GROUP):
        first = jnp.zeros((rows, LANES), F32)
        last = jnp.zeros((rows, LANES), F32)
        for k in range(GROUP):
            last = put_left(x_ref[g * GROUP + k], k, last)
            first = put_right(x_ref[g * GROUP + k], k, first)
        first_ref[g] = first
        last_ref[g] = last


def shift(x, axis, step):
    count = lax.axis_size(axis)
    pairs = [(i, i + step) for i in range(count) if 0 <= i + step < count]
    return lax.ppermute(x, axis, pairs)


def sweep(wx_ref, wy_ref, x_ref, above_ref, below_ref, side_row, grad_ref):
    levels, rows, cols = x_ref.shape
    tile, tiles = lax.axis_index("tile"), lax.axis_size("tile")
    member, parts = lax.axis_index("member"), lax.axis_size("member")
    x_flat = x_ref.reshape(levels * rows, cols)
    grad_flat = grad_ref.reshape(levels * rows, cols)
    halo = MODEL_STEPS
    pairs = above_ref.shape[0]
    above_flat = above_ref.reshape(pairs * SUB, LANES)
    below_flat = below_ref.reshape(pairs * SUB, LANES)

    half = LANES // 2
    lane = lane_iota((SUB, LANES))
    on_right = lane % half < halo
    first_of = (lane == 0, lane == half)
    last_of = (lane == LANES - 1, lane == half - 1)
    second = (lane >= half // 2) & (lane < half + half // 2)
    inside = (on_right & (member < parts - 1)) | ((lane % half >= half - halo) & (member > 0))
    side_mask = jnp.where(inside, 1.0, 0.0).astype(F32)
    has_above = jnp.where(tile > 0, 1.0, 0.0).astype(F32)
    has_below = jnp.where(tile < tiles - 1, 1.0, 0.0).astype(F32)

    def load(g, e):
        centers = []
        for q in (2 * g, 2 * g + 1):
            if e < 0:
                centers.append(above_flat[pl.ds(q * SUB * halo + e + halo, SUB, stride=halo), :])
            elif e < rows:
                centers.append(x_flat[pl.ds(q * SUB * rows + e, SUB, stride=rows), :])
            else:
                centers.append(below_flat[pl.ds(q * SUB * halo + e - rows, SUB, stride=halo), :])
        row = jnp.broadcast_to(side_row(g, e), (SUB, LANES))
        right = pltpu.roll(row, halo, 1, stride=halo, stride_axis=0)
        left = pltpu.roll(row, LANES // 4, 1, stride=halo, stride_axis=0)
        side = jnp.where(on_right, right, left) * side_mask
        return centers[0], pltpu.roll(centers[1], half, 1), side

    def advance(before, here, after, e, coefficients):
        fore = [pltpu.roll(x, LANES - 1, 1) for x in here]
        back = [pltpu.roll(x, 1, 1) for x in here]
        fore_side = jnp.where(last_of[0], fore[0], jnp.where(last_of[1], fore[1], fore[2]))
        back_side = jnp.where(first_of[0], back[0], jnp.where(first_of[1], back[1], back[2]))
        fores = [jnp.where(last_of[i], fore[2], fore[i]) for i in range(2)] + [fore_side]
        backs = [jnp.where(first_of[i], back[2], back[i]) for i in range(2)] + [back_side]
        result = []
        for i, (own, ahead_x, ahead_y) in enumerate(coefficients):
            value = own * here[i] + ahead_x * after[i] + ahead_y * fores[i] + DIFFUSION * (before[i] + backs[i])
            if e < 0:
                value = value * has_above
            if e >= rows:
                value = value * has_below
            result.append(value * side_mask if i == 2 else value)
        return tuple(result)

    def group(g, carry):
        coefficients = []
        for q in (2 * g, 2 * g + 1):
            at = pl.ds(pl.multiple_of(q * SUB, SUB), SUB)
            wx, wy = wx_ref[at, :], wy_ref[at, :]
            coefficients.append((1.0 - 4.0 * DIFFUSION - wx - wy, DIFFUSION + wx, DIFFUSION + wy))
        coefficients.append(tuple(jnp.where(second, b, a) for a, b in zip(*coefficients)))
        fields = [{} for _ in range(halo + 1)]
        for front in range(-halo, rows + halo):
            fields[0][front] = load(g, front)
            for n in range(1, halo + 1):
                e = front - n
                if -halo + n <= e < rows + halo - n:
                    old = fields[n - 1]
                    fields[n][e] = advance(old[e - 1], old[e], old[e + 1], e, coefficients)
            e = front - halo
            if 0 <= e < rows:
                grad_flat[pl.ds(2 * g * SUB * rows + e, SUB, stride=rows), :] = fields[halo][e][0]
                grad_flat[pl.ds((2 * g + 1) * SUB * rows + e, SUB, stride=rows), :] = pltpu.roll(fields[halo][e][1], half, 1)
        return carry

    lax.fori_loop(0, levels // GROUP, group, 0)


def side_rows(levels, rows, beside_ref, above_ref, below_ref):
    above_flat, below_flat = (ref.reshape(ref.shape[0] * SUB, LANES) for ref in (above_ref, below_ref))

    def side_row(g, e):
        if 0 <= e < rows:
            return beside_ref[g, pl.ds(e, 1), :]
        flat, row = (above_flat, e + MODEL_STEPS) if e < 0 else (below_flat, e - rows)
        return flat[pl.ds((levels + g) * MODEL_STEPS + row, 1), :]

    return side_row


def first_model_body(wx_ref, wy_ref, x_ref, beside_ref, above_ref, below_ref, grad_ref):
    levels, rows, cols = x_ref.shape
    side_row = side_rows(levels, rows, beside_ref, above_ref, below_ref)
    sweep(wx_ref, wy_ref, x_ref, above_ref, below_ref, side_row, grad_ref)


def second_model_body(wx_ref, wy_ref, x_ref, beside_ref, above_thin_ref, below_thin_ref, *refs):
    *others, grad_ref, above_ref, below_ref = refs
    levels, rows, cols = x_ref.shape
    above_ref[...] = above_thin_ref[...].astype(F32).reshape(above_ref.shape)
    below_ref[...] = below_thin_ref[...].astype(F32).reshape(below_ref.shape)
    side_row = side_rows(levels, rows, beside_ref, above_ref, below_ref)
    sweep(wx_ref, wy_ref, x_ref, above_ref, below_ref, side_row, grad_ref)
    project_body(grad_ref, *others)


def project_body(grad_ref, *refs):
    *member_refs, wide_ref, thin_ref = refs
    own, _, rows, cols = member_refs[0].shape
    count = len(member_refs) * own

    def step(q, carry):
        carry = list(carry)
        for u in range(2):
            g = grad_ref[2 * q + u]
            for m in range(count):
                carry[m] = carry[m] + member_refs[m // own][m % own, 2 * q + u].astype(F32) * g
        return tuple(carry)

    total = lax.fori_loop(0, grad_ref.shape[0] // 2, step, (jnp.zeros((rows, cols), F32),) * count)
    for m in range(count):
        at = neighbor_of(-(m // own)) * own + m % own
        wide_ref[at] = total[m]
        thin_ref[at] = total[m].astype(BF16)


def taper(offset):
    k = offset.astype(F32)
    w = (1.0 - (k / 17.0) * (k / 17.0)) * (1.0 / TAPER_TOTAL)
    return jnp.where(jnp.abs(offset) <= REACH, w, 0.0)


def halves(x):
    high = x.astype(BF16)
    return high, (x - high.astype(F32)).astype(BF16)


def sharp_dot(a, b):
    ah, al = halves(a)
    bh, bl = halves(b)
    dot = functools.partial(jnp.dot, preferred_element_type=F32)
    return dot(ah, bh) + dot(al, bh) + dot(ah, bl)


def columns_body(left_ref, mid_ref, right_ref, wide_ref, thin_ref):
    count, rows, cols = mid_ref.shape
    wide = jnp.concatenate(
        [r[...].astype(F32).reshape(count * rows, cols) for r in (left_ref, mid_ref, right_ref)], axis=1
    )
    shape = (3 * cols, wide_ref.shape[0] // count * cols)
    lane = lane_iota(shape)
    beside = lane % MODEL_STEPS + jnp.where((lane // (SUB * MODEL_STEPS)) % 2 == 0, -MODEL_STEPS, cols)
    target = jnp.where(lane < cols, lane, beside)
    out = sharp_dot(wide, taper(sub_iota(shape) - cols - target))
    for i in range(shape[1] // cols):
        part = out[:, i * cols : (i + 1) * cols].reshape(count, rows, cols)
        wide_ref[i * count : (i + 1) * count] = part
        thin_ref[i * count : (i + 1) * count] = part.astype(BF16)


def smooth_rows(above_ref, mid_ref, below_ref):
    count, rows, cols = mid_ref.shape
    tall = jnp.concatenate(
        [
            jnp.concatenate([above_ref[m].astype(F32), mid_ref[m], below_ref[m].astype(F32)], axis=0)
            for m in range(count)
        ],
        axis=1,
    )
    shape = (rows, 3 * rows)
    out = sharp_dot(taper(lane_iota(shape) - sub_iota(shape) - rows), tall)
    return [out[:, m * cols : (m + 1) * cols] for m in range(count)]


def increments(member_refs, local_ref, levels, emit):
    own = member_refs[0].shape[0]
    count = len(member_refs) * own
    local = [local_ref[neighbor_of(-(m // own)) * own + m % own] for m in range(count)]

    def step(q, carry):
        for u in range(2):
            level = 2 * q + u
            total = member_refs[0][0, level].astype(F32) * local[0]
            for m in range(1, count):
                total = total + member_refs[m // own][m % own, level].astype(F32) * local[m]
            emit(level, total)
        return carry

    lax.fori_loop(0, levels // 2, step, 0)


def update_body(parts, residual_ref, around_ref, above_ref, mid_ref, below_ref, *refs):
    member_refs, sides_ref = refs[:parts], refs[parts]
    analysis_ref, out_ref, beside_ref, top_ref, bottom_ref, local_ref, top_wide_ref, bottom_wide_ref = refs[parts + 1 :]
    levels, rows, cols = residual_ref.shape
    own = member_refs[0].shape[0]
    count = parts * own
    for m, value in enumerate(smooth_rows(above_ref, mid_ref, below_ref)):
        local_ref[m] = value

    def emit(level, value):
        analysis_ref[level] = value
        out_ref[level] = residual_ref[level] - RELAX * value

    increments(member_refs, local_ref, levels, emit)
    for g in range(levels // GROUP):
        total = jnp.zeros((rows, LANES), F32)
        for m in range(count):
            total = total + sides_ref[m // own, m % own, g].astype(F32) * local_ref[count + m]
        beside_ref[g] = around_ref[g] - RELAX * total
    pack_rows(out_ref, 0, top_wide_ref, bottom_wide_ref)
    pack_rows(beside_ref, levels // 2, top_wide_ref, bottom_wide_ref)
    top_ref[...] = top_wide_ref[...].reshape(top_ref.shape).astype(BF16)
    bottom_ref[...] = bottom_wide_ref[...].reshape(bottom_ref.shape).astype(BF16)


def final_body(parts, residual_ref, before_ref, above_ref, mid_ref, below_ref, *refs):
    member_refs = refs[:parts]
    analysis_ref, out_ref, local_ref = refs[parts:]
    for m, value in enumerate(smooth_rows(above_ref, mid_ref, below_ref)):
        local_ref[m] = value

    def emit(level, value):
        analysis_ref[level] = before_ref[level] + value
        out_ref[level] = residual_ref[level] - RELAX * value

    increments(member_refs, local_ref, residual_ref.shape[0], emit)


def per_device(residual_in, members, wind_x, wind_y):
    levels, rows, cols = residual_in.shape
    parts = lax.axis_size("member")
    count = members.shape[0] * parts
    groups = levels // GROUP

    def shape(*dims, kind=F32):
        return jax.ShapeDtypeStruct(dims, kind)

    def both(*dims):
        return shape(*dims), shape(*dims, kind=BF16)

    def turned(x, step):
        return lax.ppermute(x, "member", [(i, (i + step) % parts) for i in range(parts)])

    def smoothed(wide, thin, planes):
        wide, thin = call(
            columns_body, both(planes, rows, cols), shift(thin, "member", 1), wide, shift(thin, "member", -1)
        )
        return shift(thin, "tile", 1), wide, shift(thin, "tile", -1)

    like = shape(levels, rows, cols)
    halo = shape((levels + groups) // 2, SUB, LANES)
    thin_halo = shape((levels + groups) // 4, 2 * SUB, LANES, kind=BF16)
    wide_halo = [pltpu.VMEM(halo.shape, F32)] * 2
    packed = shape(groups, rows, LANES)
    wind_x, wind_y = (jnp.broadcast_to(w[:, None], (levels, LANES)) for w in (wind_x, wind_y))

    first, last = call(columns_edge_body, (packed, packed), residual_in)
    left, right = shift(last, "member", 1), shift(first, "member", -1)
    blocks, left, right = lax.optimization_barrier((split_columns(members, parts), left, right))
    blocks = [turned(x, r) if r else x for r, x in enumerate(blocks)]
    around, top, bottom = call(rows_body, (packed, halo, halo), residual_in, left, right)
    members, around = lax.optimization_barrier((members, around))
    sides = side_columns(members, parts)
    above, below = shift(bottom, "tile", 1), shift(top, "tile", -1)
    grad = call(
        first_model_body, like,
        wind_x, wind_y, residual_in, around, above, below, in_specs=[VMEM] * 6,
    )
    grad, sides = lax.optimization_barrier((grad, sides))
    sides = lax.all_to_all(sides, "member", split_axis=0, concat_axis=0, tiled=True)
    grad, sides = lax.optimization_barrier((grad, sides))
    wide, thin = call(
        project_body, both(count, rows, cols), grad, *blocks, in_specs=[VMEM] * (1 + parts)
    )

    analysis, residual, beside, top, bottom = call(
        functools.partial(update_body, parts), (like, like, packed, thin_halo, thin_halo),
        residual_in, around, *smoothed(wide, thin, 2 * count), *blocks, sides,
        in_specs=[VMEM] * (6 + parts),
        scratch=[pltpu.VMEM((2 * count, rows, cols), F32)] + wide_halo,
    )
    above, below = shift(bottom, "tile", 1), shift(top, "tile", -1)
    wide, thin = call(
        second_model_body, both(count, rows, cols),
        wind_x, wind_y, residual, beside, above, below, *blocks,
        in_specs=[VMEM] * (6 + parts), scratch=[pltpu.VMEM((levels, rows, cols), F32)] + wide_halo,
    )
    return call(
        functools.partial(final_body, parts), (like, like),
        residual, analysis, *smoothed(wide, thin, count), *blocks,
        in_specs=[VMEM] * (5 + parts), scratch=[pltpu.VMEM((count, rows, cols), F32)],
    )


def solution(mesh):
    return jax.shard_map(
        per_device,
        mesh=mesh,
        in_specs=(P(None, "tile", "member"), P("member", None, "tile", None), P(), P()),
        out_specs=(P(None, "tile", "member"), P(None, "tile", "member")),
        check_vma=False,
    )
```

```python
import functools

import jax
import jax.numpy as jnp
from jax import lax
from jax.experimental import pallas as pl
from jax.experimental.pallas import tpu as pltpu
from jax.sharding import PartitionSpec as P

ITERS = 2
MODEL_STEPS = 4
DIFFUSION = 0.1
RELAX = 0.5
REACH = 16
TAPER_TOTAL = sum(1.0 - (k / 17.0) ** 2 for k in range(-REACH, REACH + 1))
F32 = jnp.float32
BF16 = jnp.bfloat16
LANES = 128
SUB = 8
GROUP = LANES // (2 * MODEL_STEPS)

VMEM = pl.BlockSpec(memory_space=pltpu.VMEM)
PARAMS = pltpu.CompilerParams(vmem_limit_bytes=48 * 1024 * 1024)


def call(body, out_shape, *args, in_specs=None, scratch=()):
    return pl.pallas_call(
        body,
        out_shape=out_shape,
        in_specs=in_specs or [VMEM] * len(args),
        out_specs=jax.tree.map(lambda _: VMEM, out_shape),
        scratch_shapes=scratch,
        compiler_params=PARAMS,
    )(*args)


def lane_iota(shape):
    return lax.broadcasted_iota(jnp.int32, shape, len(shape) - 1)


def sub_iota(shape):
    return lax.broadcasted_iota(jnp.int32, shape, len(shape) - 2)


def neighbor_of(step):
    parts = lax.axis_size("member")
    at = lax.axis_index("member") + step
    return jnp.where(at < 0, at + parts, jnp.where(at >= parts, at - parts, at))


def columns_split_body(in_ref, *out_refs):
    cols = out_refs[0].shape[-1]
    for r, out_ref in enumerate(out_refs):
        out_ref[...] = in_ref[:, :, :, pl.ds(pl.multiple_of(neighbor_of(r) * cols, cols), cols)]


def split_columns(members, parts):
    own, levels, rows, ny = members.shape
    out = jax.ShapeDtypeStruct((own, levels, rows, ny // parts), members.dtype)
    return call(columns_split_body, (out,) * parts, members, in_specs=[VMEM])


def left_slot(k):
    return 3 * SUB - 1 - k % SUB - GROUP * (k // SUB)


def put_left(x, k, total):
    here = lane_iota(x.shape) // MODEL_STEPS == left_slot(k)
    return jnp.where(here, pltpu.roll(x, (MODEL_STEPS * (left_slot(k) + 1)) % LANES, 1), total)


def put_right(x, k, total):
    here = lane_iota(x.shape) // MODEL_STEPS == left_slot(k) + SUB
    return jnp.where(here, pltpu.roll(x, MODEL_STEPS * (left_slot(k) + SUB), 1), total)


def sides_body(in_ref, out_ref):
    parts, own, groups, rows, _ = out_ref.shape
    cols = in_ref.shape[-1] // parts
    for r in range(parts):
        before, after = (pl.ds((r + parts + d) % parts * cols, cols) for d in (-1, 1))
        for m in range(own):

            def step(g, carry):
                total = jnp.zeros((rows, LANES), F32)
                for k in range(GROUP):
                    total = put_left(in_ref[m, g * GROUP + k, :, before].astype(F32), k, total)
                    total = put_right(in_ref[m, g * GROUP + k, :, after].astype(F32), k, total)
                out_ref[r, m, g] = total.astype(out_ref.dtype)
                return carry

            lax.fori_loop(0, groups, step, 0)


def side_columns(members, parts):
    own, levels, rows, ny = members.shape
    return call(sides_body, jax.ShapeDtypeStruct((parts, own, levels // GROUP, rows, LANES), members.dtype), members)


def pack_rows(ref, at, top_ref, bottom_ref):
    upper = sub_iota((SUB, LANES)) < MODEL_STEPS
    count, rows, _ = ref.shape
    for q in range(count // 2):
        top_ref[at + q] = jnp.where(upper, ref[2 * q, :SUB], pltpu.roll(ref[2 * q + 1, :SUB], MODEL_STEPS, 0))
        bottom_ref[at + q] = jnp.where(
            upper, pltpu.roll(ref[2 * q, rows - SUB :], MODEL_STEPS, 0), ref[2 * q + 1, rows - SUB :]
        )


def rows_body(x_ref, left_ref, right_ref, beside_ref, top_ref, bottom_ref):
    beside_ref[...] = left_ref[...] + right_ref[...]
    pack_rows(x_ref, 0, top_ref, bottom_ref)
    pack_rows(beside_ref, x_ref.shape[0] // 2, top_ref, bottom_ref)


def columns_edge_body(x_ref, first_ref, last_ref):
    levels, rows, cols = x_ref.shape
    for g in range(levels // GROUP):
        first = jnp.zeros((rows, LANES), F32)
        last = jnp.zeros((rows, LANES), F32)
        for k in range(GROUP):
            last = put_left(x_ref[g * GROUP + k], k, last)
            first = put_right(x_ref[g * GROUP + k], k, first)
        first_ref[g] = first
        last_ref[g] = last


def shift(x, axis, step):
    count = lax.axis_size(axis)
    pairs = [(i, i + step) for i in range(count) if 0 <= i + step < count]
    return lax.ppermute(x, axis, pairs)


def model_parts(wx_ref, wy_ref, x_ref, above_ref, below_ref, side_row, grad_ref):
    levels, rows, cols = x_ref.shape
    tile, tiles = lax.axis_index("tile"), lax.axis_size("tile")
    member, parts = lax.axis_index("member"), lax.axis_size("member")
    x_flat = x_ref.reshape(levels * rows, cols)
    grad_flat = grad_ref.reshape(levels * rows, cols)
    halo = MODEL_STEPS
    if above_ref is not None:
        pairs = above_ref.shape[0]
        above_flat = above_ref.reshape(pairs * SUB, LANES)
        below_flat = below_ref.reshape(pairs * SUB, LANES)

    half = LANES // 2
    lane = lane_iota((SUB, LANES))
    on_right = lane % half < halo
    first_of = (lane == 0, lane == half)
    last_of = (lane == LANES - 1, lane == half - 1)
    second = (lane >= half // 2) & (lane < half + half // 2)
    inside = (on_right & (member < parts - 1)) | ((lane % half >= half - halo) & (member > 0))
    side_mask = jnp.where(inside, 1.0, 0.0).astype(F32)
    has_above = jnp.where(tile > 0, 1.0, 0.0).astype(F32)
    has_below = jnp.where(tile < tiles - 1, 1.0, 0.0).astype(F32)

    def load(g, e):
        centers = []
        for q in (2 * g, 2 * g + 1):
            if e < 0:
                centers.append(above_flat[pl.ds(q * SUB * halo + e + halo, SUB, stride=halo), :])
            elif e < rows:
                centers.append(x_flat[pl.ds(q * SUB * rows + e, SUB, stride=rows), :])
            else:
                centers.append(below_flat[pl.ds(q * SUB * halo + e - rows, SUB, stride=halo), :])
        row = jnp.broadcast_to(side_row(g, e), (SUB, LANES))
        right = pltpu.roll(row, halo, 1, stride=halo, stride_axis=0)
        left = pltpu.roll(row, LANES // 4, 1, stride=halo, stride_axis=0)
        side = jnp.where(on_right, right, left) * side_mask
        return centers[0], pltpu.roll(centers[1], half, 1), side

    def advance(before, here, after, e, coefficients):
        fore = [pltpu.roll(x, LANES - 1, 1) for x in here]
        back = [pltpu.roll(x, 1, 1) for x in here]
        fore_side = jnp.where(last_of[0], fore[0], jnp.where(last_of[1], fore[1], fore[2]))
        back_side = jnp.where(first_of[0], back[0], jnp.where(first_of[1], back[1], back[2]))
        fores = [jnp.where(last_of[i], fore[2], fore[i]) for i in range(2)] + [fore_side]
        backs = [jnp.where(first_of[i], back[2], back[i]) for i in range(2)] + [back_side]
        result = []
        for i, (own, ahead_x, ahead_y) in enumerate(coefficients):
            value = own * here[i] + ahead_x * after[i] + ahead_y * fores[i] + DIFFUSION * (before[i] + backs[i])
            if e < 0:
                value = value * has_above
            if e >= rows:
                value = value * has_below
            result.append(value * side_mask if i == 2 else value)
        return tuple(result)

    def coefficients_of(g):
        coefficients = []
        for q in (2 * g, 2 * g + 1):
            at = pl.ds(pl.multiple_of(q * SUB, SUB), SUB)
            wx, wy = wx_ref[at, :], wy_ref[at, :]
            coefficients.append((1.0 - 4.0 * DIFFUSION - wx - wy, DIFFUSION + wx, DIFFUSION + wy))
        coefficients.append(tuple(jnp.where(second, b, a) for a, b in zip(*coefficients)))
        return coefficients

    def store(g, e, field):
        grad_flat[pl.ds(2 * g * SUB * rows + e, SUB, stride=rows), :] = field[0]
        grad_flat[pl.ds((2 * g + 1) * SUB * rows + e, SUB, stride=rows), :] = pltpu.roll(field[1], half, 1)

    return load, advance, coefficients_of, store


def sweep(x_ref, parts):
    levels, rows, cols = x_ref.shape
    load, advance, coefficients_of, store = parts
    halo = MODEL_STEPS

    def group(g, carry):
        coefficients = coefficients_of(g)
        fields = [{} for _ in range(halo + 1)]
        for front in range(-halo, rows + halo):
            fields[0][front] = load(g, front)
            for n in range(1, halo + 1):
                e = front - n
                if -halo + n <= e < rows + halo - n:
                    old = fields[n - 1]
                    fields[n][e] = advance(old[e - 1], old[e], old[e + 1], e, coefficients)
            e = front - halo
            if 0 <= e < rows:
                store(g, e, fields[halo][e])
        return carry

    lax.fori_loop(0, levels // GROUP, group, 0)


def kept_rows(rows):
    return [(n, e) for n in range(1, MODEL_STEPS) for e in (n, n + 1, rows - 2 - n, rows - 1 - n)]


def inner_sweep(x_ref, parts, kept_ref):
    levels, rows, cols = x_ref.shape
    load, advance, coefficients_of, store = parts
    halo = MODEL_STEPS

    def group(g, carry):
        coefficients = coefficients_of(g)
        fields = [{} for _ in range(halo + 1)]
        for front in range(rows):
            fields[0][front] = load(g, front)
            for n in range(1, halo + 1):
                e = front - n
                if n <= e < rows - n:
                    old = fields[n - 1]
                    fields[n][e] = advance(old[e - 1], old[e], old[e + 1], e, coefficients)
            e = front - halo
            if halo <= e < rows - halo:
                store(g, e, fields[halo][e])
        for i, (n, e) in enumerate(kept_rows(rows)):
            for j in range(3):
                kept_ref[g, i, j] = fields[n][e][j]
        return carry

    lax.fori_loop(0, levels // GROUP, group, 0)


def outer_sweep(x_ref, parts, kept_ref):
    levels, rows, cols = x_ref.shape
    load, advance, coefficients_of, store = parts
    halo = MODEL_STEPS

    def group(g, carry):
        coefficients = coefficients_of(g)
        fields = [{} for _ in range(halo + 1)]
        for i, (n, e) in enumerate(kept_rows(rows)):
            fields[n][e] = tuple(kept_ref[g, i, j] for j in range(3))
        for e in (*range(-halo, 2), *range(rows - 2, rows + halo)):
            fields[0][e] = load(g, e)
        for n in range(1, halo + 1):
            old = fields[n - 1]
            for e in (*range(n - halo, n), *range(rows - n, rows + halo - n)):
                fields[n][e] = advance(old[e - 1], old[e], old[e + 1], e, coefficients)
        for e in (*range(halo), *range(rows - halo, rows)):
            store(g, e, fields[halo][e])
        return carry

    lax.fori_loop(0, levels // GROUP, group, 0)


def side_rows(levels, rows, beside_ref, above_ref, below_ref):
    def side_row(g, e):
        if 0 <= e < rows:
            return beside_ref[g, pl.ds(e, 1), :]
        ref, row = (above_ref, e + MODEL_STEPS) if e < 0 else (below_ref, e - rows)
        flat = ref.reshape(ref.shape[0] * SUB, LANES)
        return flat[pl.ds((levels + g) * MODEL_STEPS + row, 1), :]

    return side_row


def first_model_body(wx_ref, wy_ref, x_ref, beside_ref, above_ref, below_ref, grad_ref):
    levels, rows, cols = x_ref.shape
    side_row = side_rows(levels, rows, beside_ref, above_ref, below_ref)
    sweep(x_ref, model_parts(wx_ref, wy_ref, x_ref, above_ref, below_ref, side_row, grad_ref))


def inner_model_body(wx_ref, wy_ref, x_ref, beside_ref, grad_ref, kept_ref):
    levels, rows, cols = x_ref.shape
    side_row = side_rows(levels, rows, beside_ref, None, None)
    inner_sweep(x_ref, model_parts(wx_ref, wy_ref, x_ref, None, None, side_row, grad_ref), kept_ref)


def outer_model_body(wx_ref, wy_ref, x_ref, beside_ref, above_thin_ref, below_thin_ref, inner_ref, kept_ref, *refs):
    *others, grad_ref, above_ref, below_ref = refs
    levels, rows, cols = x_ref.shape
    above_ref[...] = above_thin_ref[...].astype(F32).reshape(above_ref.shape)
    below_ref[...] = below_thin_ref[...].astype(F32).reshape(below_ref.shape)
    side_row = side_rows(levels, rows, beside_ref, above_ref, below_ref)
    outer_sweep(x_ref, model_parts(wx_ref, wy_ref, x_ref, above_ref, below_ref, side_row, grad_ref), kept_ref)
    row = sub_iota((rows, cols))
    inside = (row >= MODEL_STEPS) & (row < rows - MODEL_STEPS)
    project_levels(lambda level: jnp.where(inside, inner_ref[level], grad_ref[level]), levels, *others)


def project_body(grad_ref, *refs):
    project_levels(lambda level: grad_ref[level], grad_ref.shape[0], *refs)


def project_levels(grad, levels, *refs):
    *member_refs, wide_ref, thin_ref = refs
    own, _, rows, cols = member_refs[0].shape
    count = len(member_refs) * own

    def step(q, carry):
        carry = list(carry)
        for u in range(2):
            g = grad(2 * q + u)
            for m in range(count):
                carry[m] = carry[m] + member_refs[m // own][m % own, 2 * q + u].astype(F32) * g
        return tuple(carry)

    total = lax.fori_loop(0, levels // 2, step, (jnp.zeros((rows, cols), F32),) * count)
    for m in range(count):
        at = neighbor_of(-(m // own)) * own + m % own
        wide_ref[at] = total[m]
        thin_ref[at] = total[m].astype(BF16)


def taper(offset):
    k = offset.astype(F32)
    w = (1.0 - (k / 17.0) * (k / 17.0)) * (1.0 / TAPER_TOTAL)
    return jnp.where(jnp.abs(offset) <= REACH, w, 0.0)


def halves(x):
    high = x.astype(BF16)
    return high, (x - high.astype(F32)).astype(BF16)


def sharp_dot(a, b):
    ah, al = halves(a)
    bh, bl = halves(b)
    dot = functools.partial(jnp.dot, preferred_element_type=F32)
    return dot(ah, bh) + dot(al, bh) + dot(ah, bl)


def columns_body(left_ref, mid_ref, right_ref, wide_ref, thin_ref):
    count, rows, cols = mid_ref.shape
    wide = jnp.concatenate(
        [r[...].astype(F32).reshape(count * rows, cols) for r in (left_ref, mid_ref, right_ref)], axis=1
    )
    shape = (3 * cols, wide_ref.shape[0] // count * cols)
    lane = lane_iota(shape)
    beside = lane % MODEL_STEPS + jnp.where((lane // (SUB * MODEL_STEPS)) % 2 == 0, -MODEL_STEPS, cols)
    target = jnp.where(lane < cols, lane, beside)
    out = sharp_dot(wide, taper(sub_iota(shape) - cols - target))
    for i in range(shape[1] // cols):
        part = out[:, i * cols : (i + 1) * cols].reshape(count, rows, cols)
        wide_ref[i * count : (i + 1) * count] = part
        thin_ref[i * count : (i + 1) * count] = part.astype(BF16)


def smooth_rows(above_ref, mid_ref, below_ref):
    count, rows, cols = mid_ref.shape
    tall = jnp.concatenate(
        [
            jnp.concatenate([above_ref[m].astype(F32), mid_ref[m], below_ref[m].astype(F32)], axis=0)
            for m in range(count)
        ],
        axis=1,
    )
    shape = (rows, 3 * rows)
    out = sharp_dot(taper(lane_iota(shape) - sub_iota(shape) - rows), tall)
    return [out[:, m * cols : (m + 1) * cols] for m in range(count)]


def increments(member_refs, local_ref, levels, emit):
    own = member_refs[0].shape[0]
    count = len(member_refs) * own
    local = [local_ref[neighbor_of(-(m // own)) * own + m % own] for m in range(count)]

    def step(q, carry):
        for u in range(2):
            level = 2 * q + u
            total = member_refs[0][0, level].astype(F32) * local[0]
            for m in range(1, count):
                total = total + member_refs[m // own][m % own, level].astype(F32) * local[m]
            emit(level, total)
        return carry

    lax.fori_loop(0, levels // 2, step, 0)


def update_body(parts, residual_ref, around_ref, above_ref, mid_ref, below_ref, *refs):
    member_refs, sides_ref = refs[:parts], refs[parts]
    analysis_ref, out_ref, beside_ref, top_ref, bottom_ref, local_ref, top_wide_ref, bottom_wide_ref = refs[parts + 1 :]
    levels, rows, cols = residual_ref.shape
    own = member_refs[0].shape[0]
    count = parts * own
    for m, value in enumerate(smooth_rows(above_ref, mid_ref, below_ref)):
        local_ref[m] = value

    def emit(level, value):
        analysis_ref[level] = value
        out_ref[level] = residual_ref[level] - RELAX * value

    increments(member_refs, local_ref, levels, emit)
    for g in range(levels // GROUP):
        total = jnp.zeros((rows, LANES), F32)
        for m in range(count):
            total = total + sides_ref[m // own, m % own, g].astype(F32) * local_ref[count + m]
        beside_ref[g] = around_ref[g] - RELAX * total
    pack_rows(out_ref, 0, top_wide_ref, bottom_wide_ref)
    pack_rows(beside_ref, levels // 2, top_wide_ref, bottom_wide_ref)
    top_ref[...] = top_wide_ref[...].reshape(top_ref.shape).astype(BF16)
    bottom_ref[...] = bottom_wide_ref[...].reshape(bottom_ref.shape).astype(BF16)


def final_body(parts, residual_ref, before_ref, above_ref, mid_ref, below_ref, *refs):
    member_refs = refs[:parts]
    analysis_ref, out_ref, local_ref = refs[parts:]
    for m, value in enumerate(smooth_rows(above_ref, mid_ref, below_ref)):
        local_ref[m] = value

    def emit(level, value):
        analysis_ref[level] = before_ref[level] + value
        out_ref[level] = residual_ref[level] - RELAX * value

    increments(member_refs, local_ref, residual_ref.shape[0], emit)


def per_device(residual_in, members, wind_x, wind_y):
    levels, rows, cols = residual_in.shape
    parts = lax.axis_size("member")
    count = members.shape[0] * parts
    groups = levels // GROUP

    def shape(*dims, kind=F32):
        return jax.ShapeDtypeStruct(dims, kind)

    def both(*dims):
        return shape(*dims), shape(*dims, kind=BF16)

    def turned(x, step):
        return lax.ppermute(x, "member", [(i, (i + step) % parts) for i in range(parts)])

    def smoothed(wide, thin, planes):
        wide, thin = call(
            columns_body, both(planes, rows, cols), shift(thin, "member", 1), wide, shift(thin, "member", -1)
        )
        return shift(thin, "tile", 1), wide, shift(thin, "tile", -1)

    like = shape(levels, rows, cols)
    halo = shape((levels + groups) // 2, SUB, LANES)
    thin_halo = shape((levels + groups) // 4, 2 * SUB, LANES, kind=BF16)
    wide_halo = [pltpu.VMEM(halo.shape, F32)] * 2
    packed = shape(groups, rows, LANES)
    wind_x, wind_y = (jnp.broadcast_to(w[:, None], (levels, LANES)) for w in (wind_x, wind_y))

    first, last = call(columns_edge_body, (packed, packed), residual_in)
    left, right = shift(last, "member", 1), shift(first, "member", -1)
    blocks, left, right = lax.optimization_barrier((split_columns(members, parts), left, right))
    blocks = [turned(x, r) if r else x for r, x in enumerate(blocks)]
    around, top, bottom = call(rows_body, (packed, halo, halo), residual_in, left, right)
    members, around = lax.optimization_barrier((members, around))
    sides = side_columns(members, parts)
    above, below = shift(bottom, "tile", 1), shift(top, "tile", -1)
    grad = call(
        first_model_body, like,
        wind_x, wind_y, residual_in, around, above, below, in_specs=[VMEM] * 6,
    )
    grad, sides = lax.optimization_barrier((grad, sides))
    sides = lax.all_to_all(sides, "member", split_axis=0, concat_axis=0, tiled=True)
    grad, sides = lax.optimization_barrier((grad, sides))
    wide, thin = call(
        project_body, both(count, rows, cols), grad, *blocks, in_specs=[VMEM] * (1 + parts)
    )

    analysis, residual, beside, top, bottom = call(
        functools.partial(update_body, parts), (like, like, packed, thin_halo, thin_halo),
        residual_in, around, *smoothed(wide, thin, 2 * count), *blocks, sides,
        in_specs=[VMEM] * (6 + parts),
        scratch=[pltpu.VMEM((2 * count, rows, cols), F32)] + wide_halo,
    )
    above, below = shift(bottom, "tile", 1), shift(top, "tile", -1)
    kept = shape(groups, len(kept_rows(rows)), 3, SUB, LANES)
    inner, kept = call(inner_model_body, (like, kept), wind_x, wind_y, residual, beside)
    wide, thin = call(
        outer_model_body, both(count, rows, cols),
        wind_x, wind_y, residual, beside, above, below, inner, kept, *blocks,
        scratch=[pltpu.VMEM((levels, rows, cols), F32)] + wide_halo,
    )
    return call(
        functools.partial(final_body, parts), (like, like),
        residual, analysis, *smoothed(wide, thin, count), *blocks,
        in_specs=[VMEM] * (5 + parts), scratch=[pltpu.VMEM((count, rows, cols), F32)],
    )


def solution(mesh):
    return jax.shard_map(
        per_device,
        mesh=mesh,
        in_specs=(P(None, "tile", "member"), P("member", None, "tile", None), P(), P()),
        out_specs=(P(None, "tile", "member"), P(None, "tile", "member")),
        check_vma=False,
    )
```

```python
import functools

import jax
import jax.numpy as jnp
from jax import lax
from jax.experimental import pallas as pl
from jax.experimental.pallas import tpu as pltpu
from jax.sharding import PartitionSpec as P

ITERS = 2
MODEL_STEPS = 4
DIFFUSION = 0.1
RELAX = 0.5
REACH = 16
TAPER_TOTAL = sum(1.0 - (k / 17.0) ** 2 for k in range(-REACH, REACH + 1))
F32 = jnp.float32
BF16 = jnp.bfloat16
LANES = 128
SUB = 8
GROUP = LANES // (2 * MODEL_STEPS)

VMEM = pl.BlockSpec(memory_space=pltpu.VMEM)
PARAMS = pltpu.CompilerParams(vmem_limit_bytes=48 * 1024 * 1024)


def call(body, out_shape, *args, in_specs=None, scratch=()):
    return pl.pallas_call(
        body,
        out_shape=out_shape,
        in_specs=in_specs or [VMEM] * len(args),
        out_specs=jax.tree.map(lambda _: VMEM, out_shape),
        scratch_shapes=scratch,
        compiler_params=PARAMS,
    )(*args)


def lane_iota(shape):
    return lax.broadcasted_iota(jnp.int32, shape, len(shape) - 1)


def sub_iota(shape):
    return lax.broadcasted_iota(jnp.int32, shape, len(shape) - 2)


def neighbor_of(step):
    parts = lax.axis_size("member")
    at = lax.axis_index("member") + step
    return jnp.where(at < 0, at + parts, jnp.where(at >= parts, at - parts, at))


def columns_split_body(in_ref, *out_refs):
    cols = out_refs[0].shape[-1]
    for r, out_ref in enumerate(out_refs):
        out_ref[...] = in_ref[:, :, :, pl.ds(pl.multiple_of(neighbor_of(r) * cols, cols), cols)]


def split_columns(members, parts):
    own, levels, rows, ny = members.shape
    out = jax.ShapeDtypeStruct((own, levels, rows, ny // parts), members.dtype)
    return call(columns_split_body, (out,) * parts, members, in_specs=[VMEM])


def left_slot(k):
    return 3 * SUB - 1 - k % SUB - GROUP * (k // SUB)


def put_left(x, k, total):
    here = lane_iota(x.shape) // MODEL_STEPS == left_slot(k)
    return jnp.where(here, pltpu.roll(x, (MODEL_STEPS * (left_slot(k) + 1)) % LANES, 1), total)


def put_right(x, k, total):
    here = lane_iota(x.shape) // MODEL_STEPS == left_slot(k) + SUB
    return jnp.where(here, pltpu.roll(x, MODEL_STEPS * (left_slot(k) + SUB), 1), total)


def sides_body(in_ref, out_ref):
    parts, own, groups, rows, _ = out_ref.shape
    cols = in_ref.shape[-1] // parts
    for r in range(parts):
        before, after = (pl.ds((r + parts + d) % parts * cols, cols) for d in (-1, 1))
        for m in range(own):

            def step(g, carry):
                total = jnp.zeros((rows, LANES), F32)
                for k in range(GROUP):
                    total = put_left(in_ref[m, g * GROUP + k, :, before].astype(F32), k, total)
                    total = put_right(in_ref[m, g * GROUP + k, :, after].astype(F32), k, total)
                out_ref[r, m, g] = total.astype(out_ref.dtype)
                return carry

            lax.fori_loop(0, groups, step, 0)


def side_columns(members, parts):
    own, levels, rows, ny = members.shape
    return call(sides_body, jax.ShapeDtypeStruct((parts, own, levels // GROUP, rows, LANES), members.dtype), members)


def pack_rows(ref, at, top_ref, bottom_ref):
    upper = sub_iota((SUB, LANES)) < MODEL_STEPS
    count, rows, _ = ref.shape
    for q in range(count // 2):
        top_ref[at + q] = jnp.where(upper, ref[2 * q, :SUB], pltpu.roll(ref[2 * q + 1, :SUB], MODEL_STEPS, 0))
        bottom_ref[at + q] = jnp.where(
            upper, pltpu.roll(ref[2 * q, rows - SUB :], MODEL_STEPS, 0), ref[2 * q + 1, rows - SUB :]
        )


def rows_body(x_ref, left_ref, right_ref, beside_ref, top_ref, bottom_ref):
    beside_ref[...] = left_ref[...] + right_ref[...]
    pack_rows(x_ref, 0, top_ref, bottom_ref)
    pack_rows(beside_ref, x_ref.shape[0] // 2, top_ref, bottom_ref)


def columns_edge_body(x_ref, first_ref, last_ref):
    levels, rows, cols = x_ref.shape
    for g in range(levels // GROUP):
        first = jnp.zeros((rows, LANES), F32)
        last = jnp.zeros((rows, LANES), F32)
        for k in range(GROUP):
            last = put_left(x_ref[g * GROUP + k], k, last)
            first = put_right(x_ref[g * GROUP + k], k, first)
        first_ref[g] = first
        last_ref[g] = last


def shift(x, axis, step):
    count = lax.axis_size(axis)
    pairs = [(i, i + step) for i in range(count) if 0 <= i + step < count]
    return lax.ppermute(x, axis, pairs)


def model_parts(wx_ref, wy_ref, x_ref, above_ref, below_ref, side_row, grad_ref):
    levels, rows, cols = x_ref.shape
    tile, tiles = lax.axis_index("tile"), lax.axis_size("tile")
    member, parts = lax.axis_index("member"), lax.axis_size("member")
    x_flat = x_ref.reshape(levels * rows, cols)
    grad_flat = grad_ref.reshape(levels * rows, cols)
    halo = MODEL_STEPS
    if above_ref is not None:
        pairs = above_ref.shape[0]
        above_flat = above_ref.reshape(pairs * SUB, LANES)
        below_flat = below_ref.reshape(pairs * SUB, LANES)

    half = LANES // 2
    lane = lane_iota((SUB, LANES))
    on_right = lane % half < halo
    first_of = (lane == 0, lane == half)
    last_of = (lane == LANES - 1, lane == half - 1)
    second = (lane >= half // 2) & (lane < half + half // 2)
    inside = (on_right & (member < parts - 1)) | ((lane % half >= half - halo) & (member > 0))
    side_mask = jnp.where(inside, 1.0, 0.0).astype(F32)
    has_above = jnp.where(tile > 0, 1.0, 0.0).astype(F32)
    has_below = jnp.where(tile < tiles - 1, 1.0, 0.0).astype(F32)

    def load(g, e):
        centers = []
        for q in (2 * g, 2 * g + 1):
            if e < 0:
                centers.append(above_flat[pl.ds(q * SUB * halo + e + halo, SUB, stride=halo), :])
            elif e < rows:
                centers.append(x_flat[pl.ds(q * SUB * rows + e, SUB, stride=rows), :])
            else:
                centers.append(below_flat[pl.ds(q * SUB * halo + e - rows, SUB, stride=halo), :])
        row = jnp.broadcast_to(side_row(g, e), (SUB, LANES))
        right = pltpu.roll(row, halo, 1, stride=halo, stride_axis=0)
        left = pltpu.roll(row, LANES // 4, 1, stride=halo, stride_axis=0)
        side = jnp.where(on_right, right, left) * side_mask
        return centers[0], pltpu.roll(centers[1], half, 1), side

    def advance(before, here, after, e, coefficients):
        fore = [pltpu.roll(x, LANES - 1, 1) for x in here]
        back = [pltpu.roll(x, 1, 1) for x in here]
        fore_side = jnp.where(last_of[0], fore[0], jnp.where(last_of[1], fore[1], fore[2]))
        back_side = jnp.where(first_of[0], back[0], jnp.where(first_of[1], back[1], back[2]))
        fores = [jnp.where(last_of[i], fore[2], fore[i]) for i in range(2)] + [fore_side]
        backs = [jnp.where(first_of[i], back[2], back[i]) for i in range(2)] + [back_side]
        result = []
        for i, (own, ahead_x, ahead_y) in enumerate(coefficients):
            value = own * here[i] + ahead_x * after[i] + ahead_y * fores[i] + DIFFUSION * (before[i] + backs[i])
            if e < 0:
                value = value * has_above
            if e >= rows:
                value = value * has_below
            result.append(value * side_mask if i == 2 else value)
        return tuple(result)

    def coefficients_of(g):
        coefficients = []
        for q in (2 * g, 2 * g + 1):
            at = pl.ds(pl.multiple_of(q * SUB, SUB), SUB)
            wx, wy = wx_ref[at, :], wy_ref[at, :]
            coefficients.append((1.0 - 4.0 * DIFFUSION - wx - wy, DIFFUSION + wx, DIFFUSION + wy))
        coefficients.append(tuple(jnp.where(second, b, a) for a, b in zip(*coefficients)))
        return coefficients

    def store(g, e, field):
        grad_flat[pl.ds(2 * g * SUB * rows + e, SUB, stride=rows), :] = field[0]
        grad_flat[pl.ds((2 * g + 1) * SUB * rows + e, SUB, stride=rows), :] = pltpu.roll(field[1], half, 1)

    return load, advance, coefficients_of, store


def sweep(x_ref, parts):
    levels, rows, cols = x_ref.shape
    load, advance, coefficients_of, store = parts
    halo = MODEL_STEPS

    def group(g, carry):
        coefficients = coefficients_of(g)
        fields = [{} for _ in range(halo + 1)]
        for front in range(-halo, rows + halo):
            fields[0][front] = load(g, front)
            for n in range(1, halo + 1):
                e = front - n
                if -halo + n <= e < rows + halo - n:
                    old = fields[n - 1]
                    fields[n][e] = advance(old[e - 1], old[e], old[e + 1], e, coefficients)
            e = front - halo
            if 0 <= e < rows:
                store(g, e, fields[halo][e])
        return carry

    lax.fori_loop(0, levels // GROUP, group, 0)


def kept_rows(rows):
    return [(n, e) for n in range(1, MODEL_STEPS) for e in (n, n + 1, rows - 2 - n, rows - 1 - n)]


def inner_sweep(x_ref, parts, kept_ref):
    levels, rows, cols = x_ref.shape
    load, advance, coefficients_of, store = parts
    halo = MODEL_STEPS

    def group(g, carry):
        coefficients = coefficients_of(g)
        fields = [{} for _ in range(halo + 1)]
        for front in range(rows):
            fields[0][front] = load(g, front)
            for n in range(1, halo + 1):
                e = front - n
                if n <= e < rows - n:
                    old = fields[n - 1]
                    fields[n][e] = advance(old[e - 1], old[e], old[e + 1], e, coefficients)
            e = front - halo
            if halo <= e < rows - halo:
                store(g, e, fields[halo][e])
        for i, (n, e) in enumerate(kept_rows(rows)):
            for j in range(3):
                kept_ref[g, i, j] = fields[n][e][j]
        return carry

    lax.fori_loop(0, levels // GROUP, group, 0)


def outer_sweep(x_ref, parts, kept_ref):
    levels, rows, cols = x_ref.shape
    load, advance, coefficients_of, store = parts
    halo = MODEL_STEPS

    def group(g, carry):
        coefficients = coefficients_of(g)
        fields = [{} for _ in range(halo + 1)]
        for i, (n, e) in enumerate(kept_rows(rows)):
            fields[n][e] = tuple(kept_ref[g, i, j] for j in range(3))
        for e in (*range(-halo, 2), *range(rows - 2, rows + halo)):
            fields[0][e] = load(g, e)
        for n in range(1, halo + 1):
            old = fields[n - 1]
            for e in (*range(n - halo, n), *range(rows - n, rows + halo - n)):
                fields[n][e] = advance(old[e - 1], old[e], old[e + 1], e, coefficients)
        for e in (*range(halo), *range(rows - halo, rows)):
            store(g, e, fields[halo][e])
        return carry

    lax.fori_loop(0, levels // GROUP, group, 0)


def side_rows(levels, rows, beside_ref, above_ref, below_ref):
    def side_row(g, e):
        if 0 <= e < rows:
            return beside_ref[g, pl.ds(e, 1), :]
        ref, row = (above_ref, e + MODEL_STEPS) if e < 0 else (below_ref, e - rows)
        flat = ref.reshape(ref.shape[0] * SUB, LANES)
        return flat[pl.ds((levels + g) * MODEL_STEPS + row, 1), :]

    return side_row


def first_model_body(wx_ref, wy_ref, x_ref, beside_ref, above_ref, below_ref, grad_ref):
    levels, rows, cols = x_ref.shape
    side_row = side_rows(levels, rows, beside_ref, above_ref, below_ref)
    sweep(x_ref, model_parts(wx_ref, wy_ref, x_ref, above_ref, below_ref, side_row, grad_ref))


def inner_model_body(wx_ref, wy_ref, x_ref, beside_ref, grad_ref, kept_ref):
    levels, rows, cols = x_ref.shape
    side_row = side_rows(levels, rows, beside_ref, None, None)
    inner_sweep(x_ref, model_parts(wx_ref, wy_ref, x_ref, None, None, side_row, grad_ref), kept_ref)


def outer_model_body(wx_ref, wy_ref, x_ref, beside_ref, above_thin_ref, below_thin_ref, inner_ref, kept_ref, *refs):
    *others, grad_ref, above_ref, below_ref = refs
    levels, rows, cols = x_ref.shape
    above_ref[...] = above_thin_ref[...].astype(F32).reshape(above_ref.shape)
    below_ref[...] = below_thin_ref[...].astype(F32).reshape(below_ref.shape)
    side_row = side_rows(levels, rows, beside_ref, above_ref, below_ref)
    outer_sweep(x_ref, model_parts(wx_ref, wy_ref, x_ref, above_ref, below_ref, side_row, grad_ref), kept_ref)
    row = sub_iota((rows, cols))
    inside = (row >= MODEL_STEPS) & (row < rows - MODEL_STEPS)
    project_levels(lambda level: jnp.where(inside, inner_ref[level], grad_ref[level]), levels, *others)


def project_body(grad_ref, *refs):
    project_levels(lambda level: grad_ref[level], grad_ref.shape[0], *refs)


def project_levels(grad, levels, *refs):
    *member_refs, wide_ref, thin_ref = refs
    own, _, rows, cols = member_refs[0].shape
    count = len(member_refs) * own

    def step(q, carry):
        carry = list(carry)
        for u in range(2):
            g = grad(2 * q + u)
            for m in range(count):
                carry[m] = carry[m] + member_refs[m // own][m % own, 2 * q + u].astype(F32) * g
        return tuple(carry)

    total = lax.fori_loop(0, levels // 2, step, (jnp.zeros((rows, cols), F32),) * count)
    for m in range(count):
        at = neighbor_of(-(m // own)) * own + m % own
        wide_ref[at] = total[m]
        thin_ref[at] = total[m].astype(BF16)


def taper(offset):
    k = offset.astype(F32)
    w = (1.0 - (k / 17.0) * (k / 17.0)) * (1.0 / TAPER_TOTAL)
    return jnp.where(jnp.abs(offset) <= REACH, w, 0.0)


def halves(x):
    high = x.astype(BF16)
    return high, (x - high.astype(F32)).astype(BF16)


def sharp_dot(a, b):
    ah, al = halves(a)
    bh, bl = halves(b)
    dot = functools.partial(jnp.dot, preferred_element_type=F32)
    return dot(ah, bh) + dot(al, bh) + dot(ah, bl)


def columns_body(left_ref, mid_ref, right_ref, wide_ref, thin_ref):
    count, rows, cols = mid_ref.shape
    wide = jnp.concatenate(
        [r[...].astype(F32).reshape(count * rows, cols) for r in (left_ref, mid_ref, right_ref)], axis=1
    )
    shape = (3 * cols, wide_ref.shape[0] // count * cols)
    lane = lane_iota(shape)
    beside = lane % MODEL_STEPS + jnp.where((lane // (SUB * MODEL_STEPS)) % 2 == 0, -MODEL_STEPS, cols)
    target = jnp.where(lane < cols, lane, beside)
    out = sharp_dot(wide, taper(sub_iota(shape) - cols - target))
    for i in range(shape[1] // cols):
        part = out[:, i * cols : (i + 1) * cols].reshape(count, rows, cols)
        wide_ref[i * count : (i + 1) * count] = part
        thin_ref[i * count : (i + 1) * count] = part.astype(BF16)


def smooth_rows(above_ref, mid_ref, below_ref):
    count, rows, cols = mid_ref.shape
    tall = jnp.concatenate(
        [
            jnp.concatenate([above_ref[m].astype(F32), mid_ref[m], below_ref[m].astype(F32)], axis=0)
            for m in range(count)
        ],
        axis=1,
    )
    shape = (rows, 3 * rows)
    out = sharp_dot(taper(lane_iota(shape) - sub_iota(shape) - rows), tall)
    return [out[:, m * cols : (m + 1) * cols] for m in range(count)]


def increments(member_refs, local_ref, levels, emit):
    own = member_refs[0].shape[0]
    count = len(member_refs) * own
    local = [local_ref[neighbor_of(-(m // own)) * own + m % own] for m in range(count)]

    def step(q, carry):
        for u in range(2):
            level = 2 * q + u
            total = member_refs[0][0, level].astype(F32) * local[0]
            for m in range(1, count):
                total = total + member_refs[m // own][m % own, level].astype(F32) * local[m]
            emit(level, total)
        return carry

    lax.fori_loop(0, levels // 2, step, 0)


def update_body(parts, residual_ref, around_ref, above_ref, mid_ref, below_ref, *refs):
    member_refs, sides_ref = refs[:parts], refs[parts]
    analysis_ref, out_ref, beside_ref, top_ref, bottom_ref, local_ref, top_wide_ref, bottom_wide_ref = refs[parts + 1 :]
    levels, rows, cols = residual_ref.shape
    own = member_refs[0].shape[0]
    count = parts * own
    for m, value in enumerate(smooth_rows(above_ref, mid_ref, below_ref)):
        local_ref[m] = value

    def emit(level, value):
        analysis_ref[level] = value
        out_ref[level] = residual_ref[level] - RELAX * value

    increments(member_refs, local_ref, levels, emit)
    for g in range(levels // GROUP):
        total = jnp.zeros((rows, LANES), F32)
        for m in range(count):
            total = total + sides_ref[m // own, m % own, g].astype(F32) * local_ref[count + m]
        beside_ref[g] = around_ref[g] - RELAX * total
    pack_rows(out_ref, 0, top_wide_ref, bottom_wide_ref)
    pack_rows(beside_ref, levels // 2, top_wide_ref, bottom_wide_ref)
    top_ref[...] = top_wide_ref[...].reshape(top_ref.shape).astype(BF16)
    bottom_ref[...] = bottom_wide_ref[...].reshape(bottom_ref.shape).astype(BF16)


def final_body(parts, residual_ref, before_ref, above_ref, mid_ref, below_ref, *refs):
    member_refs = refs[:parts]
    analysis_ref, out_ref, local_ref = refs[parts:]
    for m, value in enumerate(smooth_rows(above_ref, mid_ref, below_ref)):
        local_ref[m] = value

    def emit(level, value):
        analysis_ref[level] = before_ref[level] + value
        out_ref[level] = residual_ref[level] - RELAX * value

    increments(member_refs, local_ref, residual_ref.shape[0], emit)


def per_device(residual_in, members, wind_x, wind_y):
    levels, rows, cols = residual_in.shape
    parts = lax.axis_size("member")
    count = members.shape[0] * parts
    groups = levels // GROUP

    def shape(*dims, kind=F32):
        return jax.ShapeDtypeStruct(dims, kind)

    def both(*dims):
        return shape(*dims), shape(*dims, kind=BF16)

    def turned(x, step):
        return lax.ppermute(x, "member", [(i, (i + step) % parts) for i in range(parts)])

    def smoothed(wide, thin, planes):
        wide, thin = call(
            columns_body, both(planes, rows, cols), shift(thin, "member", 1), wide, shift(thin, "member", -1)
        )
        return shift(thin, "tile", 1), wide, shift(thin, "tile", -1)

    like = shape(levels, rows, cols)
    halo = shape((levels + groups) // 2, SUB, LANES)
    thin_halo = shape((levels + groups) // 4, 2 * SUB, LANES, kind=BF16)
    wide_halo = [pltpu.VMEM(halo.shape, F32)] * 2
    packed = shape(groups, rows, LANES)
    wind_x, wind_y = (jnp.broadcast_to(w[:, None], (levels, LANES)) for w in (wind_x, wind_y))

    blocks = list(split_columns(members, parts))
    blocks[1], residual_in = lax.optimization_barrier((blocks[1], residual_in))
    early = turned(blocks[1], 1)
    first, last = call(columns_edge_body, (packed, packed), residual_in)
    left, right = shift(last, "member", 1), shift(first, "member", -1)
    blocks, early, left, right = lax.optimization_barrier((blocks, early, left, right))
    blocks = [early if r == 1 else turned(x, r) if r else x for r, x in enumerate(blocks)]
    around, top, bottom = call(rows_body, (packed, halo, halo), residual_in, left, right)
    members, around = lax.optimization_barrier((members, around))
    sides = side_columns(members, parts)
    above, below = shift(bottom, "tile", 1), shift(top, "tile", -1)
    grad = call(
        first_model_body, like,
        wind_x, wind_y, residual_in, around, above, below, in_specs=[VMEM] * 6,
    )
    grad, sides = lax.optimization_barrier((grad, sides))
    sides = lax.all_to_all(sides, "member", split_axis=0, concat_axis=0, tiled=True)
    grad, sides = lax.optimization_barrier((grad, sides))
    wide, thin = call(
        project_body, both(count, rows, cols), grad, *blocks, in_specs=[VMEM] * (1 + parts)
    )

    analysis, residual, beside, top, bottom = call(
        functools.partial(update_body, parts), (like, like, packed, thin_halo, thin_halo),
        residual_in, around, *smoothed(wide, thin, 2 * count), *blocks, sides,
        in_specs=[VMEM] * (6 + parts),
        scratch=[pltpu.VMEM((2 * count, rows, cols), F32)] + wide_halo,
    )
    above, below = shift(bottom, "tile", 1), shift(top, "tile", -1)
    kept = shape(groups, len(kept_rows(rows)), 3, SUB, LANES)
    inner, kept = call(inner_model_body, (like, kept), wind_x, wind_y, residual, beside)
    wide, thin = call(
        outer_model_body, both(count, rows, cols),
        wind_x, wind_y, residual, beside, above, below, inner, kept, *blocks,
        scratch=[pltpu.VMEM((levels, rows, cols), F32)] + wide_halo,
    )
    return call(
        functools.partial(final_body, parts), (like, like),
        residual, analysis, *smoothed(wide, thin, count), *blocks,
        in_specs=[VMEM] * (5 + parts), scratch=[pltpu.VMEM((count, rows, cols), F32)],
    )


def solution(mesh):
    return jax.shard_map(
        per_device,
        mesh=mesh,
        in_specs=(P(None, "tile", "member"), P("member", None, "tile", None), P(), P()),
        out_specs=(P(None, "tile", "member"), P(None, "tile", "member")),
        check_vma=False,
    )
```

```python
import functools

import jax
import jax.numpy as jnp
from jax import lax
from jax.experimental import pallas as pl
from jax.experimental.pallas import tpu as pltpu
from jax.sharding import PartitionSpec as P

ITERS = 2
MODEL_STEPS = 4
DIFFUSION = 0.1
RELAX = 0.5
REACH = 16
TAPER_TOTAL = sum(1.0 - (k / 17.0) ** 2 for k in range(-REACH, REACH + 1))
F32 = jnp.float32
BF16 = jnp.bfloat16
LANES = 128
SUB = 8
GROUP = LANES // (2 * MODEL_STEPS)

VMEM = pl.BlockSpec(memory_space=pltpu.VMEM)
PARAMS = pltpu.CompilerParams(vmem_limit_bytes=48 * 1024 * 1024)


def call(body, out_shape, *args, in_specs=None, scratch=()):
    return pl.pallas_call(
        body,
        out_shape=out_shape,
        in_specs=in_specs or [VMEM] * len(args),
        out_specs=jax.tree.map(lambda _: VMEM, out_shape),
        scratch_shapes=scratch,
        compiler_params=PARAMS,
    )(*args)


def lane_iota(shape):
    return lax.broadcasted_iota(jnp.int32, shape, len(shape) - 1)


def sub_iota(shape):
    return lax.broadcasted_iota(jnp.int32, shape, len(shape) - 2)


def neighbor_of(step):
    parts = lax.axis_size("member")
    at = lax.axis_index("member") + step
    return jnp.where(at < 0, at + parts, jnp.where(at >= parts, at - parts, at))


def left_slot(k):
    return 3 * SUB - 1 - k % SUB - GROUP * (k // SUB)


def put_left(x, k, total):
    here = lane_iota(x.shape) // MODEL_STEPS == left_slot(k)
    return jnp.where(here, pltpu.roll(x, (MODEL_STEPS * (left_slot(k) + 1)) % LANES, 1), total)


def put_right(x, k, total):
    here = lane_iota(x.shape) // MODEL_STEPS == left_slot(k) + SUB
    return jnp.where(here, pltpu.roll(x, MODEL_STEPS * (left_slot(k) + SUB), 1), total)


def sides_body(in_ref, out_ref):
    parts, own, groups, rows, _ = out_ref.shape
    cols = in_ref.shape[-1] // parts
    for r in range(parts):
        before, after = (pl.ds((r + parts + d) % parts * cols, cols) for d in (-1, 1))
        for m in range(own):

            def step(g, carry):
                total = jnp.zeros((rows, LANES), F32)
                for k in range(GROUP):
                    total = put_left(in_ref[m, g * GROUP + k, :, before].astype(F32), k, total)
                    total = put_right(in_ref[m, g * GROUP + k, :, after].astype(F32), k, total)
                out_ref[r, m, g] = total.astype(out_ref.dtype)
                return carry

            lax.fori_loop(0, groups, step, 0)


def side_columns(members, parts):
    own, levels, rows, ny = members.shape
    return call(sides_body, jax.ShapeDtypeStruct((parts, own, levels // GROUP, rows, LANES), members.dtype), members)


def pack_rows(ref, at, top_ref, bottom_ref):
    upper = sub_iota((SUB, LANES)) < MODEL_STEPS
    count, rows, _ = ref.shape
    for q in range(count // 2):
        top_ref[at + q] = jnp.where(upper, ref[2 * q, :SUB], pltpu.roll(ref[2 * q + 1, :SUB], MODEL_STEPS, 0))
        bottom_ref[at + q] = jnp.where(
            upper, pltpu.roll(ref[2 * q, rows - SUB :], MODEL_STEPS, 0), ref[2 * q + 1, rows - SUB :]
        )


def edge_plane(ref, levels, g):
    per = ref.shape[1] - levels
    return g // per, levels + g % per


def rows_body(x_ref, left_ref, right_ref, beside_ref, top_ref, bottom_ref):
    levels = x_ref.shape[0]
    for g in range(levels // GROUP):
        left, right = (ref[edge_plane(ref, levels, g)].astype(F32) for ref in (left_ref, right_ref))
        beside_ref[g] = left + right
    pack_rows(x_ref, 0, top_ref, bottom_ref)
    pack_rows(beside_ref, levels // 2, top_ref, bottom_ref)


def opening_body(x_ref, members_ref, *block_refs):
    levels, rows, cols = x_ref.shape
    for g in range(levels // GROUP):
        first = jnp.zeros((rows, LANES), F32)
        last = jnp.zeros((rows, LANES), F32)
        for k in range(GROUP):
            last = put_left(x_ref[g * GROUP + k], k, last)
            first = put_right(x_ref[g * GROUP + k], k, first)
        for ref, edge in ((block_refs[1], last), (block_refs[-1], first)):
            ref[edge_plane(ref, levels, g)] = edge.astype(ref.dtype)
    for r, block_ref in enumerate(block_refs):
        at = pl.ds(pl.multiple_of(neighbor_of(r) * cols, cols), cols)
        block_ref[:, :levels] = members_ref[:, :, :, at]


def shift(x, axis, step):
    count = lax.axis_size(axis)
    pairs = [(i, i + step) for i in range(count) if 0 <= i + step < count]
    return lax.ppermute(x, axis, pairs)


def model_parts(wx_ref, wy_ref, x_ref, above_ref, below_ref, side_row, grad_ref):
    levels, rows, cols = x_ref.shape
    tile, tiles = lax.axis_index("tile"), lax.axis_size("tile")
    member, parts = lax.axis_index("member"), lax.axis_size("member")
    x_flat = x_ref.reshape(levels * rows, cols)
    grad_flat = grad_ref.reshape(levels * rows, cols)
    halo = MODEL_STEPS
    if above_ref is not None:
        pairs = above_ref.shape[0]
        above_flat = above_ref.reshape(pairs * SUB, LANES)
        below_flat = below_ref.reshape(pairs * SUB, LANES)

    half = LANES // 2
    lane = lane_iota((SUB, LANES))
    on_right = lane % half < halo
    first_of = (lane == 0, lane == half)
    last_of = (lane == LANES - 1, lane == half - 1)
    second = (lane >= half // 2) & (lane < half + half // 2)
    inside = (on_right & (member < parts - 1)) | ((lane % half >= half - halo) & (member > 0))
    side_mask = jnp.where(inside, 1.0, 0.0).astype(F32)
    has_above = jnp.where(tile > 0, 1.0, 0.0).astype(F32)
    has_below = jnp.where(tile < tiles - 1, 1.0, 0.0).astype(F32)

    def load(g, e):
        centers = []
        for q in (2 * g, 2 * g + 1):
            if e < 0:
                centers.append(above_flat[pl.ds(q * SUB * halo + e + halo, SUB, stride=halo), :])
            elif e < rows:
                centers.append(x_flat[pl.ds(q * SUB * rows + e, SUB, stride=rows), :])
            else:
                centers.append(below_flat[pl.ds(q * SUB * halo + e - rows, SUB, stride=halo), :])
        row = jnp.broadcast_to(side_row(g, e), (SUB, LANES))
        right = pltpu.roll(row, halo, 1, stride=halo, stride_axis=0)
        left = pltpu.roll(row, LANES // 4, 1, stride=halo, stride_axis=0)
        side = jnp.where(on_right, right, left) * side_mask
        return centers[0], pltpu.roll(centers[1], half, 1), side

    def advance(before, here, after, e, coefficients):
        fore = [pltpu.roll(x, LANES - 1, 1) for x in here]
        back = [pltpu.roll(x, 1, 1) for x in here]
        fore_side = jnp.where(last_of[0], fore[0], jnp.where(last_of[1], fore[1], fore[2]))
        back_side = jnp.where(first_of[0], back[0], jnp.where(first_of[1], back[1], back[2]))
        fores = [jnp.where(last_of[i], fore[2], fore[i]) for i in range(2)] + [fore_side]
        backs = [jnp.where(first_of[i], back[2], back[i]) for i in range(2)] + [back_side]
        result = []
        for i, (own, ahead_x, ahead_y) in enumerate(coefficients):
            value = own * here[i] + ahead_x * after[i] + ahead_y * fores[i] + DIFFUSION * (before[i] + backs[i])
            if e < 0:
                value = value * has_above
            if e >= rows:
                value = value * has_below
            result.append(value * side_mask if i == 2 else value)
        return tuple(result)

    def coefficients_of(g):
        coefficients = []
        for q in (2 * g, 2 * g + 1):
            at = pl.ds(pl.multiple_of(q * SUB, SUB), SUB)
            wx, wy = wx_ref[at, :], wy_ref[at, :]
            coefficients.append((1.0 - 4.0 * DIFFUSION - wx - wy, DIFFUSION + wx, DIFFUSION + wy))
        coefficients.append(tuple(jnp.where(second, b, a) for a, b in zip(*coefficients)))
        return coefficients

    def store(g, e, field):
        grad_flat[pl.ds(2 * g * SUB * rows + e, SUB, stride=rows), :] = field[0]
        grad_flat[pl.ds((2 * g + 1) * SUB * rows + e, SUB, stride=rows), :] = pltpu.roll(field[1], half, 1)

    return load, advance, coefficients_of, store


def sweep(x_ref, parts):
    levels, rows, cols = x_ref.shape
    load, advance, coefficients_of, store = parts
    halo = MODEL_STEPS

    def group(g, carry):
        coefficients = coefficients_of(g)
        fields = [{} for _ in range(halo + 1)]
        for front in range(-halo, rows + halo):
            fields[0][front] = load(g, front)
            for n in range(1, halo + 1):
                e = front - n
                if -halo + n <= e < rows + halo - n:
                    old = fields[n - 1]
                    fields[n][e] = advance(old[e - 1], old[e], old[e + 1], e, coefficients)
            e = front - halo
            if 0 <= e < rows:
                store(g, e, fields[halo][e])
        return carry

    lax.fori_loop(0, levels // GROUP, group, 0)


def kept_rows(rows):
    return [(n, e) for n in range(1, MODEL_STEPS) for e in (n, n + 1, rows - 2 - n, rows - 1 - n)]


def inner_sweep(x_ref, parts, kept_ref):
    levels, rows, cols = x_ref.shape
    load, advance, coefficients_of, store = parts
    halo = MODEL_STEPS

    def group(g, carry):
        coefficients = coefficients_of(g)
        fields = [{} for _ in range(halo + 1)]
        for front in range(rows):
            fields[0][front] = load(g, front)
            for n in range(1, halo + 1):
                e = front - n
                if n <= e < rows - n:
                    old = fields[n - 1]
                    fields[n][e] = advance(old[e - 1], old[e], old[e + 1], e, coefficients)
            e = front - halo
            if halo <= e < rows - halo:
                store(g, e, fields[halo][e])
        for i, (n, e) in enumerate(kept_rows(rows)):
            for j in range(3):
                kept_ref[g, i, j] = fields[n][e][j]
        return carry

    lax.fori_loop(0, levels // GROUP, group, 0)


def outer_sweep(x_ref, parts, kept_ref):
    levels, rows, cols = x_ref.shape
    load, advance, coefficients_of, store = parts
    halo = MODEL_STEPS

    def group(g, carry):
        coefficients = coefficients_of(g)
        fields = [{} for _ in range(halo + 1)]
        for i, (n, e) in enumerate(kept_rows(rows)):
            fields[n][e] = tuple(kept_ref[g, i, j] for j in range(3))
        for e in (*range(-halo, 2), *range(rows - 2, rows + halo)):
            fields[0][e] = load(g, e)
        for n in range(1, halo + 1):
            old = fields[n - 1]
            for e in (*range(n - halo, n), *range(rows - n, rows + halo - n)):
                fields[n][e] = advance(old[e - 1], old[e], old[e + 1], e, coefficients)
        for e in (*range(halo), *range(rows - halo, rows)):
            store(g, e, fields[halo][e])
        return carry

    lax.fori_loop(0, levels // GROUP, group, 0)


def side_rows(levels, rows, beside_ref, above_ref, below_ref):
    def side_row(g, e):
        if 0 <= e < rows:
            return beside_ref[g, pl.ds(e, 1), :]
        ref, row = (above_ref, e + MODEL_STEPS) if e < 0 else (below_ref, e - rows)
        flat = ref.reshape(ref.shape[0] * SUB, LANES)
        return flat[pl.ds((levels + g) * MODEL_STEPS + row, 1), :]

    return side_row


def first_model_body(wx_ref, wy_ref, x_ref, beside_ref, above_ref, below_ref, grad_ref):
    levels, rows, cols = x_ref.shape
    side_row = side_rows(levels, rows, beside_ref, above_ref, below_ref)
    sweep(x_ref, model_parts(wx_ref, wy_ref, x_ref, above_ref, below_ref, side_row, grad_ref))


def inner_model_body(wx_ref, wy_ref, x_ref, beside_ref, grad_ref, kept_ref):
    levels, rows, cols = x_ref.shape
    side_row = side_rows(levels, rows, beside_ref, None, None)
    inner_sweep(x_ref, model_parts(wx_ref, wy_ref, x_ref, None, None, side_row, grad_ref), kept_ref)


def outer_model_body(wx_ref, wy_ref, x_ref, beside_ref, above_thin_ref, below_thin_ref, inner_ref, kept_ref, *refs):
    *others, grad_ref, above_ref, below_ref = refs
    levels, rows, cols = x_ref.shape
    above_ref[...] = above_thin_ref[...].astype(F32).reshape(above_ref.shape)
    below_ref[...] = below_thin_ref[...].astype(F32).reshape(below_ref.shape)
    side_row = side_rows(levels, rows, beside_ref, above_ref, below_ref)
    outer_sweep(x_ref, model_parts(wx_ref, wy_ref, x_ref, above_ref, below_ref, side_row, grad_ref), kept_ref)
    row = sub_iota((rows, cols))
    inside = (row >= MODEL_STEPS) & (row < rows - MODEL_STEPS)
    project_levels(lambda level: jnp.where(inside, inner_ref[level], grad_ref[level]), levels, *others)


def project_body(grad_ref, *refs):
    project_levels(lambda level: grad_ref[level], grad_ref.shape[0], *refs)


def project_levels(grad, levels, *refs):
    *member_refs, wide_ref, thin_ref = refs
    own, _, rows, cols = member_refs[0].shape
    count = len(member_refs) * own

    def step(q, carry):
        carry = list(carry)
        for u in range(2):
            g = grad(2 * q + u)
            for m in range(count):
                carry[m] = carry[m] + member_refs[m // own][m % own, 2 * q + u].astype(F32) * g
        return tuple(carry)

    total = lax.fori_loop(0, levels // 2, step, (jnp.zeros((rows, cols), F32),) * count)
    for m in range(count):
        at = neighbor_of(-(m // own)) * own + m % own
        wide_ref[at] = total[m]
        thin_ref[at] = total[m].astype(BF16)


def taper(offset):
    k = offset.astype(F32)
    w = (1.0 - (k / 17.0) * (k / 17.0)) * (1.0 / TAPER_TOTAL)
    return jnp.where(jnp.abs(offset) <= REACH, w, 0.0)


def halves(x):
    high = x.astype(BF16)
    return high, (x - high.astype(F32)).astype(BF16)


def sharp_dot(a, b):
    ah, al = halves(a)
    bh, bl = halves(b)
    dot = functools.partial(jnp.dot, preferred_element_type=F32)
    return dot(ah, bh) + dot(al, bh) + dot(ah, bl)


def columns_body(left_ref, mid_ref, right_ref, wide_ref, thin_ref):
    count, rows, cols = mid_ref.shape
    wide = jnp.concatenate(
        [r[...].astype(F32).reshape(count * rows, cols) for r in (left_ref, mid_ref, right_ref)], axis=1
    )
    shape = (3 * cols, wide_ref.shape[0] // count * cols)
    lane = lane_iota(shape)
    beside = lane % MODEL_STEPS + jnp.where((lane // (SUB * MODEL_STEPS)) % 2 == 0, -MODEL_STEPS, cols)
    target = jnp.where(lane < cols, lane, beside)
    out = sharp_dot(wide, taper(sub_iota(shape) - cols - target))
    for i in range(shape[1] // cols):
        part = out[:, i * cols : (i + 1) * cols].reshape(count, rows, cols)
        wide_ref[i * count : (i + 1) * count] = part
        thin_ref[i * count : (i + 1) * count] = part.astype(BF16)


def smooth_rows(above_ref, mid_ref, below_ref):
    count, rows, cols = mid_ref.shape
    tall = jnp.concatenate(
        [
            jnp.concatenate([above_ref[m].astype(F32), mid_ref[m], below_ref[m].astype(F32)], axis=0)
            for m in range(count)
        ],
        axis=1,
    )
    shape = (rows, 3 * rows)
    out = sharp_dot(taper(lane_iota(shape) - sub_iota(shape) - rows), tall)
    return [out[:, m * cols : (m + 1) * cols] for m in range(count)]


def increments(member_refs, local_ref, levels, emit):
    own = member_refs[0].shape[0]
    count = len(member_refs) * own
    local = [local_ref[neighbor_of(-(m // own)) * own + m % own] for m in range(count)]

    def step(q, carry):
        for u in range(2):
            level = 2 * q + u
            total = member_refs[0][0, level].astype(F32) * local[0]
            for m in range(1, count):
                total = total + member_refs[m // own][m % own, level].astype(F32) * local[m]
            emit(level, total)
        return carry

    lax.fori_loop(0, levels // 2, step, 0)


def update_body(parts, residual_ref, around_ref, above_ref, mid_ref, below_ref, *refs):
    member_refs, sides_ref = refs[:parts], refs[parts]
    analysis_ref, out_ref, beside_ref, top_ref, bottom_ref, local_ref, top_wide_ref, bottom_wide_ref = refs[parts + 1 :]
    levels, rows, cols = residual_ref.shape
    own = member_refs[0].shape[0]
    count = parts * own
    for m, value in enumerate(smooth_rows(above_ref, mid_ref, below_ref)):
        local_ref[m] = value

    def emit(level, value):
        analysis_ref[level] = value
        out_ref[level] = residual_ref[level] - RELAX * value

    increments(member_refs, local_ref, levels, emit)
    for g in range(levels // GROUP):
        total = jnp.zeros((rows, LANES), F32)
        for m in range(count):
            total = total + sides_ref[m // own, m % own, g].astype(F32) * local_ref[count + m]
        beside_ref[g] = around_ref[g] - RELAX * total
    pack_rows(out_ref, 0, top_wide_ref, bottom_wide_ref)
    pack_rows(beside_ref, levels // 2, top_wide_ref, bottom_wide_ref)
    top_ref[...] = top_wide_ref[...].reshape(top_ref.shape).astype(BF16)
    bottom_ref[...] = bottom_wide_ref[...].reshape(bottom_ref.shape).astype(BF16)


def final_body(parts, residual_ref, before_ref, above_ref, mid_ref, below_ref, *refs):
    member_refs = refs[:parts]
    analysis_ref, out_ref, local_ref = refs[parts:]
    for m, value in enumerate(smooth_rows(above_ref, mid_ref, below_ref)):
        local_ref[m] = value

    def emit(level, value):
        analysis_ref[level] = before_ref[level] + value
        out_ref[level] = residual_ref[level] - RELAX * value

    increments(member_refs, local_ref, residual_ref.shape[0], emit)


def per_device(residual_in, members, wind_x, wind_y):
    levels, rows, cols = residual_in.shape
    parts = lax.axis_size("member")
    count = members.shape[0] * parts
    groups = levels // GROUP

    def shape(*dims, kind=F32):
        return jax.ShapeDtypeStruct(dims, kind)

    def both(*dims):
        return shape(*dims), shape(*dims, kind=BF16)

    def turned(x, step):
        return lax.ppermute(x, "member", [(i, (i + step) % parts) for i in range(parts)])

    def smoothed(wide, thin, planes):
        wide, thin = call(
            columns_body, both(planes, rows, cols), shift(thin, "member", 1), wide, shift(thin, "member", -1)
        )
        return shift(thin, "tile", 1), wide, shift(thin, "tile", -1)

    like = shape(levels, rows, cols)
    halo = shape((levels + groups) // 2, SUB, LANES)
    thin_halo = shape((levels + groups) // 4, 2 * SUB, LANES, kind=BF16)
    wide_halo = [pltpu.VMEM(halo.shape, F32)] * 2
    packed = shape(groups, rows, LANES)
    wind_x, wind_y = (jnp.broadcast_to(w[:, None], (levels, LANES)) for w in (wind_x, wind_y))

    own = members.shape[0]
    near = (1, parts - 1)
    extra = [groups // own if r in near else 0 for r in range(parts)]
    blocks = [shape(own, levels + n, rows, cols, kind=members.dtype) for n in extra]
    blocks = list(call(opening_body, tuple(blocks), residual_in, members))
    for r in near:
        blocks[r] = turned(blocks[r], r)
    blocks[1], members, *rest = lax.optimization_barrier((blocks[1], members, *blocks[2:-1]))
    blocks[2:-1] = [turned(x, r) for r, x in enumerate(rest, 2)]
    sides = side_columns(members, parts)
    blocks[-1], sides = lax.optimization_barrier((blocks[-1], sides))
    around, top, bottom = call(rows_body, (packed, halo, halo), residual_in, blocks[1], blocks[-1])
    above, below = shift(bottom, "tile", 1), shift(top, "tile", -1)
    grad = call(
        first_model_body, like,
        wind_x, wind_y, residual_in, around, above, below, in_specs=[VMEM] * 6,
    )
    grad, sides = lax.optimization_barrier((grad, sides))
    sides = lax.all_to_all(sides, "member", split_axis=0, concat_axis=0, tiled=True)
    grad, sides = lax.optimization_barrier((grad, sides))
    wide, thin = call(
        project_body, both(count, rows, cols), grad, *blocks, in_specs=[VMEM] * (1 + parts)
    )

    analysis, residual, beside, top, bottom = call(
        functools.partial(update_body, parts), (like, like, packed, thin_halo, thin_halo),
        residual_in, around, *smoothed(wide, thin, 2 * count), *blocks, sides,
        in_specs=[VMEM] * (6 + parts),
        scratch=[pltpu.VMEM((2 * count, rows, cols), F32)] + wide_halo,
    )
    above, below = shift(bottom, "tile", 1), shift(top, "tile", -1)
    kept = shape(groups, len(kept_rows(rows)), 3, SUB, LANES)
    inner, kept = call(inner_model_body, (like, kept), wind_x, wind_y, residual, beside)
    wide, thin = call(
        outer_model_body, both(count, rows, cols),
        wind_x, wind_y, residual, beside, above, below, inner, kept, *blocks,
        scratch=[pltpu.VMEM((levels, rows, cols), F32)] + wide_halo,
    )
    return call(
        functools.partial(final_body, parts), (like, like),
        residual, analysis, *smoothed(wide, thin, count), *blocks,
        in_specs=[VMEM] * (5 + parts), scratch=[pltpu.VMEM((count, rows, cols), F32)],
    )


def solution(mesh):
    return jax.shard_map(
        per_device,
        mesh=mesh,
        in_specs=(P(None, "tile", "member"), P("member", None, "tile", None), P(), P()),
        out_specs=(P(None, "tile", "member"), P(None, "tile", "member")),
        check_vma=False,
    )
```

```python
import functools

import jax
import jax.numpy as jnp
from jax import lax
from jax.experimental import pallas as pl
from jax.experimental.pallas import tpu as pltpu
from jax.sharding import PartitionSpec as P

ITERS = 2
MODEL_STEPS = 4
DIFFUSION = 0.1
RELAX = 0.5
REACH = 16
TAPER_TOTAL = sum(1.0 - (k / 17.0) ** 2 for k in range(-REACH, REACH + 1))
F32 = jnp.float32
BF16 = jnp.bfloat16
LANES = 128
SUB = 8
GROUP = LANES // (2 * MODEL_STEPS)

VMEM = pl.BlockSpec(memory_space=pltpu.VMEM)
PARAMS = pltpu.CompilerParams(vmem_limit_bytes=48 * 1024 * 1024)


def call(body, out_shape, *args, in_specs=None, scratch=()):
    return pl.pallas_call(
        body,
        out_shape=out_shape,
        in_specs=in_specs or [VMEM] * len(args),
        out_specs=jax.tree.map(lambda _: VMEM, out_shape),
        scratch_shapes=scratch,
        compiler_params=PARAMS,
    )(*args)


def lane_iota(shape):
    return lax.broadcasted_iota(jnp.int32, shape, len(shape) - 1)


def sub_iota(shape):
    return lax.broadcasted_iota(jnp.int32, shape, len(shape) - 2)


def neighbor_of(step):
    parts = lax.axis_size("member")
    at = lax.axis_index("member") + step
    return jnp.where(at < 0, at + parts, jnp.where(at >= parts, at - parts, at))


def block_of(step, cols):
    return pl.ds(pl.multiple_of(neighbor_of(step) * cols, cols), cols)


def columns_split_body(in_ref, *out_refs):
    cols = out_refs[0].shape[-1]
    for r, out_ref in enumerate(out_refs):
        out_ref[...] = in_ref[:, :, :, block_of(r, cols)]


def split_columns(members, parts):
    own, levels, rows, ny = members.shape
    out = jax.ShapeDtypeStruct((own, levels, rows, ny // parts), members.dtype)
    return call(columns_split_body, (out,) * 2, members)


def left_slot(k):
    return 3 * SUB - 1 - k % SUB - GROUP * (k // SUB)


def put_left(x, k, total):
    here = lane_iota(x.shape) // MODEL_STEPS == left_slot(k)
    return jnp.where(here, pltpu.roll(x, (MODEL_STEPS * (left_slot(k) + 1)) % LANES, 1), total)


def put_right(x, k, total):
    here = lane_iota(x.shape) // MODEL_STEPS == left_slot(k) + SUB
    return jnp.where(here, pltpu.roll(x, MODEL_STEPS * (left_slot(k) + SUB), 1), total)


def sides_body(in_ref, *out_refs):
    levels = in_ref.shape[1]
    own, groups, rows, _ = out_refs[0].shape
    cols = in_ref.shape[-1] // len(out_refs)
    for r, out_ref in enumerate(out_refs):
        start = out_ref.shape[1] - groups
        if start:
            out_ref[:, :start] = in_ref[:, :, :, block_of(r, cols)]
        before, after = block_of(r - 1, cols), block_of(r + 1, cols)
        for m in range(own):

            def step(g, carry):
                total = jnp.zeros((rows, LANES), F32)
                for k in range(GROUP):
                    total = put_left(in_ref[m, g * GROUP + k, :, before].astype(F32), k, total)
                    total = put_right(in_ref[m, g * GROUP + k, :, after].astype(F32), k, total)
                out_ref[m, start + g] = total.astype(out_ref.dtype)
                return carry

            lax.fori_loop(0, groups, step, 0)


def side_columns(members, parts):
    own, levels, rows, ny = members.shape
    groups = levels // GROUP
    thin = jax.ShapeDtypeStruct((own, groups, rows, LANES), members.dtype)
    full = jax.ShapeDtypeStruct((own, levels + groups, rows, LANES), members.dtype)
    return call(sides_body, (thin,) * 2 + (full,) * (parts - 2), members)


def pack_rows(ref, at, top_ref, bottom_ref):
    upper = sub_iota((SUB, LANES)) < MODEL_STEPS
    count, rows, _ = ref.shape
    for q in range(count // 2):
        top_ref[at + q] = jnp.where(upper, ref[2 * q, :SUB], pltpu.roll(ref[2 * q + 1, :SUB], MODEL_STEPS, 0))
        bottom_ref[at + q] = jnp.where(
            upper, pltpu.roll(ref[2 * q, rows - SUB :], MODEL_STEPS, 0), ref[2 * q + 1, rows - SUB :]
        )


def rows_body(x_ref, left_ref, right_ref, beside_ref, top_ref, bottom_ref):
    beside_ref[...] = left_ref[...] + right_ref[...]
    pack_rows(x_ref, 0, top_ref, bottom_ref)
    pack_rows(beside_ref, x_ref.shape[0] // 2, top_ref, bottom_ref)


def columns_edge_body(x_ref, first_ref, last_ref):
    levels, rows, cols = x_ref.shape
    for g in range(levels // GROUP):
        first = jnp.zeros((rows, LANES), F32)
        last = jnp.zeros((rows, LANES), F32)
        for k in range(GROUP):
            last = put_left(x_ref[g * GROUP + k], k, last)
            first = put_right(x_ref[g * GROUP + k], k, first)
        first_ref[g] = first
        last_ref[g] = last


def shift(x, axis, step):
    count = lax.axis_size(axis)
    pairs = [(i, i + step) for i in range(count) if 0 <= i + step < count]
    return lax.ppermute(x, axis, pairs)


def model_parts(wx_ref, wy_ref, x_ref, above_ref, below_ref, side_row, grad_ref):
    levels, rows, cols = x_ref.shape
    tile, tiles = lax.axis_index("tile"), lax.axis_size("tile")
    member, parts = lax.axis_index("member"), lax.axis_size("member")
    x_flat = x_ref.reshape(levels * rows, cols)
    grad_flat = grad_ref.reshape(levels * rows, cols)
    halo = MODEL_STEPS
    if above_ref is not None:
        pairs = above_ref.shape[0]
        above_flat = above_ref.reshape(pairs * SUB, LANES)
        below_flat = below_ref.reshape(pairs * SUB, LANES)

    half = LANES // 2
    lane = lane_iota((SUB, LANES))
    on_right = lane % half < halo
    first_of = (lane == 0, lane == half)
    last_of = (lane == LANES - 1, lane == half - 1)
    second = (lane >= half // 2) & (lane < half + half // 2)
    inside = (on_right & (member < parts - 1)) | ((lane % half >= half - halo) & (member > 0))
    side_mask = jnp.where(inside, 1.0, 0.0).astype(F32)
    has_above = jnp.where(tile > 0, 1.0, 0.0).astype(F32)
    has_below = jnp.where(tile < tiles - 1, 1.0, 0.0).astype(F32)

    def load(g, e):
        centers = []
        for q in (2 * g, 2 * g + 1):
            if e < 0:
                centers.append(above_flat[pl.ds(q * SUB * halo + e + halo, SUB, stride=halo), :])
            elif e < rows:
                centers.append(x_flat[pl.ds(q * SUB * rows + e, SUB, stride=rows), :])
            else:
                centers.append(below_flat[pl.ds(q * SUB * halo + e - rows, SUB, stride=halo), :])
        row = jnp.broadcast_to(side_row(g, e), (SUB, LANES))
        right = pltpu.roll(row, halo, 1, stride=halo, stride_axis=0)
        left = pltpu.roll(row, LANES // 4, 1, stride=halo, stride_axis=0)
        side = jnp.where(on_right, right, left) * side_mask
        return centers[0], pltpu.roll(centers[1], half, 1), side

    def advance(before, here, after, e, coefficients):
        fore = [pltpu.roll(x, LANES - 1, 1) for x in here]
        back = [pltpu.roll(x, 1, 1) for x in here]
        fore_side = jnp.where(last_of[0], fore[0], jnp.where(last_of[1], fore[1], fore[2]))
        back_side = jnp.where(first_of[0], back[0], jnp.where(first_of[1], back[1], back[2]))
        fores = [jnp.where(last_of[i], fore[2], fore[i]) for i in range(2)] + [fore_side]
        backs = [jnp.where(first_of[i], back[2], back[i]) for i in range(2)] + [back_side]
        result = []
        for i, (own, ahead_x, ahead_y) in enumerate(coefficients):
            value = own * here[i] + ahead_x * after[i] + ahead_y * fores[i] + DIFFUSION * (before[i] + backs[i])
            if e < 0:
                value = value * has_above
            if e >= rows:
                value = value * has_below
            result.append(value * side_mask if i == 2 else value)
        return tuple(result)

    def coefficients_of(g):
        coefficients = []
        for q in (2 * g, 2 * g + 1):
            at = pl.ds(pl.multiple_of(q * SUB, SUB), SUB)
            wx, wy = wx_ref[at, :], wy_ref[at, :]
            coefficients.append((1.0 - 4.0 * DIFFUSION - wx - wy, DIFFUSION + wx, DIFFUSION + wy))
        coefficients.append(tuple(jnp.where(second, b, a) for a, b in zip(*coefficients)))
        return coefficients

    def store(g, e, field):
        grad_flat[pl.ds(2 * g * SUB * rows + e, SUB, stride=rows), :] = field[0]
        grad_flat[pl.ds((2 * g + 1) * SUB * rows + e, SUB, stride=rows), :] = pltpu.roll(field[1], half, 1)

    return load, advance, coefficients_of, store


def sweep(x_ref, parts):
    levels, rows, cols = x_ref.shape
    load, advance, coefficients_of, store = parts
    halo = MODEL_STEPS

    def group(g, carry):
        coefficients = coefficients_of(g)
        fields = [{} for _ in range(halo + 1)]
        for front in range(-halo, rows + halo):
            fields[0][front] = load(g, front)
            for n in range(1, halo + 1):
                e = front - n
                if -halo + n <= e < rows + halo - n:
                    old = fields[n - 1]
                    fields[n][e] = advance(old[e - 1], old[e], old[e + 1], e, coefficients)
            e = front - halo
            if 0 <= e < rows:
                store(g, e, fields[halo][e])
        return carry

    lax.fori_loop(0, levels // GROUP, group, 0)


def kept_rows(rows):
    return [(n, e) for n in range(1, MODEL_STEPS) for e in (n, n + 1, rows - 2 - n, rows - 1 - n)]


def inner_sweep(x_ref, parts, kept_ref):
    levels, rows, cols = x_ref.shape
    load, advance, coefficients_of, store = parts
    halo = MODEL_STEPS

    def group(g, carry):
        coefficients = coefficients_of(g)
        fields = [{} for _ in range(halo + 1)]
        for front in range(rows):
            fields[0][front] = load(g, front)
            for n in range(1, halo + 1):
                e = front - n
                if n <= e < rows - n:
                    old = fields[n - 1]
                    fields[n][e] = advance(old[e - 1], old[e], old[e + 1], e, coefficients)
            e = front - halo
            if halo <= e < rows - halo:
                store(g, e, fields[halo][e])
        for i, (n, e) in enumerate(kept_rows(rows)):
            for j in range(3):
                kept_ref[g, i, j] = fields[n][e][j]
        return carry

    lax.fori_loop(0, levels // GROUP, group, 0)


def outer_sweep(x_ref, parts, kept_ref):
    levels, rows, cols = x_ref.shape
    load, advance, coefficients_of, store = parts
    halo = MODEL_STEPS

    def group(g, carry):
        coefficients = coefficients_of(g)
        fields = [{} for _ in range(halo + 1)]
        for i, (n, e) in enumerate(kept_rows(rows)):
            fields[n][e] = tuple(kept_ref[g, i, j] for j in range(3))
        for e in (*range(-halo, 2), *range(rows - 2, rows + halo)):
            fields[0][e] = load(g, e)
        for n in range(1, halo + 1):
            old = fields[n - 1]
            for e in (*range(n - halo, n), *range(rows - n, rows + halo - n)):
                fields[n][e] = advance(old[e - 1], old[e], old[e + 1], e, coefficients)
        for e in (*range(halo), *range(rows - halo, rows)):
            store(g, e, fields[halo][e])
        return carry

    lax.fori_loop(0, levels // GROUP, group, 0)


def side_rows(levels, rows, beside_ref, above_ref, below_ref):
    def side_row(g, e):
        if 0 <= e < rows:
            return beside_ref[g, pl.ds(e, 1), :]
        ref, row = (above_ref, e + MODEL_STEPS) if e < 0 else (below_ref, e - rows)
        flat = ref.reshape(ref.shape[0] * SUB, LANES)
        return flat[pl.ds((levels + g) * MODEL_STEPS + row, 1), :]

    return side_row


def first_model_body(wx_ref, wy_ref, x_ref, beside_ref, above_ref, below_ref, grad_ref):
    levels, rows, cols = x_ref.shape
    side_row = side_rows(levels, rows, beside_ref, above_ref, below_ref)
    sweep(x_ref, model_parts(wx_ref, wy_ref, x_ref, above_ref, below_ref, side_row, grad_ref))


def inner_model_body(wx_ref, wy_ref, x_ref, beside_ref, grad_ref, kept_ref):
    levels, rows, cols = x_ref.shape
    side_row = side_rows(levels, rows, beside_ref, None, None)
    inner_sweep(x_ref, model_parts(wx_ref, wy_ref, x_ref, None, None, side_row, grad_ref), kept_ref)


def outer_model_body(wx_ref, wy_ref, x_ref, beside_ref, above_thin_ref, below_thin_ref, inner_ref, kept_ref, *refs):
    *others, grad_ref, above_ref, below_ref = refs
    levels, rows, cols = x_ref.shape
    above_ref[...] = above_thin_ref[...].astype(F32).reshape(above_ref.shape)
    below_ref[...] = below_thin_ref[...].astype(F32).reshape(below_ref.shape)
    side_row = side_rows(levels, rows, beside_ref, above_ref, below_ref)
    outer_sweep(x_ref, model_parts(wx_ref, wy_ref, x_ref, above_ref, below_ref, side_row, grad_ref), kept_ref)
    row = sub_iota((rows, cols))
    inside = (row >= MODEL_STEPS) & (row < rows - MODEL_STEPS)
    project_levels(lambda level: jnp.where(inside, inner_ref[level], grad_ref[level]), levels, *others)


def project_body(grad_ref, *refs):
    project_levels(lambda level: grad_ref[level], grad_ref.shape[0], *refs)


def project_levels(grad, levels, *refs):
    *member_refs, wide_ref, thin_ref = refs
    own, _, rows, cols = member_refs[0].shape
    count = len(member_refs) * own

    def step(q, carry):
        carry = list(carry)
        for u in range(2):
            g = grad(2 * q + u)
            for m in range(count):
                carry[m] = carry[m] + member_refs[m // own][m % own, 2 * q + u].astype(F32) * g
        return tuple(carry)

    total = lax.fori_loop(0, levels // 2, step, (jnp.zeros((rows, cols), F32),) * count)
    for m in range(count):
        at = neighbor_of(-(m // own)) * own + m % own
        wide_ref[at] = total[m]
        thin_ref[at] = total[m].astype(BF16)


def taper(offset):
    k = offset.astype(F32)
    w = (1.0 - (k / 17.0) * (k / 17.0)) * (1.0 / TAPER_TOTAL)
    return jnp.where(jnp.abs(offset) <= REACH, w, 0.0)


def halves(x):
    high = x.astype(BF16)
    return high, (x - high.astype(F32)).astype(BF16)


def sharp_dot(a, b):
    ah, al = halves(a)
    bh, bl = halves(b)
    dot = functools.partial(jnp.dot, preferred_element_type=F32)
    return dot(ah, bh) + dot(al, bh) + dot(ah, bl)


def columns_body(left_ref, mid_ref, right_ref, wide_ref, thin_ref):
    count, rows, cols = mid_ref.shape
    wide = jnp.concatenate(
        [r[...].astype(F32).reshape(count * rows, cols) for r in (left_ref, mid_ref, right_ref)], axis=1
    )
    shape = (3 * cols, wide_ref.shape[0] // count * cols)
    lane = lane_iota(shape)
    beside = lane % MODEL_STEPS + jnp.where((lane // (SUB * MODEL_STEPS)) % 2 == 0, -MODEL_STEPS, cols)
    target = jnp.where(lane < cols, lane, beside)
    out = sharp_dot(wide, taper(sub_iota(shape) - cols - target))
    for i in range(shape[1] // cols):
        part = out[:, i * cols : (i + 1) * cols].reshape(count, rows, cols)
        wide_ref[i * count : (i + 1) * count] = part
        thin_ref[i * count : (i + 1) * count] = part.astype(BF16)


def smooth_rows(above_ref, mid_ref, below_ref):
    count, rows, cols = mid_ref.shape
    tall = jnp.concatenate(
        [
            jnp.concatenate([above_ref[m].astype(F32), mid_ref[m], below_ref[m].astype(F32)], axis=0)
            for m in range(count)
        ],
        axis=1,
    )
    shape = (rows, 3 * rows)
    out = sharp_dot(taper(lane_iota(shape) - sub_iota(shape) - rows), tall)
    return [out[:, m * cols : (m + 1) * cols] for m in range(count)]


def increments(member_refs, local_ref, levels, emit):
    own = member_refs[0].shape[0]
    count = len(member_refs) * own
    local = [local_ref[neighbor_of(-(m // own)) * own + m % own] for m in range(count)]

    def step(q, carry):
        for u in range(2):
            level = 2 * q + u
            total = member_refs[0][0, level].astype(F32) * local[0]
            for m in range(1, count):
                total = total + member_refs[m // own][m % own, level].astype(F32) * local[m]
            emit(level, total)
        return carry

    lax.fori_loop(0, levels // 2, step, 0)


def update_body(parts, residual_ref, around_ref, above_ref, mid_ref, below_ref, *refs):
    member_refs, side_refs = refs[:parts], refs[parts : parts + 2] + refs[2:parts]
    analysis_ref, out_ref, beside_ref, top_ref, bottom_ref, local_ref, top_wide_ref, bottom_wide_ref = refs[parts + 2 :]
    levels, rows, cols = residual_ref.shape
    own = member_refs[0].shape[0]
    count = parts * own
    for m, value in enumerate(smooth_rows(above_ref, mid_ref, below_ref)):
        local_ref[m] = value

    def emit(level, value):
        analysis_ref[level] = value
        out_ref[level] = residual_ref[level] - RELAX * value

    increments(member_refs, local_ref, levels, emit)
    for g in range(levels // GROUP):
        total = jnp.zeros((rows, LANES), F32)
        for m in range(count):
            ref = side_refs[m // own]
            at = neighbor_of(-(m // own)) * own + m % own
            member = ref[m % own, ref.shape[1] - levels // GROUP + g]
            total = total + member.astype(F32) * local_ref[count + at]
        beside_ref[g] = around_ref[g] - RELAX * total
    pack_rows(out_ref, 0, top_wide_ref, bottom_wide_ref)
    pack_rows(beside_ref, levels // 2, top_wide_ref, bottom_wide_ref)
    top_ref[...] = top_wide_ref[...].reshape(top_ref.shape).astype(BF16)
    bottom_ref[...] = bottom_wide_ref[...].reshape(bottom_ref.shape).astype(BF16)


def final_body(parts, residual_ref, before_ref, above_ref, mid_ref, below_ref, *refs):
    member_refs = refs[:parts]
    analysis_ref, out_ref, local_ref = refs[parts:]
    for m, value in enumerate(smooth_rows(above_ref, mid_ref, below_ref)):
        local_ref[m] = value

    def emit(level, value):
        analysis_ref[level] = before_ref[level] + value
        out_ref[level] = residual_ref[level] - RELAX * value

    increments(member_refs, local_ref, residual_ref.shape[0], emit)


def per_device(residual_in, members, wind_x, wind_y):
    levels, rows, cols = residual_in.shape
    parts = lax.axis_size("member")
    count = members.shape[0] * parts
    groups = levels // GROUP

    def shape(*dims, kind=F32):
        return jax.ShapeDtypeStruct(dims, kind)

    def both(*dims):
        return shape(*dims), shape(*dims, kind=BF16)

    def turned(x, step):
        return lax.ppermute(x, "member", [(i, (i + step) % parts) for i in range(parts)])

    def smoothed(wide, thin, planes):
        wide, thin = call(
            columns_body, both(planes, rows, cols), shift(thin, "member", 1), wide, shift(thin, "member", -1)
        )
        return shift(thin, "tile", 1), wide, shift(thin, "tile", -1)

    like = shape(levels, rows, cols)
    halo = shape((levels + groups) // 2, SUB, LANES)
    thin_halo = shape((levels + groups) // 4, 2 * SUB, LANES, kind=BF16)
    wide_halo = [pltpu.VMEM(halo.shape, F32)] * 2
    packed = shape(groups, rows, LANES)
    wind_x, wind_y = (jnp.broadcast_to(w[:, None], (levels, LANES)) for w in (wind_x, wind_y))

    mine, early = split_columns(members, parts)
    early, residual_in = lax.optimization_barrier((early, residual_in))
    early = turned(early, 1)
    first, last = call(columns_edge_body, (packed, packed), residual_in)
    left, right = shift(last, "member", 1), shift(first, "member", -1)
    members, first = lax.optimization_barrier((members, first))
    later, early, left, right = lax.optimization_barrier((side_columns(members, parts), early, left, right))
    blocks = [mine, early] + [turned(x, r) for r, x in enumerate(later[2:], 2)]
    sides = [later[0], turned(later[1], 1)]
    around, top, bottom = call(rows_body, (packed, halo, halo), residual_in, left, right)
    above, below = shift(bottom, "tile", 1), shift(top, "tile", -1)
    grad = call(
        first_model_body, like,
        wind_x, wind_y, residual_in, around, above, below, in_specs=[VMEM] * 6,
    )
    grad, sides = lax.optimization_barrier((grad, sides))
    wide, thin = call(
        project_body, both(count, rows, cols), grad, *blocks, in_specs=[VMEM] * (1 + parts)
    )

    analysis, residual, beside, top, bottom = call(
        functools.partial(update_body, parts), (like, like, packed, thin_halo, thin_halo),
        residual_in, around, *smoothed(wide, thin, 2 * count), *blocks, *sides,
        in_specs=[VMEM] * (7 + parts),
        scratch=[pltpu.VMEM((2 * count, rows, cols), F32)] + wide_halo,
    )
    above, below = shift(bottom, "tile", 1), shift(top, "tile", -1)
    kept = shape(groups, len(kept_rows(rows)), 3, SUB, LANES)
    inner, kept = call(inner_model_body, (like, kept), wind_x, wind_y, residual, beside)
    wide, thin = call(
        outer_model_body, both(count, rows, cols),
        wind_x, wind_y, residual, beside, above, below, inner, kept, *blocks,
        scratch=[pltpu.VMEM((levels, rows, cols), F32)] + wide_halo,
    )
    return call(
        functools.partial(final_body, parts), (like, like),
        residual, analysis, *smoothed(wide, thin, count), *blocks,
        in_specs=[VMEM] * (5 + parts), scratch=[pltpu.VMEM((count, rows, cols), F32)],
    )


def solution(mesh):
    return jax.shard_map(
        per_device,
        mesh=mesh,
        in_specs=(P(None, "tile", "member"), P("member", None, "tile", None), P(), P()),
        out_specs=(P(None, "tile", "member"), P(None, "tile", "member")),
        check_vma=False,
    )
```

```python
import functools

import jax
import jax.numpy as jnp
from jax import lax
from jax.experimental import pallas as pl
from jax.experimental.pallas import tpu as pltpu
from jax.sharding import PartitionSpec as P

ITERS = 2
MODEL_STEPS = 4
DIFFUSION = 0.1
RELAX = 0.5
REACH = 16
TAPER_TOTAL = sum(1.0 - (k / 17.0) ** 2 for k in range(-REACH, REACH + 1))
F32 = jnp.float32
BF16 = jnp.bfloat16
LANES = 128
SUB = 8
GROUP = LANES // (2 * MODEL_STEPS)

VMEM = pl.BlockSpec(memory_space=pltpu.VMEM)
PARAMS = pltpu.CompilerParams(vmem_limit_bytes=48 * 1024 * 1024)


def call(body, out_shape, *args, in_specs=None, scratch=()):
    return pl.pallas_call(
        body,
        out_shape=out_shape,
        in_specs=in_specs or [VMEM] * len(args),
        out_specs=jax.tree.map(lambda _: VMEM, out_shape),
        scratch_shapes=scratch,
        compiler_params=PARAMS,
    )(*args)


def lane_iota(shape):
    return lax.broadcasted_iota(jnp.int32, shape, len(shape) - 1)


def sub_iota(shape):
    return lax.broadcasted_iota(jnp.int32, shape, len(shape) - 2)


def neighbor_of(step):
    parts = lax.axis_size("member")
    at = lax.axis_index("member") + step
    return jnp.where(at < 0, at + parts, jnp.where(at >= parts, at - parts, at))


def block_of(step, cols):
    return pl.ds(pl.multiple_of(neighbor_of(step) * cols, cols), cols)


def columns_split_body(in_ref, *out_refs):
    cols = out_refs[0].shape[-1]
    for r, out_ref in enumerate(out_refs):
        out_ref[...] = in_ref[:, :, :, block_of(r, cols)]


def split_columns(members, parts):
    own, levels, rows, ny = members.shape
    out = jax.ShapeDtypeStruct((own, levels, rows, ny // parts), members.dtype)
    return call(columns_split_body, (out,) * 2, members)


def left_slot(k):
    return 3 * SUB - 1 - k % SUB - GROUP * (k // SUB)


def put_left(x, k, total):
    here = lane_iota(x.shape) // MODEL_STEPS == left_slot(k)
    return jnp.where(here, pltpu.roll(x, (MODEL_STEPS * (left_slot(k) + 1)) % LANES, 1), total)


def put_right(x, k, total):
    here = lane_iota(x.shape) // MODEL_STEPS == left_slot(k) + SUB
    return jnp.where(here, pltpu.roll(x, MODEL_STEPS * (left_slot(k) + SUB), 1), total)


def sides_body(in_ref, *out_refs):
    levels = in_ref.shape[1]
    own, groups, rows, _ = out_refs[0].shape
    cols = in_ref.shape[-1] // len(out_refs)
    for r, out_ref in enumerate(out_refs):
        start = out_ref.shape[1] - groups
        if start:
            out_ref[:, :start] = in_ref[:, :, :, block_of(r, cols)]
        before, after = block_of(r - 1, cols), block_of(r + 1, cols)
        for m in range(own):

            def step(g, carry):
                total = jnp.zeros((rows, LANES), F32)
                for k in range(GROUP):
                    total = put_left(in_ref[m, g * GROUP + k, :, before].astype(F32), k, total)
                    total = put_right(in_ref[m, g * GROUP + k, :, after].astype(F32), k, total)
                out_ref[m, start + g] = total.astype(out_ref.dtype)
                return carry

            lax.fori_loop(0, groups, step, 0)


def side_columns(members, parts):
    own, levels, rows, ny = members.shape
    groups = levels // GROUP
    thin = jax.ShapeDtypeStruct((own, groups, rows, LANES), members.dtype)
    full = jax.ShapeDtypeStruct((own, levels + groups, rows, LANES), members.dtype)
    return call(sides_body, (thin,) * 2 + (full,) * (parts - 2), members)


def pack_rows(ref, at, top_ref, bottom_ref):
    upper = sub_iota((SUB, LANES)) < MODEL_STEPS
    count, rows, _ = ref.shape
    for q in range(count // 2):
        top_ref[at + q] = jnp.where(upper, ref[2 * q, :SUB], pltpu.roll(ref[2 * q + 1, :SUB], MODEL_STEPS, 0))
        bottom_ref[at + q] = jnp.where(
            upper, pltpu.roll(ref[2 * q, rows - SUB :], MODEL_STEPS, 0), ref[2 * q + 1, rows - SUB :]
        )


def rows_body(x_ref, left_ref, right_ref, beside_ref, top_ref, bottom_ref):
    beside_ref[...] = left_ref[...] + right_ref[...]
    pack_rows(x_ref, 0, top_ref, bottom_ref)
    pack_rows(beside_ref, x_ref.shape[0] // 2, top_ref, bottom_ref)


def columns_edge_body(x_ref, first_ref, last_ref):
    levels, rows, cols = x_ref.shape
    for g in range(levels // GROUP):
        first = jnp.zeros((rows, LANES), F32)
        last = jnp.zeros((rows, LANES), F32)
        for k in range(GROUP):
            last = put_left(x_ref[g * GROUP + k], k, last)
            first = put_right(x_ref[g * GROUP + k], k, first)
        first_ref[g] = first
        last_ref[g] = last


def shift(x, axis, step):
    count = lax.axis_size(axis)
    pairs = [(i, i + step) for i in range(count) if 0 <= i + step < count]
    return lax.ppermute(x, axis, pairs)


def model_parts(wx_ref, wy_ref, x_ref, above_ref, below_ref, side_row, grad_ref):
    levels, rows, cols = x_ref.shape
    tile, tiles = lax.axis_index("tile"), lax.axis_size("tile")
    member, parts = lax.axis_index("member"), lax.axis_size("member")
    x_flat = x_ref.reshape(levels * rows, cols)
    grad_flat = grad_ref.reshape(levels * rows, cols)
    halo = MODEL_STEPS
    if above_ref is not None:
        pairs = above_ref.shape[0]
        above_flat = above_ref.reshape(pairs * SUB, LANES)
        below_flat = below_ref.reshape(pairs * SUB, LANES)

    half = LANES // 2
    lane = lane_iota((SUB, LANES))
    on_right = lane % half < halo
    first_of = (lane == 0, lane == half)
    last_of = (lane == LANES - 1, lane == half - 1)
    second = (lane >= half // 2) & (lane < half + half // 2)
    inside = (on_right & (member < parts - 1)) | ((lane % half >= half - halo) & (member > 0))
    side_mask = jnp.where(inside, 1.0, 0.0).astype(F32)
    has_above = jnp.where(tile > 0, 1.0, 0.0).astype(F32)
    has_below = jnp.where(tile < tiles - 1, 1.0, 0.0).astype(F32)

    def load(g, e):
        centers = []
        for q in (2 * g, 2 * g + 1):
            if e < 0:
                centers.append(above_flat[pl.ds(q * SUB * halo + e + halo, SUB, stride=halo), :])
            elif e < rows:
                centers.append(x_flat[pl.ds(q * SUB * rows + e, SUB, stride=rows), :])
            else:
                centers.append(below_flat[pl.ds(q * SUB * halo + e - rows, SUB, stride=halo), :])
        row = jnp.broadcast_to(side_row(g, e), (SUB, LANES))
        right = pltpu.roll(row, halo, 1, stride=halo, stride_axis=0)
        left = pltpu.roll(row, LANES // 4, 1, stride=halo, stride_axis=0)
        side = jnp.where(on_right, right, left) * side_mask
        return centers[0], pltpu.roll(centers[1], half, 1), side

    def advance(before, here, after, e, coefficients):
        fore = [pltpu.roll(x, LANES - 1, 1) for x in here]
        back = [pltpu.roll(x, 1, 1) for x in here]
        fore_side = jnp.where(last_of[0], fore[0], jnp.where(last_of[1], fore[1], fore[2]))
        back_side = jnp.where(first_of[0], back[0], jnp.where(first_of[1], back[1], back[2]))
        fores = [jnp.where(last_of[i], fore[2], fore[i]) for i in range(2)] + [fore_side]
        backs = [jnp.where(first_of[i], back[2], back[i]) for i in range(2)] + [back_side]
        result = []
        for i, (own, ahead_x, ahead_y) in enumerate(coefficients):
            value = own * here[i] + ahead_x * after[i] + ahead_y * fores[i] + DIFFUSION * (before[i] + backs[i])
            if e < 0:
                value = value * has_above
            if e >= rows:
                value = value * has_below
            result.append(value * side_mask if i == 2 else value)
        return tuple(result)

    def coefficients_of(g):
        coefficients = []
        for q in (2 * g, 2 * g + 1):
            at = pl.ds(pl.multiple_of(q * SUB, SUB), SUB)
            wx, wy = wx_ref[at, :], wy_ref[at, :]
            coefficients.append((1.0 - 4.0 * DIFFUSION - wx - wy, DIFFUSION + wx, DIFFUSION + wy))
        coefficients.append(tuple(jnp.where(second, b, a) for a, b in zip(*coefficients)))
        return coefficients

    def store(g, e, field):
        grad_flat[pl.ds(2 * g * SUB * rows + e, SUB, stride=rows), :] = field[0]
        grad_flat[pl.ds((2 * g + 1) * SUB * rows + e, SUB, stride=rows), :] = pltpu.roll(field[1], half, 1)

    return load, advance, coefficients_of, store


def sweep(x_ref, parts):
    levels, rows, cols = x_ref.shape
    load, advance, coefficients_of, store = parts
    halo = MODEL_STEPS

    def group(g, carry):
        coefficients = coefficients_of(g)
        fields = [{} for _ in range(halo + 1)]
        for front in range(-halo, rows + halo):
            fields[0][front] = load(g, front)
            for n in range(1, halo + 1):
                e = front - n
                if -halo + n <= e < rows + halo - n:
                    old = fields[n - 1]
                    fields[n][e] = advance(old[e - 1], old[e], old[e + 1], e, coefficients)
            e = front - halo
            if 0 <= e < rows:
                store(g, e, fields[halo][e])
        return carry

    lax.fori_loop(0, levels // GROUP, group, 0)


def kept_rows(rows):
    return [(n, e) for n in range(1, MODEL_STEPS) for e in (n, n + 1, rows - 2 - n, rows - 1 - n)]


def inner_sweep(x_ref, parts, kept_ref):
    levels, rows, cols = x_ref.shape
    load, advance, coefficients_of, store = parts
    halo = MODEL_STEPS

    def group(g, carry):
        coefficients = coefficients_of(g)
        fields = [{} for _ in range(halo + 1)]
        for front in range(rows):
            fields[0][front] = load(g, front)
            for n in range(1, halo + 1):
                e = front - n
                if n <= e < rows - n:
                    old = fields[n - 1]
                    fields[n][e] = advance(old[e - 1], old[e], old[e + 1], e, coefficients)
            e = front - halo
            if halo <= e < rows - halo:
                store(g, e, fields[halo][e])
        for i, (n, e) in enumerate(kept_rows(rows)):
            for j in range(3):
                kept_ref[g, i, j] = fields[n][e][j]
        return carry

    lax.fori_loop(0, levels // GROUP, group, 0)


def outer_sweep(x_ref, parts, kept_ref):
    levels, rows, cols = x_ref.shape
    load, advance, coefficients_of, store = parts
    halo = MODEL_STEPS

    def group(g, carry):
        coefficients = coefficients_of(g)
        fields = [{} for _ in range(halo + 1)]
        for i, (n, e) in enumerate(kept_rows(rows)):
            fields[n][e] = tuple(kept_ref[g, i, j] for j in range(3))
        for e in (*range(-halo, 2), *range(rows - 2, rows + halo)):
            fields[0][e] = load(g, e)
        for n in range(1, halo + 1):
            old = fields[n - 1]
            for e in (*range(n - halo, n), *range(rows - n, rows + halo - n)):
                fields[n][e] = advance(old[e - 1], old[e], old[e + 1], e, coefficients)
        for e in (*range(halo), *range(rows - halo, rows)):
            store(g, e, fields[halo][e])
        return carry

    lax.fori_loop(0, levels // GROUP, group, 0)


def side_rows(levels, rows, beside_ref, above_ref, below_ref):
    def side_row(g, e):
        if 0 <= e < rows:
            return beside_ref[g, pl.ds(e, 1), :]
        ref, row = (above_ref, e + MODEL_STEPS) if e < 0 else (below_ref, e - rows)
        flat = ref.reshape(ref.shape[0] * SUB, LANES)
        return flat[pl.ds((levels + g) * MODEL_STEPS + row, 1), :]

    return side_row


def first_model_body(wx_ref, wy_ref, x_ref, beside_ref, above_ref, below_ref, grad_ref):
    levels, rows, cols = x_ref.shape
    side_row = side_rows(levels, rows, beside_ref, above_ref, below_ref)
    sweep(x_ref, model_parts(wx_ref, wy_ref, x_ref, above_ref, below_ref, side_row, grad_ref))


def inner_model_body(wx_ref, wy_ref, x_ref, beside_ref, grad_ref, kept_ref):
    levels, rows, cols = x_ref.shape
    side_row = side_rows(levels, rows, beside_ref, None, None)
    inner_sweep(x_ref, model_parts(wx_ref, wy_ref, x_ref, None, None, side_row, grad_ref), kept_ref)


def outer_model_body(wx_ref, wy_ref, x_ref, beside_ref, above_thin_ref, below_thin_ref, inner_ref, kept_ref, *refs):
    *others, grad_ref, above_ref, below_ref = refs
    levels, rows, cols = x_ref.shape
    above_ref[...] = above_thin_ref[...].astype(F32).reshape(above_ref.shape)
    below_ref[...] = below_thin_ref[...].astype(F32).reshape(below_ref.shape)
    side_row = side_rows(levels, rows, beside_ref, above_ref, below_ref)
    outer_sweep(x_ref, model_parts(wx_ref, wy_ref, x_ref, above_ref, below_ref, side_row, grad_ref), kept_ref)
    row = sub_iota((rows, cols))
    inside = (row >= MODEL_STEPS) & (row < rows - MODEL_STEPS)
    project_levels(lambda level: jnp.where(inside, inner_ref[level], grad_ref[level]), levels, *others)


def project_body(grad_ref, *refs):
    project_levels(lambda level: grad_ref[level], grad_ref.shape[0], *refs)


def project_levels(grad, levels, *refs):
    *member_refs, wide_ref, thin_ref = refs
    own, _, rows, cols = member_refs[0].shape
    count = len(member_refs) * own

    def step(q, carry):
        carry = list(carry)
        for u in range(2):
            g = grad(2 * q + u)
            for m in range(count):
                carry[m] = carry[m] + member_refs[m // own][m % own, 2 * q + u].astype(F32) * g
        return tuple(carry)

    total = lax.fori_loop(0, levels // 2, step, (jnp.zeros((rows, cols), F32),) * count)
    for m in range(count):
        at = neighbor_of(-(m // own)) * own + m % own
        wide_ref[at] = total[m]
        thin_ref[at] = total[m].astype(BF16)


def taper(offset):
    k = offset.astype(F32)
    w = (1.0 - (k / 17.0) * (k / 17.0)) * (1.0 / TAPER_TOTAL)
    return jnp.where(jnp.abs(offset) <= REACH, w, 0.0)


def halves(x):
    high = x.astype(BF16)
    return high, (x - high.astype(F32)).astype(BF16)


def sharp_dot(a, b):
    ah, al = halves(a)
    bh, bl = halves(b)
    dot = functools.partial(jnp.dot, preferred_element_type=F32)
    return dot(ah, bh) + dot(al, bh) + dot(ah, bl)


def columns_body(left_ref, mid_ref, right_ref, wide_ref, thin_ref):
    count, rows, cols = mid_ref.shape
    wide = jnp.concatenate(
        [r[...].astype(F32).reshape(count * rows, cols) for r in (left_ref, mid_ref, right_ref)], axis=1
    )
    shape = (3 * cols, wide_ref.shape[0] // count * cols)
    lane = lane_iota(shape)
    beside = lane % MODEL_STEPS + jnp.where((lane // (SUB * MODEL_STEPS)) % 2 == 0, -MODEL_STEPS, cols)
    target = jnp.where(lane < cols, lane, beside)
    out = sharp_dot(wide, taper(sub_iota(shape) - cols - target))
    for i in range(shape[1] // cols):
        part = out[:, i * cols : (i + 1) * cols].reshape(count, rows, cols)
        wide_ref[i * count : (i + 1) * count] = part
        thin_ref[i * count : (i + 1) * count] = part.astype(BF16)


def smooth_rows(above_ref, mid_ref, below_ref):
    count, rows, cols = mid_ref.shape
    tall = jnp.concatenate(
        [
            jnp.concatenate([above_ref[m].astype(F32), mid_ref[m], below_ref[m].astype(F32)], axis=0)
            for m in range(count)
        ],
        axis=1,
    )
    shape = (rows, 3 * rows)
    out = sharp_dot(taper(lane_iota(shape) - sub_iota(shape) - rows), tall)
    return [out[:, m * cols : (m + 1) * cols] for m in range(count)]


def increments(member_refs, local_ref, levels, emit):
    own = member_refs[0].shape[0]
    count = len(member_refs) * own
    local = [local_ref[neighbor_of(-(m // own)) * own + m % own] for m in range(count)]

    def step(q, carry):
        for u in range(2):
            level = 2 * q + u
            total = member_refs[0][0, level].astype(F32) * local[0]
            for m in range(1, count):
                total = total + member_refs[m // own][m % own, level].astype(F32) * local[m]
            emit(level, total)
        return carry

    lax.fori_loop(0, levels // 2, step, 0)


def update_body(parts, residual_ref, around_ref, above_ref, mid_ref, below_ref, *refs):
    member_refs, side_refs = refs[:parts], refs[parts : parts + 2] + refs[2:parts]
    analysis_ref, out_ref, beside_ref, top_ref, bottom_ref, local_ref, top_wide_ref, bottom_wide_ref = refs[parts + 2 :]
    levels, rows, cols = residual_ref.shape
    own = member_refs[0].shape[0]
    count = parts * own
    for m, value in enumerate(smooth_rows(above_ref, mid_ref, below_ref)):
        local_ref[m] = value

    def emit(level, value):
        analysis_ref[level] = value
        out_ref[level] = residual_ref[level] - RELAX * value

    increments(member_refs, local_ref, levels, emit)
    for g in range(levels // GROUP):
        total = jnp.zeros((rows, LANES), F32)
        for m in range(count):
            ref = side_refs[m // own]
            at = neighbor_of(-(m // own)) * own + m % own
            member = ref[m % own, ref.shape[1] - levels // GROUP + g]
            total = total + member.astype(F32) * local_ref[count + at]
        beside_ref[g] = around_ref[g] - RELAX * total
    pack_rows(out_ref, 0, top_wide_ref, bottom_wide_ref)
    pack_rows(beside_ref, levels // 2, top_wide_ref, bottom_wide_ref)
    top_ref[...] = top_wide_ref[...].reshape(top_ref.shape).astype(BF16)
    bottom_ref[...] = bottom_wide_ref[...].reshape(bottom_ref.shape).astype(BF16)


def final_body(parts, residual_ref, before_ref, above_ref, mid_ref, below_ref, *refs):
    member_refs = refs[:parts]
    analysis_ref, out_ref, local_ref = refs[parts:]
    for m, value in enumerate(smooth_rows(above_ref, mid_ref, below_ref)):
        local_ref[m] = value

    def emit(level, value):
        analysis_ref[level] = before_ref[level] + value
        out_ref[level] = residual_ref[level] - RELAX * value

    increments(member_refs, local_ref, residual_ref.shape[0], emit)


def per_device(residual_in, members, wind_x, wind_y):
    levels, rows, cols = residual_in.shape
    parts = lax.axis_size("member")
    count = members.shape[0] * parts
    groups = levels // GROUP

    def shape(*dims, kind=F32):
        return jax.ShapeDtypeStruct(dims, kind)

    def both(*dims):
        return shape(*dims), shape(*dims, kind=BF16)

    def turned(x, step):
        return lax.ppermute(x, "member", [(i, (i + step) % parts) for i in range(parts)])

    def smoothed(wide, thin, planes):
        wide, thin = call(
            columns_body, both(planes, rows, cols), shift(thin, "member", 1), wide, shift(thin, "member", -1)
        )
        return shift(thin, "tile", 1), wide, shift(thin, "tile", -1)

    like = shape(levels, rows, cols)
    halo = shape((levels + groups) // 2, SUB, LANES)
    thin_halo = shape((levels + groups) // 4, 2 * SUB, LANES, kind=BF16)
    wide_halo = [pltpu.VMEM(halo.shape, F32)] * 2
    packed = shape(groups, rows, LANES)
    wind_x, wind_y = (jnp.broadcast_to(w[:, None], (levels, LANES)) for w in (wind_x, wind_y))

    mine, early = split_columns(members, parts)
    early, residual_in = lax.optimization_barrier((early, residual_in))
    early = turned(early, 1)
    first, last = call(columns_edge_body, (packed, packed), residual_in)
    left, right = shift(last, "member", 1), shift(first, "member", -1)
    members, first = lax.optimization_barrier((members, first))
    *later, final = side_columns(members, parts)
    final = turned(final, parts - 1)
    later, early, left, right = lax.optimization_barrier((later, early, left, right))
    blocks = [mine, early] + [turned(x, r) for r, x in enumerate(later[2:], 2)] + [final]
    sides = [later[0], turned(later[1], 1)]
    around, top, bottom = call(rows_body, (packed, halo, halo), residual_in, left, right)
    above, below = shift(bottom, "tile", 1), shift(top, "tile", -1)
    grad = call(
        first_model_body, like,
        wind_x, wind_y, residual_in, around, above, below, in_specs=[VMEM] * 6,
    )
    grad, sides = lax.optimization_barrier((grad, sides))
    wide, thin = call(
        project_body, both(count, rows, cols), grad, *blocks, in_specs=[VMEM] * (1 + parts)
    )

    analysis, residual, beside, top, bottom = call(
        functools.partial(update_body, parts), (like, like, packed, thin_halo, thin_halo),
        residual_in, around, *smoothed(wide, thin, 2 * count), *blocks, *sides,
        in_specs=[VMEM] * (7 + parts),
        scratch=[pltpu.VMEM((2 * count, rows, cols), F32)] + wide_halo,
    )
    above, below = shift(bottom, "tile", 1), shift(top, "tile", -1)
    kept = shape(groups, len(kept_rows(rows)), 3, SUB, LANES)
    inner, kept = call(inner_model_body, (like, kept), wind_x, wind_y, residual, beside)
    wide, thin = call(
        outer_model_body, both(count, rows, cols),
        wind_x, wind_y, residual, beside, above, below, inner, kept, *blocks,
        scratch=[pltpu.VMEM((levels, rows, cols), F32)] + wide_halo,
    )
    return call(
        functools.partial(final_body, parts), (like, like),
        residual, analysis, *smoothed(wide, thin, count), *blocks,
        in_specs=[VMEM] * (5 + parts), scratch=[pltpu.VMEM((count, rows, cols), F32)],
    )


def solution(mesh):
    return jax.shard_map(
        per_device,
        mesh=mesh,
        in_specs=(P(None, "tile", "member"), P("member", None, "tile", None), P(), P()),
        out_specs=(P(None, "tile", "member"), P(None, "tile", "member")),
        check_vma=False,
    )
```

```python
import functools

import jax
import jax.numpy as jnp
from jax import lax
from jax.experimental import pallas as pl
from jax.experimental.pallas import tpu as pltpu
from jax.sharding import PartitionSpec as P

ITERS = 2
MODEL_STEPS = 4
DIFFUSION = 0.1
RELAX = 0.5
REACH = 16
TAPER_TOTAL = sum(1.0 - (k / 17.0) ** 2 for k in range(-REACH, REACH + 1))
F32 = jnp.float32
BF16 = jnp.bfloat16
LANES = 128
SUB = 8
GROUP = LANES // (2 * MODEL_STEPS)

VMEM = pl.BlockSpec(memory_space=pltpu.VMEM)
PARAMS = pltpu.CompilerParams(vmem_limit_bytes=48 * 1024 * 1024)


def call(body, out_shape, *args, in_specs=None, scratch=()):
    return pl.pallas_call(
        body,
        out_shape=out_shape,
        in_specs=in_specs or [VMEM] * len(args),
        out_specs=jax.tree.map(lambda _: VMEM, out_shape),
        scratch_shapes=scratch,
        compiler_params=PARAMS,
    )(*args)


def lane_iota(shape):
    return lax.broadcasted_iota(jnp.int32, shape, len(shape) - 1)


def sub_iota(shape):
    return lax.broadcasted_iota(jnp.int32, shape, len(shape) - 2)


def neighbor_of(step):
    parts = lax.axis_size("member")
    at = lax.axis_index("member") + step
    return jnp.where(at < 0, at + parts, jnp.where(at >= parts, at - parts, at))


def block_of(step, cols):
    return pl.ds(pl.multiple_of(neighbor_of(step) * cols, cols), cols)


def columns_split_body(in_ref, *out_refs):
    cols = out_refs[0].shape[-1]
    for r, out_ref in enumerate(out_refs):
        out_ref[...] = in_ref[:, :, :, block_of(r, cols)]


def split_columns(members, parts):
    own, levels, rows, ny = members.shape
    out = jax.ShapeDtypeStruct((own, levels, rows, ny // parts), members.dtype)
    return call(columns_split_body, (out,) * 2, members)


def left_slot(k):
    return 3 * SUB - 1 - k % SUB - GROUP * (k // SUB)


def put_left(x, k, total):
    here = lane_iota(x.shape) // MODEL_STEPS == left_slot(k)
    return jnp.where(here, pltpu.roll(x, (MODEL_STEPS * (left_slot(k) + 1)) % LANES, 1), total)


def put_right(x, k, total):
    here = lane_iota(x.shape) // MODEL_STEPS == left_slot(k) + SUB
    return jnp.where(here, pltpu.roll(x, MODEL_STEPS * (left_slot(k) + SUB), 1), total)


def sides_body(in_ref, *out_refs):
    levels = in_ref.shape[1]
    own, groups, rows, _ = out_refs[0].shape
    cols = in_ref.shape[-1] // len(out_refs)
    for r, out_ref in enumerate(out_refs):
        start = out_ref.shape[1] - groups
        if start:
            out_ref[:, :start] = in_ref[:, :, :, block_of(r, cols)]
        before, after = block_of(r - 1, cols), block_of(r + 1, cols)
        for m in range(own):

            def step(g, carry):
                total = jnp.zeros((rows, LANES), F32)
                for k in range(GROUP):
                    total = put_left(in_ref[m, g * GROUP + k, :, before].astype(F32), k, total)
                    total = put_right(in_ref[m, g * GROUP + k, :, after].astype(F32), k, total)
                out_ref[m, start + g] = total.astype(out_ref.dtype)
                return carry

            lax.fori_loop(0, groups, step, 0)


def side_columns(members, parts):
    own, levels, rows, ny = members.shape
    groups = levels // GROUP
    thin = jax.ShapeDtypeStruct((own, groups, rows, LANES), members.dtype)
    full = jax.ShapeDtypeStruct((own, levels + groups, rows, LANES), members.dtype)
    return call(sides_body, (thin,) * 2 + (full,) * (parts - 2), members)


def pack_rows(ref, at, top_ref, bottom_ref):
    upper = sub_iota((SUB, LANES)) < MODEL_STEPS
    count, rows, _ = ref.shape
    for q in range(count // 2):
        top_ref[at + q] = jnp.where(upper, ref[2 * q, :SUB], pltpu.roll(ref[2 * q + 1, :SUB], MODEL_STEPS, 0))
        bottom_ref[at + q] = jnp.where(
            upper, pltpu.roll(ref[2 * q, rows - SUB :], MODEL_STEPS, 0), ref[2 * q + 1, rows - SUB :]
        )


def rows_body(x_ref, left_ref, right_ref, beside_ref, top_ref, bottom_ref):
    beside_ref[...] = left_ref[...] + right_ref[...]
    pack_rows(x_ref, 0, top_ref, bottom_ref)
    pack_rows(beside_ref, x_ref.shape[0] // 2, top_ref, bottom_ref)


def columns_edge_body(x_ref, first_ref, last_ref):
    levels, rows, cols = x_ref.shape
    for g in range(levels // GROUP):
        first = jnp.zeros((rows, LANES), F32)
        last = jnp.zeros((rows, LANES), F32)
        for k in range(GROUP):
            last = put_left(x_ref[g * GROUP + k], k, last)
            first = put_right(x_ref[g * GROUP + k], k, first)
        first_ref[g] = first
        last_ref[g] = last


def shift(x, axis, step):
    count = lax.axis_size(axis)
    pairs = [(i, i + step) for i in range(count) if 0 <= i + step < count]
    return lax.ppermute(x, axis, pairs)


def model_parts(wx_ref, wy_ref, x_ref, above_ref, below_ref, side_row, grad_ref):
    levels, rows, cols = x_ref.shape
    tile, tiles = lax.axis_index("tile"), lax.axis_size("tile")
    member, parts = lax.axis_index("member"), lax.axis_size("member")
    x_flat = x_ref.reshape(levels * rows, cols)
    grad_flat = grad_ref.reshape(levels * rows, cols)
    halo = MODEL_STEPS
    if above_ref is not None:
        pairs = above_ref.shape[0]
        above_flat = above_ref.reshape(pairs * SUB, LANES)
        below_flat = below_ref.reshape(pairs * SUB, LANES)

    half = LANES // 2
    lane = lane_iota((SUB, LANES))
    on_right = lane % half < halo
    first_of = (lane == 0, lane == half)
    last_of = (lane == LANES - 1, lane == half - 1)
    second = (lane >= half // 2) & (lane < half + half // 2)
    inside = (on_right & (member < parts - 1)) | ((lane % half >= half - halo) & (member > 0))
    side_mask = jnp.where(inside, 1.0, 0.0).astype(F32)
    has_above = jnp.where(tile > 0, 1.0, 0.0).astype(F32)
    has_below = jnp.where(tile < tiles - 1, 1.0, 0.0).astype(F32)

    def load(g, e):
        centers = []
        for q in (2 * g, 2 * g + 1):
            if e < 0:
                centers.append(above_flat[pl.ds(q * SUB * halo + e + halo, SUB, stride=halo), :])
            elif e < rows:
                centers.append(x_flat[pl.ds(q * SUB * rows + e, SUB, stride=rows), :])
            else:
                centers.append(below_flat[pl.ds(q * SUB * halo + e - rows, SUB, stride=halo), :])
        row = jnp.broadcast_to(side_row(g, e), (SUB, LANES))
        right = pltpu.roll(row, halo, 1, stride=halo, stride_axis=0)
        left = pltpu.roll(row, LANES // 4, 1, stride=halo, stride_axis=0)
        side = jnp.where(on_right, right, left) * side_mask
        return centers[0], pltpu.roll(centers[1], half, 1), side

    def advance(before, here, after, e, coefficients):
        fore = [pltpu.roll(x, LANES - 1, 1) for x in here]
        back = [pltpu.roll(x, 1, 1) for x in here]
        fore_side = jnp.where(last_of[0], fore[0], jnp.where(last_of[1], fore[1], fore[2]))
        back_side = jnp.where(first_of[0], back[0], jnp.where(first_of[1], back[1], back[2]))
        fores = [jnp.where(last_of[i], fore[2], fore[i]) for i in range(2)] + [fore_side]
        backs = [jnp.where(first_of[i], back[2], back[i]) for i in range(2)] + [back_side]
        result = []
        for i, (own, ahead_x, ahead_y) in enumerate(coefficients):
            value = own * here[i] + ahead_x * after[i] + ahead_y * fores[i] + DIFFUSION * (before[i] + backs[i])
            if e < 0:
                value = value * has_above
            if e >= rows:
                value = value * has_below
            result.append(value * side_mask if i == 2 else value)
        return tuple(result)

    def coefficients_of(g):
        coefficients = []
        for q in (2 * g, 2 * g + 1):
            at = pl.ds(pl.multiple_of(q * SUB, SUB), SUB)
            wx, wy = wx_ref[at, :], wy_ref[at, :]
            coefficients.append((1.0 - 4.0 * DIFFUSION - wx - wy, DIFFUSION + wx, DIFFUSION + wy))
        coefficients.append(tuple(jnp.where(second, b, a) for a, b in zip(*coefficients)))
        return coefficients

    def store(g, e, field):
        grad_flat[pl.ds(2 * g * SUB * rows + e, SUB, stride=rows), :] = field[0]
        grad_flat[pl.ds((2 * g + 1) * SUB * rows + e, SUB, stride=rows), :] = pltpu.roll(field[1], half, 1)

    return load, advance, coefficients_of, store


def sweep(x_ref, parts):
    levels, rows, cols = x_ref.shape
    load, advance, coefficients_of, store = parts
    halo = MODEL_STEPS

    def group(g, carry):
        coefficients = coefficients_of(g)
        fields = [{} for _ in range(halo + 1)]
        for front in range(-halo, rows + halo):
            fields[0][front] = load(g, front)
            for n in range(1, halo + 1):
                e = front - n
                if -halo + n <= e < rows + halo - n:
                    old = fields[n - 1]
                    fields[n][e] = advance(old[e - 1], old[e], old[e + 1], e, coefficients)
            e = front - halo
            if 0 <= e < rows:
                store(g, e, fields[halo][e])
        return carry

    lax.fori_loop(0, levels // GROUP, group, 0)


def kept_rows(rows):
    return [(n, e) for n in range(1, MODEL_STEPS) for e in (n, n + 1, rows - 2 - n, rows - 1 - n)]


def inner_sweep(x_ref, parts, kept_ref):
    levels, rows, cols = x_ref.shape
    load, advance, coefficients_of, store = parts
    halo = MODEL_STEPS

    def group(g, carry):
        coefficients = coefficients_of(g)
        fields = [{} for _ in range(halo + 1)]
        for front in range(rows):
            fields[0][front] = load(g, front)
            for n in range(1, halo + 1):
                e = front - n
                if n <= e < rows - n:
                    old = fields[n - 1]
                    fields[n][e] = advance(old[e - 1], old[e], old[e + 1], e, coefficients)
            e = front - halo
            if halo <= e < rows - halo:
                store(g, e, fields[halo][e])
        for i, (n, e) in enumerate(kept_rows(rows)):
            for j in range(3):
                kept_ref[g, i, j] = fields[n][e][j]
        return carry

    lax.fori_loop(0, levels // GROUP, group, 0)


def outer_sweep(x_ref, parts, kept_ref):
    levels, rows, cols = x_ref.shape
    load, advance, coefficients_of, store = parts
    halo = MODEL_STEPS

    def group(g, carry):
        coefficients = coefficients_of(g)
        fields = [{} for _ in range(halo + 1)]
        for i, (n, e) in enumerate(kept_rows(rows)):
            fields[n][e] = tuple(kept_ref[g, i, j] for j in range(3))
        for e in (*range(-halo, 2), *range(rows - 2, rows + halo)):
            fields[0][e] = load(g, e)
        for n in range(1, halo + 1):
            old = fields[n - 1]
            for e in (*range(n - halo, n), *range(rows - n, rows + halo - n)):
                fields[n][e] = advance(old[e - 1], old[e], old[e + 1], e, coefficients)
        for e in (*range(halo), *range(rows - halo, rows)):
            store(g, e, fields[halo][e])
        return carry

    lax.fori_loop(0, levels // GROUP, group, 0)


def side_rows(levels, rows, beside_ref, above_ref, below_ref):
    def side_row(g, e):
        if 0 <= e < rows:
            return beside_ref[g, pl.ds(e, 1), :]
        ref, row = (above_ref, e + MODEL_STEPS) if e < 0 else (below_ref, e - rows)
        flat = ref.reshape(ref.shape[0] * SUB, LANES)
        return flat[pl.ds((levels + g) * MODEL_STEPS + row, 1), :]

    return side_row


def first_model_body(wx_ref, wy_ref, x_ref, beside_ref, above_ref, below_ref, grad_ref):
    levels, rows, cols = x_ref.shape
    side_row = side_rows(levels, rows, beside_ref, above_ref, below_ref)
    sweep(x_ref, model_parts(wx_ref, wy_ref, x_ref, above_ref, below_ref, side_row, grad_ref))


def inner_model_body(wx_ref, wy_ref, x_ref, beside_ref, grad_ref, kept_ref):
    levels, rows, cols = x_ref.shape
    side_row = side_rows(levels, rows, beside_ref, None, None)
    inner_sweep(x_ref, model_parts(wx_ref, wy_ref, x_ref, None, None, side_row, grad_ref), kept_ref)


def outer_model_body(wx_ref, wy_ref, x_ref, beside_ref, above_thin_ref, below_thin_ref, inner_ref, kept_ref, *refs):
    *others, grad_ref, above_ref, below_ref = refs
    levels, rows, cols = x_ref.shape
    above_ref[...] = above_thin_ref[...].astype(F32).reshape(above_ref.shape)
    below_ref[...] = below_thin_ref[...].astype(F32).reshape(below_ref.shape)
    side_row = side_rows(levels, rows, beside_ref, above_ref, below_ref)
    outer_sweep(x_ref, model_parts(wx_ref, wy_ref, x_ref, above_ref, below_ref, side_row, grad_ref), kept_ref)
    row = sub_iota((rows, cols))
    inside = (row >= MODEL_STEPS) & (row < rows - MODEL_STEPS)
    project_levels(lambda level: jnp.where(inside, inner_ref[level], grad_ref[level]), levels, list(range(len(others) - 2)), *others)


def near_turns(parts):
    return [0, 1, parts - 1]


def first_project_body(parts, grad_ref, *refs):
    project_levels(lambda level: grad_ref[level], grad_ref.shape[0], near_turns(parts), *refs)


def last_project_body(parts, grad_ref, wide_in_ref, thin_in_ref, *refs):
    *member_refs, wide_ref, thin_ref = refs
    own = member_refs[0].shape[0]
    for r in near_turns(parts):
        for m in range(own):
            at = neighbor_of(-r) * own + m
            wide_ref[at] = wide_in_ref[at]
            thin_ref[at] = thin_in_ref[at]
    project_levels(lambda level: grad_ref[level], grad_ref.shape[0], list(range(2, parts - 1)), *refs)


def project_levels(grad, levels, turns, *refs):
    *member_refs, wide_ref, thin_ref = refs
    own, _, rows, cols = member_refs[0].shape
    count = len(member_refs) * own

    def step(q, carry):
        carry = list(carry)
        for u in range(2):
            g = grad(2 * q + u)
            for m in range(count):
                carry[m] = carry[m] + member_refs[m // own][m % own, 2 * q + u].astype(F32) * g
        return tuple(carry)

    total = lax.fori_loop(0, levels // 2, step, (jnp.zeros((rows, cols), F32),) * count)
    for m in range(count):
        at = neighbor_of(-turns[m // own]) * own + m % own
        wide_ref[at] = total[m]
        thin_ref[at] = total[m].astype(BF16)


def taper(offset):
    k = offset.astype(F32)
    w = (1.0 - (k / 17.0) * (k / 17.0)) * (1.0 / TAPER_TOTAL)
    return jnp.where(jnp.abs(offset) <= REACH, w, 0.0)


def halves(x):
    high = x.astype(BF16)
    return high, (x - high.astype(F32)).astype(BF16)


def sharp_dot(a, b):
    ah, al = halves(a)
    bh, bl = halves(b)
    dot = functools.partial(jnp.dot, preferred_element_type=F32)
    return dot(ah, bh) + dot(al, bh) + dot(ah, bl)


def columns_body(left_ref, mid_ref, right_ref, wide_ref, thin_ref):
    count, rows, cols = mid_ref.shape
    wide = jnp.concatenate(
        [r[...].astype(F32).reshape(count * rows, cols) for r in (left_ref, mid_ref, right_ref)], axis=1
    )
    shape = (3 * cols, wide_ref.shape[0] // count * cols)
    lane = lane_iota(shape)
    beside = lane % MODEL_STEPS + jnp.where((lane // (SUB * MODEL_STEPS)) % 2 == 0, -MODEL_STEPS, cols)
    target = jnp.where(lane < cols, lane, beside)
    out = sharp_dot(wide, taper(sub_iota(shape) - cols - target))
    for i in range(shape[1] // cols):
        part = out[:, i * cols : (i + 1) * cols].reshape(count, rows, cols)
        wide_ref[i * count : (i + 1) * count] = part
        thin_ref[i * count : (i + 1) * count] = part.astype(BF16)


def smooth_rows(above_ref, mid_ref, below_ref):
    count, rows, cols = mid_ref.shape
    tall = jnp.concatenate(
        [
            jnp.concatenate([above_ref[m].astype(F32), mid_ref[m], below_ref[m].astype(F32)], axis=0)
            for m in range(count)
        ],
        axis=1,
    )
    shape = (rows, 3 * rows)
    out = sharp_dot(taper(lane_iota(shape) - sub_iota(shape) - rows), tall)
    return [out[:, m * cols : (m + 1) * cols] for m in range(count)]


def increments(member_refs, local_ref, start, levels, emit):
    own = member_refs[0].shape[0]
    count = len(member_refs) * own
    local = [local_ref[neighbor_of(-(m // own)) * own + m % own] for m in range(count)]

    def step(q, carry):
        for u in range(2):
            level = 2 * q + u
            total = member_refs[0][0, level].astype(F32) * local[0]
            for m in range(1, count):
                total = total + member_refs[m // own][m % own, level].astype(F32) * local[m]
            emit(level, total)
        return carry

    lax.fori_loop(start // 2, (start + levels) // 2, step, 0)


def update_body(parts, residual_ref, around_ref, above_ref, mid_ref, below_ref, *refs):
    member_refs, side_refs = refs[:parts], refs[parts : parts + 2] + refs[2:parts]
    analysis_ref, out_ref, beside_ref, top_ref, bottom_ref, local_ref, top_wide_ref, bottom_wide_ref = refs[parts + 2 :]
    levels, rows, cols = residual_ref.shape
    own = member_refs[0].shape[0]
    count = parts * own
    for m, value in enumerate(smooth_rows(above_ref, mid_ref, below_ref)):
        local_ref[m] = value

    def emit(level, value):
        analysis_ref[level] = value
        out_ref[level] = residual_ref[level] - RELAX * value

    increments(member_refs, local_ref, 0, levels, emit)
    for g in range(levels // GROUP):
        total = jnp.zeros((rows, LANES), F32)
        for m in range(count):
            ref = side_refs[m // own]
            at = neighbor_of(-(m // own)) * own + m % own
            member = ref[m % own, ref.shape[1] - levels // GROUP + g]
            total = total + member.astype(F32) * local_ref[count + at]
        beside_ref[g] = around_ref[g] - RELAX * total
    pack_rows(out_ref, 0, top_wide_ref, bottom_wide_ref)
    pack_rows(beside_ref, levels // 2, top_wide_ref, bottom_wide_ref)
    top_ref[...] = top_wide_ref[...].reshape(top_ref.shape).astype(BF16)
    bottom_ref[...] = bottom_wide_ref[...].reshape(bottom_ref.shape).astype(BF16)


def final_body(parts, residual_ref, before_ref, above_ref, mid_ref, below_ref, *refs):
    member_refs = refs[:parts]
    analysis_out_ref, residual_out_ref, local_ref, analysis_ref, out_ref, sems = refs[parts:]
    levels = residual_ref.shape[0]
    for m, value in enumerate(smooth_rows(above_ref, mid_ref, below_ref)):
        local_ref[m] = value

    def emit(level, value):
        analysis_ref[level] = before_ref[level] + value
        out_ref[level] = residual_ref[level] - RELAX * value

    pieces = sems.shape[1]
    count = levels // pieces
    copies = []
    for i in range(pieces):
        increments(member_refs, local_ref, i * count, count, emit)
        at = pl.ds(i * count, count)
        for j, (source, target) in enumerate(((analysis_ref, analysis_out_ref), (out_ref, residual_out_ref))):
            copies.append(pltpu.make_async_copy(source.at[at], target.at[at], sems.at[j, i]))
            copies[-1].start()
    for copy in copies:
        copy.wait()


def per_device(residual_in, members, wind_x, wind_y):
    levels, rows, cols = residual_in.shape
    parts = lax.axis_size("member")
    count = members.shape[0] * parts
    groups = levels // GROUP

    def shape(*dims, kind=F32):
        return jax.ShapeDtypeStruct(dims, kind)

    def both(*dims):
        return shape(*dims), shape(*dims, kind=BF16)

    def turned(x, step):
        return lax.ppermute(x, "member", [(i, (i + step) % parts) for i in range(parts)])

    def smoothed(wide, thin, planes):
        wide, thin = call(
            columns_body, both(planes, rows, cols), shift(thin, "member", 1), wide, shift(thin, "member", -1)
        )
        return shift(thin, "tile", 1), wide, shift(thin, "tile", -1)

    like = shape(levels, rows, cols)
    halo = shape((levels + groups) // 2, SUB, LANES)
    thin_halo = shape((levels + groups) // 4, 2 * SUB, LANES, kind=BF16)
    wide_halo = [pltpu.VMEM(halo.shape, F32)] * 2
    packed = shape(groups, rows, LANES)
    wind_x, wind_y = (jnp.broadcast_to(w[:, None], (levels, LANES)) for w in (wind_x, wind_y))

    mine, early = split_columns(members, parts)
    early, residual_in = lax.optimization_barrier((early, residual_in))
    early = turned(early, 1)
    first, last = call(columns_edge_body, (packed, packed), residual_in)
    left, right = shift(last, "member", 1), shift(first, "member", -1)
    members, first = lax.optimization_barrier((members, first))
    *later, final = side_columns(members, parts)
    final = turned(final, parts - 1)
    later, early, left, right = lax.optimization_barrier((later, early, left, right))
    blocks = [mine, early] + [turned(x, r) for r, x in enumerate(later[2:], 2)] + [final]
    sides = [later[0], turned(later[1], 1)]
    around, top, bottom = call(rows_body, (packed, halo, halo), residual_in, left, right)
    above, below = shift(bottom, "tile", 1), shift(top, "tile", -1)
    grad = call(
        first_model_body, like,
        wind_x, wind_y, residual_in, around, above, below, in_specs=[VMEM] * 6,
    )
    grad, sides = lax.optimization_barrier((grad, sides))
    near = [blocks[r] for r in near_turns(parts)]
    wide, thin = call(functools.partial(first_project_body, parts), both(count, rows, cols), grad, *near)
    wide, thin = call(
        functools.partial(last_project_body, parts), both(count, rows, cols), grad, wide, thin, *blocks[2:-1]
    )

    analysis, residual, beside, top, bottom = call(
        functools.partial(update_body, parts), (like, like, packed, thin_halo, thin_halo),
        residual_in, around, *smoothed(wide, thin, 2 * count), *blocks, *sides,
        in_specs=[VMEM] * (7 + parts),
        scratch=[pltpu.VMEM((2 * count, rows, cols), F32)] + wide_halo,
    )
    above, below = shift(bottom, "tile", 1), shift(top, "tile", -1)
    kept = shape(groups, len(kept_rows(rows)), 3, SUB, LANES)
    inner, kept = call(inner_model_body, (like, kept), wind_x, wind_y, residual, beside)
    wide, thin = call(
        outer_model_body, both(count, rows, cols),
        wind_x, wind_y, residual, beside, above, below, inner, kept, *blocks,
        scratch=[pltpu.VMEM((levels, rows, cols), F32)] + wide_halo,
    )
    return pl.pallas_call(
        functools.partial(final_body, parts),
        out_shape=(like, like),
        in_specs=[VMEM] * (5 + parts),
        out_specs=(pl.BlockSpec(memory_space=pl.ANY),) * 2,
        scratch_shapes=[
            pltpu.VMEM((count, rows, cols), F32),
            pltpu.VMEM(like.shape, F32),
            pltpu.VMEM(like.shape, F32),
            pltpu.SemaphoreType.DMA((2, 4)),
        ],
        compiler_params=PARAMS,
    )(residual, analysis, *smoothed(wide, thin, count), *blocks)


def solution(mesh):
    return jax.shard_map(
        per_device,
        mesh=mesh,
        in_specs=(P(None, "tile", "member"), P("member", None, "tile", None), P(), P()),
        out_specs=(P(None, "tile", "member"), P(None, "tile", "member")),
        check_vma=False,
    )
```

```python
import functools

import jax
import jax.numpy as jnp
from jax import lax
from jax.experimental import pallas as pl
from jax.experimental.pallas import tpu as pltpu
from jax.sharding import PartitionSpec as P

ITERS = 2
MODEL_STEPS = 4
DIFFUSION = 0.1
RELAX = 0.5
REACH = 16
TAPER_TOTAL = sum(1.0 - (k / 17.0) ** 2 for k in range(-REACH, REACH + 1))
F32 = jnp.float32
BF16 = jnp.bfloat16
LANES = 128
SUB = 8
GROUP = LANES // (2 * MODEL_STEPS)

VMEM = pl.BlockSpec(memory_space=pltpu.VMEM)
PARAMS = pltpu.CompilerParams(vmem_limit_bytes=48 * 1024 * 1024)


def call(body, out_shape, *args, in_specs=None, scratch=()):
    return pl.pallas_call(
        body,
        out_shape=out_shape,
        in_specs=in_specs or [VMEM] * len(args),
        out_specs=jax.tree.map(lambda _: VMEM, out_shape),
        scratch_shapes=scratch,
        compiler_params=PARAMS,
    )(*args)


def lane_iota(shape):
    return lax.broadcasted_iota(jnp.int32, shape, len(shape) - 1)


def sub_iota(shape):
    return lax.broadcasted_iota(jnp.int32, shape, len(shape) - 2)


def neighbor_of(step):
    parts = lax.axis_size("member")
    at = lax.axis_index("member") + step
    return jnp.where(at < 0, at + parts, jnp.where(at >= parts, at - parts, at))


def block_of(step, cols):
    return pl.ds(pl.multiple_of(neighbor_of(step) * cols, cols), cols)


def columns_split_body(in_ref, *out_refs):
    cols = out_refs[0].shape[-1]
    for r, out_ref in enumerate(out_refs):
        out_ref[...] = in_ref[:, :, :, block_of(r, cols)]


def split_columns(members, parts):
    own, levels, rows, ny = members.shape
    out = jax.ShapeDtypeStruct((own, levels, rows, ny // parts), members.dtype)
    return call(columns_split_body, (out,) * 2, members)


def left_slot(k):
    return 3 * SUB - 1 - k % SUB - GROUP * (k // SUB)


def put_left(x, k, total):
    here = lane_iota(x.shape) // MODEL_STEPS == left_slot(k)
    return jnp.where(here, pltpu.roll(x, (MODEL_STEPS * (left_slot(k) + 1)) % LANES, 1), total)


def put_right(x, k, total):
    here = lane_iota(x.shape) // MODEL_STEPS == left_slot(k) + SUB
    return jnp.where(here, pltpu.roll(x, MODEL_STEPS * (left_slot(k) + SUB), 1), total)


def sides_body(turns, parts, in_ref, *out_refs):
    own, levels, rows, ny = in_ref.shape
    groups = levels // GROUP
    cols = ny // parts
    for r, out_ref in zip(turns, out_refs):
        start = out_ref.shape[1] - groups
        if start:
            out_ref[:, :start] = in_ref[:, :, :, block_of(r, cols)]
        before, after = block_of(r - 1, cols), block_of(r + 1, cols)
        for m in range(own):

            def step(g, carry):
                total = jnp.zeros((rows, LANES), F32)
                for k in range(GROUP):
                    total = put_left(in_ref[m, g * GROUP + k, :, before].astype(F32), k, total)
                    total = put_right(in_ref[m, g * GROUP + k, :, after].astype(F32), k, total)
                out_ref[m, start + g] = total.astype(out_ref.dtype)
                return carry

            lax.fori_loop(0, groups, step, 0)


def side_columns(members, parts, turns):
    own, levels, rows, ny = members.shape
    groups = levels // GROUP
    out = [
        jax.ShapeDtypeStruct((own, (levels if r > 1 else 0) + groups, rows, LANES), members.dtype) for r in turns
    ]
    return call(functools.partial(sides_body, turns, parts), tuple(out), members)


def pack_rows(ref, at, top_ref, bottom_ref):
    upper = sub_iota((SUB, LANES)) < MODEL_STEPS
    count, rows, _ = ref.shape
    for q in range(count // 2):
        top_ref[at + q] = jnp.where(upper, ref[2 * q, :SUB], pltpu.roll(ref[2 * q + 1, :SUB], MODEL_STEPS, 0))
        bottom_ref[at + q] = jnp.where(
            upper, pltpu.roll(ref[2 * q, rows - SUB :], MODEL_STEPS, 0), ref[2 * q + 1, rows - SUB :]
        )


def rows_body(x_ref, left_ref, right_ref, beside_ref, top_ref, bottom_ref):
    beside_ref[...] = left_ref[...] + right_ref[...]
    pack_rows(x_ref, 0, top_ref, bottom_ref)
    pack_rows(beside_ref, x_ref.shape[0] // 2, top_ref, bottom_ref)


def columns_edge_body(x_ref, first_ref, last_ref):
    levels, rows, cols = x_ref.shape
    for g in range(levels // GROUP):
        first = jnp.zeros((rows, LANES), F32)
        last = jnp.zeros((rows, LANES), F32)
        for k in range(GROUP):
            last = put_left(x_ref[g * GROUP + k], k, last)
            first = put_right(x_ref[g * GROUP + k], k, first)
        first_ref[g] = first
        last_ref[g] = last


def shift(x, axis, step):
    count = lax.axis_size(axis)
    pairs = [(i, i + step) for i in range(count) if 0 <= i + step < count]
    return lax.ppermute(x, axis, pairs)


def model_parts(wx_ref, wy_ref, x_ref, above_ref, below_ref, side_row, grad_ref):
    levels, rows, cols = x_ref.shape
    tile, tiles = lax.axis_index("tile"), lax.axis_size("tile")
    member, parts = lax.axis_index("member"), lax.axis_size("member")
    x_flat = x_ref.reshape(levels * rows, cols)
    grad_flat = grad_ref.reshape(levels * rows, cols)
    halo = MODEL_STEPS
    if above_ref is not None:
        pairs = above_ref.shape[0]
        above_flat = above_ref.reshape(pairs * SUB, LANES)
        below_flat = below_ref.reshape(pairs * SUB, LANES)

    half = LANES // 2
    lane = lane_iota((SUB, LANES))
    on_right = lane % half < halo
    first_of = (lane == 0, lane == half)
    last_of = (lane == LANES - 1, lane == half - 1)
    second = (lane >= half // 2) & (lane < half + half // 2)
    inside = (on_right & (member < parts - 1)) | ((lane % half >= half - halo) & (member > 0))
    side_mask = jnp.where(inside, 1.0, 0.0).astype(F32)
    has_above = jnp.where(tile > 0, 1.0, 0.0).astype(F32)
    has_below = jnp.where(tile < tiles - 1, 1.0, 0.0).astype(F32)

    def load(g, e):
        centers = []
        for q in (2 * g, 2 * g + 1):
            if e < 0:
                centers.append(above_flat[pl.ds(q * SUB * halo + e + halo, SUB, stride=halo), :])
            elif e < rows:
                centers.append(x_flat[pl.ds(q * SUB * rows + e, SUB, stride=rows), :])
            else:
                centers.append(below_flat[pl.ds(q * SUB * halo + e - rows, SUB, stride=halo), :])
        row = jnp.broadcast_to(side_row(g, e), (SUB, LANES))
        right = pltpu.roll(row, halo, 1, stride=halo, stride_axis=0)
        left = pltpu.roll(row, LANES // 4, 1, stride=halo, stride_axis=0)
        side = jnp.where(on_right, right, left) * side_mask
        return centers[0], pltpu.roll(centers[1], half, 1), side

    def advance(before, here, after, e, coefficients):
        fore = [pltpu.roll(x, LANES - 1, 1) for x in here]
        back = [pltpu.roll(x, 1, 1) for x in here]
        fore_side = jnp.where(last_of[0], fore[0], jnp.where(last_of[1], fore[1], fore[2]))
        back_side = jnp.where(first_of[0], back[0], jnp.where(first_of[1], back[1], back[2]))
        fores = [jnp.where(last_of[i], fore[2], fore[i]) for i in range(2)] + [fore_side]
        backs = [jnp.where(first_of[i], back[2], back[i]) for i in range(2)] + [back_side]
        result = []
        for i, (own, ahead_x, ahead_y) in enumerate(coefficients):
            value = own * here[i] + ahead_x * after[i] + ahead_y * fores[i] + DIFFUSION * (before[i] + backs[i])
            if e < 0:
                value = value * has_above
            if e >= rows:
                value = value * has_below
            result.append(value * side_mask if i == 2 else value)
        return tuple(result)

    def coefficients_of(g):
        coefficients = []
        for q in (2 * g, 2 * g + 1):
            at = pl.ds(pl.multiple_of(q * SUB, SUB), SUB)
            wx, wy = wx_ref[at, :], wy_ref[at, :]
            coefficients.append((1.0 - 4.0 * DIFFUSION - wx - wy, DIFFUSION + wx, DIFFUSION + wy))
        coefficients.append(tuple(jnp.where(second, b, a) for a, b in zip(*coefficients)))
        return coefficients

    def store(g, e, field):
        grad_flat[pl.ds(2 * g * SUB * rows + e, SUB, stride=rows), :] = field[0]
        grad_flat[pl.ds((2 * g + 1) * SUB * rows + e, SUB, stride=rows), :] = pltpu.roll(field[1], half, 1)

    return load, advance, coefficients_of, store


def sweep(x_ref, parts):
    levels, rows, cols = x_ref.shape
    load, advance, coefficients_of, store = parts
    halo = MODEL_STEPS

    def group(g, carry):
        coefficients = coefficients_of(g)
        fields = [{} for _ in range(halo + 1)]
        for front in range(-halo, rows + halo):
            fields[0][front] = load(g, front)
            for n in range(1, halo + 1):
                e = front - n
                if -halo + n <= e < rows + halo - n:
                    old = fields[n - 1]
                    fields[n][e] = advance(old[e - 1], old[e], old[e + 1], e, coefficients)
            e = front - halo
            if 0 <= e < rows:
                store(g, e, fields[halo][e])
        return carry

    lax.fori_loop(0, levels // GROUP, group, 0)


def kept_rows(rows):
    return [(n, e) for n in range(1, MODEL_STEPS) for e in (n, n + 1, rows - 2 - n, rows - 1 - n)]


def inner_sweep(x_ref, parts, kept_ref):
    levels, rows, cols = x_ref.shape
    load, advance, coefficients_of, store = parts
    halo = MODEL_STEPS

    def group(g, carry):
        coefficients = coefficients_of(g)
        fields = [{} for _ in range(halo + 1)]
        for front in range(rows):
            fields[0][front] = load(g, front)
            for n in range(1, halo + 1):
                e = front - n
                if n <= e < rows - n:
                    old = fields[n - 1]
                    fields[n][e] = advance(old[e - 1], old[e], old[e + 1], e, coefficients)
            e = front - halo
            if halo <= e < rows - halo:
                store(g, e, fields[halo][e])
        for i, (n, e) in enumerate(kept_rows(rows)):
            for j in range(3):
                kept_ref[g, i, j] = fields[n][e][j]
        return carry

    lax.fori_loop(0, levels // GROUP, group, 0)


def outer_sweep(x_ref, parts, kept_ref):
    levels, rows, cols = x_ref.shape
    load, advance, coefficients_of, store = parts
    halo = MODEL_STEPS

    def group(g, carry):
        coefficients = coefficients_of(g)
        fields = [{} for _ in range(halo + 1)]
        for i, (n, e) in enumerate(kept_rows(rows)):
            fields[n][e] = tuple(kept_ref[g, i, j] for j in range(3))
        for e in (*range(-halo, 2), *range(rows - 2, rows + halo)):
            fields[0][e] = load(g, e)
        for n in range(1, halo + 1):
            old = fields[n - 1]
            for e in (*range(n - halo, n), *range(rows - n, rows + halo - n)):
                fields[n][e] = advance(old[e - 1], old[e], old[e + 1], e, coefficients)
        for e in (*range(halo), *range(rows - halo, rows)):
            store(g, e, fields[halo][e])
        return carry

    lax.fori_loop(0, levels // GROUP, group, 0)


def side_rows(levels, rows, beside_ref, above_ref, below_ref):
    def side_row(g, e):
        if 0 <= e < rows:
            return beside_ref[g, pl.ds(e, 1), :]
        ref, row = (above_ref, e + MODEL_STEPS) if e < 0 else (below_ref, e - rows)
        flat = ref.reshape(ref.shape[0] * SUB, LANES)
        return flat[pl.ds((levels + g) * MODEL_STEPS + row, 1), :]

    return side_row


def first_model_body(wx_ref, wy_ref, x_ref, beside_ref, above_ref, below_ref, grad_ref):
    levels, rows, cols = x_ref.shape
    side_row = side_rows(levels, rows, beside_ref, above_ref, below_ref)
    sweep(x_ref, model_parts(wx_ref, wy_ref, x_ref, above_ref, below_ref, side_row, grad_ref))


def inner_model_body(wx_ref, wy_ref, x_ref, beside_ref, grad_ref, kept_ref):
    levels, rows, cols = x_ref.shape
    side_row = side_rows(levels, rows, beside_ref, None, None)
    inner_sweep(x_ref, model_parts(wx_ref, wy_ref, x_ref, None, None, side_row, grad_ref), kept_ref)


def outer_model_body(wx_ref, wy_ref, x_ref, beside_ref, above_thin_ref, below_thin_ref, inner_ref, kept_ref, *refs):
    *others, grad_ref, above_ref, below_ref = refs
    levels, rows, cols = x_ref.shape
    above_ref[...] = above_thin_ref[...].astype(F32).reshape(above_ref.shape)
    below_ref[...] = below_thin_ref[...].astype(F32).reshape(below_ref.shape)
    side_row = side_rows(levels, rows, beside_ref, above_ref, below_ref)
    outer_sweep(x_ref, model_parts(wx_ref, wy_ref, x_ref, above_ref, below_ref, side_row, grad_ref), kept_ref)
    row = sub_iota((rows, cols))
    inside = (row >= MODEL_STEPS) & (row < rows - MODEL_STEPS)
    project_levels(lambda level: jnp.where(inside, inner_ref[level], grad_ref[level]), levels, list(range(len(others) - 2)), *others)


def near_turns(parts):
    return [0, 1, parts - 1]


def first_project_body(parts, grad_ref, *refs):
    project_levels(lambda level: grad_ref[level], grad_ref.shape[0], near_turns(parts), *refs)


def last_project_body(parts, grad_ref, wide_in_ref, thin_in_ref, *refs):
    *member_refs, wide_ref, thin_ref = refs
    own = member_refs[0].shape[0]
    for r in near_turns(parts):
        for m in range(own):
            at = neighbor_of(-r) * own + m
            wide_ref[at] = wide_in_ref[at]
            thin_ref[at] = thin_in_ref[at]
    project_levels(lambda level: grad_ref[level], grad_ref.shape[0], list(range(2, parts - 1)), *refs)


def project_levels(grad, levels, turns, *refs):
    *member_refs, wide_ref, thin_ref = refs
    own, _, rows, cols = member_refs[0].shape
    count = len(member_refs) * own

    def step(q, carry):
        carry = list(carry)
        for u in range(2):
            g = grad(2 * q + u)
            for m in range(count):
                carry[m] = carry[m] + member_refs[m // own][m % own, 2 * q + u].astype(F32) * g
        return tuple(carry)

    total = lax.fori_loop(0, levels // 2, step, (jnp.zeros((rows, cols), F32),) * count)
    for m in range(count):
        at = neighbor_of(-turns[m // own]) * own + m % own
        wide_ref[at] = total[m]
        thin_ref[at] = total[m].astype(BF16)


def taper(offset):
    k = offset.astype(F32)
    w = (1.0 - (k / 17.0) * (k / 17.0)) * (1.0 / TAPER_TOTAL)
    return jnp.where(jnp.abs(offset) <= REACH, w, 0.0)


def halves(x):
    high = x.astype(BF16)
    return high, (x - high.astype(F32)).astype(BF16)


def sharp_dot(a, b):
    ah, al = halves(a)
    bh, bl = halves(b)
    dot = functools.partial(jnp.dot, preferred_element_type=F32)
    return dot(ah, bh) + dot(al, bh) + dot(ah, bl)


def columns_body(left_ref, mid_ref, right_ref, wide_ref, thin_ref):
    count, rows, cols = mid_ref.shape
    wide = jnp.concatenate(
        [r[...].astype(F32).reshape(count * rows, cols) for r in (left_ref, mid_ref, right_ref)], axis=1
    )
    shape = (3 * cols, wide_ref.shape[0] // count * cols)
    lane = lane_iota(shape)
    beside = lane % MODEL_STEPS + jnp.where((lane // (SUB * MODEL_STEPS)) % 2 == 0, -MODEL_STEPS, cols)
    target = jnp.where(lane < cols, lane, beside)
    out = sharp_dot(wide, taper(sub_iota(shape) - cols - target))
    for i in range(shape[1] // cols):
        part = out[:, i * cols : (i + 1) * cols].reshape(count, rows, cols)
        wide_ref[i * count : (i + 1) * count] = part
        thin_ref[i * count : (i + 1) * count] = part.astype(BF16)


def smooth_rows(above_ref, mid_ref, below_ref):
    count, rows, cols = mid_ref.shape
    tall = jnp.concatenate(
        [
            jnp.concatenate([above_ref[m].astype(F32), mid_ref[m], below_ref[m].astype(F32)], axis=0)
            for m in range(count)
        ],
        axis=1,
    )
    shape = (rows, 3 * rows)
    out = sharp_dot(taper(lane_iota(shape) - sub_iota(shape) - rows), tall)
    return [out[:, m * cols : (m + 1) * cols] for m in range(count)]


def increments(member_refs, local_ref, start, levels, emit):
    own = member_refs[0].shape[0]
    count = len(member_refs) * own
    local = [local_ref[neighbor_of(-(m // own)) * own + m % own] for m in range(count)]

    def step(q, carry):
        for u in range(2):
            level = 2 * q + u
            total = member_refs[0][0, level].astype(F32) * local[0]
            for m in range(1, count):
                total = total + member_refs[m // own][m % own, level].astype(F32) * local[m]
            emit(level, total)
        return carry

    lax.fori_loop(start // 2, (start + levels) // 2, step, 0)


def update_body(parts, residual_ref, around_ref, above_ref, mid_ref, below_ref, *refs):
    member_refs, side_refs = refs[:parts], refs[parts : parts + 2] + refs[2:parts]
    analysis_ref, out_ref, beside_ref, top_ref, bottom_ref, local_ref, top_wide_ref, bottom_wide_ref = refs[parts + 2 :]
    levels, rows, cols = residual_ref.shape
    own = member_refs[0].shape[0]
    count = parts * own
    for m, value in enumerate(smooth_rows(above_ref, mid_ref, below_ref)):
        local_ref[m] = value

    def emit(level, value):
        analysis_ref[level] = value
        out_ref[level] = residual_ref[level] - RELAX * value

    increments(member_refs, local_ref, 0, levels, emit)
    for g in range(levels // GROUP):
        total = jnp.zeros((rows, LANES), F32)
        for m in range(count):
            ref = side_refs[m // own]
            at = neighbor_of(-(m // own)) * own + m % own
            member = ref[m % own, ref.shape[1] - levels // GROUP + g]
            total = total + member.astype(F32) * local_ref[count + at]
        beside_ref[g] = around_ref[g] - RELAX * total
    pack_rows(out_ref, 0, top_wide_ref, bottom_wide_ref)
    pack_rows(beside_ref, levels // 2, top_wide_ref, bottom_wide_ref)
    top_ref[...] = top_wide_ref[...].reshape(top_ref.shape).astype(BF16)
    bottom_ref[...] = bottom_wide_ref[...].reshape(bottom_ref.shape).astype(BF16)


def final_body(parts, residual_ref, before_ref, above_ref, mid_ref, below_ref, *refs):
    member_refs = refs[:parts]
    analysis_out_ref, residual_out_ref, local_ref, analysis_ref, out_ref, sems = refs[parts:]
    levels = residual_ref.shape[0]
    for m, value in enumerate(smooth_rows(above_ref, mid_ref, below_ref)):
        local_ref[m] = value

    def emit(level, value):
        analysis_ref[level] = before_ref[level] + value
        out_ref[level] = residual_ref[level] - RELAX * value

    pieces = sems.shape[1]
    count = levels // pieces
    copies = []
    for i in range(pieces):
        increments(member_refs, local_ref, i * count, count, emit)
        at = pl.ds(i * count, count)
        for j, (source, target) in enumerate(((analysis_ref, analysis_out_ref), (out_ref, residual_out_ref))):
            copies.append(pltpu.make_async_copy(source.at[at], target.at[at], sems.at[j, i]))
            copies[-1].start()
    for copy in copies:
        copy.wait()


def per_device(residual_in, members, wind_x, wind_y):
    levels, rows, cols = residual_in.shape
    parts = lax.axis_size("member")
    count = members.shape[0] * parts
    groups = levels // GROUP

    def shape(*dims, kind=F32):
        return jax.ShapeDtypeStruct(dims, kind)

    def both(*dims):
        return shape(*dims), shape(*dims, kind=BF16)

    def turned(x, step):
        return lax.ppermute(x, "member", [(i, (i + step) % parts) for i in range(parts)])

    def smoothed(wide, thin, planes):
        wide, thin = call(
            columns_body, both(planes, rows, cols), shift(thin, "member", 1), wide, shift(thin, "member", -1)
        )
        return shift(thin, "tile", 1), wide, shift(thin, "tile", -1)

    like = shape(levels, rows, cols)
    halo = shape((levels + groups) // 2, SUB, LANES)
    thin_halo = shape((levels + groups) // 4, 2 * SUB, LANES, kind=BF16)
    wide_halo = [pltpu.VMEM(halo.shape, F32)] * 2
    packed = shape(groups, rows, LANES)
    wind_x, wind_y = (jnp.broadcast_to(w[:, None], (levels, LANES)) for w in (wind_x, wind_y))

    mine, early = split_columns(members, parts)
    early, residual_in = lax.optimization_barrier((early, residual_in))
    early = turned(early, 1)
    first, last = call(columns_edge_body, (packed, packed), residual_in)
    left, right = shift(last, "member", 1), shift(first, "member", -1)
    members, first = lax.optimization_barrier((members, first))
    (final,) = side_columns(members, parts, [parts - 1])
    final, members = lax.optimization_barrier((final, members))
    final = turned(final, parts - 1)
    later = side_columns(members, parts, list(range(parts - 1)))
    later, early, left, right = lax.optimization_barrier((later, early, left, right))
    blocks = [mine, early] + [turned(x, r) for r, x in enumerate(later[2:], 2)] + [final]
    sides = [later[0], turned(later[1], 1)]
    around, top, bottom = call(rows_body, (packed, halo, halo), residual_in, left, right)
    above, below = shift(bottom, "tile", 1), shift(top, "tile", -1)
    grad = call(
        first_model_body, like,
        wind_x, wind_y, residual_in, around, above, below, in_specs=[VMEM] * 6,
    )
    grad, sides = lax.optimization_barrier((grad, sides))
    near = [blocks[r] for r in near_turns(parts)]
    wide, thin = call(functools.partial(first_project_body, parts), both(count, rows, cols), grad, *near)
    wide, thin = call(
        functools.partial(last_project_body, parts), both(count, rows, cols), grad, wide, thin, *blocks[2:-1]
    )

    analysis, residual, beside, top, bottom = call(
        functools.partial(update_body, parts), (like, like, packed, thin_halo, thin_halo),
        residual_in, around, *smoothed(wide, thin, 2 * count), *blocks, *sides,
        in_specs=[VMEM] * (7 + parts),
        scratch=[pltpu.VMEM((2 * count, rows, cols), F32)] + wide_halo,
    )
    above, below = shift(bottom, "tile", 1), shift(top, "tile", -1)
    kept = shape(groups, len(kept_rows(rows)), 3, SUB, LANES)
    inner, kept = call(inner_model_body, (like, kept), wind_x, wind_y, residual, beside)
    wide, thin = call(
        outer_model_body, both(count, rows, cols),
        wind_x, wind_y, residual, beside, above, below, inner, kept, *blocks,
        scratch=[pltpu.VMEM((levels, rows, cols), F32)] + wide_halo,
    )
    return pl.pallas_call(
        functools.partial(final_body, parts),
        out_shape=(like, like),
        in_specs=[VMEM] * (5 + parts),
        out_specs=(pl.BlockSpec(memory_space=pl.ANY),) * 2,
        scratch_shapes=[
            pltpu.VMEM((count, rows, cols), F32),
            pltpu.VMEM(like.shape, F32),
            pltpu.VMEM(like.shape, F32),
            pltpu.SemaphoreType.DMA((2, 4)),
        ],
        compiler_params=PARAMS,
    )(residual, analysis, *smoothed(wide, thin, count), *blocks)


def solution(mesh):
    return jax.shard_map(
        per_device,
        mesh=mesh,
        in_specs=(P(None, "tile", "member"), P("member", None, "tile", None), P(), P()),
        out_specs=(P(None, "tile", "member"), P(None, "tile", "member")),
        check_vma=False,
    )
```

```python
import functools

import jax
import jax.numpy as jnp
from jax import lax
from jax.experimental import pallas as pl
from jax.experimental.pallas import tpu as pltpu
from jax.sharding import PartitionSpec as P

ITERS = 2
MODEL_STEPS = 4
DIFFUSION = 0.1
RELAX = 0.5
REACH = 16
TAPER_TOTAL = sum(1.0 - (k / 17.0) ** 2 for k in range(-REACH, REACH + 1))
F32 = jnp.float32
BF16 = jnp.bfloat16
LANES = 128
SUB = 8
GROUP = LANES // (2 * MODEL_STEPS)

VMEM = pl.BlockSpec(memory_space=pltpu.VMEM)
PARAMS = pltpu.CompilerParams(vmem_limit_bytes=48 * 1024 * 1024)


def call(body, out_shape, *args, in_specs=None, scratch=()):
    return pl.pallas_call(
        body,
        out_shape=out_shape,
        in_specs=in_specs or [VMEM] * len(args),
        out_specs=jax.tree.map(lambda _: VMEM, out_shape),
        scratch_shapes=scratch,
        compiler_params=PARAMS,
    )(*args)


def lane_iota(shape):
    return lax.broadcasted_iota(jnp.int32, shape, len(shape) - 1)


def sub_iota(shape):
    return lax.broadcasted_iota(jnp.int32, shape, len(shape) - 2)


def neighbor_of(step):
    parts = lax.axis_size("member")
    at = lax.axis_index("member") + step
    return jnp.where(at < 0, at + parts, jnp.where(at >= parts, at - parts, at))


def block_of(step, cols):
    return pl.ds(pl.multiple_of(neighbor_of(step) * cols, cols), cols)


def columns_split_body(in_ref, *out_refs):
    cols = out_refs[0].shape[-1]
    for r, out_ref in enumerate(out_refs):
        out_ref[...] = in_ref[:, :, :, block_of(r, cols)]


def split_columns(members, parts):
    own, levels, rows, ny = members.shape
    out = jax.ShapeDtypeStruct((own, levels, rows, ny // parts), members.dtype)
    return call(columns_split_body, (out,) * 2, members)


def left_slot(k):
    return 3 * SUB - 1 - k % SUB - GROUP * (k // SUB)


def put_left(x, k, total):
    here = lane_iota(x.shape) // MODEL_STEPS == left_slot(k)
    return jnp.where(here, pltpu.roll(x, (MODEL_STEPS * (left_slot(k) + 1)) % LANES, 1), total)


def put_right(x, k, total):
    here = lane_iota(x.shape) // MODEL_STEPS == left_slot(k) + SUB
    return jnp.where(here, pltpu.roll(x, MODEL_STEPS * (left_slot(k) + SUB), 1), total)


def sides_body(turns, parts, in_ref, *out_refs):
    own, levels, rows, ny = in_ref.shape
    groups = levels // GROUP
    cols = ny // parts
    for r, out_ref in zip(turns, out_refs):
        start = out_ref.shape[1] - groups
        if start:
            out_ref[:, :start] = in_ref[:, :, :, block_of(r, cols)]
        before, after = block_of(r - 1, cols), block_of(r + 1, cols)
        for m in range(own):

            def step(g, carry):
                total = jnp.zeros((rows, LANES), F32)
                for k in range(GROUP):
                    total = put_left(in_ref[m, g * GROUP + k, :, before].astype(F32), k, total)
                    total = put_right(in_ref[m, g * GROUP + k, :, after].astype(F32), k, total)
                out_ref[m, start + g] = total.astype(out_ref.dtype)
                return carry

            lax.fori_loop(0, groups, step, 0)


def side_columns(members, parts, turns):
    own, levels, rows, ny = members.shape
    groups = levels // GROUP
    out = [
        jax.ShapeDtypeStruct((own, (levels if r > 1 else 0) + groups, rows, LANES), members.dtype) for r in turns
    ]
    return call(functools.partial(sides_body, turns, parts), tuple(out), members)


def pack_rows(ref, at, top_ref, bottom_ref):
    upper = sub_iota((SUB, LANES)) < MODEL_STEPS
    count, rows, _ = ref.shape
    for q in range(count // 2):
        top_ref[at + q] = jnp.where(upper, ref[2 * q, :SUB], pltpu.roll(ref[2 * q + 1, :SUB], MODEL_STEPS, 0))
        bottom_ref[at + q] = jnp.where(
            upper, pltpu.roll(ref[2 * q, rows - SUB :], MODEL_STEPS, 0), ref[2 * q + 1, rows - SUB :]
        )


def rows_body(x_ref, left_ref, right_ref, beside_ref, top_ref, bottom_ref):
    beside_ref[...] = left_ref[...] + right_ref[...]
    pack_rows(x_ref, 0, top_ref, bottom_ref)
    pack_rows(beside_ref, x_ref.shape[0] // 2, top_ref, bottom_ref)


def columns_edge_body(x_ref, first_ref, last_ref):
    levels, rows, cols = x_ref.shape
    for g in range(levels // GROUP):
        first = jnp.zeros((rows, LANES), F32)
        last = jnp.zeros((rows, LANES), F32)
        for k in range(GROUP):
            last = put_left(x_ref[g * GROUP + k], k, last)
            first = put_right(x_ref[g * GROUP + k], k, first)
        first_ref[g] = first
        last_ref[g] = last


def shift(x, axis, step):
    count = lax.axis_size(axis)
    pairs = [(i, i + step) for i in range(count) if 0 <= i + step < count]
    return lax.ppermute(x, axis, pairs)


def model_parts(wx_ref, wy_ref, x_ref, above_ref, below_ref, side_row, grad_ref):
    levels, rows, cols = x_ref.shape
    tile, tiles = lax.axis_index("tile"), lax.axis_size("tile")
    member, parts = lax.axis_index("member"), lax.axis_size("member")
    x_flat = x_ref.reshape(levels * rows, cols)
    grad_flat = grad_ref.reshape(levels * rows, cols)
    halo = MODEL_STEPS
    if above_ref is not None:
        pairs = above_ref.shape[0]
        above_flat = above_ref.reshape(pairs * SUB, LANES)
        below_flat = below_ref.reshape(pairs * SUB, LANES)

    half = LANES // 2
    lane = lane_iota((SUB, LANES))
    on_right = lane % half < halo
    first_of = (lane == 0, lane == half)
    last_of = (lane == LANES - 1, lane == half - 1)
    second = (lane >= half // 2) & (lane < half + half // 2)
    inside = (on_right & (member < parts - 1)) | ((lane % half >= half - halo) & (member > 0))
    side_mask = jnp.where(inside, 1.0, 0.0).astype(F32)
    has_above = jnp.where(tile > 0, 1.0, 0.0).astype(F32)
    has_below = jnp.where(tile < tiles - 1, 1.0, 0.0).astype(F32)

    def load(g, e):
        centers = []
        for q in (2 * g, 2 * g + 1):
            if e < 0:
                centers.append(above_flat[pl.ds(q * SUB * halo + e + halo, SUB, stride=halo), :])
            elif e < rows:
                centers.append(x_flat[pl.ds(q * SUB * rows + e, SUB, stride=rows), :])
            else:
                centers.append(below_flat[pl.ds(q * SUB * halo + e - rows, SUB, stride=halo), :])
        row = jnp.broadcast_to(side_row(g, e), (SUB, LANES))
        right = pltpu.roll(row, halo, 1, stride=halo, stride_axis=0)
        left = pltpu.roll(row, LANES // 4, 1, stride=halo, stride_axis=0)
        side = jnp.where(on_right, right, left) * side_mask
        return centers[0], pltpu.roll(centers[1], half, 1), side

    def advance(before, here, after, e, coefficients):
        fore = [pltpu.roll(x, LANES - 1, 1) for x in here]
        back = [pltpu.roll(x, 1, 1) for x in here]
        fore_side = jnp.where(last_of[0], fore[0], jnp.where(last_of[1], fore[1], fore[2]))
        back_side = jnp.where(first_of[0], back[0], jnp.where(first_of[1], back[1], back[2]))
        fores = [jnp.where(last_of[i], fore[2], fore[i]) for i in range(2)] + [fore_side]
        backs = [jnp.where(first_of[i], back[2], back[i]) for i in range(2)] + [back_side]
        result = []
        for i, (own, ahead_x, ahead_y) in enumerate(coefficients):
            value = own * here[i] + ahead_x * after[i] + ahead_y * fores[i] + DIFFUSION * (before[i] + backs[i])
            if e < 0:
                value = value * has_above
            if e >= rows:
                value = value * has_below
            result.append(value * side_mask if i == 2 else value)
        return tuple(result)

    def coefficients_of(g):
        coefficients = []
        for q in (2 * g, 2 * g + 1):
            at = pl.ds(pl.multiple_of(q * SUB, SUB), SUB)
            wx, wy = wx_ref[at, :], wy_ref[at, :]
            coefficients.append((1.0 - 4.0 * DIFFUSION - wx - wy, DIFFUSION + wx, DIFFUSION + wy))
        coefficients.append(tuple(jnp.where(second, b, a) for a, b in zip(*coefficients)))
        return coefficients

    def store(g, e, field):
        grad_flat[pl.ds(2 * g * SUB * rows + e, SUB, stride=rows), :] = field[0]
        grad_flat[pl.ds((2 * g + 1) * SUB * rows + e, SUB, stride=rows), :] = pltpu.roll(field[1], half, 1)

    return load, advance, coefficients_of, store


def sweep(x_ref, parts):
    levels, rows, cols = x_ref.shape
    load, advance, coefficients_of, store = parts
    halo = MODEL_STEPS

    def group(g, carry):
        coefficients = coefficients_of(g)
        fields = [{} for _ in range(halo + 1)]
        for front in range(-halo, rows + halo):
            fields[0][front] = load(g, front)
            for n in range(1, halo + 1):
                e = front - n
                if -halo + n <= e < rows + halo - n:
                    old = fields[n - 1]
                    fields[n][e] = advance(old[e - 1], old[e], old[e + 1], e, coefficients)
            e = front - halo
            if 0 <= e < rows:
                store(g, e, fields[halo][e])
        return carry

    lax.fori_loop(0, levels // GROUP, group, 0)


def kept_rows(rows):
    return [(n, e) for n in range(1, MODEL_STEPS) for e in (n, n + 1, rows - 2 - n, rows - 1 - n)]


def inner_sweep(x_ref, parts, kept_ref):
    levels, rows, cols = x_ref.shape
    load, advance, coefficients_of, store = parts
    halo = MODEL_STEPS

    def group(g, carry):
        coefficients = coefficients_of(g)
        fields = [{} for _ in range(halo + 1)]
        for front in range(rows):
            fields[0][front] = load(g, front)
            for n in range(1, halo + 1):
                e = front - n
                if n <= e < rows - n:
                    old = fields[n - 1]
                    fields[n][e] = advance(old[e - 1], old[e], old[e + 1], e, coefficients)
            e = front - halo
            if halo <= e < rows - halo:
                store(g, e, fields[halo][e])
        for i, (n, e) in enumerate(kept_rows(rows)):
            for j in range(3):
                kept_ref[g, i, j] = fields[n][e][j]
        return carry

    lax.fori_loop(0, levels // GROUP, group, 0)


def outer_sweep(x_ref, parts, kept_ref):
    levels, rows, cols = x_ref.shape
    load, advance, coefficients_of, store = parts
    halo = MODEL_STEPS

    def group(g, carry):
        coefficients = coefficients_of(g)
        fields = [{} for _ in range(halo + 1)]
        for i, (n, e) in enumerate(kept_rows(rows)):
            fields[n][e] = tuple(kept_ref[g, i, j] for j in range(3))
        for e in (*range(-halo, 2), *range(rows - 2, rows + halo)):
            fields[0][e] = load(g, e)
        for n in range(1, halo + 1):
            old = fields[n - 1]
            for e in (*range(n - halo, n), *range(rows - n, rows + halo - n)):
                fields[n][e] = advance(old[e - 1], old[e], old[e + 1], e, coefficients)
        for e in (*range(halo), *range(rows - halo, rows)):
            store(g, e, fields[halo][e])
        return carry

    lax.fori_loop(0, levels // GROUP, group, 0)


def side_rows(levels, rows, beside_ref, above_ref, below_ref):
    def side_row(g, e):
        if 0 <= e < rows:
            return beside_ref[g, pl.ds(e, 1), :]
        ref, row = (above_ref, e + MODEL_STEPS) if e < 0 else (below_ref, e - rows)
        flat = ref.reshape(ref.shape[0] * SUB, LANES)
        return flat[pl.ds((levels + g) * MODEL_STEPS + row, 1), :]

    return side_row


def first_model_body(wx_ref, wy_ref, x_ref, beside_ref, above_ref, below_ref, grad_ref):
    levels, rows, cols = x_ref.shape
    side_row = side_rows(levels, rows, beside_ref, above_ref, below_ref)
    sweep(x_ref, model_parts(wx_ref, wy_ref, x_ref, above_ref, below_ref, side_row, grad_ref))


def inner_model_body(wx_ref, wy_ref, x_ref, beside_ref, grad_ref, kept_ref):
    levels, rows, cols = x_ref.shape
    side_row = side_rows(levels, rows, beside_ref, None, None)
    inner_sweep(x_ref, model_parts(wx_ref, wy_ref, x_ref, None, None, side_row, grad_ref), kept_ref)


def outer_model_body(wx_ref, wy_ref, x_ref, beside_ref, above_thin_ref, below_thin_ref, inner_ref, kept_ref, *refs):
    *others, grad_ref, above_ref, below_ref = refs
    levels, rows, cols = x_ref.shape
    above_ref[...] = above_thin_ref[...].astype(F32).reshape(above_ref.shape)
    below_ref[...] = below_thin_ref[...].astype(F32).reshape(below_ref.shape)
    side_row = side_rows(levels, rows, beside_ref, above_ref, below_ref)
    outer_sweep(x_ref, model_parts(wx_ref, wy_ref, x_ref, above_ref, below_ref, side_row, grad_ref), kept_ref)
    row = sub_iota((rows, cols))
    inside = (row >= MODEL_STEPS) & (row < rows - MODEL_STEPS)
    project_levels(lambda level: jnp.where(inside, inner_ref[level], grad_ref[level]), levels, list(range(len(others) - 2)), *others)


def near_turns(parts):
    return [0, 1, parts - 1]


def first_project_body(parts, grad_ref, *refs):
    project_levels(lambda level: grad_ref[level], grad_ref.shape[0], near_turns(parts), *refs)


def last_project_body(parts, grad_ref, wide_in_ref, thin_in_ref, *refs):
    *member_refs, wide_ref, thin_ref = refs
    own = member_refs[0].shape[0]
    for r in near_turns(parts):
        for m in range(own):
            at = neighbor_of(-r) * own + m
            wide_ref[at] = wide_in_ref[at]
            thin_ref[at] = thin_in_ref[at]
    project_levels(lambda level: grad_ref[level], grad_ref.shape[0], list(range(2, parts - 1)), *refs)


def project_levels(grad, levels, turns, *refs):
    *member_refs, wide_ref, thin_ref = refs
    own, _, rows, cols = member_refs[0].shape
    count = len(member_refs) * own

    def step(q, carry):
        carry = list(carry)
        for u in range(2):
            g = grad(2 * q + u)
            for m in range(count):
                carry[m] = carry[m] + member_refs[m // own][m % own, 2 * q + u].astype(F32) * g
        return tuple(carry)

    total = lax.fori_loop(0, levels // 2, step, (jnp.zeros((rows, cols), F32),) * count)
    for m in range(count):
        at = neighbor_of(-turns[m // own]) * own + m % own
        wide_ref[at] = total[m]
        thin_ref[at] = total[m].astype(BF16)


def taper(offset):
    k = offset.astype(F32)
    w = (1.0 - (k / 17.0) * (k / 17.0)) * (1.0 / TAPER_TOTAL)
    return jnp.where(jnp.abs(offset) <= REACH, w, 0.0)


def halves(x):
    high = x.astype(BF16)
    return high, (x - high.astype(F32)).astype(BF16)


def sharp_dot(a, b):
    ah, al = halves(a)
    bh, bl = halves(b)
    dot = functools.partial(jnp.dot, preferred_element_type=F32)
    return dot(ah, bh) + dot(al, bh) + dot(ah, bl)


def columns_body(left_ref, mid_ref, right_ref, wide_ref, thin_ref):
    count, rows, cols = mid_ref.shape
    wide = jnp.concatenate(
        [r[...].astype(F32).reshape(count * rows, cols) for r in (left_ref, mid_ref, right_ref)], axis=1
    )
    shape = (3 * cols, wide_ref.shape[0] // count * cols)
    lane = lane_iota(shape)
    beside = lane % MODEL_STEPS + jnp.where((lane // (SUB * MODEL_STEPS)) % 2 == 0, -MODEL_STEPS, cols)
    target = jnp.where(lane < cols, lane, beside)
    out = sharp_dot(wide, taper(sub_iota(shape) - cols - target))
    for i in range(shape[1] // cols):
        part = out[:, i * cols : (i + 1) * cols].reshape(count, rows, cols)
        wide_ref[i * count : (i + 1) * count] = part
        thin_ref[i * count : (i + 1) * count] = part.astype(BF16)


def smooth_rows(above_ref, mid_ref, below_ref):
    count, rows, cols = mid_ref.shape
    tall = jnp.concatenate(
        [
            jnp.concatenate([above_ref[m].astype(F32), mid_ref[m], below_ref[m].astype(F32)], axis=0)
            for m in range(count)
        ],
        axis=1,
    )
    shape = (rows, 3 * rows)
    out = sharp_dot(taper(lane_iota(shape) - sub_iota(shape) - rows), tall)
    return [out[:, m * cols : (m + 1) * cols] for m in range(count)]


def increments(member_refs, local_ref, start, levels, emit):
    own = member_refs[0].shape[0]
    count = len(member_refs) * own
    local = [local_ref[neighbor_of(-(m // own)) * own + m % own] for m in range(count)]

    def step(q, carry):
        for u in range(2):
            level = 2 * q + u
            total = member_refs[0][0, level].astype(F32) * local[0]
            for m in range(1, count):
                total = total + member_refs[m // own][m % own, level].astype(F32) * local[m]
            emit(level, total)
        return carry

    lax.fori_loop(start // 2, (start + levels) // 2, step, 0)


def update_body(parts, residual_ref, around_ref, above_ref, mid_ref, below_ref, *refs):
    member_refs, side_refs = refs[:parts], refs[parts : parts + 2] + refs[2:parts]
    analysis_ref, out_ref, beside_ref, top_ref, bottom_ref, local_ref, top_wide_ref, bottom_wide_ref = refs[parts + 2 :]
    levels, rows, cols = residual_ref.shape
    own = member_refs[0].shape[0]
    count = parts * own
    for m, value in enumerate(smooth_rows(above_ref, mid_ref, below_ref)):
        local_ref[m] = value

    def emit(level, value):
        analysis_ref[level] = value
        out_ref[level] = residual_ref[level] - RELAX * value

    increments(member_refs, local_ref, 0, levels, emit)
    for g in range(levels // GROUP):
        total = jnp.zeros((rows, LANES), F32)
        for m in range(count):
            ref = side_refs[m // own]
            at = neighbor_of(-(m // own)) * own + m % own
            member = ref[m % own, ref.shape[1] - levels // GROUP + g]
            total = total + member.astype(F32) * local_ref[count + at]
        beside_ref[g] = around_ref[g] - RELAX * total
    pack_rows(out_ref, 0, top_wide_ref, bottom_wide_ref)
    pack_rows(beside_ref, levels // 2, top_wide_ref, bottom_wide_ref)
    top_ref[...] = top_wide_ref[...].reshape(top_ref.shape).astype(BF16)
    bottom_ref[...] = bottom_wide_ref[...].reshape(bottom_ref.shape).astype(BF16)


def final_body(parts, residual_ref, before_ref, above_ref, mid_ref, below_ref, *refs):
    member_refs = refs[:parts]
    analysis_out_ref, residual_out_ref, local_ref, analysis_ref, out_ref, sems = refs[parts:]
    levels = residual_ref.shape[0]
    for m, value in enumerate(smooth_rows(above_ref, mid_ref, below_ref)):
        local_ref[m] = value

    def emit(level, value):
        analysis_ref[level] = before_ref[level] + value
        out_ref[level] = residual_ref[level] - RELAX * value

    pieces = sems.shape[1]
    count = levels // pieces
    copies = []
    for i in range(pieces):
        increments(member_refs, local_ref, i * count, count, emit)
        at = pl.ds(i * count, count)
        for j, (source, target) in enumerate(((analysis_ref, analysis_out_ref), (out_ref, residual_out_ref))):
            copies.append(pltpu.make_async_copy(source.at[at], target.at[at], sems.at[j, i]))
            copies[-1].start()
    for copy in copies:
        copy.wait()


def per_device(residual_in, members, wind_x, wind_y):
    levels, rows, cols = residual_in.shape
    parts = lax.axis_size("member")
    count = members.shape[0] * parts
    groups = levels // GROUP

    def shape(*dims, kind=F32):
        return jax.ShapeDtypeStruct(dims, kind)

    def both(*dims):
        return shape(*dims), shape(*dims, kind=BF16)

    def turned(x, step):
        return lax.ppermute(x, "member", [(i, (i + step) % parts) for i in range(parts)])

    def smoothed(wide, thin, planes):
        wide, thin = call(
            columns_body, both(planes, rows, cols), shift(thin, "member", 1), wide, shift(thin, "member", -1)
        )
        return shift(thin, "tile", 1), wide, shift(thin, "tile", -1)

    like = shape(levels, rows, cols)
    halo = shape((levels + groups) // 2, SUB, LANES)
    thin_halo = shape((levels + groups) // 4, 2 * SUB, LANES, kind=BF16)
    wide_halo = [pltpu.VMEM(halo.shape, F32)] * 2
    packed = shape(groups, rows, LANES)
    wind_x, wind_y = (jnp.broadcast_to(w[:, None], (levels, LANES)) for w in (wind_x, wind_y))

    mine, early = split_columns(members, parts)
    early, residual_in = lax.optimization_barrier((early, residual_in))
    early = turned(early, 1)
    first, last = call(columns_edge_body, (packed, packed), residual_in)
    left, right = shift(last, "member", 1), shift(first, "member", -1)
    members, first = lax.optimization_barrier((members, first))
    (final,) = side_columns(members, parts, [parts - 1])
    final, members = lax.optimization_barrier((final, members))
    final = turned(final, parts - 1)
    later = side_columns(members, parts, list(range(parts - 1)))
    later, left, right = lax.optimization_barrier((later, left, right))
    blocks = [mine, early] + [turned(x, r) for r, x in enumerate(later[2:], 2)] + [final]
    sides = [later[0], turned(later[1], 1)]
    around, top, bottom = call(rows_body, (packed, halo, halo), residual_in, left, right)
    above, below = shift(bottom, "tile", 1), shift(top, "tile", -1)
    grad = call(
        first_model_body, like,
        wind_x, wind_y, residual_in, around, above, below, in_specs=[VMEM] * 6,
    )
    grad, sides = lax.optimization_barrier((grad, sides))
    near = [blocks[r] for r in near_turns(parts)]
    wide, thin = call(functools.partial(first_project_body, parts), both(count, rows, cols), grad, *near)
    wide, thin = call(
        functools.partial(last_project_body, parts), both(count, rows, cols), grad, wide, thin, *blocks[2:-1]
    )

    analysis, residual, beside, top, bottom = call(
        functools.partial(update_body, parts), (like, like, packed, thin_halo, thin_halo),
        residual_in, around, *smoothed(wide, thin, 2 * count), *blocks, *sides,
        in_specs=[VMEM] * (7 + parts),
        scratch=[pltpu.VMEM((2 * count, rows, cols), F32)] + wide_halo,
    )
    above, below = shift(bottom, "tile", 1), shift(top, "tile", -1)
    kept = shape(groups, len(kept_rows(rows)), 3, SUB, LANES)
    inner, kept = call(inner_model_body, (like, kept), wind_x, wind_y, residual, beside)
    wide, thin = call(
        outer_model_body, both(count, rows, cols),
        wind_x, wind_y, residual, beside, above, below, inner, kept, *blocks,
        scratch=[pltpu.VMEM((levels, rows, cols), F32)] + wide_halo,
    )
    return pl.pallas_call(
        functools.partial(final_body, parts),
        out_shape=(like, like),
        in_specs=[VMEM] * (5 + parts),
        out_specs=(pl.BlockSpec(memory_space=pl.ANY),) * 2,
        scratch_shapes=[
            pltpu.VMEM((count, rows, cols), F32),
            pltpu.VMEM(like.shape, F32),
            pltpu.VMEM(like.shape, F32),
            pltpu.SemaphoreType.DMA((2, 4)),
        ],
        compiler_params=PARAMS,
    )(residual, analysis, *smoothed(wide, thin, count), *blocks)


def solution(mesh):
    return jax.shard_map(
        per_device,
        mesh=mesh,
        in_specs=(P(None, "tile", "member"), P("member", None, "tile", None), P(), P()),
        out_specs=(P(None, "tile", "member"), P(None, "tile", "member")),
        check_vma=False,
    )
```
